512 devices in a mesh: panel: 2 (over x_hi), lat: 16 (over z, core), lon: 16 (over x_lo, y).
Axes of the slice: x: 4 (x_hi: 2, x_lo: 2; x = x_hi * 2 + x_lo), y: 8, z: 8, core: 2. Of those that a mesh axis runs over, the one named last changes fastest.
Arguments:
- state: float32 [2, 8, 4, 256, 768], P('panel', None, None, 'lat', 'lon'), as said below
- donor_cell: int32 [2, 16, 16, 33], P('panel', 'lat', 'lon'), may hold values from 0 to 767, as said below
- donor_weights: float32 [2, 16, 16, 4, 33], P('panel', 'lat', 'lon'), as said below
- donor_turn: float32 [2, 16, 16, 33], P('panel', 'lat', 'lon'), may hold values from -3.140625 to 3.140625
- border_source: int32 [2, 8256], P('panel'), may hold values from 0 to 8446, as said below
- diffusion: float32 [2], replicated, may hold values from 0.01 to 0.1
Outputs:
- accumulated: float32 [2, 8, 4, 256, 768], P('panel', None, None, 'lat', 'lon')
- section_three: float32 [2, 8, 4, 256, 768], P('panel', None, None, 'lat', 'lon')
The draws below stay inside these ranges and needn't reach their ends.
Inputs may be any that keep to these rules, and one draw needn't show every extreme that they name: `state`: eight fields in order: log density, velocity (r, theta, phi), magnetic field (r, theta, phi), pressure; pressure is positive. `donor_cell`: c names the cell at row c // 48, column c % 48 of the block; the cells one row and one column further lie inside the panel. `donor_weights`: the four weights of a slot are nonnegative and sum to one. `border_source`: entry n of panel p names slot s % 33 of block s // 33 of the other panel, blocks numbered colatitude-major; no slot is named twice; each block serves 33 or 32 ghost cells, from its first slots.
All inputs are finite; a program needn't handle non-finite values.
Results may differ from the reference program's by a relative error of at most 0.00002.
Values sent between devices are 32-bit elements; how exact they have to be, the bound alone decides.
No kernel may reach another device: no remote copies, remote signals or barrier semaphores. Data moves between devices by JAX's collectives and lax.ppermute only.
A program may use at most 64 MiB of HBM per device.

```python
import math
import jax
import jax.numpy as jnp

LEV = 4
CT = 16
CP = 48
NT = 256
NP = 768
NB = 8256
SLOT = 33
N_LAT = 16
N_LON = 16


def draw_state(key, part):
    key = jax.random.fold_in(key, 11)
    keys = jax.random.split(key, 4)
    scalar_shape = (2, 1, LEV, NT, NP)
    vector_shape = (2, 3, LEV, NT, NP)
    log_rho = jnp.clip(0.2 * jax.random.normal(keys[0], scalar_shape, jnp.float32), -0.5, 0.5)
    velocity = jnp.clip(jax.random.normal(keys[1], vector_shape, jnp.float32), -4.0, 4.0)
    magnetic = jnp.clip(jax.random.normal(keys[2], vector_shape, jnp.float32), -4.0, 4.0)
    pressure = jax.random.uniform(keys[3], scalar_shape, jnp.float32, 0.5, 2.0)
    return jnp.concatenate([log_rho, velocity, magnetic, pressure], axis=1)


def draw_donor_cell(key, part):
    key = jax.random.fold_in(key, 23)
    row_key, col_key = jax.random.split(key)
    lat_ids = jnp.arange(N_LAT, dtype=jnp.int32)[None, :, None, None]
    lon_ids = jnp.arange(N_LON, dtype=jnp.int32)[None, None, :, None]
    row_top = CT - (lat_ids == N_LAT - 1).astype(jnp.int32)
    col_top = CP - (lon_ids == N_LON - 1).astype(jnp.int32)
    shape = (2, N_LAT, N_LON, SLOT)
    row_pick = jax.random.randint(row_key, shape, 0, row_top, dtype=jnp.int32)
    col_pick = jax.random.randint(col_key, shape, 0, col_top, dtype=jnp.int32)
    cells = row_pick * CP + col_pick
    cells = cells.at[:, 0, 0, 0].set(CT * CP - 1).at[:, 0, 0, 1].set(0)
    return cells.astype(jnp.int32)


def draw_donor_weights(key, part):
    key = jax.random.fold_in(key, 29)
    first_key, second_key = jax.random.split(key)
    shape = (2, N_LAT, N_LON, SLOT)
    along_row = jax.random.uniform(first_key, shape, jnp.float32)
    along_col = jax.random.uniform(second_key, shape, jnp.float32)
    return jnp.stack([(1.0 - along_row) * (1.0 - along_col), (1.0 - along_row) * along_col, along_row * (1.0 - along_col), along_row * along_col], axis=3)


def draw_border_source(key, part):
    key = jax.random.fold_in(key, 37)
    first_key, second_key = jax.random.split(key)
    blocks = N_LAT * N_LON
    ranks = jnp.stack([jax.random.permutation(first_key, NB), jax.random.permutation(second_key, NB)])
    return (ranks % blocks * SLOT + ranks // blocks).astype(jnp.int32)


def setup_inputs(seed: int = 0) -> dict:
    key_list = jax.random.split(jax.random.key(seed), 7)
    state = draw_state(jax.random.fold_in(key_list[6], 71), 0)
    donor_cell = draw_donor_cell(jax.random.fold_in(key_list[6], 71), 0)
    donor_weights = draw_donor_weights(jax.random.fold_in(key_list[6], 71), 0)
    donor_turn = jnp.clip(jax.random.uniform(key_list[3], (2, N_LAT, N_LON, SLOT), jnp.float32, -3.140625, 3.140625), -3.140625, 3.140625)
    border_source = draw_border_source(jax.random.fold_in(key_list[6], 71), 0)
    diffusion = jnp.clip(jnp.exp(jax.random.uniform(key_list[5], (2,), jnp.float32, math.log(0.01), math.log(0.1))), 0.01, 0.1)
    return dict(state=state, donor_cell=donor_cell, donor_weights=donor_weights, donor_turn=donor_turn, border_source=border_source, diffusion=diffusion)


GAMMA = 5.0 / 3.0
RADIAL_STEP = 0.65 / 32.0


def radii(levels):
    level_ids = jnp.arange(levels, dtype=jnp.float32)
    offset = 16 - levels // 2
    return 0.35 + 0.65 * (level_ids + offset + 0.5) / 32.0


def along_colatitude(field, dtheta):
    return (field[..., :-4, 2:-2] - 8.0 * field[..., 1:-3, 2:-2] + 8.0 * field[..., 3:-1, 2:-2] - field[..., 4:, 2:-2]) / (12.0 * dtheta)


def along_longitude(field, dlongitude):
    return (field[..., 2:-2, :-4] - 8.0 * field[..., 2:-2, 1:-3] + 8.0 * field[..., 2:-2, 3:-1] - field[..., 2:-2, 4:]) / (12.0 * dlongitude)


def along_radius(field):
    inner_part = (field[2:] - field[:-2]) / (2.0 * RADIAL_STEP)
    first_end = (field[1:2] - field[0:1]) / RADIAL_STEP
    last_end = (field[-1:] - field[-2:-1]) / RADIAL_STEP
    return jnp.concatenate([first_end, inner_part, last_end], axis=0)[:, 2:-2, 2:-2]


def shrink(field):
    return field[..., 2:-2, 2:-2]


def curl(vector, band):
    radius, sine_in, sine_out, dtheta, dlongitude = band
    part_r, part_t, part_p = vector
    curl_r = (along_colatitude(sine_in * part_p, dtheta) - along_longitude(part_t, dlongitude)) / (radius * sine_out)
    curl_t = (along_longitude(part_r, dlongitude) / sine_out - along_radius(radius * part_p)) / radius
    curl_p = (along_radius(radius * part_t) - along_colatitude(part_r, dtheta)) / radius
    return (curl_r, curl_t, curl_p)


def divergence(vector, band):
    radius, sine_in, sine_out, dtheta, dlongitude = band
    part_r, part_t, part_p = vector
    radial = along_radius(radius * radius * part_r) / (radius * radius)
    return radial + (along_colatitude(sine_in * part_t, dtheta) + along_longitude(part_p, dlongitude)) / (radius * sine_out)


def gradient(field, band):
    radius, sine_in, sine_out, dtheta, dlongitude = band
    return (along_radius(field), along_colatitude(field, dtheta) / radius, along_longitude(field, dlongitude) / (radius * sine_out))


def cross(left, right):
    return (left[1] * right[2] - left[2] * right[1], left[2] * right[0] - left[0] * right[2], left[0] * right[1] - left[1] * right[0])


def advect(velocity, grad_field):
    return velocity[0] * grad_field[0] + velocity[1] * grad_field[1] + velocity[2] * grad_field[2]


def tendency(extended, colatitude, longitude, panel_flag, diffusion, dtheta, dlongitude, time_step):
    levels = extended.shape[1]
    radius = radii(levels)[:, None, None]
    sine_four = jnp.sin(colatitude)[:, None]
    sine_two = sine_four[2:-2]
    sine_zero = sine_four[4:-4]
    outer_band = (radius, sine_four, sine_two, dtheta, dlongitude)
    inner_band = (radius, sine_two, sine_zero, dtheta, dlongitude)
    finest = min(dtheta, dlongitude)
    viscosity = diffusion[0] * (finest * finest / time_step)
    resistivity = diffusion[1] * (finest * finest / time_step)
    rotation = 0.25 / time_step
    log_rho, vel_r, vel_t, vel_p, mag_r, mag_t, mag_p, pressure = [extended[which] for which in range(8)]
    vorticity = curl((vel_r, vel_t, vel_p), outer_band)
    current = curl((mag_r, mag_t, mag_p), outer_band)
    div_two = divergence((vel_r, vel_t, vel_p), outer_band)
    vel_two = [shrink(piece) for piece in (vel_r, vel_t, vel_p)]
    mag_two = [shrink(piece) for piece in (mag_r, mag_t, mag_p)]
    induced = cross(vel_two, mag_two)
    electric = tuple(induced[which] - resistivity * current[which] for which in range(3))
    kinetic = 0.5 * (vel_two[0] * vel_two[0] + vel_two[1] * vel_two[1] + vel_two[2] * vel_two[2])
    grad_kin = gradient(kinetic, inner_band)
    grad_pres = gradient(shrink(pressure), inner_band)
    grad_rho = gradient(shrink(log_rho), inner_band)
    curl_vort = curl(vorticity, inner_band)
    curl_elec = curl(electric, inner_band)
    velocity = [shrink(piece) for piece in vel_two]
    magnetic = [shrink(piece) for piece in mag_two]
    vort_zero = [shrink(piece) for piece in vorticity]
    curr_zero = [shrink(piece) for piece in current]
    div_vel = shrink(div_two)
    inv_rho = jnp.exp(-shrink(shrink(log_rho)))
    pres_zero = shrink(shrink(pressure))
    colat_zero = colatitude[4:-4][:, None]
    longi_zero = longitude[4:-4][None, :]
    omega_r = rotation * ((1.0 - panel_flag) * jnp.cos(colat_zero) + panel_flag * jnp.sin(colat_zero) * jnp.sin(longi_zero))
    omega_t = rotation * ((1.0 - panel_flag) * (-jnp.sin(colat_zero)) + panel_flag * jnp.cos(colat_zero) * jnp.sin(longi_zero))
    omega_p = rotation * panel_flag * jnp.cos(longi_zero)
    lamb_term = cross(velocity, vort_zero)
    lorentz = cross(curr_zero, magnetic)
    spin_term = cross((omega_r, omega_t, omega_p), velocity)
    vel_rates = [lamb_term[which] - grad_kin[which] - inv_rho * grad_pres[which] + inv_rho * lorentz[which]
                 - 2.0 * spin_term[which] - viscosity * curl_vort[which] for which in range(3)]
    rho_rate = -advect(velocity, grad_rho) - div_vel
    pres_rate = -advect(velocity, grad_pres) - GAMMA * pres_zero * div_vel
    return jnp.stack([rho_rate] + vel_rates + list(curl_elec) + [pres_rate])


def blend(flat, base, stride, weights, turn):
    corner_aa = jnp.take(flat, base, axis=2, mode="clip")
    corner_ab = jnp.take(flat, base + 1, axis=2, mode="clip")
    corner_ba = jnp.take(flat, base + stride, axis=2, mode="clip")
    corner_bb = jnp.take(flat, base + stride + 1, axis=2, mode="clip")
    mixed = corner_aa * weights[0] + corner_ab * weights[1] + corner_ba * weights[2] + corner_bb * weights[3]
    cosine = jnp.cos(turn)
    sine_turn = jnp.sin(turn)
    vel_t = cosine * mixed[2] + sine_turn * mixed[3]
    vel_p = -sine_turn * mixed[2] + cosine * mixed[3]
    mag_t = cosine * mixed[5] + sine_turn * mixed[6]
    mag_p = -sine_turn * mixed[5] + cosine * mixed[6]
    return jnp.stack([mixed[0], mixed[1], vel_t, vel_p, mixed[4], mag_t, mag_p, mixed[7]])


def border_index(row_ids, col_ids, panel_rows, panel_cols):
    width = panel_cols + 8
    top_band = (row_ids + 4) * width + col_ids + 4
    bottom_band = 4 * width + (row_ids - panel_rows) * width + col_ids + 4
    left_band = 8 * width + row_ids * 8 + col_ids + 4
    right_band = 8 * width + row_ids * 8 + 4 + col_ids - panel_cols
    border_at = jnp.where(row_ids < 0, top_band, jnp.where(row_ids >= panel_rows, bottom_band,
                          jnp.where(col_ids < 0, left_band, right_band)))
    outside = (row_ids < 0) | (row_ids >= panel_rows) | (col_ids < 0) | (col_ids >= panel_cols)
    return jnp.where(outside, border_at, 0).astype(jnp.int32), outside


def angles(row_ids, col_ids, dtheta, dlongitude):
    colatitude = 0.25 * math.pi + (row_ids.astype(jnp.float32) + 0.5) * dtheta
    longitude = -0.75 * math.pi + (col_ids.astype(jnp.float32) + 0.5) * dlongitude
    return colatitude, longitude


def donor_values(panel_state, donor_at, weights, turn, block_rows, block_cols, panel_cols):
    lat_blocks, lon_blocks, slots = donor_at.shape
    lat_ids = jnp.arange(lat_blocks, dtype=jnp.int32)[:, None, None]
    lon_ids = jnp.arange(lon_blocks, dtype=jnp.int32)[None, :, None]
    row_at = lat_ids * block_rows + donor_at // block_cols
    col_at = lon_ids * block_cols + donor_at % block_cols
    base = (row_at * panel_cols + col_at).reshape(-1).astype(jnp.int32)
    flat = panel_state.reshape(panel_state.shape[0], panel_state.shape[1], -1)
    weight_rows = jnp.moveaxis(weights, 2, 0).reshape(4, -1)
    return blend(flat, base, panel_cols, weight_rows, turn.reshape(-1))


def reference(state, donor_cell, donor_weights, donor_turn, border_source, diffusion):
    panel_rows = CT * N_LAT
    panel_cols = CP * N_LON
    dtheta = 0.5 * math.pi / panel_rows
    dlongitude = 1.5 * math.pi / panel_cols
    time_step = 0.1 * min(dtheta, dlongitude)
    row_ids = jnp.arange(-4, panel_rows + 4, dtype=jnp.int32)
    col_ids = jnp.arange(-4, panel_cols + 4, dtype=jnp.int32)
    colatitude, longitude = angles(row_ids, col_ids, dtheta, dlongitude)
    border_at, outside = border_index(row_ids[:, None], col_ids[None, :], panel_rows, panel_cols)
    flat_border = border_at.reshape(-1)

    def rates(current_state):
        donors = [donor_values(current_state[donor_panel], donor_cell[donor_panel], donor_weights[donor_panel],
                               donor_turn[donor_panel], CT, CP, panel_cols) for donor_panel in range(2)]
        results = []
        for panel_id in range(2):
            padded = jnp.pad(current_state[panel_id], ((0, 0), (0, 0), (4, 4), (4, 4)))
            sources = jnp.take(border_source[panel_id], flat_border, mode="clip")
            fill = jnp.take(donors[1 - panel_id], sources, axis=2, mode="clip").reshape(padded.shape)
            extended = jnp.where(outside, fill, padded)
            results.append(tendency(extended, colatitude, longitude, float(panel_id), diffusion,
                                    dtheta, dlongitude, time_step))
        return jnp.stack(results)

    first = rates(state)
    second = rates(state + (0.5 * time_step) * first)
    accumulated = state + (time_step / 6.0) * (first + 2.0 * second)
    section_three = state + (0.5 * time_step) * second
    return accumulated, section_three
```

```python
import math

import jax
import jax.numpy as jnp
from jax import lax
from jax.sharding import PartitionSpec as P

GAMMA = 5.0 / 3.0
RADIAL_STEP = 0.65 / 32.0
HIGHEST = lax.Precision.HIGHEST

def radii(levels):
    level_ids = jnp.arange(levels, dtype=jnp.float32)
    offset = 16 - levels // 2
    return 0.35 + 0.65 * (level_ids + offset + 0.5) / 32.0


def along_colatitude(field, dtheta):
    return (
        field[..., :-4, 2:-2]
        - 8.0 * field[..., 1:-3, 2:-2]
        + 8.0 * field[..., 3:-1, 2:-2]
        - field[..., 4:, 2:-2]
    ) / (12.0 * dtheta)


def along_longitude(field, dlongitude):
    return (
        field[..., 2:-2, :-4]
        - 8.0 * field[..., 2:-2, 1:-3]
        + 8.0 * field[..., 2:-2, 3:-1]
        - field[..., 2:-2, 4:]
    ) / (12.0 * dlongitude)


def along_radius(field):
    inner_part = (field[2:] - field[:-2]) / (2.0 * RADIAL_STEP)
    first_end = (field[1:2] - field[0:1]) / RADIAL_STEP
    last_end = (field[-1:] - field[-2:-1]) / RADIAL_STEP
    return jnp.concatenate([first_end, inner_part, last_end], axis=0)[:, 2:-2, 2:-2]


def shrink(field):
    return field[..., 2:-2, 2:-2]


def curl(vector, band):
    radius, sine_in, sine_out, dtheta, dlongitude = band
    part_r, part_t, part_p = vector
    curl_r = (along_colatitude(sine_in * part_p, dtheta) - along_longitude(part_t, dlongitude)) / (
        radius * sine_out
    )
    curl_t = (
        along_longitude(part_r, dlongitude) / sine_out - along_radius(radius * part_p)
    ) / radius
    curl_p = (along_radius(radius * part_t) - along_colatitude(part_r, dtheta)) / radius
    return (curl_r, curl_t, curl_p)


def divergence(vector, band):
    radius, sine_in, sine_out, dtheta, dlongitude = band
    part_r, part_t, part_p = vector
    radial = along_radius(radius * radius * part_r) / (radius * radius)
    return radial + (
        along_colatitude(sine_in * part_t, dtheta) + along_longitude(part_p, dlongitude)
    ) / (radius * sine_out)


def gradient(field, band):
    radius, sine_in, sine_out, dtheta, dlongitude = band
    return (
        along_radius(field),
        along_colatitude(field, dtheta) / radius,
        along_longitude(field, dlongitude) / (radius * sine_out),
    )


def cross(left, right):
    return (
        left[1] * right[2] - left[2] * right[1],
        left[2] * right[0] - left[0] * right[2],
        left[0] * right[1] - left[1] * right[0],
    )


def advect(velocity, grad_field):
    return velocity[0] * grad_field[0] + velocity[1] * grad_field[1] + velocity[2] * grad_field[2]


def tendency(extended, colatitude, longitude, panel_flag, diffusion, dtheta, dlongitude, time_step):
    levels = extended.shape[1]
    radius = radii(levels)[:, None, None]
    sine_four = jnp.sin(colatitude)[:, None]
    sine_two = sine_four[2:-2]
    sine_zero = sine_four[4:-4]
    outer_band = (radius, sine_four, sine_two, dtheta, dlongitude)
    inner_band = (radius, sine_two, sine_zero, dtheta, dlongitude)
    finest = min(dtheta, dlongitude)
    viscosity = diffusion[0] * (finest * finest / time_step)
    resistivity = diffusion[1] * (finest * finest / time_step)
    rotation = 0.25 / time_step
    log_rho, vel_r, vel_t, vel_p, mag_r, mag_t, mag_p, pressure = [
        extended[which] for which in range(8)
    ]
    vorticity = curl((vel_r, vel_t, vel_p), outer_band)
    current = curl((mag_r, mag_t, mag_p), outer_band)
    div_two = divergence((vel_r, vel_t, vel_p), outer_band)
    vel_two = [shrink(piece) for piece in (vel_r, vel_t, vel_p)]
    mag_two = [shrink(piece) for piece in (mag_r, mag_t, mag_p)]
    induced = cross(vel_two, mag_two)
    electric = tuple((induced[which] - resistivity * current[which] for which in range(3)))
    kinetic = 0.5 * (vel_two[0] * vel_two[0] + vel_two[1] * vel_two[1] + vel_two[2] * vel_two[2])
    grad_kin = gradient(kinetic, inner_band)
    grad_pres = gradient(shrink(pressure), inner_band)
    grad_rho = gradient(shrink(log_rho), inner_band)
    curl_vort = curl(vorticity, inner_band)
    curl_elec = curl(electric, inner_band)
    velocity = [shrink(piece) for piece in vel_two]
    magnetic = [shrink(piece) for piece in mag_two]
    vort_zero = [shrink(piece) for piece in vorticity]
    curr_zero = [shrink(piece) for piece in current]
    div_vel = shrink(div_two)
    inv_rho = jnp.exp(-shrink(shrink(log_rho)))
    pres_zero = shrink(shrink(pressure))
    colat_zero = colatitude[4:-4][:, None]
    longi_zero = longitude[4:-4][None, :]
    omega_r = rotation * (
        (1.0 - panel_flag) * jnp.cos(colat_zero)
        + panel_flag * jnp.sin(colat_zero) * jnp.sin(longi_zero)
    )
    omega_t = rotation * (
        (1.0 - panel_flag) * -jnp.sin(colat_zero)
        + panel_flag * jnp.cos(colat_zero) * jnp.sin(longi_zero)
    )
    omega_p = rotation * panel_flag * jnp.cos(longi_zero)
    lamb_term = cross(velocity, vort_zero)
    lorentz = cross(curr_zero, magnetic)
    spin_term = cross((omega_r, omega_t, omega_p), velocity)
    vel_rates = [
        lamb_term[which]
        - grad_kin[which]
        - inv_rho * grad_pres[which]
        + inv_rho * lorentz[which]
        - 2.0 * spin_term[which]
        - viscosity * curl_vort[which]
        for which in range(3)
    ]
    rho_rate = -advect(velocity, grad_rho) - div_vel
    pres_rate = -advect(velocity, grad_pres) - GAMMA * pres_zero * div_vel
    return jnp.stack([rho_rate] + vel_rates + list(curl_elec) + [pres_rate])


def angles(row_ids, col_ids, dtheta, dlongitude):
    colatitude = 0.25 * math.pi + (row_ids.astype(jnp.float32) + 0.5) * dtheta
    longitude = -0.75 * math.pi + (col_ids.astype(jnp.float32) + 0.5) * dlongitude
    return (colatitude, longitude)


def own_shift(value, axes, sizes, moves):
    pairs = []
    total = math.prod(sizes)
    for source in range(total):
        rest = source
        place = []
        for size in reversed(sizes):
            place.append(rest % size)
            rest //= size
        place = place[::-1]
        goal = [at + move for at, move in zip(place, moves)]
        if all(0 <= at < size for at, size in zip(goal, sizes)):
            target = 0
            for at, size in zip(goal, sizes):
                target = target * size + at
            pairs.append((source, target))
    return lax.ppermute(value, axes, pairs)


def donors(cells, donor_at, weights, turn, block_cols):
    rows = cells.shape[2]
    cols = cells.shape[3]
    row_at = donor_at // block_cols
    col_at = donor_at % block_cols
    col_ids = jnp.arange(cols, dtype=jnp.int32)[:, None]
    row_ids = jnp.arange(rows, dtype=jnp.int32)[:, None]
    pick = jnp.concatenate([col_ids == col_at, col_ids == col_at + 1], axis=1).astype(jnp.float32)
    here = row_ids == row_at
    below = row_ids == row_at + 1
    mix = jnp.concatenate(
        [
            jnp.where(here, weights[0], 0.0) + jnp.where(below, weights[2], 0.0),
            jnp.where(here, weights[1], 0.0) + jnp.where(below, weights[3], 0.0),
        ],
        axis=1,
    )
    chosen = jnp.einsum("flij,jk->flik", cells, pick, precision=HIGHEST)
    both = jnp.sum(chosen * mix, axis=2)
    slots = donor_at.shape[0]
    mixed = both[..., :slots] + both[..., slots:]
    cosine = jnp.cos(turn)
    sine_turn = jnp.sin(turn)
    vel_t = cosine * mixed[2] + sine_turn * mixed[3]
    vel_p = -sine_turn * mixed[2] + cosine * mixed[3]
    mag_t = cosine * mixed[5] + sine_turn * mixed[6]
    mag_p = -sine_turn * mixed[5] + cosine * mixed[6]
    out = jnp.stack([mixed[0], mixed[1], vel_t, vel_p, mixed[4], mag_t, mag_p, mixed[7]])
    return out.reshape(-1, slots)


def shards(state, donor_cell, donor_weights, donor_turn, border_source, diffusion):
    fields = state[0]
    field_count, levels, block_rows, block_cols = fields.shape
    planes = field_count * levels
    lats = lax.axis_size("lat")
    lons = lax.axis_size("lon")
    panels = lax.axis_size("panel")
    slots = donor_cell.shape[-1]
    panel_rows = block_rows * lats
    panel_cols = block_cols * lons
    dtheta = 0.5 * math.pi / panel_rows
    dlongitude = 1.5 * math.pi / panel_cols
    time_step = 0.1 * min(dtheta, dlongitude)
    panel = lax.axis_index("panel")
    lat = lax.axis_index("lat")
    lon = lax.axis_index("lon")
    row_ids = lat * block_rows + jnp.arange(-8, block_rows + 8, dtype=jnp.int32)
    col_ids = lon * block_cols + jnp.arange(-8, block_cols + 8, dtype=jnp.int32)
    colatitude, longitude = angles(row_ids, col_ids, dtheta, dlongitude)
    panel_flag = panel.astype(jnp.float32)
    donor_at = donor_cell[0, 0, 0]
    slot_weights = donor_weights[0, 0, 0]
    slot_turn = donor_turn[0, 0, 0]

    both = (("lat", "lon"), (lats, lons))
    below = own_shift(fields[:, :, 0, :].reshape(planes, -1), *both, (-1, 0))
    right = own_shift(fields[:, :, :, 0].reshape(planes, -1), *both, (0, -1))
    corner = own_shift(fields[:, :, 0, 0].reshape(planes, 1), *both, (-1, -1))
    lead = (field_count, levels)
    near = jnp.concatenate(
        [
            jnp.concatenate([fields, below.reshape(*lead, 1, block_cols)], axis=2),
            jnp.concatenate([right, corner], axis=1).reshape(*lead, block_rows + 1, 1),
        ],
        axis=3,
    )
    north = own_shift(fields[:, :, -8:], *both, (1, 0))
    south = own_shift(fields[:, :, :8], *both, (-1, 0))
    tall = jnp.concatenate([north, fields, south], axis=2)
    height = block_rows + 16
    width = block_cols + 16
    west = own_shift(tall[..., -8:].reshape(planes, -1), *both, (0, 1))
    east = own_shift(tall[..., :8].reshape(planes, -1), *both, (0, -1))
    wide = jnp.concatenate(
        [west.reshape(*lead, height, 8), tall, east.reshape(*lead, height, 8)], axis=3
    )

    ring = panel_cols + 8
    border = border_source[0]
    bands = border[: 8 * ring].reshape(8, ring)
    bands = jnp.pad(bands, ((0, 0), (4, 4)), constant_values=-1)
    bands = lax.dynamic_slice(bands, (0, lon * block_cols), (8, width))
    sides = border[8 * ring :].reshape(panel_rows, 2, 4)
    sides = jnp.where(lon == 0, sides[:, 0], sides[:, 1])
    wanted = jnp.concatenate([bands.reshape(-1), sides.reshape(-1)])
    band_cells = 4 * width
    local = wanted - lat * (lons * slots)
    slot_ids = jnp.arange(lons * slots, dtype=jnp.int32)[:, None]

    def split_cells(chosen):
        top = chosen[:, :band_cells]
        bottom = chosen[:, band_cells : 2 * band_cells]
        side = chosen[:, 2 * band_cells :].reshape(planes, lats, block_rows * 4)
        half = 8 * 4
        empty = jnp.zeros((planes, 1, half), jnp.float32)
        prev = jnp.concatenate([empty, side[:, :-1, -half:]], axis=1)
        post = jnp.concatenate([side[:, 1:, :half], empty], axis=1)
        side = jnp.concatenate([prev, side, post], axis=2)
        return top, bottom, side

    def by_permutes(mine):
        axes = ("panel", "lon")
        pieces = []
        for shift in range(lons):
            pairs = [
                (q * lons + b, (1 - q) * lons + (b + shift) % lons)
                for q in range(panels)
                for b in range(lons)
            ]
            pieces.append(lax.ppermute(mine, axes, pairs))
        row = jnp.concatenate(pieces, axis=1)
        block = local // slots
        turned = jnp.where(
            (local >= 0) & (local < lons * slots),
            (lon + lons - block) % lons * slots + local % slots,
            -1,
        )
        chosen = jnp.dot(row, (slot_ids == turned).astype(jnp.float32), precision=HIGHEST)
        top, bottom, side = split_cells(chosen)
        band_sum = jnp.where(lat == 0, top, bottom)
        side_sum = lax.dynamic_index_in_dim(side, lat, 1, keepdims=False)
        axes = ("lat", "lon")
        for shift in range(1, lats):
            goal = (lat + shift) % lats
            pairs = [
                ((a - shift) % lats * lons + b, a * lons + b)
                for a in (0, lats - 1)
                for b in range(lons)
            ]
            band_sum = band_sum + lax.ppermute(jnp.where(goal == 0, top, bottom), axes, pairs)
            pairs = [
                (a * lons + b, (a + shift) % lats * lons + b)
                for a in range(lats)
                for b in (0, lons - 1)
            ]
            part = lax.dynamic_index_in_dim(side, goal, 1, keepdims=False)
            side_sum = side_sum + lax.ppermute(part, axes, pairs)
        return band_sum, side_sum

    def by_exchange(mine):
        target = jnp.arange(panels * lons, dtype=jnp.int32) // lons
        sent = jnp.where((target != panel)[:, None, None], mine[None], 0.0)
        got = lax.all_to_all(sent, ("panel", "lon"), 0, 0, tiled=True)
        got = lax.dynamic_slice_in_dim(got, (1 - panel) * lons, lons, 0)
        row = jnp.moveaxis(got, 0, 1).reshape(planes, -1)
        chosen = jnp.dot(row, (slot_ids == local).astype(jnp.float32), precision=HIGHEST)
        top, bottom, side = split_cells(chosen)
        empty = jnp.zeros((lats - 2, planes, band_cells), jnp.float32)
        band = jnp.concatenate([top[None], empty, bottom[None]], axis=0)
        sent = jnp.concatenate([band, jnp.moveaxis(side, 1, 0)], axis=2)
        got = lax.all_to_all(sent, "lat", 0, 0, tiled=True).sum(axis=0)
        return got[:, :band_cells], got[:, band_cells:]

    def filled(cells, band, side, trim):
        band = band.reshape(*lead, 4, width)[..., trim : width - trim]
        side = side.reshape(*lead, height, 4)[:, :, trim : height - trim]
        top = 8 - trim
        end = top + block_rows
        cells = jnp.concatenate(
            [
                cells[..., : top - 4],
                jnp.where(lon == 0, side, cells[..., top - 4 : top]),
                cells[..., top : top + block_cols],
                jnp.where(lon == lons - 1, side, cells[..., top + block_cols : top + block_cols + 4]),
                cells[..., top + block_cols + 4 :],
            ],
            axis=3,
        )
        return jnp.concatenate(
            [
                cells[:, :, : top - 4],
                jnp.where(lat == 0, band, cells[:, :, top - 4 : top]),
                cells[:, :, top:end],
                jnp.where(lat == lats - 1, band, cells[:, :, end : end + 4]),
                cells[:, :, end + 4 :],
            ],
            axis=2,
        )

    mine = donors(near, donor_at, slot_weights, slot_turn, block_cols)
    band, side = by_permutes(mine)
    first = tendency(
        filled(wide, band, side, 0),
        colatitude,
        longitude,
        panel_flag,
        diffusion,
        dtheta,
        dlongitude,
        time_step,
    )
    middle = wide[:, :, 4:-4, 4:-4] + 0.5 * time_step * first
    mine = donors(
        middle[:, :, 4 : block_rows + 5, 4 : block_cols + 5],
        donor_at,
        slot_weights,
        slot_turn,
        block_cols,
    )
    band, side = by_exchange(mine)
    second = tendency(
        filled(middle, band, side, 4),
        colatitude[4:-4],
        longitude[4:-4],
        panel_flag,
        diffusion,
        dtheta,
        dlongitude,
        time_step,
    )
    first = first[:, :, 4:-4, 4:-4]
    accumulated = fields + time_step / 6.0 * (first + 2.0 * second)
    section_three = fields + 0.5 * time_step * second
    return (accumulated[None], section_three[None])


def solution(mesh):
    return jax.shard_map(
        shards,
        mesh=mesh,
        in_specs=(
            P("panel", None, None, "lat", "lon"),
            P("panel", "lat", "lon", None),
            P("panel", "lat", "lon", None, None),
            P("panel", "lat", "lon", None),
            P("panel", None),
            P(),
        ),
        out_specs=(P("panel", None, None, "lat", "lon"), P("panel", None, None, "lat", "lon")),
        check_vma=False,
    )
```

```python
import math

import jax
import jax.numpy as jnp
from jax import lax
from jax.sharding import PartitionSpec as P

GAMMA = 5.0 / 3.0
RADIAL_STEP = 0.65 / 32.0
HIGHEST = lax.Precision.HIGHEST

def radii(levels):
    level_ids = jnp.arange(levels, dtype=jnp.float32)
    offset = 16 - levels // 2
    return 0.35 + 0.65 * (level_ids + offset + 0.5) / 32.0


def along_colatitude(field, dtheta):
    return (
        field[..., :-4, 2:-2]
        - 8.0 * field[..., 1:-3, 2:-2]
        + 8.0 * field[..., 3:-1, 2:-2]
        - field[..., 4:, 2:-2]
    ) / (12.0 * dtheta)


def along_longitude(field, dlongitude):
    return (
        field[..., 2:-2, :-4]
        - 8.0 * field[..., 2:-2, 1:-3]
        + 8.0 * field[..., 2:-2, 3:-1]
        - field[..., 2:-2, 4:]
    ) / (12.0 * dlongitude)


def along_radius(field):
    inner_part = (field[2:] - field[:-2]) / (2.0 * RADIAL_STEP)
    first_end = (field[1:2] - field[0:1]) / RADIAL_STEP
    last_end = (field[-1:] - field[-2:-1]) / RADIAL_STEP
    return jnp.concatenate([first_end, inner_part, last_end], axis=0)[:, 2:-2, 2:-2]


def shrink(field):
    return field[..., 2:-2, 2:-2]


def curl(vector, band):
    radius, sine_in, sine_out, dtheta, dlongitude = band
    part_r, part_t, part_p = vector
    curl_r = (along_colatitude(sine_in * part_p, dtheta) - along_longitude(part_t, dlongitude)) / (
        radius * sine_out
    )
    curl_t = (
        along_longitude(part_r, dlongitude) / sine_out - along_radius(radius * part_p)
    ) / radius
    curl_p = (along_radius(radius * part_t) - along_colatitude(part_r, dtheta)) / radius
    return (curl_r, curl_t, curl_p)


def divergence(vector, band):
    radius, sine_in, sine_out, dtheta, dlongitude = band
    part_r, part_t, part_p = vector
    radial = along_radius(radius * radius * part_r) / (radius * radius)
    return radial + (
        along_colatitude(sine_in * part_t, dtheta) + along_longitude(part_p, dlongitude)
    ) / (radius * sine_out)


def gradient(field, band):
    radius, sine_in, sine_out, dtheta, dlongitude = band
    return (
        along_radius(field),
        along_colatitude(field, dtheta) / radius,
        along_longitude(field, dlongitude) / (radius * sine_out),
    )


def cross(left, right):
    return (
        left[1] * right[2] - left[2] * right[1],
        left[2] * right[0] - left[0] * right[2],
        left[0] * right[1] - left[1] * right[0],
    )


def advect(velocity, grad_field):
    return velocity[0] * grad_field[0] + velocity[1] * grad_field[1] + velocity[2] * grad_field[2]


def tendency(extended, colatitude, longitude, panel_flag, diffusion, dtheta, dlongitude, time_step):
    levels = extended.shape[1]
    radius = radii(levels)[:, None, None]
    sine_four = jnp.sin(colatitude)[:, None]
    sine_two = sine_four[2:-2]
    sine_zero = sine_four[4:-4]
    outer_band = (radius, sine_four, sine_two, dtheta, dlongitude)
    inner_band = (radius, sine_two, sine_zero, dtheta, dlongitude)
    finest = min(dtheta, dlongitude)
    viscosity = diffusion[0] * (finest * finest / time_step)
    resistivity = diffusion[1] * (finest * finest / time_step)
    rotation = 0.25 / time_step
    log_rho, vel_r, vel_t, vel_p, mag_r, mag_t, mag_p, pressure = [
        extended[which] for which in range(8)
    ]
    vorticity = curl((vel_r, vel_t, vel_p), outer_band)
    current = curl((mag_r, mag_t, mag_p), outer_band)
    div_two = divergence((vel_r, vel_t, vel_p), outer_band)
    vel_two = [shrink(piece) for piece in (vel_r, vel_t, vel_p)]
    mag_two = [shrink(piece) for piece in (mag_r, mag_t, mag_p)]
    induced = cross(vel_two, mag_two)
    electric = tuple((induced[which] - resistivity * current[which] for which in range(3)))
    kinetic = 0.5 * (vel_two[0] * vel_two[0] + vel_two[1] * vel_two[1] + vel_two[2] * vel_two[2])
    grad_kin = gradient(kinetic, inner_band)
    grad_pres = gradient(shrink(pressure), inner_band)
    grad_rho = gradient(shrink(log_rho), inner_band)
    curl_vort = curl(vorticity, inner_band)
    curl_elec = curl(electric, inner_band)
    velocity = [shrink(piece) for piece in vel_two]
    magnetic = [shrink(piece) for piece in mag_two]
    vort_zero = [shrink(piece) for piece in vorticity]
    curr_zero = [shrink(piece) for piece in current]
    div_vel = shrink(div_two)
    inv_rho = jnp.exp(-shrink(shrink(log_rho)))
    pres_zero = shrink(shrink(pressure))
    colat_zero = colatitude[4:-4][:, None]
    longi_zero = longitude[4:-4][None, :]
    omega_r = rotation * (
        (1.0 - panel_flag) * jnp.cos(colat_zero)
        + panel_flag * jnp.sin(colat_zero) * jnp.sin(longi_zero)
    )
    omega_t = rotation * (
        (1.0 - panel_flag) * -jnp.sin(colat_zero)
        + panel_flag * jnp.cos(colat_zero) * jnp.sin(longi_zero)
    )
    omega_p = rotation * panel_flag * jnp.cos(longi_zero)
    lamb_term = cross(velocity, vort_zero)
    lorentz = cross(curr_zero, magnetic)
    spin_term = cross((omega_r, omega_t, omega_p), velocity)
    vel_rates = [
        lamb_term[which]
        - grad_kin[which]
        - inv_rho * grad_pres[which]
        + inv_rho * lorentz[which]
        - 2.0 * spin_term[which]
        - viscosity * curl_vort[which]
        for which in range(3)
    ]
    rho_rate = -advect(velocity, grad_rho) - div_vel
    pres_rate = -advect(velocity, grad_pres) - GAMMA * pres_zero * div_vel
    return jnp.stack([rho_rate] + vel_rates + list(curl_elec) + [pres_rate])


def angles(row_ids, col_ids, dtheta, dlongitude):
    colatitude = 0.25 * math.pi + (row_ids.astype(jnp.float32) + 0.5) * dtheta
    longitude = -0.75 * math.pi + (col_ids.astype(jnp.float32) + 0.5) * dlongitude
    return (colatitude, longitude)


def own_shift(value, axes, sizes, moves):
    pairs = []
    total = math.prod(sizes)
    for source in range(total):
        rest = source
        place = []
        for size in reversed(sizes):
            place.append(rest % size)
            rest //= size
        place = place[::-1]
        goal = [at + move for at, move in zip(place, moves)]
        if all(0 <= at < size for at, size in zip(goal, sizes)):
            target = 0
            for at, size in zip(goal, sizes):
                target = target * size + at
            pairs.append((source, target))
    return lax.ppermute(value, axes, pairs)


def donors(cells, donor_at, weights, turn, block_cols):
    rows = cells.shape[2]
    cols = cells.shape[3]
    row_at = donor_at // block_cols
    col_at = donor_at % block_cols
    col_ids = jnp.arange(cols, dtype=jnp.int32)[:, None]
    row_ids = jnp.arange(rows, dtype=jnp.int32)[:, None]
    pick = jnp.concatenate([col_ids == col_at, col_ids == col_at + 1], axis=1).astype(jnp.float32)
    here = row_ids == row_at
    below = row_ids == row_at + 1
    mix = jnp.concatenate(
        [
            jnp.where(here, weights[0], 0.0) + jnp.where(below, weights[2], 0.0),
            jnp.where(here, weights[1], 0.0) + jnp.where(below, weights[3], 0.0),
        ],
        axis=1,
    )
    chosen = jnp.einsum("flij,jk->flik", cells, pick, precision=HIGHEST)
    both = jnp.sum(chosen * mix, axis=2)
    slots = donor_at.shape[0]
    mixed = both[..., :slots] + both[..., slots:]
    cosine = jnp.cos(turn)
    sine_turn = jnp.sin(turn)
    vel_t = cosine * mixed[2] + sine_turn * mixed[3]
    vel_p = -sine_turn * mixed[2] + cosine * mixed[3]
    mag_t = cosine * mixed[5] + sine_turn * mixed[6]
    mag_p = -sine_turn * mixed[5] + cosine * mixed[6]
    out = jnp.stack([mixed[0], mixed[1], vel_t, vel_p, mixed[4], mag_t, mag_p, mixed[7]])
    return out.reshape(-1, slots)


def shards(state, donor_cell, donor_weights, donor_turn, border_source, diffusion):
    fields = state[0]
    field_count, levels, block_rows, block_cols = fields.shape
    planes = field_count * levels
    lats = lax.axis_size("lat")
    lons = lax.axis_size("lon")
    panels = lax.axis_size("panel")
    slots = donor_cell.shape[-1]
    panel_rows = block_rows * lats
    panel_cols = block_cols * lons
    dtheta = 0.5 * math.pi / panel_rows
    dlongitude = 1.5 * math.pi / panel_cols
    time_step = 0.1 * min(dtheta, dlongitude)
    panel = lax.axis_index("panel")
    lat = lax.axis_index("lat")
    lon = lax.axis_index("lon")
    row_ids = lat * block_rows + jnp.arange(-8, block_rows + 8, dtype=jnp.int32)
    col_ids = lon * block_cols + jnp.arange(-8, block_cols + 8, dtype=jnp.int32)
    colatitude, longitude = angles(row_ids, col_ids, dtheta, dlongitude)
    panel_flag = panel.astype(jnp.float32)
    donor_at = donor_cell[0, 0, 0]
    slot_weights = donor_weights[0, 0, 0]
    slot_turn = donor_turn[0, 0, 0]

    both = (("lat", "lon"), (lats, lons))
    below = own_shift(fields[:, :, 0, :].reshape(planes, -1), *both, (-1, 0))
    right = own_shift(fields[:, :, :, 0].reshape(planes, -1), *both, (0, -1))
    corner = own_shift(fields[:, :, 0, 0].reshape(planes, 1), *both, (-1, -1))
    lead = (field_count, levels)
    near = jnp.concatenate(
        [
            jnp.concatenate([fields, below.reshape(*lead, 1, block_cols)], axis=2),
            jnp.concatenate([right, corner], axis=1).reshape(*lead, block_rows + 1, 1),
        ],
        axis=3,
    )
    north = own_shift(fields[:, :, -8:], *both, (1, 0))
    south = own_shift(fields[:, :, :8], *both, (-1, 0))
    tall = jnp.concatenate([north, fields, south], axis=2)
    height = block_rows + 16
    width = block_cols + 16
    west = own_shift(tall[..., -8:].reshape(planes, -1), *both, (0, 1))
    east = own_shift(tall[..., :8].reshape(planes, -1), *both, (0, -1))
    wide = jnp.concatenate(
        [west.reshape(*lead, height, 8), tall, east.reshape(*lead, height, 8)], axis=3
    )

    ring = panel_cols + 8
    border = border_source[0]
    bands = border[: 8 * ring].reshape(8, ring)
    bands = jnp.pad(bands, ((0, 0), (4, 4)), constant_values=-1)
    bands = lax.dynamic_slice(bands, (0, lon * block_cols), (8, width))
    sides = border[8 * ring :].reshape(panel_rows, 2, 4)
    sides = jnp.where(lon == 0, sides[:, 0], sides[:, 1])
    wanted = jnp.concatenate([bands.reshape(-1), sides.reshape(-1)])
    band_cells = 4 * width
    local = wanted - lat * (lons * slots)
    slot_ids = jnp.arange(lons * slots, dtype=jnp.int32)[:, None]

    quad = 4
    lon_far, lon_near = lon // quad, lon % quad
    lat_far, lat_near = lat // quad, lat % quad
    block = local // slots
    valid = (local >= 0) & (local < lons * slots)

    def pick_cells(pieces, place):
        row = jnp.concatenate(pieces, axis=1)
        at = jnp.where(valid, place * slots + local % slots, -1)
        chosen = jnp.dot(row, (slot_ids == at).astype(jnp.float32), precision=HIGHEST)
        top = chosen[:, :band_cells]
        bottom = chosen[:, band_cells : 2 * band_cells]
        side = chosen[:, 2 * band_cells :].reshape(planes, lats, block_rows * 4)
        half = 8 * 4
        empty = jnp.zeros((planes, 1, half), jnp.float32)
        prev = jnp.concatenate([empty, side[:, :-1, -half:]], axis=1)
        post = jnp.concatenate([side[:, 1:, :half], empty], axis=1)
        side = jnp.concatenate([prev, side, post], axis=2)
        side = jnp.moveaxis(side, 1, 0).reshape(quad, quad, planes, -1)
        return top, bottom, side

    def near_chunks(pieces, place):
        top, bottom, side = pick_cells(pieces, place)
        empty = jnp.zeros((quad - 2, planes, band_cells), jnp.float32)
        band = jnp.concatenate([top[None], empty, bottom[None]], axis=0)
        side = jnp.moveaxis(side, 0, 2).reshape(quad, planes, -1)
        return jnp.concatenate([band, side], axis=2)

    def far_chunks(got):
        band = got[:, :band_cells]
        side = jnp.moveaxis(got[:, band_cells:].reshape(planes, quad, -1), 1, 0)
        far = jnp.arange(quad, dtype=jnp.int32)
        goal = jnp.where(lat_near == 0, 0, quad - 1)
        band = jnp.where((far == goal)[:, None, None], band[None], 0.0)
        return jnp.concatenate([band, side], axis=2)

    def by_permutes(mine):
        axes = ("panel", "lon")
        pieces = []
        for shift in range(quad):
            pairs = [
                (q * lons + b, (1 - q) * lons + (b + quad * shift) % lons)
                for q in range(panels)
                for b in range(lons)
            ]
            pieces.append(lax.ppermute(mine, axes, pairs))
        held = jnp.stack(pieces)
        whole = list(pieces)
        for shift in range(1, quad):
            pairs = [(b, b - b % quad + (b + shift) % quad) for b in range(lons)]
            got = lax.ppermute(held, "lon", pairs)
            whole += [got[which] for which in range(quad)]
        far_turn = (lon_far + quad - block // quad) % quad
        near_turn = (lon_near + quad - block % quad) % quad
        chunks = near_chunks(whole, near_turn * quad + far_turn)
        axes = ("lat", "lon")
        total = lax.dynamic_index_in_dim(chunks, lat_near, 0, keepdims=False)
        for shift in range(1, quad):
            pairs = []
            for a in range(lats):
                goal = a - a % quad + (a + shift) % quad
                for b in range(lons):
                    if b in (0, lons - 1) or goal % quad in (0, quad - 1):
                        pairs.append((a * lons + b, goal * lons + b))
            part = lax.dynamic_index_in_dim(
                chunks, (lat_near + shift) % quad, 0, keepdims=False
            )
            total = total + lax.ppermute(part, axes, pairs)
        chunks = far_chunks(total)
        total = lax.dynamic_index_in_dim(chunks, lat_far, 0, keepdims=False)
        for shift in range(1, quad):
            pairs = []
            for a in range(lats):
                goal = (a + quad * shift) % lats
                for b in range(lons):
                    if b in (0, lons - 1) or goal in (0, lats - 1):
                        pairs.append((a * lons + b, goal * lons + b))
            part = lax.dynamic_index_in_dim(
                chunks, (lat_far + shift) % quad, 0, keepdims=False
            )
            total = total + lax.ppermute(part, axes, pairs)
        return total[:, :band_cells], total[:, band_cells:]

    def by_exchange(mine):
        far_groups = [[quad * i + j for i in range(quad)] for j in range(quad)]
        near_groups = [[quad * i + j for j in range(quad)] for i in range(quad)]
        both_groups = [[q * lons + b for q in range(panels) for b in group] for group in far_groups]
        target = jnp.arange(panels * quad, dtype=jnp.int32) // quad
        sent = jnp.where((target != panel)[:, None, None], mine[None], 0.0)
        got = lax.all_to_all(
            sent, ("panel", "lon"), 0, 0, axis_index_groups=both_groups, tiled=True
        )
        got = lax.dynamic_slice_in_dim(got, (1 - panel) * quad, quad, 0)
        sent = jnp.broadcast_to(got[None], (quad, *got.shape))
        got = lax.all_to_all(sent, "lon", 0, 0, axis_index_groups=near_groups, tiled=True)
        whole = [got[near, far] for near in range(quad) for far in range(quad)]
        chunks = near_chunks(whole, block % quad * quad + block // quad)
        got = lax.all_to_all(chunks, "lat", 0, 0, axis_index_groups=near_groups, tiled=True)
        chunks = far_chunks(got.sum(axis=0))
        got = lax.all_to_all(chunks, "lat", 0, 0, axis_index_groups=far_groups, tiled=True)
        got = got.sum(axis=0)
        return got[:, :band_cells], got[:, band_cells:]

    def filled(cells, band, side, trim):
        band = band.reshape(*lead, 4, width)[..., trim : width - trim]
        side = side.reshape(*lead, height, 4)[:, :, trim : height - trim]
        top = 8 - trim
        end = top + block_rows
        cells = jnp.concatenate(
            [
                cells[..., : top - 4],
                jnp.where(lon == 0, side, cells[..., top - 4 : top]),
                cells[..., top : top + block_cols],
                jnp.where(lon == lons - 1, side, cells[..., top + block_cols : top + block_cols + 4]),
                cells[..., top + block_cols + 4 :],
            ],
            axis=3,
        )
        return jnp.concatenate(
            [
                cells[:, :, : top - 4],
                jnp.where(lat == 0, band, cells[:, :, top - 4 : top]),
                cells[:, :, top:end],
                jnp.where(lat == lats - 1, band, cells[:, :, end : end + 4]),
                cells[:, :, end + 4 :],
            ],
            axis=2,
        )

    mine = donors(near, donor_at, slot_weights, slot_turn, block_cols)
    band, side = by_permutes(mine)
    first = tendency(
        filled(wide, band, side, 0),
        colatitude,
        longitude,
        panel_flag,
        diffusion,
        dtheta,
        dlongitude,
        time_step,
    )
    middle = wide[:, :, 4:-4, 4:-4] + 0.5 * time_step * first
    mine = donors(
        middle[:, :, 4 : block_rows + 5, 4 : block_cols + 5],
        donor_at,
        slot_weights,
        slot_turn,
        block_cols,
    )
    band, side = by_exchange(mine)
    second = tendency(
        filled(middle, band, side, 4),
        colatitude[4:-4],
        longitude[4:-4],
        panel_flag,
        diffusion,
        dtheta,
        dlongitude,
        time_step,
    )
    first = first[:, :, 4:-4, 4:-4]
    accumulated = fields + time_step / 6.0 * (first + 2.0 * second)
    section_three = fields + 0.5 * time_step * second
    return (accumulated[None], section_three[None])


def solution(mesh):
    return jax.shard_map(
        shards,
        mesh=mesh,
        in_specs=(
            P("panel", None, None, "lat", "lon"),
            P("panel", "lat", "lon", None),
            P("panel", "lat", "lon", None, None),
            P("panel", "lat", "lon", None),
            P("panel", None),
            P(),
        ),
        out_specs=(P("panel", None, None, "lat", "lon"), P("panel", None, None, "lat", "lon")),
        check_vma=False,
    )
```

```python
import math

import jax
import jax.numpy as jnp
from jax import lax
from jax.experimental import pallas as pl
from jax.experimental.pallas import tpu as pltpu
from jax.sharding import PartitionSpec as P

GAMMA = 5.0 / 3.0
RADIAL_STEP = 0.65 / 32.0
FIELDS = 8
LEVELS = 4
PLANES = FIELDS * LEVELS
ROWS = 16
COLS = 48
SLOTS = 33
LATS = 16
LONS = 16
TILE = 4
WIDE = 128
TALL = ROWS + 16
MID = ROWS + 8
BAND = 4 * 64
SIDE = 4 * TALL
CHUNK = BAND + SIDE
PEERS = 16
PANEL_ROWS = ROWS * LATS
PANEL_COLS = COLS * LONS
DTHETA = 0.5 * math.pi / PANEL_ROWS
DPHI = 1.5 * math.pi / PANEL_COLS
FINEST = min(DTHETA, DPHI)
TIME_STEP = 0.1 * FINEST
RADII = [0.35 + 0.65 * (k + 16 - LEVELS // 2 + 0.5) / 32.0 for k in range(LEVELS)]
VMEM = pl.BlockSpec(memory_space=pltpu.VMEM)
SMEM = pl.BlockSpec(memory_space=pltpu.SMEM)
PARAMS = pltpu.CompilerParams(vmem_limit_bytes=40 * 1024 * 1024)


def iota(shape, axis):
    return lax.broadcasted_iota(jnp.int32, shape, axis)


def split_dot(left, right):
    total = None
    for _ in range(3):
        part = left.astype(jnp.bfloat16)
        left = left - part.astype(jnp.float32)
        term = jnp.dot(part, right, preferred_element_type=jnp.float32)
        total = term if total is None else total + term
    return total


def donor_message(planes, rows, pick, mix, spin):
    chosen = split_dot(planes, pick).reshape(PLANES, rows, WIDE)
    both = jnp.sum(chosen * mix[None], axis=1)
    mixed = both + pltpu.roll(both, WIDE // 2, 1)
    cosine = spin[0:1]
    sine = spin[1:2]
    at = iota((PLANES, WIDE), 0) // LEVELS
    theta = (at == 2) | (at == 5)
    phi = (at == 3) | (at == 6)
    other = jnp.where(
        theta, pltpu.roll(mixed, PLANES - LEVELS, 0), -pltpu.roll(mixed, LEVELS, 0)
    )
    turned = jnp.where(theta | phi, cosine * mixed + sine * other, mixed)
    half = PLANES // 2
    return jnp.where(iota((half, WIDE), 1) < WIDE // 2, turned[:half], turned[half:])


def post_message(place_ref, packed, out_ref):
    panel = place_ref[0]
    out_ref[pl.ds((1 - panel) * PEERS, PEERS)] = jnp.broadcast_to(packed[None], (PEERS, 16, WIDE))
    out_ref[pl.ds(panel * PEERS, PEERS)] = jnp.zeros((PEERS, 16, WIDE), jnp.float32)


def donor_kernel(place_ref, near_ref, pick_ref, mix_ref, spin_ref, out_ref):
    planes = near_ref[...].reshape(PLANES * MID, WIDE)
    packed = donor_message(planes, MID, pick_ref[...], mix_ref[...], spin_ref[...])
    post_message(place_ref, packed, out_ref)


def choice_kernel(place_ref, got_ref, index_ref, out_ref):
    panel, lat, lon = place_ref[0], place_ref[1], place_ref[2]
    low = iota((16, WIDE), 1) < WIDE // 2
    tiles = []
    base = (1 - panel) * PEERS
    for pair in range(PEERS // 2):
        one = got_ref[base + 2 * pair]
        two = got_ref[base + 2 * pair + 1]
        top = jnp.where(low, one, pltpu.roll(two, WIDE // 2, 1))
        end = jnp.where(low, pltpu.roll(one, WIDE // 2, 1), two)
        tiles.append(jnp.concatenate([top, end], axis=0))
    held = jnp.concatenate(tiles, axis=1)
    depth = PEERS * WIDE // 2
    parts = []
    for _ in range(3):
        part = held.astype(jnp.bfloat16)
        held = held - part.astype(jnp.float32)
        parts.append(part)
    parts = jnp.concatenate(parts, axis=0)

    def chosen(start, count):
        wanted = index_ref[:, start : start + count]
        spot = iota((depth, count), 0) == wanted
        hot = jnp.where(spot, 1.0, 0.0).astype(jnp.bfloat16)
        terms = jnp.dot(parts, hot, preferred_element_type=jnp.float32)
        return terms[:PLANES] + terms[PLANES : 2 * PLANES] + terms[2 * PLANES :]

    out_ref[...] = jnp.zeros(out_ref.shape, jnp.float32)
    tile_row = lat // TILE
    tile_col = lon % 8 // 2

    @pl.when((tile_row == 0) | (tile_row == LATS // TILE - 1))
    def _():
        first = jnp.where(tile_row == 0, 0, (TILE - 1) * TILE)
        for which in range(TILE):
            out_ref[first + which, :, :BAND] = chosen(which * BAND, BAND)

    @pl.when((tile_col == 0) | (tile_col == 3))
    def _():
        first = jnp.where(tile_col == 0, 0, TILE - 1)
        sides = chosen(TILE * BAND, TILE * SIDE)
        for which in range(TILE):
            out_ref[which * TILE + first, :, BAND:] = sides[:, which * SIDE : (which + 1) * SIDE]


def fill_ghosts(place_ref, got_ref, work_ref, rows):
    lat, lon = place_ref[1], place_ref[2]
    trim = (TALL - rows) // 2
    top = 8 - trim

    @pl.when((lon == 0) | (lon == LONS - 1))
    def _():
        side = jnp.sum(got_ref[:, :, BAND:], axis=0)
        first = jnp.where(lon == 0, 4, 8 + COLS)
        lane = iota((rows, WIDE), 1)
        own = lane // 4 == iota((rows, WIDE), 0) + trim
        spread = jnp.where(own[None], side[:, None, :], 0.0).reshape(PLANES * rows, WIDE)
        target = iota((WIDE, WIDE), 1) - first
        hot = jnp.where(target == iota((WIDE, WIDE), 0) % 4, 1.0, 0.0).astype(jnp.bfloat16)
        moved = split_dot(spread, hot).reshape(PLANES, rows, WIDE)
        ghost = (lane >= first) & (lane < first + 4)
        work_ref[...] = jnp.where(ghost[None], moved, work_ref[...])

    @pl.when((lat == 0) | (lat == LATS - 1))
    def _():
        band = jnp.sum(got_ref[:, :, :BAND], axis=0)
        lines = []
        for half in range(2):
            piece = band[:, half * WIDE : (half + 1) * WIDE]
            lines += [piece, pltpu.roll(piece, WIDE // 2, 1)]

        @pl.when(lat == 0)
        def _():
            for row in range(4):
                work_ref[:, top - 4 + row, :] = lines[row]

        @pl.when(lat == LATS - 1)
        def _():
            for row in range(4):
                work_ref[:, top + ROWS + row, :] = lines[row]


def rates(load, rows, coef_ref, diffusion_ref):
    def on_levels(value, factors):
        return jnp.concatenate(
            [value[k * rows : (k + 1) * rows] * factors[k] for k in range(LEVELS)], axis=0
        )

    def whole(which):
        return jnp.concatenate([coef_ref[which]] * LEVELS, axis=0)

    sine = whole(0)
    per_sine = whole(1)
    inverse = [1.0 / r for r in RADII]
    viscosity = diffusion_ref[0] * (FINEST * FINEST / TIME_STEP)
    resistivity = diffusion_ref[1] * (FINEST * FINEST / TIME_STEP)

    def slope(value, axis, step):
        size = value.shape[axis]
        near = pltpu.roll(value, size - 1, axis) - pltpu.roll(value, 1, axis)
        far = pltpu.roll(value, size - 2, axis) - pltpu.roll(value, 2, axis)
        return near * (8.0 / (12.0 * step)) - far * (1.0 / (12.0 * step))

    def d_theta(value):
        return slope(value, 0, DTHETA)

    def d_phi(value):
        return slope(value, 1, DPHI)

    def d_radius(value):
        part = [value[k * rows : (k + 1) * rows] for k in range(LEVELS)]
        slopes = [(part[1] - part[0]) * (1.0 / RADIAL_STEP)]
        for k in range(1, LEVELS - 1):
            slopes.append((part[k + 1] - part[k - 1]) * (1.0 / (2.0 * RADIAL_STEP)))
        slopes.append((part[-1] - part[-2]) * (1.0 / RADIAL_STEP))
        return jnp.concatenate(slopes, axis=0)

    def by_radius(value):
        return on_levels(value, RADII)

    def per_radius(value):
        return on_levels(value, inverse)

    def curl(vector):
        part_r, part_t, part_p = vector
        return (
            per_radius((d_theta(sine * part_p) - d_phi(part_t)) * per_sine),
            per_radius(d_phi(part_r) * per_sine - d_radius(by_radius(part_p))),
            per_radius(d_radius(by_radius(part_t)) - d_theta(part_r)),
        )

    def gradient(value):
        return (
            d_radius(value),
            per_radius(d_theta(value)),
            per_radius(d_phi(value) * per_sine),
        )

    def cross(left, right):
        return (
            left[1] * right[2] - left[2] * right[1],
            left[2] * right[0] - left[0] * right[2],
            left[0] * right[1] - left[1] * right[0],
        )

    def advect(vector, slopes):
        return vector[0] * slopes[0] + vector[1] * slopes[1] + vector[2] * slopes[2]

    velocity = [load(which) for which in (1, 2, 3)]
    magnetic = [load(which) for which in (4, 5, 6)]
    vorticity = curl(velocity)
    current = curl(magnetic)
    squares = [r * r for r in RADII]
    spread = on_levels(
        d_radius(on_levels(velocity[0], squares)), [1.0 / square for square in squares]
    ) + per_radius((d_theta(sine * velocity[1]) + d_phi(velocity[2])) * per_sine)
    induced = cross(velocity, magnetic)
    electric = [induced[k] - resistivity * current[k] for k in range(3)]
    kinetic = 0.5 * (
        velocity[0] * velocity[0] + velocity[1] * velocity[1] + velocity[2] * velocity[2]
    )
    curl_electric = curl(electric)
    log_rho = load(0)
    rho_rate = -advect(velocity, gradient(log_rho)) - spread
    pressure = load(7)
    slope_pressure = gradient(pressure)
    pressure_rate = -advect(velocity, slope_pressure) - GAMMA * pressure * spread
    lorentz = cross(current, magnetic)
    per_rho = jnp.exp(-log_rho)
    slope_kinetic = gradient(kinetic)
    curl_vorticity = curl(vorticity)
    lamb = cross(velocity, vorticity)
    turning = cross((whole(2), whole(3), whole(4)), velocity)
    momentum = [
        lamb[k]
        - slope_kinetic[k]
        + per_rho * (lorentz[k] - slope_pressure[k])
        - turning[k]
        - viscosity * curl_vorticity[k]
        for k in range(3)
    ]
    return [rho_rate, *momentum, *curl_electric, pressure_rate]


def first_kernel(
    place_ref,
    diffusion_ref,
    wide_ref,
    got_ref,
    coef_ref,
    pick_ref,
    mix_ref,
    spin_ref,
    middle_ref,
    out_ref,
    work_ref,
    next_ref,
):
    work_ref[...] = wide_ref[...]
    fill_ghosts(place_ref, got_ref, work_ref, TALL)

    def load(which):
        return work_ref[which * LEVELS : (which + 1) * LEVELS].reshape(LEVELS * TALL, WIDE)

    found = rates(load, TALL, coef_ref, diffusion_ref)
    lane = iota((TALL, WIDE), 1)
    row = iota((TALL, WIDE), 0)
    inside = (lane >= 4) & (lane < 12 + COLS) & (row >= 4) & (row < 12 + ROWS)
    for which in range(FIELDS):
        value = load(which) + (0.5 * TIME_STEP) * found[which]
        for level in range(LEVELS):
            plane = which * LEVELS + level
            part = jnp.where(inside, value[level * TALL : (level + 1) * TALL], 0.0)
            next_ref[plane] = part[8:]
            middle_ref[plane] = pltpu.roll(part, TALL - 4, 0)[:MID]
    planes = next_ref[...].reshape(PLANES * MID, WIDE)
    packed = donor_message(planes, MID, pick_ref[...], mix_ref[...], spin_ref[...])
    post_message(place_ref, packed, out_ref)


def second_kernel(
    place_ref,
    diffusion_ref,
    middle_ref,
    got_ref,
    coef_ref,
    state_ref,
    whole_ref,
    third_ref,
    work_ref,
):
    work_ref[...] = middle_ref[...]
    fill_ghosts(place_ref, got_ref, work_ref, MID)

    def load(which):
        return work_ref[which * LEVELS : (which + 1) * LEVELS].reshape(LEVELS * MID, WIDE)

    found = rates(load, MID, coef_ref, diffusion_ref)

    def centre(value):
        return pltpu.roll(pltpu.roll(value, MID - 4, 0)[:ROWS], WIDE - 8, 1)[:, :COLS]

    for which in range(FIELDS):
        for level in range(LEVELS):
            rate = found[which][level * MID : (level + 1) * MID]
            held = state_ref[which, level]
            step = centre(rate * (0.5 * TIME_STEP))
            middle = centre(middle_ref[which * LEVELS + level])
            third_ref[which, level] = held + step
            whole_ref[which, level] = held + ((middle - held) + 2.0 * step) * (1.0 / 3.0)


def shift(value, move_lat, move_lon):
    pairs = []
    for a in range(LATS):
        for b in range(LONS):
            goal_a, goal_b = a + move_lat, b + move_lon
            if 0 <= goal_a < LATS and 0 <= goal_b < LONS:
                pairs.append((a * LONS + b, goal_a * LONS + goal_b))
    return lax.ppermute(value, ("lat", "lon"), pairs)


def lon_of(x_half, tile, step):
    return x_half * 8 + tile * 2 + step


def far_groups():
    groups = []
    for u in range(TILE):
        for x_half in range(2):
            for step in range(2):
                groups.append(
                    [
                        (q * LATS + ti * TILE + u) * LONS + lon_of(x_half, tj, step)
                        for q in range(2)
                        for ti in range(TILE)
                        for tj in range(TILE)
                    ]
                )
    return groups


def near_groups():
    groups = []
    for ti in range(TILE):
        for tj in range(TILE):
            groups.append(
                [
                    (ti * TILE + u) * LONS + lon_of(x_half, tj, step)
                    for u in range(TILE)
                    for x_half in range(2)
                    for step in range(2)
                ]
            )
    return groups


def shards(state, donor_cell, donor_weights, donor_turn, border_source, diffusion):
    fields = state[0]
    panel = lax.axis_index("panel")
    lat = lax.axis_index("lat")
    lon = lax.axis_index("lon")
    place = jnp.stack([panel, lat, lon]).astype(jnp.int32)
    f32 = jnp.float32

    below = shift(fields[:, :, 0, :].reshape(PLANES, COLS), -1, 0)
    right = shift(fields[:, :, :, 0].reshape(PLANES, ROWS), 0, -1)
    corner = shift(fields[:, :, 0, 0].reshape(PLANES, 1), -1, -1)

    donor_at = donor_cell[0, 0, 0]
    weights = donor_weights[0, 0, 0]
    turn = donor_turn[0, 0, 0]
    late = (jnp.arange(WIDE) >= WIDE // 2)[None]

    def twice(value, fill):
        value = jnp.pad(value, (0, WIDE // 2 - SLOTS), constant_values=fill)
        return jnp.concatenate([value, value])[None]

    col_at = twice(donor_at % COLS, -100) + late
    row_at = twice(donor_at // COLS, -100)
    upper = jnp.where(late, twice(weights[1], 0), twice(weights[0], 0))
    lower = jnp.where(late, twice(weights[3], 0), twice(weights[2], 0))
    spin = jnp.concatenate([jnp.cos(twice(turn, 0)), jnp.sin(twice(turn, 0))])

    def pick_at(offset):
        return (jnp.arange(WIDE)[:, None] == col_at + offset).astype(jnp.bfloat16)

    row_ids = jnp.arange(MID)[:, None]
    mix = jnp.where(row_ids == row_at, upper, 0.0) + jnp.where(row_ids == row_at + 1, lower, 0.0)

    near = jnp.concatenate([fields.reshape(PLANES, ROWS, COLS), below[:, None, :]], axis=1)
    edge = jnp.concatenate([right, corner], axis=1)[:, :, None]
    near = jnp.concatenate([near, edge], axis=2)
    near = jnp.pad(near, ((0, 0), (0, MID - ROWS - 1), (0, WIDE - COLS - 1)))
    message = jax.ShapeDtypeStruct((2 * PEERS, 16, WIDE), f32)
    sent = pl.pallas_call(
        donor_kernel,
        out_shape=message,
        in_specs=[SMEM, VMEM, VMEM, VMEM, VMEM],
        out_specs=VMEM,
        compiler_params=PARAMS,
    )(place, near, pick_at(0), mix, spin)

    def to_holders(sent):
        return lax.all_to_all(
            sent, ("panel", "lat", "lon"), 0, 0, axis_index_groups=far_groups(), tiled=True
        )

    got = to_holders(sent)

    late_fields, _ = lax.optimization_barrier((fields, sent))
    north = shift(late_fields[:, :, -8:], 1, 0)
    south = shift(late_fields[:, :, :8], -1, 0)
    tall = jnp.concatenate([north, late_fields, south], axis=2).reshape(PLANES, TALL, COLS)
    west = shift(tall[..., -8:].reshape(PLANES, TALL * 8), 0, 1).reshape(PLANES, TALL, 8)
    east = shift(tall[..., :8].reshape(PLANES, TALL * 8), 0, -1).reshape(PLANES, TALL, 8)
    blank = jnp.zeros((PLANES, TALL, WIDE - COLS - 16), f32)
    wide = jnp.concatenate([west, tall, east, blank], axis=2)

    ring = PANEL_COLS + 8
    border = border_source[0]
    tile_row = lat // TILE
    tile_col = lon % 8 // 2
    bands = border[: 8 * ring].reshape(2, 4, ring)
    bands = jnp.where(tile_row == 0, bands[0], bands[1])
    bands = jnp.pad(bands, ((0, 0), (4, 4)), constant_values=-1)
    windows = []
    for x_half in range(2):
        for step in range(2):
            start = lon_of(x_half, tile_col, step) * COLS
            windows.append(lax.dynamic_slice(bands, (0, start), (4, 64)).reshape(1, BAND))
    sides = border[8 * ring :].reshape(PANEL_ROWS, 2, 4)
    sides = jnp.where(tile_col == 0, sides[:, 0], sides[:, 1])
    sides = jnp.pad(sides, ((8, 8), (0, 0)), constant_values=-1)
    sides = lax.dynamic_slice(sides, (tile_row * TILE * ROWS, 0), (TILE * ROWS + 16, 4))
    for u in range(TILE):
        windows.append(sides[u * ROWS : u * ROWS + TALL].reshape(1, SIDE))
    wanted = jnp.concatenate(windows, axis=1)
    block = wanted // SLOTS
    from_lat, from_lon = block // LONS, block % LONS
    mine = (from_lat % TILE == lat % TILE) & (from_lon // 8 == lon // 8)
    mine = mine & (from_lon % 2 == lon % 2) & (wanted >= 0)
    spot = (from_lat // TILE * TILE + from_lon % 8 // 2) * (WIDE // 2) + wanted % SLOTS
    index = jnp.where(mine, spot, -1).astype(jnp.int32)

    def to_blocks(got):
        chunks = pl.pallas_call(
            choice_kernel,
            out_shape=jax.ShapeDtypeStruct((PEERS, PLANES, CHUNK), f32),
            in_specs=[SMEM, VMEM, VMEM],
            out_specs=VMEM,
            compiler_params=PARAMS,
        )(place, got, index)
        return lax.all_to_all(
            chunks, ("lat", "lon"), 0, 0, axis_index_groups=near_groups(), tiled=True
        )

    row_ids = lat * ROWS + jnp.arange(-8, ROWS + 8, dtype=jnp.int32)
    col_ids = lon * COLS + jnp.arange(-8, WIDE - 8, dtype=jnp.int32)
    colatitude = (0.25 * math.pi + (row_ids.astype(f32) + 0.5) * DTHETA)[:, None]
    longitude = (-0.75 * math.pi + (col_ids.astype(f32) + 0.5) * DPHI)[None, :]
    sine, cosine = jnp.sin(colatitude), jnp.cos(colatitude)
    sine_lon, cosine_lon = jnp.sin(longitude), jnp.cos(longitude)
    twirl = 2.0 * 0.25 / TIME_STEP
    flat = jnp.ones((TALL, WIDE), f32)
    yang = panel == 1
    coef = jnp.stack(
        [
            sine * flat,
            1.0 / sine * flat,
            twirl * jnp.where(yang, sine * sine_lon, cosine * flat),
            twirl * jnp.where(yang, cosine * sine_lon, -sine * flat),
            twirl * jnp.where(yang, cosine_lon * flat, 0.0),
        ]
    )

    got = to_blocks(got)
    middle, sent = pl.pallas_call(
        first_kernel,
        out_shape=(jax.ShapeDtypeStruct((PLANES, MID, WIDE), f32), message),
        in_specs=[SMEM, SMEM] + [VMEM] * 6,
        out_specs=(VMEM, VMEM),
        scratch_shapes=[
            pltpu.VMEM((PLANES, TALL, WIDE), f32),
            pltpu.VMEM((PLANES, MID, WIDE), f32),
        ],
        compiler_params=PARAMS,
    )(place, diffusion, wide, got, coef, pick_at(8), mix, spin)
    got = to_blocks(to_holders(sent))
    block_shape = jax.ShapeDtypeStruct(fields.shape, f32)
    accumulated, section_three = pl.pallas_call(
        second_kernel,
        out_shape=(block_shape, block_shape),
        in_specs=[SMEM, SMEM] + [VMEM] * 4,
        out_specs=(VMEM, VMEM),
        scratch_shapes=[pltpu.VMEM((PLANES, MID, WIDE), f32)],
        compiler_params=PARAMS,
    )(place, diffusion, middle, got, coef[:, 4 : 4 + MID], fields)
    return (accumulated[None], section_three[None])


def solution(mesh):
    return jax.shard_map(
        shards,
        mesh=mesh,
        in_specs=(
            P("panel", None, None, "lat", "lon"),
            P("panel", "lat", "lon", None),
            P("panel", "lat", "lon", None, None),
            P("panel", "lat", "lon", None),
            P("panel", None),
            P(),
        ),
        out_specs=(P("panel", None, None, "lat", "lon"), P("panel", None, None, "lat", "lon")),
        check_vma=False,
    )
```

```python
import math

import jax
import jax.numpy as jnp
from jax import lax
from jax.experimental import pallas as pl
from jax.experimental.pallas import tpu as pltpu
from jax.sharding import PartitionSpec as P

GAMMA = 5.0 / 3.0
RADIAL_STEP = 0.65 / 32.0
FIELDS = 8
LEVELS = 4
PLANES = FIELDS * LEVELS
ROWS = 16
COLS = 48
SLOTS = 33
LATS = 16
LONS = 16
ROOM = 63
WIDE = 128
TALL = ROWS + 16
MID = ROWS + 8
BAND = 4 * 64
SIDE = 4 * TALL
CHUNK = BAND + SIDE
PEERS = 16
DEPTH = PEERS * WIDE // 2
PANEL_ROWS = ROWS * LATS
PANEL_COLS = COLS * LONS
DTHETA = 0.5 * math.pi / PANEL_ROWS
DPHI = 1.5 * math.pi / PANEL_COLS
FINEST = min(DTHETA, DPHI)
TIME_STEP = 0.1 * FINEST
RADII = [0.35 + 0.65 * (k + 16 - LEVELS // 2 + 0.5) / 32.0 for k in range(LEVELS)]
VMEM = pl.BlockSpec(memory_space=pltpu.VMEM)
SMEM = pl.BlockSpec(memory_space=pltpu.SMEM)
PARAMS = pltpu.CompilerParams(vmem_limit_bytes=40 * 1024 * 1024)


def iota(shape, axis):
    return lax.broadcasted_iota(jnp.int32, shape, axis)


def split_dot(left, right):
    total = None
    for _ in range(3):
        part = left.astype(jnp.bfloat16)
        left = left - part.astype(jnp.float32)
        term = jnp.dot(part, right, preferred_element_type=jnp.float32)
        total = term if total is None else total + term
    return total


def donor_message(planes, rows, pick, mix, spin):
    chosen = split_dot(planes, pick).reshape(PLANES, rows, WIDE)
    both = jnp.sum(chosen * mix[None], axis=1)
    mixed = both + pltpu.roll(both, WIDE // 2, 1)
    cosine = spin[0:1]
    sine = spin[1:2]
    at = iota((PLANES, WIDE), 0) // LEVELS
    theta = (at == 2) | (at == 5)
    phi = (at == 3) | (at == 6)
    other = jnp.where(
        theta, pltpu.roll(mixed, PLANES - LEVELS, 0), -pltpu.roll(mixed, LEVELS, 0)
    )
    turned = jnp.where(theta | phi, cosine * mixed + sine * other, mixed)
    half = PLANES // 2
    return jnp.where(iota((half, WIDE), 1) < WIDE // 2, turned[:half], turned[half:])


def post_message(place_ref, packed, out_ref):
    panel = place_ref[0]
    out_ref[pl.ds((1 - panel) * PEERS, PEERS)] = jnp.broadcast_to(packed[None], (PEERS, 16, WIDE))
    out_ref[pl.ds(panel * PEERS, PEERS)] = jnp.zeros((PEERS, 16, WIDE), jnp.float32)


def donor_kernel(place_ref, near_ref, pick_ref, mix_ref, spin_ref, out_ref):
    planes = near_ref[...].reshape(PLANES * MID, WIDE)
    packed = donor_message(planes, MID, pick_ref[...], mix_ref[...], spin_ref[...])
    post_message(place_ref, packed, out_ref)


def unpack(read):
    low = iota((16, WIDE), 1) < WIDE // 2
    tiles = []
    for pair in range(PEERS // 2):
        one = read(2 * pair)
        two = read(2 * pair + 1)
        top = jnp.where(low, one, pltpu.roll(two, WIDE // 2, 1))
        end = jnp.where(low, pltpu.roll(one, WIDE // 2, 1), two)
        tiles.append(jnp.concatenate([top, end], axis=0))
    return jnp.concatenate(tiles, axis=1)


def split_parts(held):
    parts = []
    for _ in range(3):
        part = held.astype(jnp.bfloat16)
        held = held - part.astype(jnp.float32)
        parts.append(part)
    return jnp.concatenate(parts, axis=0)


def join_parts(terms):
    return terms[:PLANES] + terms[PLANES : 2 * PLANES] + terms[2 * PLANES :]


def from_row(place_ref, got_ref):
    base = (1 - place_ref[0]) * PEERS
    return split_parts(unpack(lambda which: got_ref[base + which]))


def plan_kernel(place_ref, holder_ref, spot_ref, send_ref, take_ref, rest_ref):
    lat = place_ref[1]
    order = iota((CHUNK, CHUNK), 0) < iota((CHUNK, CHUNK), 1)
    order = jnp.where(order, 1.0, 0.0).astype(jnp.bfloat16)

    def ranks(chosen):
        ones = jnp.where(chosen, 1.0, 0.0).astype(jnp.bfloat16)
        return jnp.dot(ones, order, preferred_element_type=jnp.float32)

    holder = holder_ref[...]
    mine = holder == lat
    spot = spot_ref[...].astype(jnp.float32)
    rank = ranks(mine)
    rest_ref[...] = jnp.where(mine & (rank >= ROOM), spot, -1.0)
    key = jnp.where(mine & (rank < ROOM), rank, -1.0)
    half = WIDE // 2
    place_at = iota((half, CHUNK), 0).astype(jnp.float32)
    lane = iota((half, DEPTH), 1).astype(jnp.float32)
    for block in range(LATS):
        found = place_at == key[block : block + 1]
        table = jnp.sum(
            jnp.where(found, spot[block : block + 1] + 1.0, 0.0), axis=1, keepdims=True
        )
        hot = jnp.where(lane + 1.0 == table, 1.0, 0.0)
        send_ref[block * half : (block + 1) * half] = hot.astype(jnp.bfloat16)
    own = holder_ref[pl.ds(lat, 1)]
    masks = iota((PEERS, CHUNK), 0) == own
    rank = jnp.sum(jnp.where(masks, ranks(masks), 0.0), axis=0, keepdims=True)
    fits = (own >= 0) & (rank < ROOM)
    index = jnp.where(fits, own.astype(jnp.float32) * half + rank, -1.0)
    hot = iota((DEPTH, CHUNK), 0).astype(jnp.float32) == index
    take_ref[...] = jnp.where(hot, 1.0, 0.0).astype(jnp.bfloat16)


def count_kernel(bands_ref, sides_ref, out_ref):
    width = bands_ref.shape[1]
    column = iota((width, WIDE), 0) - 4
    start = iota((width, WIDE), 1) * COLS - 8
    within = (column >= start) & (column < start + 64) & (start < PANEL_COLS)
    columns = jnp.where(within, 1.0, 0.0).astype(jnp.bfloat16)
    row = iota((PANEL_ROWS, WIDE), 0)
    start = iota((PANEL_ROWS, WIDE), 1) * ROWS - 8
    within = (row >= start) & (row < start + TALL) & (start < PANEL_ROWS)
    rows = jnp.where(within, 1.0, 0.0).astype(jnp.bfloat16)

    def most(ref, windows):
        ones = []
        for which in range(LATS):
            ones.append(jnp.where(ref[...] == which, 1.0, 0.0))
        ones = jnp.concatenate(ones, axis=0).astype(jnp.bfloat16)
        counts = jnp.dot(ones, windows, preferred_element_type=jnp.float32)
        counts = jnp.sum(counts.reshape(2 * LATS, 4, WIDE), axis=1)
        return jnp.max(counts)

    total = most(bands_ref, columns) + most(sides_ref, rows)
    out_ref[...] = jnp.full(out_ref.shape, total, jnp.float32)


def choice_kernel(place_ref, got_ref, send_ref, out_ref):
    parts = from_row(place_ref, got_ref)
    terms = lax.dot_general(
        parts, send_ref[...], (((1,), (1,)), ((), ())), preferred_element_type=jnp.float32
    )
    chosen = join_parts(terms)
    low = iota((16, WIDE), 1) < WIDE // 2
    for pair in range(PEERS // 2):
        tile = chosen[:, pair * WIDE : (pair + 1) * WIDE]
        top, end = tile[:16], tile[16:]
        out_ref[2 * pair] = jnp.where(low, top, pltpu.roll(end, WIDE // 2, 1))
        out_ref[2 * pair + 1] = jnp.where(low, pltpu.roll(top, WIDE // 2, 1), end)


def rest_kernel(place_ref, got_ref, rest_ref, out_ref):
    parts = from_row(place_ref, got_ref)
    at = iota((DEPTH, CHUNK), 0).astype(jnp.float32)
    for block in range(LATS):
        hot = jnp.where(at == rest_ref[block : block + 1], 1.0, 0.0).astype(jnp.bfloat16)
        out_ref[block] = join_parts(jnp.dot(parts, hot, preferred_element_type=jnp.float32))


def ghost_values(got_ref, take_ref, rest_ref):
    parts = split_parts(unpack(lambda which: got_ref[which]))
    terms = jnp.dot(parts, take_ref[...], preferred_element_type=jnp.float32)
    return join_parts(terms) + rest_ref[...]


def fill_ghosts(place_ref, ghosts, work_ref, rows):
    lat, lon = place_ref[1], place_ref[2]
    trim = (TALL - rows) // 2
    top = 8 - trim

    @pl.when((lon == 0) | (lon == LONS - 1))
    def _():
        side = ghosts[:, BAND:]
        first = jnp.where(lon == 0, 4, 8 + COLS)
        lane = iota((rows, WIDE), 1)
        own = lane // 4 == iota((rows, WIDE), 0) + trim
        spread = jnp.where(own[None], side[:, None, :], 0.0).reshape(PLANES * rows, WIDE)
        target = iota((WIDE, WIDE), 1) - first
        hot = jnp.where(target == iota((WIDE, WIDE), 0) % 4, 1.0, 0.0).astype(jnp.bfloat16)
        moved = split_dot(spread, hot).reshape(PLANES, rows, WIDE)
        ghost = (lane >= first) & (lane < first + 4)
        work_ref[...] = jnp.where(ghost[None], moved, work_ref[...])

    @pl.when((lat == 0) | (lat == LATS - 1))
    def _():
        band = ghosts[:, :BAND]
        lines = []
        for half in range(2):
            piece = band[:, half * WIDE : (half + 1) * WIDE]
            lines += [piece, pltpu.roll(piece, WIDE // 2, 1)]

        @pl.when(lat == 0)
        def _():
            for row in range(4):
                work_ref[:, top - 4 + row, :] = lines[row]

        @pl.when(lat == LATS - 1)
        def _():
            for row in range(4):
                work_ref[:, top + ROWS + row, :] = lines[row]


def rates(load, rows, coef_ref, diffusion_ref):
    def on_levels(value, factors):
        return jnp.concatenate(
            [value[k * rows : (k + 1) * rows] * factors[k] for k in range(LEVELS)], axis=0
        )

    def whole(which):
        return jnp.concatenate([coef_ref[which]] * LEVELS, axis=0)

    sine = whole(0)
    per_sine = whole(1)
    inverse = [1.0 / r for r in RADII]
    viscosity = diffusion_ref[0] * (FINEST * FINEST / TIME_STEP)
    resistivity = diffusion_ref[1] * (FINEST * FINEST / TIME_STEP)

    def slope(value, axis, step):
        size = value.shape[axis]
        near = pltpu.roll(value, size - 1, axis) - pltpu.roll(value, 1, axis)
        far = pltpu.roll(value, size - 2, axis) - pltpu.roll(value, 2, axis)
        return near * (8.0 / (12.0 * step)) - far * (1.0 / (12.0 * step))

    def d_theta(value):
        return slope(value, 0, DTHETA)

    def d_phi(value):
        return slope(value, 1, DPHI)

    def d_radius(value):
        part = [value[k * rows : (k + 1) * rows] for k in range(LEVELS)]
        slopes = [(part[1] - part[0]) * (1.0 / RADIAL_STEP)]
        for k in range(1, LEVELS - 1):
            slopes.append((part[k + 1] - part[k - 1]) * (1.0 / (2.0 * RADIAL_STEP)))
        slopes.append((part[-1] - part[-2]) * (1.0 / RADIAL_STEP))
        return jnp.concatenate(slopes, axis=0)

    def by_radius(value):
        return on_levels(value, RADII)

    def per_radius(value):
        return on_levels(value, inverse)

    def curl(vector):
        part_r, part_t, part_p = vector
        return (
            per_radius((d_theta(sine * part_p) - d_phi(part_t)) * per_sine),
            per_radius(d_phi(part_r) * per_sine - d_radius(by_radius(part_p))),
            per_radius(d_radius(by_radius(part_t)) - d_theta(part_r)),
        )

    def gradient(value):
        return (
            d_radius(value),
            per_radius(d_theta(value)),
            per_radius(d_phi(value) * per_sine),
        )

    def cross(left, right):
        return (
            left[1] * right[2] - left[2] * right[1],
            left[2] * right[0] - left[0] * right[2],
            left[0] * right[1] - left[1] * right[0],
        )

    def advect(vector, slopes):
        return vector[0] * slopes[0] + vector[1] * slopes[1] + vector[2] * slopes[2]

    velocity = [load(which) for which in (1, 2, 3)]
    magnetic = [load(which) for which in (4, 5, 6)]
    vorticity = curl(velocity)
    current = curl(magnetic)
    squares = [r * r for r in RADII]
    spread = on_levels(
        d_radius(on_levels(velocity[0], squares)), [1.0 / square for square in squares]
    ) + per_radius((d_theta(sine * velocity[1]) + d_phi(velocity[2])) * per_sine)
    induced = cross(velocity, magnetic)
    electric = [induced[k] - resistivity * current[k] for k in range(3)]
    kinetic = 0.5 * (
        velocity[0] * velocity[0] + velocity[1] * velocity[1] + velocity[2] * velocity[2]
    )
    curl_electric = curl(electric)
    log_rho = load(0)
    rho_rate = -advect(velocity, gradient(log_rho)) - spread
    pressure = load(7)
    slope_pressure = gradient(pressure)
    pressure_rate = -advect(velocity, slope_pressure) - GAMMA * pressure * spread
    lorentz = cross(current, magnetic)
    per_rho = jnp.exp(-log_rho)
    slope_kinetic = gradient(kinetic)
    curl_vorticity = curl(vorticity)
    lamb = cross(velocity, vorticity)
    turning = cross((whole(2), whole(3), whole(4)), velocity)
    momentum = [
        lamb[k]
        - slope_kinetic[k]
        + per_rho * (lorentz[k] - slope_pressure[k])
        - turning[k]
        - viscosity * curl_vorticity[k]
        for k in range(3)
    ]
    return [rho_rate, *momentum, *curl_electric, pressure_rate]


def first_kernel(
    place_ref,
    diffusion_ref,
    wide_ref,
    got_ref,
    take_ref,
    rest_ref,
    coef_ref,
    pick_ref,
    mix_ref,
    spin_ref,
    middle_ref,
    out_ref,
    work_ref,
    next_ref,
):
    work_ref[...] = wide_ref[...]
    ghosts = ghost_values(got_ref, take_ref, rest_ref)
    fill_ghosts(place_ref, ghosts, work_ref, TALL)

    def load(which):
        return work_ref[which * LEVELS : (which + 1) * LEVELS].reshape(LEVELS * TALL, WIDE)

    found = rates(load, TALL, coef_ref, diffusion_ref)
    lane = iota((TALL, WIDE), 1)
    row = iota((TALL, WIDE), 0)
    inside = (lane >= 4) & (lane < 12 + COLS) & (row >= 4) & (row < 12 + ROWS)
    for which in range(FIELDS):
        value = load(which) + (0.5 * TIME_STEP) * found[which]
        for level in range(LEVELS):
            plane = which * LEVELS + level
            part = jnp.where(inside, value[level * TALL : (level + 1) * TALL], 0.0)
            next_ref[plane] = part[8:]
            middle_ref[plane] = pltpu.roll(part, TALL - 4, 0)[:MID]
    planes = next_ref[...].reshape(PLANES * MID, WIDE)
    packed = donor_message(planes, MID, pick_ref[...], mix_ref[...], spin_ref[...])
    post_message(place_ref, packed, out_ref)


def second_kernel(
    place_ref,
    diffusion_ref,
    middle_ref,
    got_ref,
    take_ref,
    rest_ref,
    coef_ref,
    state_ref,
    whole_ref,
    third_ref,
    work_ref,
):
    work_ref[...] = middle_ref[...]
    ghosts = ghost_values(got_ref, take_ref, rest_ref)
    fill_ghosts(place_ref, ghosts, work_ref, MID)

    def load(which):
        return work_ref[which * LEVELS : (which + 1) * LEVELS].reshape(LEVELS * MID, WIDE)

    found = rates(load, MID, coef_ref, diffusion_ref)

    def centre(value):
        return pltpu.roll(pltpu.roll(value, MID - 4, 0)[:ROWS], WIDE - 8, 1)[:, :COLS]

    for which in range(FIELDS):
        for level in range(LEVELS):
            rate = found[which][level * MID : (level + 1) * MID]
            held = state_ref[which, level]
            step = centre(rate * (0.5 * TIME_STEP))
            middle = centre(middle_ref[which * LEVELS + level])
            third_ref[which, level] = held + step
            whole_ref[which, level] = held + ((middle - held) + 2.0 * step) * (1.0 / 3.0)


def shift(value, move_lat, move_lon):
    pairs = []
    for a in range(LATS):
        for b in range(LONS):
            goal_a, goal_b = a + move_lat, b + move_lon
            if 0 <= goal_a < LATS and 0 <= goal_b < LONS:
                pairs.append((a * LONS + b, goal_a * LONS + goal_b))
    return lax.ppermute(value, ("lat", "lon"), pairs)


def shards(state, donor_cell, donor_weights, donor_turn, border_source, diffusion):
    fields = state[0]
    panel = lax.axis_index("panel")
    lat = lax.axis_index("lat")
    lon = lax.axis_index("lon")
    place = jnp.stack([panel, lat, lon]).astype(jnp.int32)
    f32 = jnp.float32

    below = shift(fields[:, :, 0, :].reshape(PLANES, COLS), -1, 0)
    right = shift(fields[:, :, :, 0].reshape(PLANES, ROWS), 0, -1)
    corner = shift(fields[:, :, 0, 0].reshape(PLANES, 1), -1, -1)

    donor_at = donor_cell[0, 0, 0]
    weights = donor_weights[0, 0, 0]
    turn = donor_turn[0, 0, 0]
    late = (jnp.arange(WIDE) >= WIDE // 2)[None]

    def twice(value, fill):
        value = jnp.pad(value, (0, WIDE // 2 - SLOTS), constant_values=fill)
        return jnp.concatenate([value, value])[None]

    col_at = twice(donor_at % COLS, -100) + late
    row_at = twice(donor_at // COLS, -100)
    upper = jnp.where(late, twice(weights[1], 0), twice(weights[0], 0))
    lower = jnp.where(late, twice(weights[3], 0), twice(weights[2], 0))
    spin = jnp.concatenate([jnp.cos(twice(turn, 0)), jnp.sin(twice(turn, 0))])

    def pick_at(offset):
        return (jnp.arange(WIDE)[:, None] == col_at + offset).astype(jnp.bfloat16)

    row_ids = jnp.arange(MID)[:, None]
    mix = jnp.where(row_ids == row_at, upper, 0.0) + jnp.where(row_ids == row_at + 1, lower, 0.0)

    near = jnp.concatenate([fields.reshape(PLANES, ROWS, COLS), below[:, None, :]], axis=1)
    edge = jnp.concatenate([right, corner], axis=1)[:, :, None]
    near = jnp.concatenate([near, edge], axis=2)
    near = jnp.pad(near, ((0, 0), (0, MID - ROWS - 1), (0, WIDE - COLS - 1)))
    message = jax.ShapeDtypeStruct((2 * PEERS, 16, WIDE), f32)
    sent = pl.pallas_call(
        donor_kernel,
        out_shape=message,
        in_specs=[SMEM, VMEM, VMEM, VMEM, VMEM],
        out_specs=VMEM,
        compiler_params=PARAMS,
    )(place, near, pick_at(0), mix, spin)

    def to_holders(sent):
        return lax.all_to_all(sent, ("panel", "lon"), 0, 0, tiled=True)

    got = to_holders(sent)

    late_fields, border, late_lat, late_lon, _ = lax.optimization_barrier(
        (fields, border_source[0], lat, lon, sent)
    )
    north = shift(late_fields[:, :, -8:], 1, 0)
    south = shift(late_fields[:, :, :8], -1, 0)
    got, north, south = lax.optimization_barrier((got, north, south))
    tall = jnp.concatenate([north, late_fields, south], axis=2).reshape(PLANES, TALL, COLS)
    west = shift(tall[..., -8:].reshape(PLANES, TALL * 8), 0, 1).reshape(PLANES, TALL, 8)
    east = shift(tall[..., :8].reshape(PLANES, TALL * 8), 0, -1).reshape(PLANES, TALL, 8)
    blank = jnp.zeros((PLANES, TALL, WIDE - COLS - 16), f32)
    wide = jnp.concatenate([west, tall, east, blank], axis=2)

    ring = PANEL_COLS + 8
    row_slots = LONS * SLOTS
    bands = border[: 8 * ring].reshape(8, ring)
    sides = border[8 * ring :].reshape(PANEL_ROWS, 8)
    window = jnp.pad(bands, ((0, 0), (4, 4)), constant_values=-1)
    window = lax.dynamic_slice(window, (0, late_lon * COLS), (8, 64)).reshape(2, BAND)
    side = jnp.where(late_lon == 0, sides[:, :4], sides[:, 4:])
    side = jnp.where((late_lon == 0) | (late_lon == LONS - 1), side, -1)
    side = jnp.pad(side, ((8, 8), (0, 0)), constant_values=-1)
    side = jnp.concatenate(
        [
            side[:PANEL_ROWS].reshape(LATS, ROWS, 4),
            side[ROWS:].reshape(LATS, ROWS, 4),
        ],
        axis=1,
    ).reshape(LATS, SIDE)
    at_lat = jnp.arange(LATS)[:, None]
    band = jnp.where(at_lat == 0, window[:1], jnp.where(at_lat == LATS - 1, window[1:], -1))
    wanted = jnp.concatenate([band, side], axis=1)
    holder = jnp.where(wanted >= 0, wanted // row_slots, -1)
    local = wanted - late_lat * row_slots
    spot = local // SLOTS * (WIDE // 2) + local % SLOTS
    send, take, rest = pl.pallas_call(
        plan_kernel,
        out_shape=(
            jax.ShapeDtypeStruct((DEPTH, DEPTH), jnp.bfloat16),
            jax.ShapeDtypeStruct((DEPTH, CHUNK), jnp.bfloat16),
            jax.ShapeDtypeStruct((LATS, CHUNK), f32),
        ),
        in_specs=[SMEM, VMEM, VMEM],
        out_specs=(VMEM, VMEM, VMEM),
        compiler_params=PARAMS,
    )(place, holder, spot)
    most = pl.pallas_call(
        count_kernel,
        out_shape=jax.ShapeDtypeStruct((8, WIDE), f32),
        in_specs=[VMEM, VMEM],
        out_specs=VMEM,
        compiler_params=PARAMS,
    )(
        jnp.pad(bands // row_slots, ((0, 0), (0, 7 * WIDE - ring)), constant_values=-1),
        (sides // row_slots).T,
    )
    other = lax.ppermute(most, "panel", [(0, 1), (1, 0)])
    crowded = jnp.maximum(most, other)[0, 0] > ROOM

    def to_blocks(got):
        chunks = pl.pallas_call(
            choice_kernel,
            out_shape=jax.ShapeDtypeStruct((PEERS, 16, WIDE), f32),
            in_specs=[SMEM, VMEM, VMEM],
            out_specs=VMEM,
            compiler_params=PARAMS,
        )(place, got, send)
        fitting = lax.all_to_all(chunks, "lat", 0, 0, tiled=True)
        got, fitting = lax.optimization_barrier((got, fitting))

        def send_rest():
            chunks = pl.pallas_call(
                rest_kernel,
                out_shape=jax.ShapeDtypeStruct((PEERS, PLANES, CHUNK), f32),
                in_specs=[SMEM, VMEM, VMEM],
                out_specs=VMEM,
                compiler_params=PARAMS,
            )(place, got, rest)
            return lax.all_to_all(chunks, "lat", 0, 0, tiled=True).sum(axis=0)

        return fitting, lax.cond(crowded, send_rest, lambda: jnp.zeros((PLANES, CHUNK), f32))

    row_ids = late_lat * ROWS + jnp.arange(-8, ROWS + 8, dtype=jnp.int32)
    col_ids = late_lon * COLS + jnp.arange(-8, WIDE - 8, dtype=jnp.int32)
    colatitude = (0.25 * math.pi + (row_ids.astype(f32) + 0.5) * DTHETA)[:, None]
    longitude = (-0.75 * math.pi + (col_ids.astype(f32) + 0.5) * DPHI)[None, :]
    sine, cosine = jnp.sin(colatitude), jnp.cos(colatitude)
    sine_lon, cosine_lon = jnp.sin(longitude), jnp.cos(longitude)
    twirl = 2.0 * 0.25 / TIME_STEP
    flat = jnp.ones((TALL, WIDE), f32)
    yang = panel == 1
    coef = jnp.stack(
        [
            sine * flat,
            1.0 / sine * flat,
            twirl * jnp.where(yang, sine * sine_lon, cosine * flat),
            twirl * jnp.where(yang, cosine * sine_lon, -sine * flat),
            twirl * jnp.where(yang, cosine_lon * flat, 0.0),
        ]
    )

    got, extra = to_blocks(got)
    middle, sent = pl.pallas_call(
        first_kernel,
        out_shape=(jax.ShapeDtypeStruct((PLANES, MID, WIDE), f32), message),
        in_specs=[SMEM, SMEM] + [VMEM] * 8,
        out_specs=(VMEM, VMEM),
        scratch_shapes=[
            pltpu.VMEM((PLANES, TALL, WIDE), f32),
            pltpu.VMEM((PLANES, MID, WIDE), f32),
        ],
        compiler_params=PARAMS,
    )(place, diffusion, wide, got, take, extra, coef, pick_at(8), mix, spin)
    got, extra = to_blocks(to_holders(sent))
    block_shape = jax.ShapeDtypeStruct(fields.shape, f32)
    accumulated, section_three = pl.pallas_call(
        second_kernel,
        out_shape=(block_shape, block_shape),
        in_specs=[SMEM, SMEM] + [VMEM] * 6,
        out_specs=(VMEM, VMEM),
        scratch_shapes=[pltpu.VMEM((PLANES, MID, WIDE), f32)],
        compiler_params=PARAMS,
    )(place, diffusion, middle, got, take, extra, coef[:, 4 : 4 + MID], fields)
    return (accumulated[None], section_three[None])


def solution(mesh):
    return jax.shard_map(
        shards,
        mesh=mesh,
        in_specs=(
            P("panel", None, None, "lat", "lon"),
            P("panel", "lat", "lon", None),
            P("panel", "lat", "lon", None, None),
            P("panel", "lat", "lon", None),
            P("panel", None),
            P(),
        ),
        out_specs=(P("panel", None, None, "lat", "lon"), P("panel", None, None, "lat", "lon")),
        check_vma=False,
    )
```

```python
import math

import jax
import jax.numpy as jnp
from jax import lax
from jax.experimental import pallas as pl
from jax.experimental.pallas import tpu as pltpu
from jax.sharding import PartitionSpec as P

GAMMA = 5.0 / 3.0
RADIAL_STEP = 0.65 / 32.0
FIELDS = 8
LEVELS = 4
PLANES = FIELDS * LEVELS
ROWS = 16
COLS = 48
SLOTS = 33
LATS = 16
LONS = 16
ROOM = 63
FLAG_LANE = 63
WIDE = 128
TALL = ROWS + 16
MID = ROWS + 8
BAND = 4 * 64
SIDE = 4 * TALL
CHUNK = BAND + SIDE
PEERS = 16
DEPTH = PEERS * WIDE // 2
PANEL_ROWS = ROWS * LATS
PANEL_COLS = COLS * LONS
DTHETA = 0.5 * math.pi / PANEL_ROWS
DPHI = 1.5 * math.pi / PANEL_COLS
FINEST = min(DTHETA, DPHI)
TIME_STEP = 0.1 * FINEST
RADII = [0.35 + 0.65 * (k + 16 - LEVELS // 2 + 0.5) / 32.0 for k in range(LEVELS)]
VMEM = pl.BlockSpec(memory_space=pltpu.VMEM)
SMEM = pl.BlockSpec(memory_space=pltpu.SMEM)
PARAMS = pltpu.CompilerParams(vmem_limit_bytes=40 * 1024 * 1024)


def iota(shape, axis):
    return lax.broadcasted_iota(jnp.int32, shape, axis)


def split_dot(left, right):
    total = None
    for _ in range(3):
        part = left.astype(jnp.bfloat16)
        left = left - part.astype(jnp.float32)
        term = jnp.dot(part, right, preferred_element_type=jnp.float32)
        total = term if total is None else total + term
    return total


def donor_message(planes, rows, pick, mix, spin):
    chosen = split_dot(planes, pick).reshape(PLANES, rows, WIDE)
    both = jnp.sum(chosen * mix[None], axis=1)
    mixed = both + pltpu.roll(both, WIDE // 2, 1)
    cosine = spin[0:1]
    sine = spin[1:2]
    at = iota((PLANES, WIDE), 0) // LEVELS
    theta = (at == 2) | (at == 5)
    phi = (at == 3) | (at == 6)
    other = jnp.where(
        theta, pltpu.roll(mixed, PLANES - LEVELS, 0), -pltpu.roll(mixed, LEVELS, 0)
    )
    turned = jnp.where(theta | phi, cosine * mixed + sine * other, mixed)
    half = PLANES // 2
    return jnp.where(iota((half, WIDE), 1) < WIDE // 2, turned[:half], turned[half:])


def post_message(place_ref, packed, flag, out_ref):
    panel = place_ref[0]
    spot = (iota((16, WIDE), 0) == 0) & (iota((16, WIDE), 1) == FLAG_LANE)
    blank = jnp.where(spot, flag[0:1], 0.0)
    packed = jnp.where(spot, blank, packed)
    out_ref[pl.ds((1 - panel) * PEERS, PEERS)] = jnp.broadcast_to(packed[None], (PEERS, 16, WIDE))
    out_ref[pl.ds(panel * PEERS, PEERS)] = jnp.broadcast_to(blank[None], (PEERS, 16, WIDE))


def cut_kernel(state_ref, south_ref, east_ref, corner_ref, held_ref):
    for plane in range(PLANES):
        held_ref[plane, :, :COLS] = state_ref[plane // LEVELS, plane % LEVELS]
    lane = iota((ROWS, WIDE), 1)
    for pair in range(PLANES // 2):
        south_ref[pair] = pack_pair(held_ref[2 * pair, :8], held_ref[2 * pair + 1, :8])
    for group in range(2):
        columns = jnp.zeros((ROWS, WIDE), jnp.float32)
        for which in range(16):
            moved = pltpu.roll(held_ref[16 * group + which], 8 * which, 1)
            columns = jnp.where(lane // 8 == which, moved, columns)
        east_ref[group] = columns
        corner_ref[group] = columns[:8]


def pack_pair(one, two):
    return jnp.where(iota(one.shape, 1) < WIDE // 2, one, pltpu.roll(two, WIDE // 2, 1))


def prepare_kernel(
    cell_ref, weight_ref, turn_ref, bands_ref, sides_ref,
    pick_ref, mix_ref, spin_ref, flag_ref, line_ref
):
    half = WIDE // 2
    late = iota((1, WIDE), 1) >= half

    def twice(value, fill):
        line_ref[...] = jnp.full((1, WIDE), fill, jnp.float32)
        line_ref[:, :SLOTS] = value.astype(jnp.float32)
        line = line_ref[...]
        return jnp.where(late, pltpu.roll(line, half, 1), line)

    cell = twice(cell_ref[...], -10 * COLS)
    row_at = jnp.floor((cell + 0.5) * (1.0 / COLS))
    col_at = cell - row_at * COLS + jnp.where(late, 1.0, 0.0)
    upper = jnp.where(late, twice(weight_ref[1:2], 0.0), twice(weight_ref[0:1], 0.0))
    lower = jnp.where(late, twice(weight_ref[3:4], 0.0), twice(weight_ref[2:3], 0.0))
    turn = twice(turn_ref[...], 0.0)
    spin_ref[0:1] = jnp.cos(turn)
    spin_ref[1:2] = jnp.sin(turn)
    lane = iota((WIDE, WIDE), 0).astype(jnp.float32)
    real = jnp.where(row_at >= 0, col_at + 8.0, -1.0)
    pick_ref[...] = jnp.where(lane == real, 1.0, 0.0).astype(jnp.bfloat16)
    row = iota((MID, WIDE), 0).astype(jnp.float32)
    mix = jnp.where(row == row_at, upper, 0.0) + jnp.where(row == row_at + 1.0, lower, 0.0)
    mix_ref[...] = mix

    width = bands_ref.shape[1]
    column = iota((width, WIDE), 0) - 4
    start = iota((width, WIDE), 1) * COLS - 8
    within = (column >= start) & (column < start + 64) & (start < PANEL_COLS)
    columns = jnp.where(within, 1.0, 0.0).astype(jnp.bfloat16)
    row = iota((PANEL_ROWS, WIDE), 0)
    start = iota((PANEL_ROWS, WIDE), 1) * ROWS - 8
    within = (row >= start) & (row < start + TALL) & (start < PANEL_ROWS)
    rows = jnp.where(within, 1.0, 0.0).astype(jnp.bfloat16)

    def most(slots, windows):
        ones = []
        for which in range(LATS):
            first = which * LONS * SLOTS
            inside = (slots >= first) & (slots < first + LONS * SLOTS)
            ones.append(jnp.where(inside, 1.0, 0.0))
        ones = jnp.concatenate(ones, axis=0).astype(jnp.bfloat16)
        counts = jnp.dot(ones, windows, preferred_element_type=jnp.float32)
        return jnp.max(jnp.sum(counts.reshape(2 * LATS, 4, WIDE), axis=1))

    total = most(bands_ref[...], columns) + most(sides_ref[...], rows)
    flag_ref[...] = jnp.full(flag_ref.shape, total, jnp.float32)


def donor_kernel(
    place_ref, state_ref, south_ref, east_ref, corner_ref, pick_ref, mix_ref, spin_ref, flag_ref,
    wide_ref, north_ref, west_ref, corner_out_ref, out_ref, held_ref
):
    for plane in range(PLANES):
        held_ref[plane, :, :COLS] = state_ref[plane // LEVELS, plane % LEVELS]
    lane = iota((ROWS, WIDE), 1)
    own = (lane >= 8) & (lane < 8 + COLS)
    beyond = (lane >= 8 + COLS) & (lane < 16 + COLS)
    for plane in range(PLANES):
        group, which = plane // 16, plane % 16
        turn = (8 + COLS - 8 * which) % WIDE
        middle = pltpu.roll(held_ref[plane], 8, 1)
        east = pltpu.roll(east_ref[group], turn, 1)
        wide_ref[plane, :8] = jnp.zeros((8, WIDE), jnp.float32)
        wide_ref[plane, 8:24] = jnp.where(own, middle, jnp.where(beyond, east, 0.0))
        south = pltpu.roll(south_ref[plane // 2], 8 + plane % 2 * (WIDE // 2), 1)
        corner = pltpu.roll(corner_ref[group], turn, 1)
        wide_ref[plane, 24:] = jnp.where(own[:8], south, jnp.where(beyond[:8], corner, 0.0))
    planes = wide_ref[:, 8:, :].reshape(PLANES * MID, WIDE)
    packed = donor_message(planes, MID, pick_ref[...], mix_ref[...], spin_ref[...])
    post_message(place_ref, packed, flag_ref[...], out_ref)
    for pair in range(PLANES // 2):
        north_ref[pair] = pack_pair(wide_ref[2 * pair, 16:24], wide_ref[2 * pair + 1, 16:24])
    lane = iota((MID, WIDE), 1)
    for group in range(2):
        columns = jnp.zeros((MID, WIDE), jnp.float32)
        for which in range(16):
            turn = (8 * which - COLS) % WIDE
            moved = pltpu.roll(wide_ref[16 * group + which, 8:], turn, 1)
            columns = jnp.where(lane // 8 == which, moved, columns)
        west_ref[group] = columns
        corner_out_ref[group] = columns[8:16]


def unpack(read):
    low = iota((16, WIDE), 1) < WIDE // 2
    tiles = []
    for pair in range(PEERS // 2):
        one = read(2 * pair)
        two = read(2 * pair + 1)
        top = jnp.where(low, one, pltpu.roll(two, WIDE // 2, 1))
        end = jnp.where(low, pltpu.roll(one, WIDE // 2, 1), two)
        tiles.append(jnp.concatenate([top, end], axis=0))
    return jnp.concatenate(tiles, axis=1)


def split_parts(held):
    parts = []
    for _ in range(3):
        part = held.astype(jnp.bfloat16)
        held = held - part.astype(jnp.float32)
        parts.append(part)
    return jnp.concatenate(parts, axis=0)


def join_parts(terms):
    return terms[:PLANES] + terms[PLANES : 2 * PLANES] + terms[2 * PLANES :]


def from_row(place_ref, got_ref):
    base = (1 - place_ref[0]) * PEERS
    return split_parts(unpack(lambda which: got_ref[base + which]))


def plan_kernel(place_ref, holder_ref, spot_ref, send_ref, take_ref, rest_ref, coef_ref):
    lat = place_ref[1]
    order = iota((CHUNK, CHUNK), 0) < iota((CHUNK, CHUNK), 1)
    order = jnp.where(order, 1.0, 0.0).astype(jnp.bfloat16)

    def ranks(chosen):
        ones = jnp.where(chosen, 1.0, 0.0).astype(jnp.bfloat16)
        return jnp.dot(ones, order, preferred_element_type=jnp.float32)

    holder = holder_ref[...]
    mine = holder == lat
    spot = spot_ref[...].astype(jnp.float32)
    rank = ranks(mine)
    rest_ref[...] = jnp.where(mine & (rank >= ROOM), spot, -1.0)
    key = jnp.where(mine & (rank < ROOM), rank, -1.0)
    half = WIDE // 2
    place_at = iota((half, CHUNK), 0).astype(jnp.float32)
    lane = iota((half, DEPTH), 1).astype(jnp.float32)
    for block in range(LATS):
        found = place_at == key[block : block + 1]
        table = jnp.sum(
            jnp.where(found, spot[block : block + 1] + 1.0, 0.0), axis=1, keepdims=True
        )
        hot = jnp.where(lane + 1.0 == table, 1.0, 0.0)
        send_ref[block * half : (block + 1) * half] = hot.astype(jnp.bfloat16)
    own = holder_ref[pl.ds(lat, 1)]
    masks = iota((PEERS, CHUNK), 0) == own
    rank = jnp.sum(jnp.where(masks, ranks(masks), 0.0), axis=0, keepdims=True)
    fits = (own >= 0) & (rank < ROOM)
    index = jnp.where(fits, own.astype(jnp.float32) * half + rank, -1.0)
    hot = iota((DEPTH, CHUNK), 0).astype(jnp.float32) == index
    take_ref[...] = jnp.where(hot, 1.0, 0.0).astype(jnp.bfloat16)
    row = (lat * ROWS - 8 + iota((TALL, WIDE), 0)).astype(jnp.float32)
    column = (place_ref[2] * COLS - 8 + iota((TALL, WIDE), 1)).astype(jnp.float32)
    colatitude = 0.25 * math.pi + (row + 0.5) * DTHETA
    longitude = -0.75 * math.pi + (column + 0.5) * DPHI
    sine, cosine = jnp.sin(colatitude), jnp.cos(colatitude)
    twirl = 2.0 * 0.25 / TIME_STEP
    yang = place_ref[0] == 1
    coef_ref[0] = sine
    coef_ref[1] = 1.0 / sine
    coef_ref[2] = twirl * jnp.where(yang, sine * jnp.sin(longitude), cosine)
    coef_ref[3] = twirl * jnp.where(yang, cosine * jnp.sin(longitude), -sine)
    coef_ref[4] = twirl * jnp.where(yang, jnp.cos(longitude), 0.0)


def choice_kernel(place_ref, got_ref, send_ref, out_ref):
    parts = from_row(place_ref, got_ref)
    terms = lax.dot_general(
        parts, send_ref[...], (((1,), (1,)), ((), ())), preferred_element_type=jnp.float32
    )
    chosen = join_parts(terms)
    low = iota((16, WIDE), 1) < WIDE // 2
    for pair in range(PEERS // 2):
        tile = chosen[:, pair * WIDE : (pair + 1) * WIDE]
        top, end = tile[:16], tile[16:]
        out_ref[2 * pair] = jnp.where(low, top, pltpu.roll(end, WIDE // 2, 1))
        out_ref[2 * pair + 1] = jnp.where(low, pltpu.roll(top, WIDE // 2, 1), end)


def rest_kernel(place_ref, got_ref, rest_ref, out_ref):
    parts = from_row(place_ref, got_ref)
    at = iota((DEPTH, CHUNK), 0).astype(jnp.float32)
    for block in range(LATS):
        hot = jnp.where(at == rest_ref[block : block + 1], 1.0, 0.0).astype(jnp.bfloat16)
        out_ref[block] = join_parts(jnp.dot(parts, hot, preferred_element_type=jnp.float32))


def ghost_values(got_ref, take_ref, rest_ref):
    parts = split_parts(unpack(lambda which: got_ref[which]))
    terms = jnp.dot(parts, take_ref[...], preferred_element_type=jnp.float32)
    return join_parts(terms) + rest_ref[...]


def fill_ghosts(place_ref, ghosts, work_ref, rows):
    lat, lon = place_ref[1], place_ref[2]
    trim = (TALL - rows) // 2
    top = 8 - trim

    @pl.when((lon == 0) | (lon == LONS - 1))
    def _():
        side = ghosts[:, BAND:]
        first = jnp.where(lon == 0, 4, 8 + COLS)
        lane = iota((rows, WIDE), 1)
        own = lane // 4 == iota((rows, WIDE), 0) + trim
        spread = jnp.where(own[None], side[:, None, :], 0.0).reshape(PLANES * rows, WIDE)
        target = iota((WIDE, WIDE), 1) - first
        hot = jnp.where(target == iota((WIDE, WIDE), 0) % 4, 1.0, 0.0).astype(jnp.bfloat16)
        moved = split_dot(spread, hot).reshape(PLANES, rows, WIDE)
        ghost = (lane >= first) & (lane < first + 4)
        work_ref[...] = jnp.where(ghost[None], moved, work_ref[...])

    @pl.when((lat == 0) | (lat == LATS - 1))
    def _():
        band = ghosts[:, :BAND]
        lines = []
        for half in range(2):
            piece = band[:, half * WIDE : (half + 1) * WIDE]
            lines += [piece, pltpu.roll(piece, WIDE // 2, 1)]

        @pl.when(lat == 0)
        def _():
            for row in range(4):
                work_ref[:, top - 4 + row, :] = lines[row]

        @pl.when(lat == LATS - 1)
        def _():
            for row in range(4):
                work_ref[:, top + ROWS + row, :] = lines[row]


def rates(load, rows, coef_ref, diffusion_ref):
    def on_levels(value, factors):
        return jnp.concatenate(
            [value[k * rows : (k + 1) * rows] * factors[k] for k in range(LEVELS)], axis=0
        )

    def whole(which):
        value = coef_ref[which]
        if rows < TALL:
            value = pltpu.roll(value, TALL - (TALL - rows) // 2, 0)[:rows]
        return jnp.concatenate([value] * LEVELS, axis=0)

    sine = whole(0)
    per_sine = whole(1)
    inverse = [1.0 / r for r in RADII]
    viscosity = diffusion_ref[0] * (FINEST * FINEST / TIME_STEP)
    resistivity = diffusion_ref[1] * (FINEST * FINEST / TIME_STEP)

    def slope(value, axis, step):
        size = value.shape[axis]
        near = pltpu.roll(value, size - 1, axis) - pltpu.roll(value, 1, axis)
        far = pltpu.roll(value, size - 2, axis) - pltpu.roll(value, 2, axis)
        return near * (8.0 / (12.0 * step)) - far * (1.0 / (12.0 * step))

    def d_theta(value):
        return slope(value, 0, DTHETA)

    def d_phi(value):
        return slope(value, 1, DPHI)

    def d_radius(value):
        part = [value[k * rows : (k + 1) * rows] for k in range(LEVELS)]
        slopes = [(part[1] - part[0]) * (1.0 / RADIAL_STEP)]
        for k in range(1, LEVELS - 1):
            slopes.append((part[k + 1] - part[k - 1]) * (1.0 / (2.0 * RADIAL_STEP)))
        slopes.append((part[-1] - part[-2]) * (1.0 / RADIAL_STEP))
        return jnp.concatenate(slopes, axis=0)

    def by_radius(value):
        return on_levels(value, RADII)

    def per_radius(value):
        return on_levels(value, inverse)

    def curl(vector):
        part_r, part_t, part_p = vector
        return (
            per_radius((d_theta(sine * part_p) - d_phi(part_t)) * per_sine),
            per_radius(d_phi(part_r) * per_sine - d_radius(by_radius(part_p))),
            per_radius(d_radius(by_radius(part_t)) - d_theta(part_r)),
        )

    def gradient(value):
        return (
            d_radius(value),
            per_radius(d_theta(value)),
            per_radius(d_phi(value) * per_sine),
        )

    def cross(left, right):
        return (
            left[1] * right[2] - left[2] * right[1],
            left[2] * right[0] - left[0] * right[2],
            left[0] * right[1] - left[1] * right[0],
        )

    def advect(vector, slopes):
        return vector[0] * slopes[0] + vector[1] * slopes[1] + vector[2] * slopes[2]

    velocity = [load(which) for which in (1, 2, 3)]
    magnetic = [load(which) for which in (4, 5, 6)]
    vorticity = curl(velocity)
    current = curl(magnetic)
    squares = [r * r for r in RADII]
    spread = on_levels(
        d_radius(on_levels(velocity[0], squares)), [1.0 / square for square in squares]
    ) + per_radius((d_theta(sine * velocity[1]) + d_phi(velocity[2])) * per_sine)
    induced = cross(velocity, magnetic)
    electric = [induced[k] - resistivity * current[k] for k in range(3)]
    kinetic = 0.5 * (
        velocity[0] * velocity[0] + velocity[1] * velocity[1] + velocity[2] * velocity[2]
    )
    curl_electric = curl(electric)
    log_rho = load(0)
    rho_rate = -advect(velocity, gradient(log_rho)) - spread
    pressure = load(7)
    slope_pressure = gradient(pressure)
    pressure_rate = -advect(velocity, slope_pressure) - GAMMA * pressure * spread
    lorentz = cross(current, magnetic)
    per_rho = jnp.exp(-log_rho)
    slope_kinetic = gradient(kinetic)
    curl_vorticity = curl(vorticity)
    lamb = cross(velocity, vorticity)
    turning = cross((whole(2), whole(3), whole(4)), velocity)
    momentum = [
        lamb[k]
        - slope_kinetic[k]
        + per_rho * (lorentz[k] - slope_pressure[k])
        - turning[k]
        - viscosity * curl_vorticity[k]
        for k in range(3)
    ]
    return [rho_rate, *momentum, *curl_electric, pressure_rate]


def first_kernel(
    place_ref,
    diffusion_ref,
    wide_ref,
    north_ref,
    west_ref,
    corner_ref,
    got_ref,
    take_ref,
    rest_ref,
    coef_ref,
    pick_ref,
    mix_ref,
    spin_ref,
    flag_ref,
    middle_ref,
    out_ref,
    work_ref,
    next_ref,
):
    lane = iota((TALL, WIDE), 1)
    for plane in range(PLANES):
        group, which = plane // 16, plane % 16
        turn = (WIDE - 8 * which) % WIDE
        north = north_ref[plane // 2]
        if plane % 2:
            north = pltpu.roll(north, WIDE // 2, 1)
        corner = pltpu.roll(corner_ref[group], turn, 1)
        west = pltpu.roll(west_ref[group], turn, 1)
        north = jnp.where(lane[:8] < 16 + COLS, north, 0.0)
        work_ref[plane, :8] = jnp.where(lane[:8] < 8, corner, north)
        work_ref[plane, 8:] = jnp.where(lane[8:] < 8, west, wide_ref[plane, 8:])
    ghosts = ghost_values(got_ref, take_ref, rest_ref)
    fill_ghosts(place_ref, ghosts, work_ref, TALL)

    def load(which):
        return work_ref[which * LEVELS : (which + 1) * LEVELS].reshape(LEVELS * TALL, WIDE)

    found = rates(load, TALL, coef_ref, diffusion_ref)
    row = iota((TALL, WIDE), 0)
    inside = (lane >= 4) & (lane < 12 + COLS) & (row >= 4) & (row < 12 + ROWS)
    for which in range(FIELDS):
        value = load(which) + (0.5 * TIME_STEP) * found[which]
        for level in range(LEVELS):
            plane = which * LEVELS + level
            part = jnp.where(inside, value[level * TALL : (level + 1) * TALL], 0.0)
            next_ref[plane] = part[8:]
            middle_ref[plane] = pltpu.roll(part, TALL - 4, 0)[:MID]
    planes = next_ref[...].reshape(PLANES * MID, WIDE)
    packed = donor_message(planes, MID, pick_ref[...], mix_ref[...], spin_ref[...])
    post_message(place_ref, packed, flag_ref[...], out_ref)


def second_kernel(
    place_ref,
    diffusion_ref,
    middle_ref,
    got_ref,
    take_ref,
    rest_ref,
    coef_ref,
    state_ref,
    whole_ref,
    third_ref,
    work_ref,
):
    work_ref[...] = middle_ref[...]
    ghosts = ghost_values(got_ref, take_ref, rest_ref)
    fill_ghosts(place_ref, ghosts, work_ref, MID)

    def load(which):
        return work_ref[which * LEVELS : (which + 1) * LEVELS].reshape(LEVELS * MID, WIDE)

    found = rates(load, MID, coef_ref, diffusion_ref)

    def centre(value):
        return pltpu.roll(pltpu.roll(value, MID - 4, 0)[:ROWS], WIDE - 8, 1)[:, :COLS]

    for which in range(FIELDS):
        for level in range(LEVELS):
            rate = found[which][level * MID : (level + 1) * MID]
            held = state_ref[which, level]
            step = centre(rate * (0.5 * TIME_STEP))
            middle = centre(middle_ref[which * LEVELS + level])
            third_ref[which, level] = held + step
            whole_ref[which, level] = held + ((middle - held) + 2.0 * step) * (1.0 / 3.0)


def shift(value, move_lat, move_lon):
    pairs = []
    for a in range(LATS):
        for b in range(LONS):
            goal_a, goal_b = a + move_lat, b + move_lon
            if 0 <= goal_a < LATS and 0 <= goal_b < LONS:
                pairs.append((a * LONS + b, goal_a * LONS + goal_b))
    return lax.ppermute(value, ("lat", "lon"), pairs)


def shards(state, donor_cell, donor_weights, donor_turn, border_source, diffusion):
    fields = state[0]
    panel = lax.axis_index("panel")
    lat = lax.axis_index("lat")
    lon = lax.axis_index("lon")
    place = jnp.stack([panel, lat, lon]).astype(jnp.int32)
    f32 = jnp.float32

    def call(kernel, outs, *args, smem=0, scratch=()):
        shapes = [jax.ShapeDtypeStruct(shape, dtype) for shape, dtype in outs]
        return pl.pallas_call(
            kernel,
            out_shape=shapes,
            in_specs=[SMEM] * smem + [VMEM] * (len(args) - smem),
            out_specs=[VMEM] * len(outs),
            scratch_shapes=[pltpu.VMEM(shape, f32) for shape in scratch],
            compiler_params=PARAMS,
        )(*args)

    bf16 = jnp.bfloat16
    pairs, groups = PLANES // 2, PLANES // 16
    south, east, corner = call(
        cut_kernel,
        [((pairs, 8, WIDE), f32), ((groups, ROWS, WIDE), f32), ((groups, 8, WIDE), f32)],
        fields,
        scratch=[(PLANES, ROWS, WIDE)],
    )
    south = shift(south, -1, 0)
    east = shift(east, 0, -1)
    corner = shift(corner, -1, -1)

    ring = PANEL_COLS + 8
    row_slots = LONS * SLOTS
    border = border_source[0]
    bands = border[: 8 * ring].reshape(8, ring)
    sides = border[8 * ring :].reshape(PANEL_ROWS, 8)
    pick, mix, spin, flag = call(
        prepare_kernel,
        [((WIDE, WIDE), bf16), ((MID, WIDE), f32), ((2, WIDE), f32), ((8, WIDE), f32)],
        donor_cell[0, 0],
        donor_weights[0, 0, 0],
        donor_turn[0, 0],
        jnp.pad(bands, ((0, 0), (0, 7 * WIDE - ring)), constant_values=-1),
        sides.T,
        scratch=[(1, WIDE)],
    )
    message = ((2 * PEERS, 16, WIDE), f32)
    wide, north, west, corner, sent = call(
        donor_kernel,
        [
            ((PLANES, TALL, WIDE), f32),
            ((pairs, 8, WIDE), f32),
            ((groups, MID, WIDE), f32),
            ((groups, 8, WIDE), f32),
            message,
        ],
        place,
        fields,
        south,
        east,
        corner,
        pick,
        mix,
        spin,
        flag,
        smem=1,
        scratch=[(PLANES, ROWS, WIDE)],
    )

    def to_holders(sent):
        return lax.all_to_all(sent, ("panel", "lon"), 0, 0, tiled=True)

    got = to_holders(sent)

    crowded = jnp.maximum(got[0, 0, FLAG_LANE], got[PEERS, 0, FLAG_LANE]) > ROOM

    north = shift(north, 1, 0)
    west = shift(west, 0, 1)
    corner = shift(corner, 1, 1)
    late_lat, late_lon, bands, sides, _ = lax.optimization_barrier((lat, lon, bands, sides, sent))

    window = jnp.pad(bands, ((0, 0), (4, 4)), constant_values=-1)
    window = lax.dynamic_slice(window, (0, late_lon * COLS), (8, 64)).reshape(2, BAND)
    side = jnp.where(late_lon == 0, sides[:, :4], sides[:, 4:])
    side = jnp.where((late_lon == 0) | (late_lon == LONS - 1), side, -1)
    side = jnp.pad(side, ((8, 8), (0, 0)), constant_values=-1)
    side = jnp.concatenate(
        [
            side[:PANEL_ROWS].reshape(LATS, ROWS, 4),
            side[ROWS:].reshape(LATS, ROWS, 4),
        ],
        axis=1,
    ).reshape(LATS, SIDE)
    at_lat = jnp.arange(LATS)[:, None]
    band = jnp.where(at_lat == 0, window[:1], jnp.where(at_lat == LATS - 1, window[1:], -1))
    wanted = jnp.concatenate([band, side], axis=1)
    holder = jnp.where(wanted >= 0, wanted // row_slots, -1)
    local = wanted - late_lat * row_slots
    spot = local // SLOTS * (WIDE // 2) + local % SLOTS
    send, take, rest, coef = call(
        plan_kernel,
        [
            ((DEPTH, DEPTH), bf16),
            ((DEPTH, CHUNK), bf16),
            ((LATS, CHUNK), f32),
            ((5, TALL, WIDE), f32),
        ],
        place,
        holder,
        spot,
        smem=1,
    )

    def to_blocks(got):
        (chunks,) = call(choice_kernel, [((PEERS, 16, WIDE), f32)], place, got, send, smem=1)
        fitting = lax.all_to_all(chunks, "lat", 0, 0, tiled=True)
        got, fitting = lax.optimization_barrier((got, fitting))

        def send_rest():
            (chunks,) = call(
                rest_kernel, [((PEERS, PLANES, CHUNK), f32)], place, got, rest, smem=1
            )
            return lax.all_to_all(chunks, "lat", 0, 0, tiled=True).sum(axis=0)

        return fitting, lax.cond(crowded, send_rest, lambda: jnp.zeros((PLANES, CHUNK), f32))

    got, extra = to_blocks(got)
    middle, sent = call(
        first_kernel,
        [((PLANES, MID, WIDE), f32), message],
        place,
        diffusion,
        wide,
        north,
        west,
        corner,
        got,
        take,
        extra,
        coef,
        pick,
        mix,
        spin,
        flag,
        smem=2,
        scratch=[(PLANES, TALL, WIDE), (PLANES, MID, WIDE)],
    )
    got, extra = to_blocks(to_holders(sent))
    accumulated, section_three = call(
        second_kernel,
        [(fields.shape, f32), (fields.shape, f32)],
        place,
        diffusion,
        middle,
        got,
        take,
        extra,
        coef,
        fields,
        smem=2,
        scratch=[(PLANES, MID, WIDE)],
    )
    return (accumulated[None], section_three[None])


def solution(mesh):
    return jax.shard_map(
        shards,
        mesh=mesh,
        in_specs=(
            P("panel", None, None, "lat", "lon"),
            P("panel", "lat", "lon", None),
            P("panel", "lat", "lon", None, None),
            P("panel", "lat", "lon", None),
            P("panel", None),
            P(),
        ),
        out_specs=(P("panel", None, None, "lat", "lon"), P("panel", None, None, "lat", "lon")),
        check_vma=False,
    )
```

```python
import math

import jax
import jax.numpy as jnp
from jax import lax
from jax.experimental import pallas as pl
from jax.experimental.pallas import tpu as pltpu
from jax.sharding import PartitionSpec as P

GAMMA = 5.0 / 3.0
RADIAL_STEP = 0.65 / 32.0
FIELDS = 8
LEVELS = 4
PLANES = FIELDS * LEVELS
ROWS = 16
COLS = 48
SLOTS = 33
LATS = 16
LONS = 16
ROOM = 63
FLAG_LANE = 63
WIDE = 128
TALL = ROWS + 16
MID = ROWS + 8
BAND = 4 * 64
SIDE = 4 * TALL
CHUNK = BAND + SIDE
PEERS = 16
DEPTH = PEERS * WIDE // 2
PANEL_ROWS = ROWS * LATS
PANEL_COLS = COLS * LONS
DTHETA = 0.5 * math.pi / PANEL_ROWS
DPHI = 1.5 * math.pi / PANEL_COLS
FINEST = min(DTHETA, DPHI)
TIME_STEP = 0.1 * FINEST
RADII = [0.35 + 0.65 * (k + 16 - LEVELS // 2 + 0.5) / 32.0 for k in range(LEVELS)]
VMEM = pl.BlockSpec(memory_space=pltpu.VMEM)
SMEM = pl.BlockSpec(memory_space=pltpu.SMEM)
ANY = pl.BlockSpec(memory_space=pl.ANY)
MIB = 1024 * 1024


def iota(shape, axis):
    return lax.broadcasted_iota(jnp.int32, shape, axis)


def split_dot(left, right):
    total = None
    for _ in range(3):
        part = left.astype(jnp.bfloat16)
        left = left - part.astype(jnp.float32)
        term = jnp.dot(part, right, preferred_element_type=jnp.float32)
        total = term if total is None else total + term
    return total


def donor_message(planes, rows, pick, mix, spin):
    chosen = split_dot(planes, pick).reshape(PLANES, rows, WIDE)
    both = jnp.sum(chosen * mix[None], axis=1)
    mixed = both + pltpu.roll(both, WIDE // 2, 1)
    cosine = spin[0:1]
    sine = spin[1:2]
    at = iota((PLANES, WIDE), 0) // LEVELS
    theta = (at == 2) | (at == 5)
    phi = (at == 3) | (at == 6)
    other = jnp.where(
        theta, pltpu.roll(mixed, PLANES - LEVELS, 0), -pltpu.roll(mixed, LEVELS, 0)
    )
    turned = jnp.where(theta | phi, cosine * mixed + sine * other, mixed)
    half = PLANES // 2
    return jnp.where(iota((half, WIDE), 1) < WIDE // 2, turned[:half], turned[half:])


def post_message(place_ref, packed, flag, out_ref):
    panel = place_ref[0]
    spot = (iota((16, WIDE), 0) == 0) & (iota((16, WIDE), 1) == FLAG_LANE)
    blank = jnp.where(spot, flag[0:1], 0.0)
    packed = jnp.where(spot, blank, packed)
    out_ref[pl.ds((1 - panel) * PEERS, PEERS)] = jnp.broadcast_to(packed[None], (PEERS, 16, WIDE))
    out_ref[pl.ds(panel * PEERS, PEERS)] = jnp.broadcast_to(blank[None], (PEERS, 16, WIDE))


def cut_kernel(
    state_any, cell_any, weight_any, turn_any,
    held_ref, south_ref, east_ref, corner_ref, pick_ref, mix_ref, spin_ref,
    state_ref, cell_ref, weight_ref, turn_ref, line_ref, sems
):
    loads = [
        pltpu.make_async_copy(source, target, sems.at[which])
        for which, (source, target) in enumerate(
            [
                (state_any, state_ref),
                (cell_any, cell_ref),
                (weight_any, weight_ref),
                (turn_any, turn_ref),
            ]
        )
    ]
    for load in loads:
        load.start()
    for load in loads:
        load.wait()
    held_ref[:, :, COLS:] = jnp.zeros((PLANES, ROWS, WIDE - COLS), jnp.float32)
    for plane in range(PLANES):
        held_ref[plane, :, :COLS] = state_ref[plane // LEVELS, plane % LEVELS]
    lane = iota((ROWS, WIDE), 1)
    for pair in range(PLANES // 2):
        south_ref[pair] = pack_pair(held_ref[2 * pair, :8], held_ref[2 * pair + 1, :8])
    for group in range(2):
        columns = jnp.zeros((ROWS, WIDE), jnp.float32)
        for which in range(16):
            moved = pltpu.roll(held_ref[16 * group + which], 8 * which, 1)
            columns = jnp.where(lane // 8 == which, moved, columns)
        east_ref[group] = columns
        corner_ref[group] = columns[:8]
    donor_tables(cell_ref, weight_ref, turn_ref, pick_ref, mix_ref, spin_ref, line_ref)


def pack_pair(one, two):
    return jnp.where(iota(one.shape, 1) < WIDE // 2, one, pltpu.roll(two, WIDE // 2, 1))


def donor_tables(cell_ref, weight_ref, turn_ref, pick_ref, mix_ref, spin_ref, line_ref):
    half = WIDE // 2
    late = iota((1, WIDE), 1) >= half

    def twice(value, fill):
        line_ref[...] = jnp.full((1, WIDE), fill, jnp.float32)
        line_ref[:, :SLOTS] = value.astype(jnp.float32)
        line = line_ref[...]
        return jnp.where(late, pltpu.roll(line, half, 1), line)

    cell = twice(cell_ref[...], -10 * COLS)
    row_at = jnp.floor((cell + 0.5) * (1.0 / COLS))
    col_at = cell - row_at * COLS + jnp.where(late, 1.0, 0.0)
    upper = jnp.where(late, twice(weight_ref[1:2], 0.0), twice(weight_ref[0:1], 0.0))
    lower = jnp.where(late, twice(weight_ref[3:4], 0.0), twice(weight_ref[2:3], 0.0))
    turn = twice(turn_ref[...], 0.0)
    spin_ref[0:1] = jnp.cos(turn)
    spin_ref[1:2] = jnp.sin(turn)
    lane = iota((WIDE, WIDE), 0).astype(jnp.float32)
    real = jnp.where(row_at >= 0, col_at + 8.0, -1.0)
    pick_ref[...] = jnp.where(lane == real, 1.0, 0.0).astype(jnp.bfloat16)
    row = iota((MID, WIDE), 0).astype(jnp.float32)
    mix = jnp.where(row == row_at, upper, 0.0) + jnp.where(row == row_at + 1.0, lower, 0.0)
    mix_ref[...] = mix


def count_kernel(bands_ref, sides_ref, flag_ref):
    width = bands_ref.shape[1]
    column = iota((width, WIDE), 0) - 4
    start = iota((width, WIDE), 1) * COLS - 8
    within = (column >= start) & (column < start + 64) & (start < PANEL_COLS)
    columns = jnp.where(within, 1.0, 0.0).astype(jnp.bfloat16)
    row = iota((PANEL_ROWS, WIDE), 0)
    start = iota((PANEL_ROWS, WIDE), 1) * ROWS - 8
    within = (row >= start) & (row < start + TALL) & (start < PANEL_ROWS)
    rows = jnp.where(within, 1.0, 0.0).astype(jnp.bfloat16)

    def most(slots, windows):
        ones = []
        for which in range(LATS):
            first = which * LONS * SLOTS
            inside = (slots >= first) & (slots < first + LONS * SLOTS)
            ones.append(jnp.where(inside, 1.0, 0.0))
        ones = jnp.concatenate(ones, axis=0).astype(jnp.bfloat16)
        counts = jnp.dot(ones, windows, preferred_element_type=jnp.float32)
        return jnp.max(jnp.sum(counts.reshape(2 * LATS, 4, WIDE), axis=1))

    total = most(bands_ref[...], columns) + most(sides_ref[...], rows)
    flag_ref[...] = jnp.full(flag_ref.shape, total, jnp.float32)


def donor_kernel(
    place_ref, held_ref, south_ref, east_ref, corner_ref, pick_ref, mix_ref, spin_ref, flag_ref,
    wide_ref, north_ref, west_ref, corner_out_ref, out_ref
):
    lane = iota((ROWS, WIDE), 1)
    own = (lane >= 8) & (lane < 8 + COLS)
    beyond = (lane >= 8 + COLS) & (lane < 16 + COLS)
    for plane in range(PLANES):
        group, which = plane // 16, plane % 16
        turn = (8 + COLS - 8 * which) % WIDE
        middle = pltpu.roll(held_ref[plane], 8, 1)
        east = pltpu.roll(east_ref[group], turn, 1)
        wide_ref[plane, :8] = jnp.zeros((8, WIDE), jnp.float32)
        wide_ref[plane, 8:24] = jnp.where(own, middle, jnp.where(beyond, east, 0.0))
        south = pltpu.roll(south_ref[plane // 2], 8 + plane % 2 * (WIDE // 2), 1)
        corner = pltpu.roll(corner_ref[group], turn, 1)
        wide_ref[plane, 24:] = jnp.where(own[:8], south, jnp.where(beyond[:8], corner, 0.0))
    planes = wide_ref[:, 8:, :].reshape(PLANES * MID, WIDE)
    packed = donor_message(planes, MID, pick_ref[...], mix_ref[...], spin_ref[...])
    post_message(place_ref, packed, flag_ref[...], out_ref)
    for pair in range(PLANES // 2):
        north_ref[pair] = pack_pair(wide_ref[2 * pair, 16:24], wide_ref[2 * pair + 1, 16:24])
    lane = iota((MID, WIDE), 1)
    for group in range(2):
        columns = jnp.zeros((MID, WIDE), jnp.float32)
        for which in range(16):
            turn = (8 * which - COLS) % WIDE
            moved = pltpu.roll(wide_ref[16 * group + which, 8:], turn, 1)
            columns = jnp.where(lane // 8 == which, moved, columns)
        west_ref[group] = columns
        corner_out_ref[group] = columns[8:16]


def unpack(read):
    low = iota((16, WIDE), 1) < WIDE // 2
    tiles = []
    for pair in range(PEERS // 2):
        one = read(2 * pair)
        two = read(2 * pair + 1)
        top = jnp.where(low, one, pltpu.roll(two, WIDE // 2, 1))
        end = jnp.where(low, pltpu.roll(one, WIDE // 2, 1), two)
        tiles.append(jnp.concatenate([top, end], axis=0))
    return jnp.concatenate(tiles, axis=1)


def split_parts(held):
    parts = []
    for _ in range(3):
        part = held.astype(jnp.bfloat16)
        held = held - part.astype(jnp.float32)
        parts.append(part)
    return jnp.concatenate(parts, axis=0)


def join_parts(terms):
    return terms[:PLANES] + terms[PLANES : 2 * PLANES] + terms[2 * PLANES :]


def from_row(place_ref, got_ref):
    base = (1 - place_ref[0]) * PEERS
    return split_parts(unpack(lambda which: got_ref[base + which]))


def plan_kernel(place_ref, holder_ref, spot_ref, send_ref, take_ref, rest_ref, coef_ref):
    lat = place_ref[1]
    order = iota((CHUNK, CHUNK), 0) < iota((CHUNK, CHUNK), 1)
    order = jnp.where(order, 1.0, 0.0).astype(jnp.bfloat16)

    def ranks(chosen):
        ones = jnp.where(chosen, 1.0, 0.0).astype(jnp.bfloat16)
        return jnp.dot(ones, order, preferred_element_type=jnp.float32)

    holder = holder_ref[...]
    mine = holder == lat
    spot = spot_ref[...].astype(jnp.float32)
    rank = ranks(mine)
    rest_ref[...] = jnp.where(mine & (rank >= ROOM), spot, -1.0)
    key = jnp.where(mine & (rank < ROOM), rank, -1.0)
    half = WIDE // 2
    place_at = iota((half, CHUNK), 0).astype(jnp.float32)
    lane = iota((half, DEPTH), 1).astype(jnp.float32)
    for block in range(LATS):
        found = place_at == key[block : block + 1]
        table = jnp.sum(
            jnp.where(found, spot[block : block + 1] + 1.0, 0.0), axis=1, keepdims=True
        )
        hot = jnp.where(lane + 1.0 == table, 1.0, 0.0)
        send_ref[block * half : (block + 1) * half] = hot.astype(jnp.bfloat16)
    own = holder_ref[pl.ds(lat, 1)]
    masks = iota((PEERS, CHUNK), 0) == own
    rank = jnp.sum(jnp.where(masks, ranks(masks), 0.0), axis=0, keepdims=True)
    fits = (own >= 0) & (rank < ROOM)
    index = jnp.where(fits, own.astype(jnp.float32) * half + rank, -1.0)
    hot = iota((DEPTH, CHUNK), 0).astype(jnp.float32) == index
    take_ref[...] = jnp.where(hot, 1.0, 0.0).astype(jnp.bfloat16)
    row = (lat * ROWS - 8 + iota((TALL, WIDE), 0)).astype(jnp.float32)
    column = (place_ref[2] * COLS - 8 + iota((TALL, WIDE), 1)).astype(jnp.float32)
    colatitude = 0.25 * math.pi + (row + 0.5) * DTHETA
    longitude = -0.75 * math.pi + (column + 0.5) * DPHI
    sine, cosine = jnp.sin(colatitude), jnp.cos(colatitude)
    twirl = 2.0 * 0.25 / TIME_STEP
    yang = place_ref[0] == 1
    coef_ref[0] = sine
    coef_ref[1] = 1.0 / sine
    coef_ref[2] = twirl * jnp.where(yang, sine * jnp.sin(longitude), cosine)
    coef_ref[3] = twirl * jnp.where(yang, cosine * jnp.sin(longitude), -sine)
    coef_ref[4] = twirl * jnp.where(yang, jnp.cos(longitude), 0.0)


def choice_kernel(place_ref, got_ref, send_ref, out_ref):
    parts = from_row(place_ref, got_ref)
    terms = lax.dot_general(
        parts, send_ref[...], (((1,), (1,)), ((), ())), preferred_element_type=jnp.float32
    )
    chosen = join_parts(terms)
    low = iota((16, WIDE), 1) < WIDE // 2
    for pair in range(PEERS // 2):
        tile = chosen[:, pair * WIDE : (pair + 1) * WIDE]
        top, end = tile[:16], tile[16:]
        out_ref[2 * pair] = jnp.where(low, top, pltpu.roll(end, WIDE // 2, 1))
        out_ref[2 * pair + 1] = jnp.where(low, pltpu.roll(top, WIDE // 2, 1), end)


def rest_kernel(place_ref, got_ref, rest_ref, out_ref):
    parts = from_row(place_ref, got_ref)
    at = iota((DEPTH, CHUNK), 0).astype(jnp.float32)
    for block in range(LATS):
        hot = jnp.where(at == rest_ref[block : block + 1], 1.0, 0.0).astype(jnp.bfloat16)
        out_ref[block] = join_parts(jnp.dot(parts, hot, preferred_element_type=jnp.float32))


def ghost_values(got_ref, take_ref, rest_ref):
    parts = split_parts(unpack(lambda which: got_ref[which]))
    terms = jnp.dot(parts, take_ref[...], preferred_element_type=jnp.float32)
    return join_parts(terms) + rest_ref[...]


def fill_ghosts(place_ref, ghosts, work_ref, rows):
    lat, lon = place_ref[1], place_ref[2]
    trim = (TALL - rows) // 2
    top = 8 - trim

    @pl.when((lon == 0) | (lon == LONS - 1))
    def _():
        side = ghosts[:, BAND:]
        first = jnp.where(lon == 0, 4, 8 + COLS)
        lane = iota((rows, WIDE), 1)
        own = lane // 4 == iota((rows, WIDE), 0) + trim
        spread = jnp.where(own[None], side[:, None, :], 0.0).reshape(PLANES * rows, WIDE)
        target = iota((WIDE, WIDE), 1) - first
        hot = jnp.where(target == iota((WIDE, WIDE), 0) % 4, 1.0, 0.0).astype(jnp.bfloat16)
        moved = split_dot(spread, hot).reshape(PLANES, rows, WIDE)
        ghost = (lane >= first) & (lane < first + 4)
        work_ref[...] = jnp.where(ghost[None], moved, work_ref[...])

    @pl.when((lat == 0) | (lat == LATS - 1))
    def _():
        band = ghosts[:, :BAND]
        lines = []
        for half in range(2):
            piece = band[:, half * WIDE : (half + 1) * WIDE]
            lines += [piece, pltpu.roll(piece, WIDE // 2, 1)]

        @pl.when(lat == 0)
        def _():
            for row in range(4):
                work_ref[:, top - 4 + row, :] = lines[row]

        @pl.when(lat == LATS - 1)
        def _():
            for row in range(4):
                work_ref[:, top + ROWS + row, :] = lines[row]


def rates(load, rows, coef_ref, diffusion_ref):
    def on_levels(value, factors):
        return jnp.concatenate(
            [value[k * rows : (k + 1) * rows] * factors[k] for k in range(LEVELS)], axis=0
        )

    def whole(which):
        value = coef_ref[which]
        if rows < TALL:
            value = pltpu.roll(value, TALL - (TALL - rows) // 2, 0)[:rows]
        return jnp.concatenate([value] * LEVELS, axis=0)

    sine = whole(0)
    per_sine = whole(1)
    inverse = [1.0 / r for r in RADII]
    viscosity = diffusion_ref[0] * (FINEST * FINEST / TIME_STEP)
    resistivity = diffusion_ref[1] * (FINEST * FINEST / TIME_STEP)

    def slope(value, axis, step):
        size = value.shape[axis]
        near = pltpu.roll(value, size - 1, axis) - pltpu.roll(value, 1, axis)
        far = pltpu.roll(value, size - 2, axis) - pltpu.roll(value, 2, axis)
        return near * (8.0 / (12.0 * step)) - far * (1.0 / (12.0 * step))

    def d_theta(value):
        return slope(value, 0, DTHETA)

    def d_phi(value):
        return slope(value, 1, DPHI)

    def d_radius(value):
        part = [value[k * rows : (k + 1) * rows] for k in range(LEVELS)]
        slopes = [(part[1] - part[0]) * (1.0 / RADIAL_STEP)]
        for k in range(1, LEVELS - 1):
            slopes.append((part[k + 1] - part[k - 1]) * (1.0 / (2.0 * RADIAL_STEP)))
        slopes.append((part[-1] - part[-2]) * (1.0 / RADIAL_STEP))
        return jnp.concatenate(slopes, axis=0)

    def by_radius(value):
        return on_levels(value, RADII)

    def per_radius(value):
        return on_levels(value, inverse)

    def curl(vector):
        part_r, part_t, part_p = vector
        return (
            per_radius((d_theta(sine * part_p) - d_phi(part_t)) * per_sine),
            per_radius(d_phi(part_r) * per_sine - d_radius(by_radius(part_p))),
            per_radius(d_radius(by_radius(part_t)) - d_theta(part_r)),
        )

    def gradient(value):
        return (
            d_radius(value),
            per_radius(d_theta(value)),
            per_radius(d_phi(value) * per_sine),
        )

    def cross(left, right):
        return (
            left[1] * right[2] - left[2] * right[1],
            left[2] * right[0] - left[0] * right[2],
            left[0] * right[1] - left[1] * right[0],
        )

    def advect(vector, slopes):
        return vector[0] * slopes[0] + vector[1] * slopes[1] + vector[2] * slopes[2]

    velocity = [load(which) for which in (1, 2, 3)]
    magnetic = [load(which) for which in (4, 5, 6)]
    vorticity = curl(velocity)
    current = curl(magnetic)
    squares = [r * r for r in RADII]
    spread = on_levels(
        d_radius(on_levels(velocity[0], squares)), [1.0 / square for square in squares]
    ) + per_radius((d_theta(sine * velocity[1]) + d_phi(velocity[2])) * per_sine)
    induced = cross(velocity, magnetic)
    electric = [induced[k] - resistivity * current[k] for k in range(3)]
    kinetic = 0.5 * (
        velocity[0] * velocity[0] + velocity[1] * velocity[1] + velocity[2] * velocity[2]
    )
    curl_electric = curl(electric)
    log_rho = load(0)
    rho_rate = -advect(velocity, gradient(log_rho)) - spread
    pressure = load(7)
    slope_pressure = gradient(pressure)
    pressure_rate = -advect(velocity, slope_pressure) - GAMMA * pressure * spread
    lorentz = cross(current, magnetic)
    per_rho = jnp.exp(-log_rho)
    slope_kinetic = gradient(kinetic)
    curl_vorticity = curl(vorticity)
    lamb = cross(velocity, vorticity)
    turning = cross((whole(2), whole(3), whole(4)), velocity)
    momentum = [
        lamb[k]
        - slope_kinetic[k]
        + per_rho * (lorentz[k] - slope_pressure[k])
        - turning[k]
        - viscosity * curl_vorticity[k]
        for k in range(3)
    ]
    return [rho_rate, *momentum, *curl_electric, pressure_rate]


def first_kernel(
    place_ref,
    diffusion_ref,
    wide_ref,
    north_ref,
    west_ref,
    corner_ref,
    got_ref,
    take_ref,
    rest_ref,
    coef_ref,
    pick_ref,
    mix_ref,
    spin_ref,
    flag_ref,
    middle_ref,
    out_ref,
    work_ref,
    next_ref,
):
    lane = iota((TALL, WIDE), 1)
    for plane in range(PLANES):
        group, which = plane // 16, plane % 16
        turn = (WIDE - 8 * which) % WIDE
        north = north_ref[plane // 2]
        if plane % 2:
            north = pltpu.roll(north, WIDE // 2, 1)
        corner = pltpu.roll(corner_ref[group], turn, 1)
        west = pltpu.roll(west_ref[group], turn, 1)
        north = jnp.where(lane[:8] < 16 + COLS, north, 0.0)
        work_ref[plane, :8] = jnp.where(lane[:8] < 8, corner, north)
        work_ref[plane, 8:] = jnp.where(lane[8:] < 8, west, wide_ref[plane, 8:])
    ghosts = ghost_values(got_ref, take_ref, rest_ref)
    fill_ghosts(place_ref, ghosts, work_ref, TALL)

    def load(which):
        return work_ref[which * LEVELS : (which + 1) * LEVELS].reshape(LEVELS * TALL, WIDE)

    found = rates(load, TALL, coef_ref, diffusion_ref)
    row = iota((TALL, WIDE), 0)
    inside = (lane >= 4) & (lane < 12 + COLS) & (row >= 4) & (row < 12 + ROWS)
    for which in range(FIELDS):
        value = load(which) + (0.5 * TIME_STEP) * found[which]
        for level in range(LEVELS):
            plane = which * LEVELS + level
            part = jnp.where(inside, value[level * TALL : (level + 1) * TALL], 0.0)
            next_ref[plane] = part[8:]
            middle_ref[plane] = pltpu.roll(part, TALL - 4, 0)[:MID]
    planes = next_ref[...].reshape(PLANES * MID, WIDE)
    packed = donor_message(planes, MID, pick_ref[...], mix_ref[...], spin_ref[...])
    post_message(place_ref, packed, flag_ref[...], out_ref)


def second_kernel(
    place_ref,
    diffusion_ref,
    middle_ref,
    got_ref,
    take_ref,
    rest_ref,
    coef_ref,
    state_ref,
    whole_ref,
    third_ref,
    work_ref,
):
    work_ref[...] = middle_ref[...]
    ghosts = ghost_values(got_ref, take_ref, rest_ref)
    fill_ghosts(place_ref, ghosts, work_ref, MID)

    def load(which):
        return work_ref[which * LEVELS : (which + 1) * LEVELS].reshape(LEVELS * MID, WIDE)

    found = rates(load, MID, coef_ref, diffusion_ref)

    def centre(value):
        return pltpu.roll(pltpu.roll(value, MID - 4, 0)[:ROWS], WIDE - 8, 1)[:, :COLS]

    for which in range(FIELDS):
        for level in range(LEVELS):
            rate = found[which][level * MID : (level + 1) * MID]
            held = state_ref[which, level]
            step = centre(rate * (0.5 * TIME_STEP))
            middle = centre(middle_ref[which * LEVELS + level])
            third_ref[which, level] = held + step
            whole_ref[which, level] = held + ((middle - held) + 2.0 * step) * (1.0 / 3.0)


def shift(value, move_lat, move_lon):
    pairs = []
    for a in range(LATS):
        for b in range(LONS):
            goal_a, goal_b = a + move_lat, b + move_lon
            if 0 <= goal_a < LATS and 0 <= goal_b < LONS:
                pairs.append((a * LONS + b, goal_a * LONS + goal_b))
    return lax.ppermute(value, ("lat", "lon"), pairs)


def shards(state, donor_cell, donor_weights, donor_turn, border_source, diffusion):
    fields = state[0]
    panel = lax.axis_index("panel")
    lat = lax.axis_index("lat")
    lon = lax.axis_index("lon")
    place = jnp.stack([panel, lat, lon]).astype(jnp.int32)
    f32 = jnp.float32

    def call(kernel, outs, *args, smem=0, specs=None, scratch=(), limit=10):
        shapes = [jax.ShapeDtypeStruct(shape, dtype) for shape, dtype in outs]
        return pl.pallas_call(
            kernel,
            out_shape=shapes,
            in_specs=specs or [SMEM] * smem + [VMEM] * (len(args) - smem),
            out_specs=[VMEM] * len(outs),
            scratch_shapes=scratch,
            compiler_params=pltpu.CompilerParams(vmem_limit_bytes=limit * MIB),
        )(*args)

    bf16 = jnp.bfloat16
    pairs, groups = PLANES // 2, PLANES // 16
    held, south, east, corner, pick, mix, spin = call(
        cut_kernel,
        [
            ((PLANES, ROWS, WIDE), f32),
            ((pairs, 8, WIDE), f32),
            ((groups, ROWS, WIDE), f32),
            ((groups, 8, WIDE), f32),
            ((WIDE, WIDE), bf16),
            ((MID, WIDE), f32),
            ((2, WIDE), f32),
        ],
        fields,
        donor_cell[0, 0],
        donor_weights[0, 0, 0],
        donor_turn[0, 0],
        specs=[ANY] * 4,
        scratch=[
            pltpu.VMEM(fields.shape, f32),
            pltpu.VMEM((1, SLOTS), jnp.int32),
            pltpu.VMEM((4, SLOTS), f32),
            pltpu.VMEM((1, SLOTS), f32),
            pltpu.VMEM((1, WIDE), f32),
            pltpu.SemaphoreType.DMA((4,)),
        ],
    )
    south = shift(south, -1, 0)
    east = shift(east, 0, -1)
    corner = shift(corner, -1, -1)

    ring = PANEL_COLS + 8
    row_slots = LONS * SLOTS
    border = border_source[0]
    bands = border[: 8 * ring].reshape(8, ring)
    sides = border[8 * ring :].reshape(PANEL_ROWS, 8)
    (flag,) = call(
        count_kernel,
        [((8, WIDE), f32)],
        jnp.pad(bands, ((0, 0), (0, 7 * WIDE - ring)), constant_values=-1),
        sides.T,
    )
    message = ((2 * PEERS, 16, WIDE), f32)
    wide, north, west, corner, sent = call(
        donor_kernel,
        [
            ((PLANES, TALL, WIDE), f32),
            ((pairs, 8, WIDE), f32),
            ((groups, MID, WIDE), f32),
            ((groups, 8, WIDE), f32),
            message,
        ],
        place,
        held,
        south,
        east,
        corner,
        pick,
        mix,
        spin,
        flag,
        smem=1,
    )

    def to_holders(sent):
        return lax.all_to_all(sent, ("panel", "lon"), 0, 0, tiled=True)

    got = to_holders(sent)

    crowded = jnp.maximum(got[0, 0, FLAG_LANE], got[PEERS, 0, FLAG_LANE]) > ROOM

    north = shift(north, 1, 0)
    west = shift(west, 0, 1)
    corner = shift(corner, 1, 1)
    late_lat, late_lon, bands, sides, _ = lax.optimization_barrier((lat, lon, bands, sides, sent))

    window = jnp.pad(bands, ((0, 0), (4, 4)), constant_values=-1)
    window = lax.dynamic_slice(window, (0, late_lon * COLS), (8, 64)).reshape(2, BAND)
    side = jnp.where(late_lon == 0, sides[:, :4], sides[:, 4:])
    side = jnp.where((late_lon == 0) | (late_lon == LONS - 1), side, -1)
    side = jnp.pad(side, ((8, 8), (0, 0)), constant_values=-1)
    side = jnp.concatenate(
        [
            side[:PANEL_ROWS].reshape(LATS, ROWS, 4),
            side[ROWS:].reshape(LATS, ROWS, 4),
        ],
        axis=1,
    ).reshape(LATS, SIDE)
    at_lat = jnp.arange(LATS)[:, None]
    band = jnp.where(at_lat == 0, window[:1], jnp.where(at_lat == LATS - 1, window[1:], -1))
    wanted = jnp.concatenate([band, side], axis=1)
    holder = jnp.where(wanted >= 0, wanted // row_slots, -1)
    local = wanted - late_lat * row_slots
    spot = local // SLOTS * (WIDE // 2) + local % SLOTS
    send, take, rest, coef = call(
        plan_kernel,
        [
            ((DEPTH, DEPTH), bf16),
            ((DEPTH, CHUNK), bf16),
            ((LATS, CHUNK), f32),
            ((5, TALL, WIDE), f32),
        ],
        place,
        holder,
        spot,
        smem=1,
        limit=16,
    )

    def to_blocks(got):
        (chunks,) = call(choice_kernel, [((PEERS, 16, WIDE), f32)], place, got, send, smem=1)
        fitting = lax.all_to_all(chunks, "lat", 0, 0, tiled=True)
        got, fitting = lax.optimization_barrier((got, fitting))

        def send_rest():
            (chunks,) = call(
                rest_kernel, [((PEERS, PLANES, CHUNK), f32)], place, got, rest, smem=1, limit=16
            )
            return lax.all_to_all(chunks, "lat", 0, 0, tiled=True).sum(axis=0)

        return fitting, lax.cond(crowded, send_rest, lambda: jnp.zeros((PLANES, CHUNK), f32))

    got, north, west, corner = lax.optimization_barrier((got, north, west, corner))
    got, extra = to_blocks(got)
    middle, sent = call(
        first_kernel,
        [((PLANES, MID, WIDE), f32), message],
        place,
        diffusion,
        wide,
        north,
        west,
        corner,
        got,
        take,
        extra,
        coef,
        pick,
        mix,
        spin,
        flag,
        smem=2,
        scratch=[pltpu.VMEM((PLANES, TALL, WIDE), f32), pltpu.VMEM((PLANES, MID, WIDE), f32)],
    )
    got, extra = to_blocks(to_holders(sent))
    accumulated, section_three = call(
        second_kernel,
        [(fields.shape, f32), (fields.shape, f32)],
        place,
        diffusion,
        middle,
        got,
        take,
        extra,
        coef,
        fields,
        smem=2,
        scratch=[pltpu.VMEM((PLANES, MID, WIDE), f32)],
    )
    return (accumulated[None], section_three[None])


def solution(mesh):
    return jax.shard_map(
        shards,
        mesh=mesh,
        in_specs=(
            P("panel", None, None, "lat", "lon"),
            P("panel", "lat", "lon", None),
            P("panel", "lat", "lon", None, None),
            P("panel", "lat", "lon", None),
            P("panel", None),
            P(),
        ),
        out_specs=(P("panel", None, None, "lat", "lon"), P("panel", None, None, "lat", "lon")),
        check_vma=False,
    )
```

```python
import math

import jax
import jax.numpy as jnp
from jax import lax
from jax.experimental import pallas as pl
from jax.experimental.pallas import tpu as pltpu
from jax.sharding import PartitionSpec as P

GAMMA = 5.0 / 3.0
RADIAL_STEP = 0.65 / 32.0
FIELDS = 8
LEVELS = 4
PLANES = FIELDS * LEVELS
ROWS = 16
COLS = 48
SLOTS = 33
LATS = 16
LONS = 16
ROOM = 63
FLAG_LANE = 63
WIDE = 128
TALL = ROWS + 16
MID = ROWS + 8
BAND = 4 * 64
SIDE = 4 * TALL
CHUNK = BAND + SIDE
PEERS = 16
DEPTH = PEERS * WIDE // 2
PANEL_ROWS = ROWS * LATS
PANEL_COLS = COLS * LONS
DTHETA = 0.5 * math.pi / PANEL_ROWS
DPHI = 1.5 * math.pi / PANEL_COLS
FINEST = min(DTHETA, DPHI)
TIME_STEP = 0.1 * FINEST
RADII = [0.35 + 0.65 * (k + 16 - LEVELS // 2 + 0.5) / 32.0 for k in range(LEVELS)]
VMEM = pl.BlockSpec(memory_space=pltpu.VMEM)
SMEM = pl.BlockSpec(memory_space=pltpu.SMEM)
HBM = pl.BlockSpec(memory_space=pltpu.HBM)
MIB = 1024 * 1024


def iota(shape, axis):
    return lax.broadcasted_iota(jnp.int32, shape, axis)


def split_dot(left, right):
    total = None
    for _ in range(3):
        part = left.astype(jnp.bfloat16)
        left = left - part.astype(jnp.float32)
        term = jnp.dot(part, right, preferred_element_type=jnp.float32)
        total = term if total is None else total + term
    return total


def donor_message(planes, rows, pick, mix, spin):
    chosen = split_dot(planes, pick).reshape(PLANES, rows, WIDE)
    both = jnp.sum(chosen * mix[None], axis=1)
    mixed = both + pltpu.roll(both, WIDE // 2, 1)
    cosine = spin[0:1]
    sine = spin[1:2]
    at = iota((PLANES, WIDE), 0) // LEVELS
    theta = (at == 2) | (at == 5)
    phi = (at == 3) | (at == 6)
    other = jnp.where(
        theta, pltpu.roll(mixed, PLANES - LEVELS, 0), -pltpu.roll(mixed, LEVELS, 0)
    )
    turned = jnp.where(theta | phi, cosine * mixed + sine * other, mixed)
    half = PLANES // 2
    return jnp.where(iota((half, WIDE), 1) < WIDE // 2, turned[:half], turned[half:])


def post_message(place_ref, packed, flag, out_ref):
    panel = place_ref[0]
    spot = (iota((16, WIDE), 0) == 0) & (iota((16, WIDE), 1) == FLAG_LANE)
    blank = jnp.where(spot, flag[0:1], 0.0)
    packed = jnp.where(spot, blank, packed)
    out_ref[pl.ds((1 - panel) * PEERS, PEERS)] = jnp.broadcast_to(packed[None], (PEERS, 16, WIDE))
    out_ref[pl.ds(panel * PEERS, PEERS)] = jnp.broadcast_to(blank[None], (PEERS, 16, WIDE))


def fetch(sources, targets, sems):
    loads = [
        pltpu.make_async_copy(source, target, sems.at[which])
        for which, (source, target) in enumerate(zip(sources, targets))
    ]
    for load in loads:
        load.start()
    for load in loads:
        load.wait()


def cut_kernel(state_ref, held_ref, south_ref, east_ref, corner_ref):
    held_ref[:, :, COLS:] = jnp.zeros((PLANES, ROWS, WIDE - COLS), jnp.float32)
    for plane in range(PLANES):
        held_ref[plane, :, :COLS] = state_ref[plane // LEVELS, plane % LEVELS]
    lane = iota((ROWS, WIDE), 1)
    for pair in range(PLANES // 2):
        south_ref[pair] = pack_pair(held_ref[2 * pair, :8], held_ref[2 * pair + 1, :8])
    for group in range(2):
        columns = jnp.zeros((ROWS, WIDE), jnp.float32)
        for which in range(16):
            moved = pltpu.roll(held_ref[16 * group + which], 8 * which, 1)
            columns = jnp.where(lane // 8 == which, moved, columns)
        east_ref[group] = columns
        corner_ref[group] = columns[:8]


def pack_pair(one, two):
    return jnp.where(iota(one.shape, 1) < WIDE // 2, one, pltpu.roll(two, WIDE // 2, 1))


def donor_tables(donor_ref, pick_ref, mix_ref, spin_ref, line_ref):
    half = WIDE // 2
    late = iota((1, WIDE), 1) >= half

    def twice(value, fill):
        line_ref[...] = jnp.full((1, WIDE), fill, jnp.float32)
        line_ref[:, :SLOTS] = value
        line = line_ref[...]
        return jnp.where(late, pltpu.roll(line, half, 1), line)

    cell = twice(donor_ref[0:1], -10.0 * COLS)
    row_at = jnp.floor((cell + 0.5) * (1.0 / COLS))
    col_at = cell - row_at * COLS + jnp.where(late, 1.0, 0.0)
    upper = jnp.where(late, twice(donor_ref[2:3], 0.0), twice(donor_ref[1:2], 0.0))
    lower = jnp.where(late, twice(donor_ref[4:5], 0.0), twice(donor_ref[3:4], 0.0))
    turn = twice(donor_ref[5:6], 0.0)
    spin_ref[0:1] = jnp.cos(turn)
    spin_ref[1:2] = jnp.sin(turn)
    lane = iota((WIDE, WIDE), 0).astype(jnp.float32)
    real = jnp.where(row_at >= 0, col_at + 8.0, -1.0)
    pick_ref[...] = jnp.where(lane == real, 1.0, 0.0).astype(jnp.bfloat16)
    row = iota((MID, WIDE), 0).astype(jnp.float32)
    mix = jnp.where(row == row_at, upper, 0.0) + jnp.where(row == row_at + 1.0, lower, 0.0)
    mix_ref[...] = mix


def prepare_kernel(
    donor_ref, bands_ref, sides_ref, pick_ref, mix_ref, spin_ref, flag_ref, line_ref
):
    donor_tables(donor_ref, pick_ref, mix_ref, spin_ref, line_ref)
    width = bands_ref.shape[1]
    column = iota((width, WIDE), 0) - 4
    start = iota((width, WIDE), 1) * COLS - 8
    within = (column >= start) & (column < start + 64) & (start < PANEL_COLS)
    columns = jnp.where(within, 1.0, 0.0).astype(jnp.bfloat16)
    row = iota((PANEL_ROWS, WIDE), 0)
    start = iota((PANEL_ROWS, WIDE), 1) * ROWS - 8
    within = (row >= start) & (row < start + TALL) & (start < PANEL_ROWS)
    rows = jnp.where(within, 1.0, 0.0).astype(jnp.bfloat16)

    def most(slots, windows):
        ones = []
        for which in range(LATS):
            first = which * LONS * SLOTS
            inside = (slots >= first) & (slots < first + LONS * SLOTS)
            ones.append(jnp.where(inside, 1.0, 0.0))
        ones = jnp.concatenate(ones, axis=0).astype(jnp.bfloat16)
        counts = jnp.dot(ones, windows, preferred_element_type=jnp.float32)
        return jnp.max(jnp.sum(counts.reshape(2 * LATS, 4, WIDE), axis=1))

    total = most(bands_ref[...], columns) + most(sides_ref[...], rows)
    flag_ref[...] = jnp.full(flag_ref.shape, total, jnp.float32)


def donor_kernel(
    place_ref, held_ref, south_ref, east_ref, corner_ref, pick_ref, mix_ref, spin_ref, flag_ref,
    wide_ref, north_ref, west_ref, out_ref
):
    lane = iota((ROWS, WIDE), 1)
    own = (lane >= 8) & (lane < 8 + COLS)
    beyond = (lane >= 8 + COLS) & (lane < 16 + COLS)
    for plane in range(PLANES):
        group, which = plane // 16, plane % 16
        turn = (8 + COLS - 8 * which) % WIDE
        middle = pltpu.roll(held_ref[plane], 8, 1)
        east = pltpu.roll(east_ref[group], turn, 1)
        wide_ref[plane, :8] = jnp.zeros((8, WIDE), jnp.float32)
        wide_ref[plane, 8:24] = jnp.where(own, middle, jnp.where(beyond, east, 0.0))
        south = pltpu.roll(south_ref[plane // 2], 8 + plane % 2 * (WIDE // 2), 1)
        corner = pltpu.roll(corner_ref[group], turn, 1)
        wide_ref[plane, 24:] = jnp.where(own[:8], south, jnp.where(beyond[:8], corner, 0.0))
    planes = wide_ref[:, 8:, :].reshape(PLANES * MID, WIDE)
    packed = donor_message(planes, MID, pick_ref[...], mix_ref[...], spin_ref[...])
    post_message(place_ref, packed, flag_ref[...], out_ref)
    for pair in range(PLANES // 2):
        north_ref[pair] = pack_pair(wide_ref[2 * pair, 16:24], wide_ref[2 * pair + 1, 16:24])
    lane = iota((MID, WIDE), 1)
    for group in range(2):
        columns = jnp.zeros((MID, WIDE), jnp.float32)
        for which in range(16):
            turn = (8 * which - COLS) % WIDE
            moved = pltpu.roll(wide_ref[16 * group + which, 8:], turn, 1)
            columns = jnp.where(lane // 8 == which, moved, columns)
        west_ref[group] = columns


def unpack(read):
    low = iota((16, WIDE), 1) < WIDE // 2
    tiles = []
    for pair in range(PEERS // 2):
        one = read(2 * pair)
        two = read(2 * pair + 1)
        top = jnp.where(low, one, pltpu.roll(two, WIDE // 2, 1))
        end = jnp.where(low, pltpu.roll(one, WIDE // 2, 1), two)
        tiles.append(jnp.concatenate([top, end], axis=0))
    return jnp.concatenate(tiles, axis=1)


def split_parts(held):
    parts = []
    for _ in range(3):
        part = held.astype(jnp.bfloat16)
        held = held - part.astype(jnp.float32)
        parts.append(part)
    return jnp.concatenate(parts, axis=0)


def join_parts(terms):
    return terms[:PLANES] + terms[PLANES : 2 * PLANES] + terms[2 * PLANES :]


def from_row(place_ref, got_ref):
    base = (1 - place_ref[0]) * PEERS
    return split_parts(unpack(lambda which: got_ref[base + which]))


def rank_of(chosen):
    order = iota((CHUNK, CHUNK), 0) < iota((CHUNK, CHUNK), 1)
    order = jnp.where(order, 1.0, 0.0).astype(jnp.bfloat16)
    ones = jnp.where(chosen, 1.0, 0.0).astype(jnp.bfloat16)
    return jnp.dot(ones, order, preferred_element_type=jnp.float32)


def send_kernel(place_ref, holder_ref, spot_ref, send_ref, rest_ref):
    mine = holder_ref[...] == place_ref[1]
    spot = spot_ref[...].astype(jnp.float32)
    rank = rank_of(mine)
    rest_ref[...] = jnp.where(mine & (rank >= ROOM), spot, -1.0)
    key = jnp.where(mine & (rank < ROOM), rank, -1.0)
    half = WIDE // 2
    place_at = iota((half, CHUNK), 0).astype(jnp.float32)
    lane = iota((half, DEPTH), 1).astype(jnp.float32)
    for block in range(LATS):
        found = place_at == key[block : block + 1]
        table = jnp.sum(
            jnp.where(found, spot[block : block + 1] + 1.0, 0.0), axis=1, keepdims=True
        )
        hot = jnp.where(lane + 1.0 == table, 1.0, 0.0)
        send_ref[block * half : (block + 1) * half] = hot.astype(jnp.bfloat16)


def take_kernel(place_ref, holder_ref, take_ref, coef_ref):
    lat = place_ref[1]
    own = holder_ref[pl.ds(lat, 1)]
    masks = iota((PEERS, CHUNK), 0) == own
    rank = jnp.sum(jnp.where(masks, rank_of(masks), 0.0), axis=0, keepdims=True)
    fits = (own >= 0) & (rank < ROOM)
    index = jnp.where(fits, own.astype(jnp.float32) * (WIDE // 2) + rank, -1.0)
    hot = iota((DEPTH, CHUNK), 0).astype(jnp.float32) == index
    take_ref[...] = jnp.where(hot, 1.0, 0.0).astype(jnp.bfloat16)
    row = (lat * ROWS - 8 + iota((TALL, WIDE), 0)).astype(jnp.float32)
    column = (place_ref[2] * COLS - 8 + iota((TALL, WIDE), 1)).astype(jnp.float32)
    colatitude = 0.25 * math.pi + (row + 0.5) * DTHETA
    longitude = -0.75 * math.pi + (column + 0.5) * DPHI
    sine, cosine = jnp.sin(colatitude), jnp.cos(colatitude)
    twirl = 2.0 * 0.25 / TIME_STEP
    yang = place_ref[0] == 1
    coef_ref[0] = sine
    coef_ref[1] = 1.0 / sine
    coef_ref[2] = twirl * jnp.where(yang, sine * jnp.sin(longitude), cosine)
    coef_ref[3] = twirl * jnp.where(yang, cosine * jnp.sin(longitude), -sine)
    coef_ref[4] = twirl * jnp.where(yang, jnp.cos(longitude), 0.0)


def widen_kernel(place_ref, got_ref, send_ref, north_ref, west_ref, out_ref, edge_ref):
    lane = iota((8, WIDE), 1)
    half = WIDE // 2
    for pair in range(PLANES // 2):
        group, which = pair // 8, 2 * pair % 16
        rows = west_ref[group, 8:16]
        one = pltpu.roll(rows, (WIDE - 8 * which) % WIDE, 1)
        two = pltpu.roll(rows, (half - 8 * which - 8) % WIDE, 1)
        edge = jnp.where(lane < 8, one, north_ref[pair])
        edge_ref[pair] = jnp.where((lane >= half) & (lane < half + 8), two, edge)
    choice_kernel(place_ref, got_ref, send_ref, out_ref)


def choice_kernel(place_ref, got_ref, send_ref, out_ref):
    parts = from_row(place_ref, got_ref)
    terms = lax.dot_general(
        parts, send_ref[...], (((1,), (1,)), ((), ())), preferred_element_type=jnp.float32
    )
    chosen = join_parts(terms)
    low = iota((16, WIDE), 1) < WIDE // 2
    for pair in range(PEERS // 2):
        tile = chosen[:, pair * WIDE : (pair + 1) * WIDE]
        top, end = tile[:16], tile[16:]
        out_ref[2 * pair] = jnp.where(low, top, pltpu.roll(end, WIDE // 2, 1))
        out_ref[2 * pair + 1] = jnp.where(low, pltpu.roll(top, WIDE // 2, 1), end)


def rest_kernel(place_ref, got_ref, rest_ref, out_ref):
    parts = from_row(place_ref, got_ref)
    at = iota((DEPTH, CHUNK), 0).astype(jnp.float32)
    for block in range(LATS):
        hot = jnp.where(at == rest_ref[block : block + 1], 1.0, 0.0).astype(jnp.bfloat16)
        out_ref[block] = join_parts(jnp.dot(parts, hot, preferred_element_type=jnp.float32))


def ghost_values(got_ref, take_ref, rest_ref):
    parts = split_parts(unpack(lambda which: got_ref[which]))
    terms = jnp.dot(parts, take_ref[...], preferred_element_type=jnp.float32)
    return join_parts(terms) + rest_ref[...]


def fill_ghosts(place_ref, ghosts, work_ref, rows):
    lat, lon = place_ref[1], place_ref[2]
    trim = (TALL - rows) // 2
    top = 8 - trim

    @pl.when((lon == 0) | (lon == LONS - 1))
    def _():
        side = ghosts[:, BAND:]
        first = jnp.where(lon == 0, 4, 8 + COLS)
        lane = iota((rows, WIDE), 1)
        own = lane // 4 == iota((rows, WIDE), 0) + trim
        spread = jnp.where(own[None], side[:, None, :], 0.0).reshape(PLANES * rows, WIDE)
        target = iota((WIDE, WIDE), 1) - first
        hot = jnp.where(target == iota((WIDE, WIDE), 0) % 4, 1.0, 0.0).astype(jnp.bfloat16)
        moved = split_dot(spread, hot).reshape(PLANES, rows, WIDE)
        ghost = (lane >= first) & (lane < first + 4)
        work_ref[...] = jnp.where(ghost[None], moved, work_ref[...])

    @pl.when((lat == 0) | (lat == LATS - 1))
    def _():
        band = ghosts[:, :BAND]
        lines = []
        for half in range(2):
            piece = band[:, half * WIDE : (half + 1) * WIDE]
            lines += [piece, pltpu.roll(piece, WIDE // 2, 1)]

        @pl.when(lat == 0)
        def _():
            for row in range(4):
                work_ref[:, top - 4 + row, :] = lines[row]

        @pl.when(lat == LATS - 1)
        def _():
            for row in range(4):
                work_ref[:, top + ROWS + row, :] = lines[row]


def rates(load, rows, coef_ref, diffusion_ref):
    def on_levels(value, factors):
        return jnp.concatenate(
            [value[k * rows : (k + 1) * rows] * factors[k] for k in range(LEVELS)], axis=0
        )

    def whole(which):
        value = coef_ref[which]
        if rows < TALL:
            value = pltpu.roll(value, TALL - (TALL - rows) // 2, 0)[:rows]
        return jnp.concatenate([value] * LEVELS, axis=0)

    sine = whole(0)
    per_sine = whole(1)
    inverse = [1.0 / r for r in RADII]
    viscosity = diffusion_ref[0] * (FINEST * FINEST / TIME_STEP)
    resistivity = diffusion_ref[1] * (FINEST * FINEST / TIME_STEP)

    def slope(value, axis, step):
        size = value.shape[axis]
        near = pltpu.roll(value, size - 1, axis) - pltpu.roll(value, 1, axis)
        far = pltpu.roll(value, size - 2, axis) - pltpu.roll(value, 2, axis)
        return near * (8.0 / (12.0 * step)) - far * (1.0 / (12.0 * step))

    def d_theta(value):
        return slope(value, 0, DTHETA)

    def d_phi(value):
        return slope(value, 1, DPHI)

    def d_radius(value):
        part = [value[k * rows : (k + 1) * rows] for k in range(LEVELS)]
        slopes = [(part[1] - part[0]) * (1.0 / RADIAL_STEP)]
        for k in range(1, LEVELS - 1):
            slopes.append((part[k + 1] - part[k - 1]) * (1.0 / (2.0 * RADIAL_STEP)))
        slopes.append((part[-1] - part[-2]) * (1.0 / RADIAL_STEP))
        return jnp.concatenate(slopes, axis=0)

    def by_radius(value):
        return on_levels(value, RADII)

    def per_radius(value):
        return on_levels(value, inverse)

    def curl(vector):
        part_r, part_t, part_p = vector
        return (
            per_radius((d_theta(sine * part_p) - d_phi(part_t)) * per_sine),
            per_radius(d_phi(part_r) * per_sine - d_radius(by_radius(part_p))),
            per_radius(d_radius(by_radius(part_t)) - d_theta(part_r)),
        )

    def gradient(value):
        return (
            d_radius(value),
            per_radius(d_theta(value)),
            per_radius(d_phi(value) * per_sine),
        )

    def cross(left, right):
        return (
            left[1] * right[2] - left[2] * right[1],
            left[2] * right[0] - left[0] * right[2],
            left[0] * right[1] - left[1] * right[0],
        )

    def advect(vector, slopes):
        return vector[0] * slopes[0] + vector[1] * slopes[1] + vector[2] * slopes[2]

    velocity = [load(which) for which in (1, 2, 3)]
    magnetic = [load(which) for which in (4, 5, 6)]
    vorticity = curl(velocity)
    current = curl(magnetic)
    squares = [r * r for r in RADII]
    spread = on_levels(
        d_radius(on_levels(velocity[0], squares)), [1.0 / square for square in squares]
    ) + per_radius((d_theta(sine * velocity[1]) + d_phi(velocity[2])) * per_sine)
    induced = cross(velocity, magnetic)
    electric = [induced[k] - resistivity * current[k] for k in range(3)]
    kinetic = 0.5 * (
        velocity[0] * velocity[0] + velocity[1] * velocity[1] + velocity[2] * velocity[2]
    )
    curl_electric = curl(electric)
    log_rho = load(0)
    rho_rate = -advect(velocity, gradient(log_rho)) - spread
    pressure = load(7)
    slope_pressure = gradient(pressure)
    pressure_rate = -advect(velocity, slope_pressure) - GAMMA * pressure * spread
    lorentz = cross(current, magnetic)
    per_rho = jnp.exp(-log_rho)
    slope_kinetic = gradient(kinetic)
    curl_vorticity = curl(vorticity)
    lamb = cross(velocity, vorticity)
    turning = cross((whole(2), whole(3), whole(4)), velocity)
    momentum = [
        lamb[k]
        - slope_kinetic[k]
        + per_rho * (lorentz[k] - slope_pressure[k])
        - turning[k]
        - viscosity * curl_vorticity[k]
        for k in range(3)
    ]
    return [rho_rate, *momentum, *curl_electric, pressure_rate]


def first_kernel(
    place_ref,
    diffusion_ref,
    wide_any,
    north_any,
    west_any,
    got_any,
    take_any,
    rest_any,
    coef_any,
    pick_any,
    mix_any,
    spin_any,
    middle_ref,
    out_ref,
    wide_ref,
    north_ref,
    west_ref,
    got_ref,
    take_ref,
    rest_ref,
    coef_ref,
    pick_ref,
    mix_ref,
    spin_ref,
    work_ref,
    next_ref,
    sems,
):
    fetch(
        (wide_any, north_any, west_any, got_any, take_any, rest_any, coef_any)
        + (pick_any, mix_any, spin_any),
        (wide_ref, north_ref, west_ref, got_ref, take_ref, rest_ref, coef_ref)
        + (pick_ref, mix_ref, spin_ref),
        sems,
    )
    lane = iota((TALL, WIDE), 1)
    for plane in range(PLANES):
        group, which = plane // 16, plane % 16
        north = north_ref[plane // 2]
        if plane % 2:
            north = pltpu.roll(north, WIDE // 2, 1)
        west = pltpu.roll(west_ref[group], (WIDE - 8 * which) % WIDE, 1)
        work_ref[plane, :8] = jnp.where(lane[:8] < 16 + COLS, north, 0.0)
        work_ref[plane, 8:] = jnp.where(lane[8:] < 8, west, wide_ref[plane, 8:])
    ghosts = ghost_values(got_ref, take_ref, rest_ref)
    fill_ghosts(place_ref, ghosts, work_ref, TALL)

    def load(which):
        return work_ref[which * LEVELS : (which + 1) * LEVELS].reshape(LEVELS * TALL, WIDE)

    found = rates(load, TALL, coef_ref, diffusion_ref)
    row = iota((TALL, WIDE), 0)
    inside = (lane >= 4) & (lane < 12 + COLS) & (row >= 4) & (row < 12 + ROWS)
    for which in range(FIELDS):
        value = load(which) + (0.5 * TIME_STEP) * found[which]
        for level in range(LEVELS):
            plane = which * LEVELS + level
            part = jnp.where(inside, value[level * TALL : (level + 1) * TALL], 0.0)
            next_ref[plane] = part[8:]
            middle_ref[plane] = pltpu.roll(part, TALL - 4, 0)[:MID]
    planes = next_ref[...].reshape(PLANES * MID, WIDE)
    packed = donor_message(planes, MID, pick_ref[...], mix_ref[...], spin_ref[...])
    out_ref[...] = packed


def second_kernel(
    place_ref,
    diffusion_ref,
    middle_ref,
    got_ref,
    take_ref,
    rest_ref,
    coef_ref,
    state_ref,
    whole_ref,
    third_ref,
    work_ref,
):
    work_ref[...] = middle_ref[...]
    ghosts = ghost_values(got_ref, take_ref, rest_ref)
    fill_ghosts(place_ref, ghosts, work_ref, MID)

    def load(which):
        return work_ref[which * LEVELS : (which + 1) * LEVELS].reshape(LEVELS * MID, WIDE)

    found = rates(load, MID, coef_ref, diffusion_ref)

    def centre(value):
        return pltpu.roll(pltpu.roll(value, MID - 4, 0)[:ROWS], WIDE - 8, 1)[:, :COLS]

    for which in range(FIELDS):
        for level in range(LEVELS):
            rate = found[which][level * MID : (level + 1) * MID]
            held = state_ref[which, level]
            step = centre(rate * (0.5 * TIME_STEP))
            middle = centre(middle_ref[which * LEVELS + level])
            third_ref[which, level] = held + step
            whole_ref[which, level] = held + ((middle - held) + 2.0 * step) * (1.0 / 3.0)


def shift(value, move_lat, move_lon):
    pairs = []
    for a in range(LATS):
        for b in range(LONS):
            goal_a, goal_b = a + move_lat, b + move_lon
            if 0 <= goal_a < LATS and 0 <= goal_b < LONS:
                pairs.append((a * LONS + b, goal_a * LONS + goal_b))
    return lax.ppermute(value, ("lat", "lon"), pairs)


def shards(state, donor_cell, donor_weights, donor_turn, border_source, diffusion):
    fields = state[0]
    panel = lax.axis_index("panel")
    lat = lax.axis_index("lat")
    lon = lax.axis_index("lon")
    place = jnp.stack([panel, lat, lon]).astype(jnp.int32)
    f32 = jnp.float32

    def call(kernel, outs, *args, smem=0, specs=None, scratch=(), limit=10):
        shapes = [jax.ShapeDtypeStruct(shape, dtype) for shape, dtype in outs]
        return pl.pallas_call(
            kernel,
            out_shape=shapes,
            in_specs=specs or [SMEM] * smem + [VMEM] * (len(args) - smem),
            out_specs=[VMEM] * len(outs),
            scratch_shapes=scratch,
            compiler_params=pltpu.CompilerParams(vmem_limit_bytes=limit * MIB),
        )(*args)

    bf16 = jnp.bfloat16
    pairs, groups = PLANES // 2, PLANES // 16
    held, south, east, corner = call(
        cut_kernel,
        [
            ((PLANES, ROWS, WIDE), f32),
            ((pairs, 8, WIDE), f32),
            ((groups, ROWS, WIDE), f32),
            ((groups, 8, WIDE), f32),
        ],
        fields,
    )
    south = shift(south, -1, 0)
    east = shift(east, 0, -1)
    corner = shift(corner, -1, -1)

    ring = PANEL_COLS + 8
    row_slots = LONS * SLOTS
    border = border_source[0]
    bands = border[: 8 * ring].reshape(8, ring)
    sides = border[8 * ring :].reshape(PANEL_ROWS, 8)
    donor = jnp.concatenate(
        [donor_cell[0, 0].astype(f32), donor_weights[0, 0, 0], donor_turn[0, 0]], axis=0
    )
    pick, mix, spin, flag = call(
        prepare_kernel,
        [((WIDE, WIDE), bf16), ((MID, WIDE), f32), ((2, WIDE), f32), ((8, WIDE), f32)],
        donor,
        jnp.pad(bands, ((0, 0), (0, 7 * WIDE - ring)), constant_values=-1),
        sides.T,
        scratch=[pltpu.VMEM((1, WIDE), f32)],
    )
    message = ((2 * PEERS, 16, WIDE), f32)
    wide, north, west, sent = call(
        donor_kernel,
        [
            ((PLANES, TALL, WIDE), f32),
            ((pairs, 8, WIDE), f32),
            ((groups, MID, WIDE), f32),
            message,
        ],
        place,
        held,
        south,
        east,
        corner,
        pick,
        mix,
        spin,
        flag,
        smem=1,
    )

    def to_holders(sent):
        return lax.all_to_all(sent, ("panel", "lon"), 0, 0, tiled=True)

    got = to_holders(sent)

    crowded = jnp.maximum(got[0, 0, FLAG_LANE], got[PEERS, 0, FLAG_LANE]) > ROOM

    west = shift(west, 0, 1)
    late_lat, late_lon, bands, sides, _ = lax.optimization_barrier((lat, lon, bands, sides, sent))

    window = jnp.pad(bands, ((0, 0), (4, 4)), constant_values=-1)
    window = lax.dynamic_slice(window, (0, late_lon * COLS), (8, 64)).reshape(2, BAND)
    side = jnp.where(late_lon == 0, sides[:, :4], sides[:, 4:])
    side = jnp.where((late_lon == 0) | (late_lon == LONS - 1), side, -1)
    side = jnp.pad(side, ((8, 8), (0, 0)), constant_values=-1)
    side = jnp.concatenate(
        [
            side[:PANEL_ROWS].reshape(LATS, ROWS, 4),
            side[ROWS:].reshape(LATS, ROWS, 4),
        ],
        axis=1,
    ).reshape(LATS, SIDE)
    at_lat = jnp.arange(LATS)[:, None]
    band = jnp.where(at_lat == 0, window[:1], jnp.where(at_lat == LATS - 1, window[1:], -1))
    wanted = jnp.concatenate([band, side], axis=1)
    holder = jnp.where(wanted >= 0, wanted // row_slots, -1)
    local = wanted - late_lat * row_slots
    spot = local // SLOTS * (WIDE // 2) + local % SLOTS
    send, rest = call(
        send_kernel,
        [((DEPTH, DEPTH), bf16), ((LATS, CHUNK), f32)],
        place,
        holder,
        spot,
        smem=1,
    )

    def to_blocks(got, chunks):
        fitting = lax.all_to_all(chunks, "lat", 0, 0, tiled=True)
        got, fitting = lax.optimization_barrier((got, fitting))

        def send_rest():
            (chunks,) = call(
                rest_kernel, [((PEERS, PLANES, CHUNK), f32)], place, got, rest, smem=1, limit=16
            )
            return lax.all_to_all(chunks, "lat", 0, 0, tiled=True).sum(axis=0)

        return fitting, lax.cond(crowded, send_rest, lambda: jnp.zeros((PLANES, CHUNK), f32))

    chunks, north = call(
        widen_kernel,
        [((PEERS, 16, WIDE), f32), ((pairs, 8, WIDE), f32)],
        place,
        got,
        send,
        north,
        west,
        smem=1,
    )
    north = shift(north, 1, 0)
    late_holder, _ = lax.optimization_barrier((holder, chunks))
    take, coef = call(
        take_kernel,
        [((DEPTH, CHUNK), bf16), ((5, TALL, WIDE), f32)],
        place,
        late_holder,
        smem=1,
    )
    got, extra = to_blocks(got, chunks)
    loaded = (wide, north, west, got, take, extra, coef, pick, mix, spin)
    middle, sent = call(
        first_kernel,
        [((PLANES, MID, WIDE), f32), ((16, WIDE), f32)],
        place,
        diffusion,
        *loaded,
        specs=[SMEM] * 2 + [HBM] * len(loaded),
        limit=60,
        scratch=[pltpu.VMEM(value.shape, value.dtype) for value in loaded]
        + [
            pltpu.VMEM((PLANES, TALL, WIDE), f32),
            pltpu.VMEM((PLANES, MID, WIDE), f32),
            pltpu.SemaphoreType.DMA((len(loaded),)),
        ],
    )
    got = lax.all_gather(sent, ("panel", "lon"))
    (chunks,) = call(choice_kernel, [((PEERS, 16, WIDE), f32)], place, got, send, smem=1)
    got, extra = to_blocks(got, chunks)
    accumulated, section_three = call(
        second_kernel,
        [(fields.shape, f32), (fields.shape, f32)],
        place,
        diffusion,
        middle,
        got,
        take,
        extra,
        coef,
        fields,
        smem=2,
        scratch=[pltpu.VMEM((PLANES, MID, WIDE), f32)],
    )
    return (accumulated[None], section_three[None])


def solution(mesh):
    return jax.shard_map(
        shards,
        mesh=mesh,
        in_specs=(
            P("panel", None, None, "lat", "lon"),
            P("panel", "lat", "lon", None),
            P("panel", "lat", "lon", None, None),
            P("panel", "lat", "lon", None),
            P("panel", None),
            P(),
        ),
        out_specs=(P("panel", None, None, "lat", "lon"), P("panel", None, None, "lat", "lon")),
        check_vma=False,
    )
```

```python
import math

import jax
import jax.numpy as jnp
from jax import lax
from jax.experimental import pallas as pl
from jax.experimental.pallas import tpu as pltpu
from jax.sharding import PartitionSpec as P

GAMMA = 5.0 / 3.0
RADIAL_STEP = 0.65 / 32.0
FIELDS = 8
LEVELS = 4
PLANES = FIELDS * LEVELS
ROWS = 16
COLS = 48
SLOTS = 33
LATS = 16
LONS = 16
ROOM = 63
FLAG_LANE = 63
WIDE = 128
TALL = ROWS + 16
MID = ROWS + 8
BAND = 4 * 64
SIDE = 4 * TALL
CHUNK = BAND + SIDE
PEERS = 16
DEPTH = PEERS * WIDE // 2
PANEL_ROWS = ROWS * LATS
PANEL_COLS = COLS * LONS
DTHETA = 0.5 * math.pi / PANEL_ROWS
DPHI = 1.5 * math.pi / PANEL_COLS
FINEST = min(DTHETA, DPHI)
TIME_STEP = 0.1 * FINEST
RADII = [0.35 + 0.65 * (k + 16 - LEVELS // 2 + 0.5) / 32.0 for k in range(LEVELS)]
VMEM = pl.BlockSpec(memory_space=pltpu.VMEM)
SMEM = pl.BlockSpec(memory_space=pltpu.SMEM)
MIB = 1024 * 1024


def iota(shape, axis):
    return lax.broadcasted_iota(jnp.int32, shape, axis)


def split_dot(left, right):
    total = None
    for _ in range(3):
        part = left.astype(jnp.bfloat16)
        left = left - part.astype(jnp.float32)
        term = jnp.dot(part, right, preferred_element_type=jnp.float32)
        total = term if total is None else total + term
    return total


def donor_message(planes, rows, pick, mix, spin):
    chosen = split_dot(planes, pick).reshape(PLANES, rows, WIDE)
    both = jnp.sum(chosen * mix[None], axis=1)
    mixed = both + pltpu.roll(both, WIDE // 2, 1)
    cosine = spin[0:1]
    sine = spin[1:2]
    at = iota((PLANES, WIDE), 0) // LEVELS
    theta = (at == 2) | (at == 5)
    phi = (at == 3) | (at == 6)
    other = jnp.where(
        theta, pltpu.roll(mixed, PLANES - LEVELS, 0), -pltpu.roll(mixed, LEVELS, 0)
    )
    turned = jnp.where(theta | phi, cosine * mixed + sine * other, mixed)
    half = PLANES // 2
    return jnp.where(iota((half, WIDE), 1) < WIDE // 2, turned[:half], turned[half:])


def post_message(place_ref, packed, flag, out_ref):
    panel = place_ref[0]
    spot = (iota((16, WIDE), 0) == 0) & (iota((16, WIDE), 1) == FLAG_LANE)
    blank = jnp.where(spot, flag[0:1], 0.0)
    packed = jnp.where(spot, blank, packed)
    out_ref[pl.ds((1 - panel) * PEERS, PEERS)] = jnp.broadcast_to(packed[None], (PEERS, 16, WIDE))
    out_ref[pl.ds(panel * PEERS, PEERS)] = jnp.broadcast_to(blank[None], (PEERS, 16, WIDE))


def cut_kernel(state_ref, held_ref, south_ref, east_ref, corner_ref):
    held_ref[:, :, COLS:] = jnp.zeros((PLANES, ROWS, WIDE - COLS), jnp.float32)
    for plane in range(PLANES):
        held_ref[plane, :, :COLS] = state_ref[plane // LEVELS, plane % LEVELS]
    lane = iota((ROWS, WIDE), 1)
    for pair in range(PLANES // 2):
        south_ref[pair] = pack_pair(held_ref[2 * pair, :8], held_ref[2 * pair + 1, :8])
    for group in range(2):
        columns = jnp.zeros((ROWS, WIDE), jnp.float32)
        for which in range(16):
            moved = pltpu.roll(held_ref[16 * group + which], 8 * which, 1)
            columns = jnp.where(lane // 8 == which, moved, columns)
        east_ref[group] = columns
        corner_ref[group] = columns[:8]


def pack_pair(one, two):
    return jnp.where(iota(one.shape, 1) < WIDE // 2, one, pltpu.roll(two, WIDE // 2, 1))


def donor_tables(donor_ref, pick_ref, mix_ref, spin_ref, line_ref):
    half = WIDE // 2
    late = iota((1, WIDE), 1) >= half

    def twice(value, fill):
        line_ref[...] = jnp.full((1, WIDE), fill, jnp.float32)
        line_ref[:, :SLOTS] = value
        line = line_ref[...]
        return jnp.where(late, pltpu.roll(line, half, 1), line)

    cell = twice(donor_ref[0:1], -10.0 * COLS)
    row_at = jnp.floor((cell + 0.5) * (1.0 / COLS))
    col_at = cell - row_at * COLS + jnp.where(late, 1.0, 0.0)
    upper = jnp.where(late, twice(donor_ref[2:3], 0.0), twice(donor_ref[1:2], 0.0))
    lower = jnp.where(late, twice(donor_ref[4:5], 0.0), twice(donor_ref[3:4], 0.0))
    turn = twice(donor_ref[5:6], 0.0)
    spin_ref[0:1] = jnp.cos(turn)
    spin_ref[1:2] = jnp.sin(turn)
    lane = iota((WIDE, WIDE), 0).astype(jnp.float32)
    real = jnp.where(row_at >= 0, col_at + 8.0, -1.0)
    pick_ref[...] = jnp.where(lane == real, 1.0, 0.0).astype(jnp.bfloat16)
    row = iota((MID, WIDE), 0).astype(jnp.float32)
    mix = jnp.where(row == row_at, upper, 0.0) + jnp.where(row == row_at + 1.0, lower, 0.0)
    mix_ref[...] = mix


def prepare_kernel(
    donor_ref, bands_ref, sides_ref, pick_ref, mix_ref, spin_ref, flag_ref, line_ref
):
    donor_tables(donor_ref, pick_ref, mix_ref, spin_ref, line_ref)
    width = bands_ref.shape[1]
    column = iota((width, WIDE), 0) - 4
    start = iota((width, WIDE), 1) * COLS - 8
    within = (column >= start) & (column < start + 64) & (start < PANEL_COLS)
    columns = jnp.where(within, 1.0, 0.0).astype(jnp.bfloat16)
    row = iota((PANEL_ROWS, WIDE), 0)
    start = iota((PANEL_ROWS, WIDE), 1) * ROWS - 8
    within = (row >= start) & (row < start + TALL) & (start < PANEL_ROWS)
    rows = jnp.where(within, 1.0, 0.0).astype(jnp.bfloat16)

    def most(slots, windows):
        ones = []
        for which in range(LATS):
            first = which * LONS * SLOTS
            inside = (slots >= first) & (slots < first + LONS * SLOTS)
            ones.append(jnp.where(inside, 1.0, 0.0))
        ones = jnp.concatenate(ones, axis=0).astype(jnp.bfloat16)
        counts = jnp.dot(ones, windows, preferred_element_type=jnp.float32)
        return jnp.max(jnp.sum(counts.reshape(2 * LATS, 4, WIDE), axis=1))

    total = most(bands_ref[...], columns) + most(sides_ref[...], rows)
    flag_ref[...] = jnp.full(flag_ref.shape, total, jnp.float32)


def donor_kernel(
    place_ref, held_ref, south_ref, east_ref, corner_ref, pick_ref, mix_ref, spin_ref, flag_ref,
    wide_ref, north_ref, west_ref, out_ref
):
    lane = iota((ROWS, WIDE), 1)
    own = (lane >= 8) & (lane < 8 + COLS)
    beyond = (lane >= 8 + COLS) & (lane < 16 + COLS)
    for plane in range(PLANES):
        group, which = plane // 16, plane % 16
        turn = (8 + COLS - 8 * which) % WIDE
        middle = pltpu.roll(held_ref[plane], 8, 1)
        east = pltpu.roll(east_ref[group], turn, 1)
        wide_ref[plane, :8] = jnp.zeros((8, WIDE), jnp.float32)
        wide_ref[plane, 8:24] = jnp.where(own, middle, jnp.where(beyond, east, 0.0))
        south = pltpu.roll(south_ref[plane // 2], 8 + plane % 2 * (WIDE // 2), 1)
        corner = pltpu.roll(corner_ref[group], turn, 1)
        wide_ref[plane, 24:] = jnp.where(own[:8], south, jnp.where(beyond[:8], corner, 0.0))
    planes = wide_ref[:, 8:, :].reshape(PLANES * MID, WIDE)
    packed = donor_message(planes, MID, pick_ref[...], mix_ref[...], spin_ref[...])
    post_message(place_ref, packed, flag_ref[...], out_ref)
    for pair in range(PLANES // 2):
        north_ref[pair] = pack_pair(wide_ref[2 * pair, 16:24], wide_ref[2 * pair + 1, 16:24])
    lane = iota((MID, WIDE), 1)
    for group in range(2):
        columns = jnp.zeros((MID, WIDE), jnp.float32)
        for which in range(16):
            turn = (8 * which - COLS) % WIDE
            moved = pltpu.roll(wide_ref[16 * group + which, 8:], turn, 1)
            columns = jnp.where(lane // 8 == which, moved, columns)
        west_ref[group] = columns


def unpack(read):
    low = iota((16, WIDE), 1) < WIDE // 2
    tiles = []
    for pair in range(PEERS // 2):
        one = read(2 * pair)
        two = read(2 * pair + 1)
        top = jnp.where(low, one, pltpu.roll(two, WIDE // 2, 1))
        end = jnp.where(low, pltpu.roll(one, WIDE // 2, 1), two)
        tiles.append(jnp.concatenate([top, end], axis=0))
    return jnp.concatenate(tiles, axis=1)


def split_parts(held):
    parts = []
    for _ in range(3):
        part = held.astype(jnp.bfloat16)
        held = held - part.astype(jnp.float32)
        parts.append(part)
    return jnp.concatenate(parts, axis=0)


def join_parts(terms):
    return terms[:PLANES] + terms[PLANES : 2 * PLANES] + terms[2 * PLANES :]


def from_row(place_ref, got_ref):
    base = (1 - place_ref[0]) * PEERS
    return split_parts(unpack(lambda which: got_ref[base + which]))


def rank_of(chosen):
    order = iota((CHUNK, CHUNK), 0) < iota((CHUNK, CHUNK), 1)
    order = jnp.where(order, 1.0, 0.0).astype(jnp.bfloat16)
    ones = jnp.where(chosen, 1.0, 0.0).astype(jnp.bfloat16)
    return jnp.dot(ones, order, preferred_element_type=jnp.float32)


def send_kernel(place_ref, holder_ref, spot_ref, send_ref):
    mine = holder_ref[...] == place_ref[1]
    spot = spot_ref[...].astype(jnp.float32)
    rank = rank_of(mine)
    key = jnp.where(mine & (rank < ROOM), rank, -1.0)
    half = WIDE // 2
    place_at = iota((half, CHUNK), 0).astype(jnp.float32)
    lane = iota((half, DEPTH), 1).astype(jnp.float32)
    for block in range(LATS):
        found = place_at == key[block : block + 1]
        table = jnp.sum(
            jnp.where(found, spot[block : block + 1] + 1.0, 0.0), axis=1, keepdims=True
        )
        hot = jnp.where(lane + 1.0 == table, 1.0, 0.0)
        send_ref[block * half : (block + 1) * half] = hot.astype(jnp.bfloat16)


def take_kernel(place_ref, holder_ref, take_ref, coef_ref):
    lat = place_ref[1]
    own = holder_ref[pl.ds(lat, 1)]
    masks = iota((PEERS, CHUNK), 0) == own
    rank = jnp.sum(jnp.where(masks, rank_of(masks), 0.0), axis=0, keepdims=True)
    fits = (own >= 0) & (rank < ROOM)
    index = jnp.where(fits, own.astype(jnp.float32) * (WIDE // 2) + rank, -1.0)
    hot = iota((DEPTH, CHUNK), 0).astype(jnp.float32) == index
    take_ref[...] = jnp.where(hot, 1.0, 0.0).astype(jnp.bfloat16)
    row = (lat * ROWS - 8 + iota((TALL, WIDE), 0)).astype(jnp.float32)
    column = (place_ref[2] * COLS - 8 + iota((TALL, WIDE), 1)).astype(jnp.float32)
    colatitude = 0.25 * math.pi + (row + 0.5) * DTHETA
    longitude = -0.75 * math.pi + (column + 0.5) * DPHI
    sine, cosine = jnp.sin(colatitude), jnp.cos(colatitude)
    twirl = 2.0 * 0.25 / TIME_STEP
    yang = place_ref[0] == 1
    coef_ref[0] = sine
    coef_ref[1] = 1.0 / sine
    coef_ref[2] = twirl * jnp.where(yang, sine * jnp.sin(longitude), cosine)
    coef_ref[3] = twirl * jnp.where(yang, cosine * jnp.sin(longitude), -sine)
    coef_ref[4] = twirl * jnp.where(yang, jnp.cos(longitude), 0.0)


def widen_kernel(place_ref, got_ref, send_ref, north_ref, west_ref, out_ref, edge_ref):
    lane = iota((8, WIDE), 1)
    half = WIDE // 2
    for pair in range(PLANES // 2):
        group, which = pair // 8, 2 * pair % 16
        rows = west_ref[group, 8:16]
        one = pltpu.roll(rows, (WIDE - 8 * which) % WIDE, 1)
        two = pltpu.roll(rows, (half - 8 * which - 8) % WIDE, 1)
        edge = jnp.where(lane < 8, one, north_ref[pair])
        edge_ref[pair] = jnp.where((lane >= half) & (lane < half + 8), two, edge)
    choice_kernel(place_ref, got_ref, send_ref, out_ref)


def choice_kernel(place_ref, got_ref, send_ref, out_ref):
    parts = from_row(place_ref, got_ref)
    terms = lax.dot_general(
        parts, send_ref[...], (((1,), (1,)), ((), ())), preferred_element_type=jnp.float32
    )
    chosen = join_parts(terms)
    low = iota((16, WIDE), 1) < WIDE // 2
    for pair in range(PEERS // 2):
        tile = chosen[:, pair * WIDE : (pair + 1) * WIDE]
        top, end = tile[:16], tile[16:]
        out_ref[2 * pair] = jnp.where(low, top, pltpu.roll(end, WIDE // 2, 1))
        out_ref[2 * pair + 1] = jnp.where(low, pltpu.roll(top, WIDE // 2, 1), end)


def dense_kernel(place_ref, got_ref, holder_ref, spot_ref, out_ref):
    parts = from_row(place_ref, got_ref)
    index = jnp.where(holder_ref[...] == place_ref[1], spot_ref[...], -1)
    at = iota((DEPTH, CHUNK), 0)
    for block in range(LATS):
        hot = jnp.where(at == index[block : block + 1], 1.0, 0.0).astype(jnp.bfloat16)
        out_ref[block] = join_parts(jnp.dot(parts, hot, preferred_element_type=jnp.float32))


def ghost_values(got_ref, take_ref):
    if len(got_ref.shape) == 2:
        return got_ref[...]
    parts = split_parts(unpack(lambda which: got_ref[which]))
    return join_parts(jnp.dot(parts, take_ref[...], preferred_element_type=jnp.float32))


def fill_ghosts(place_ref, ghosts, work_ref, rows):
    lat, lon = place_ref[1], place_ref[2]
    trim = (TALL - rows) // 2
    top = 8 - trim

    @pl.when((lon == 0) | (lon == LONS - 1))
    def _():
        side = ghosts[:, BAND:]
        first = jnp.where(lon == 0, 4, 8 + COLS)
        lane = iota((rows, WIDE), 1)
        own = lane // 4 == iota((rows, WIDE), 0) + trim
        spread = jnp.where(own[None], side[:, None, :], 0.0).reshape(PLANES * rows, WIDE)
        target = iota((WIDE, WIDE), 1) - first
        hot = jnp.where(target == iota((WIDE, WIDE), 0) % 4, 1.0, 0.0).astype(jnp.bfloat16)
        moved = split_dot(spread, hot).reshape(PLANES, rows, WIDE)
        ghost = (lane >= first) & (lane < first + 4)
        work_ref[...] = jnp.where(ghost[None], moved, work_ref[...])

    @pl.when((lat == 0) | (lat == LATS - 1))
    def _():
        band = ghosts[:, :BAND]
        lines = []
        for half in range(2):
            piece = band[:, half * WIDE : (half + 1) * WIDE]
            lines += [piece, pltpu.roll(piece, WIDE // 2, 1)]

        @pl.when(lat == 0)
        def _():
            for row in range(4):
                work_ref[:, top - 4 + row, :] = lines[row]

        @pl.when(lat == LATS - 1)
        def _():
            for row in range(4):
                work_ref[:, top + ROWS + row, :] = lines[row]


def rates(load, rows, coef_ref, diffusion_ref):
    def on_levels(value, factors):
        return jnp.concatenate(
            [value[k * rows : (k + 1) * rows] * factors[k] for k in range(LEVELS)], axis=0
        )

    def whole(which):
        value = coef_ref[which]
        if rows < TALL:
            value = pltpu.roll(value, TALL - (TALL - rows) // 2, 0)[:rows]
        return jnp.concatenate([value] * LEVELS, axis=0)

    sine = whole(0)
    per_sine = whole(1)
    inverse = [1.0 / r for r in RADII]
    viscosity = diffusion_ref[0] * (FINEST * FINEST / TIME_STEP)
    resistivity = diffusion_ref[1] * (FINEST * FINEST / TIME_STEP)

    def slope(value, axis, step):
        size = value.shape[axis]
        near = pltpu.roll(value, size - 1, axis) - pltpu.roll(value, 1, axis)
        far = pltpu.roll(value, size - 2, axis) - pltpu.roll(value, 2, axis)
        return near * (8.0 / (12.0 * step)) - far * (1.0 / (12.0 * step))

    def d_theta(value):
        return slope(value, 0, DTHETA)

    def d_phi(value):
        return slope(value, 1, DPHI)

    def d_radius(value):
        part = [value[k * rows : (k + 1) * rows] for k in range(LEVELS)]
        slopes = [(part[1] - part[0]) * (1.0 / RADIAL_STEP)]
        for k in range(1, LEVELS - 1):
            slopes.append((part[k + 1] - part[k - 1]) * (1.0 / (2.0 * RADIAL_STEP)))
        slopes.append((part[-1] - part[-2]) * (1.0 / RADIAL_STEP))
        return jnp.concatenate(slopes, axis=0)

    def by_radius(value):
        return on_levels(value, RADII)

    def per_radius(value):
        return on_levels(value, inverse)

    def curl(vector):
        part_r, part_t, part_p = vector
        return (
            per_radius((d_theta(sine * part_p) - d_phi(part_t)) * per_sine),
            per_radius(d_phi(part_r) * per_sine - d_radius(by_radius(part_p))),
            per_radius(d_radius(by_radius(part_t)) - d_theta(part_r)),
        )

    def gradient(value):
        return (
            d_radius(value),
            per_radius(d_theta(value)),
            per_radius(d_phi(value) * per_sine),
        )

    def cross(left, right):
        return (
            left[1] * right[2] - left[2] * right[1],
            left[2] * right[0] - left[0] * right[2],
            left[0] * right[1] - left[1] * right[0],
        )

    def advect(vector, slopes):
        return vector[0] * slopes[0] + vector[1] * slopes[1] + vector[2] * slopes[2]

    velocity = [load(which) for which in (1, 2, 3)]
    magnetic = [load(which) for which in (4, 5, 6)]
    vorticity = curl(velocity)
    current = curl(magnetic)
    squares = [r * r for r in RADII]
    spread = on_levels(
        d_radius(on_levels(velocity[0], squares)), [1.0 / square for square in squares]
    ) + per_radius((d_theta(sine * velocity[1]) + d_phi(velocity[2])) * per_sine)
    induced = cross(velocity, magnetic)
    electric = [induced[k] - resistivity * current[k] for k in range(3)]
    kinetic = 0.5 * (
        velocity[0] * velocity[0] + velocity[1] * velocity[1] + velocity[2] * velocity[2]
    )
    curl_electric = curl(electric)
    log_rho = load(0)
    rho_rate = -advect(velocity, gradient(log_rho)) - spread
    pressure = load(7)
    slope_pressure = gradient(pressure)
    pressure_rate = -advect(velocity, slope_pressure) - GAMMA * pressure * spread
    lorentz = cross(current, magnetic)
    per_rho = jnp.exp(-log_rho)
    slope_kinetic = gradient(kinetic)
    curl_vorticity = curl(vorticity)
    lamb = cross(velocity, vorticity)
    turning = cross((whole(2), whole(3), whole(4)), velocity)
    momentum = [
        lamb[k]
        - slope_kinetic[k]
        + per_rho * (lorentz[k] - slope_pressure[k])
        - turning[k]
        - viscosity * curl_vorticity[k]
        for k in range(3)
    ]
    return [rho_rate, *momentum, *curl_electric, pressure_rate]


def first_kernel(
    place_ref,
    diffusion_ref,
    wide_ref,
    north_ref,
    west_ref,
    got_ref,
    take_ref,
    coef_ref,
    pick_ref,
    mix_ref,
    spin_ref,
    flag_ref,
    middle_ref,
    out_ref,
    work_ref,
    next_ref,
):
    lane = iota((TALL, WIDE), 1)
    for plane in range(PLANES):
        group, which = plane // 16, plane % 16
        north = north_ref[plane // 2]
        if plane % 2:
            north = pltpu.roll(north, WIDE // 2, 1)
        west = pltpu.roll(west_ref[group], (WIDE - 8 * which) % WIDE, 1)
        work_ref[plane, :8] = jnp.where(lane[:8] < 16 + COLS, north, 0.0)
        work_ref[plane, 8:] = jnp.where(lane[8:] < 8, west, wide_ref[plane, 8:])
    ghosts = ghost_values(got_ref, take_ref)
    fill_ghosts(place_ref, ghosts, work_ref, TALL)

    def load(which):
        return work_ref[which * LEVELS : (which + 1) * LEVELS].reshape(LEVELS * TALL, WIDE)

    found = rates(load, TALL, coef_ref, diffusion_ref)
    row = iota((TALL, WIDE), 0)
    inside = (lane >= 4) & (lane < 12 + COLS) & (row >= 4) & (row < 12 + ROWS)
    for which in range(FIELDS):
        value = load(which) + (0.5 * TIME_STEP) * found[which]
        for level in range(LEVELS):
            plane = which * LEVELS + level
            part = jnp.where(inside, value[level * TALL : (level + 1) * TALL], 0.0)
            next_ref[plane] = part[8:]
            middle_ref[plane] = pltpu.roll(part, TALL - 4, 0)[:MID]
    planes = next_ref[...].reshape(PLANES * MID, WIDE)
    packed = donor_message(planes, MID, pick_ref[...], mix_ref[...], spin_ref[...])
    post_message(place_ref, packed, flag_ref[...], out_ref)


def second_kernel(
    place_ref,
    diffusion_ref,
    middle_ref,
    got_ref,
    take_ref,
    coef_ref,
    state_ref,
    whole_ref,
    third_ref,
    work_ref,
):
    work_ref[...] = middle_ref[...]
    ghosts = ghost_values(got_ref, take_ref)
    fill_ghosts(place_ref, ghosts, work_ref, MID)

    def load(which):
        return work_ref[which * LEVELS : (which + 1) * LEVELS].reshape(LEVELS * MID, WIDE)

    found = rates(load, MID, coef_ref, diffusion_ref)

    def centre(value):
        return pltpu.roll(pltpu.roll(value, MID - 4, 0)[:ROWS], WIDE - 8, 1)[:, :COLS]

    for which in range(FIELDS):
        for level in range(LEVELS):
            rate = found[which][level * MID : (level + 1) * MID]
            held = state_ref[which, level]
            step = centre(rate * (0.5 * TIME_STEP))
            middle = centre(middle_ref[which * LEVELS + level])
            third_ref[which, level] = held + step
            whole_ref[which, level] = held + ((middle - held) + 2.0 * step) * (1.0 / 3.0)


def shift(value, move_lat, move_lon):
    pairs = []
    for a in range(LATS):
        for b in range(LONS):
            goal_a, goal_b = a + move_lat, b + move_lon
            if 0 <= goal_a < LATS and 0 <= goal_b < LONS:
                pairs.append((a * LONS + b, goal_a * LONS + goal_b))
    return lax.ppermute(value, ("lat", "lon"), pairs)


def shards(state, donor_cell, donor_weights, donor_turn, border_source, diffusion):
    fields = state[0]
    panel = lax.axis_index("panel")
    lat = lax.axis_index("lat")
    lon = lax.axis_index("lon")
    place = jnp.stack([panel, lat, lon]).astype(jnp.int32)
    f32 = jnp.float32

    def call(kernel, outs, *args, smem=0, specs=None, scratch=(), limit=10):
        shapes = [jax.ShapeDtypeStruct(shape, dtype) for shape, dtype in outs]
        return pl.pallas_call(
            kernel,
            out_shape=shapes,
            in_specs=specs or [SMEM] * smem + [VMEM] * (len(args) - smem),
            out_specs=[VMEM] * len(outs),
            scratch_shapes=scratch,
            compiler_params=pltpu.CompilerParams(vmem_limit_bytes=limit * MIB),
        )(*args)

    bf16 = jnp.bfloat16
    pairs, groups = PLANES // 2, PLANES // 16
    held, south, east, corner = call(
        cut_kernel,
        [
            ((PLANES, ROWS, WIDE), f32),
            ((pairs, 8, WIDE), f32),
            ((groups, ROWS, WIDE), f32),
            ((groups, 8, WIDE), f32),
        ],
        fields,
    )
    south = shift(south, -1, 0)
    east = shift(east, 0, -1)
    corner = shift(corner, -1, -1)

    ring = PANEL_COLS + 8
    row_slots = LONS * SLOTS
    border = border_source[0]
    bands = border[: 8 * ring].reshape(8, ring)
    sides = border[8 * ring :].reshape(PANEL_ROWS, 8)
    donor = jnp.concatenate(
        [donor_cell[0, 0].astype(f32), donor_weights[0, 0, 0], donor_turn[0, 0]], axis=0
    )
    pick, mix, spin, flag = call(
        prepare_kernel,
        [((WIDE, WIDE), bf16), ((MID, WIDE), f32), ((2, WIDE), f32), ((8, WIDE), f32)],
        donor,
        jnp.pad(bands, ((0, 0), (0, 7 * WIDE - ring)), constant_values=-1),
        sides.T,
        scratch=[pltpu.VMEM((1, WIDE), f32)],
    )
    message = ((2 * PEERS, 16, WIDE), f32)
    wide, north, west, sent = call(
        donor_kernel,
        [
            ((PLANES, TALL, WIDE), f32),
            ((pairs, 8, WIDE), f32),
            ((groups, MID, WIDE), f32),
            message,
        ],
        place,
        held,
        south,
        east,
        corner,
        pick,
        mix,
        spin,
        flag,
        smem=1,
    )

    def to_holders(sent):
        return lax.all_to_all(sent, ("panel", "lon"), 0, 0, tiled=True)

    got = to_holders(sent)

    crowded = jnp.maximum(got[0, 0, FLAG_LANE], got[PEERS, 0, FLAG_LANE]) > ROOM

    west = shift(west, 0, 1)
    late_lat, late_lon, bands, sides, _ = lax.optimization_barrier((lat, lon, bands, sides, sent))

    window = jnp.pad(bands, ((0, 0), (4, 4)), constant_values=-1)
    window = lax.dynamic_slice(window, (0, late_lon * COLS), (8, 64)).reshape(2, BAND)
    side = jnp.where(late_lon == 0, sides[:, :4], sides[:, 4:])
    side = jnp.where((late_lon == 0) | (late_lon == LONS - 1), side, -1)
    side = jnp.pad(side, ((8, 8), (0, 0)), constant_values=-1)
    side = jnp.concatenate(
        [
            side[:PANEL_ROWS].reshape(LATS, ROWS, 4),
            side[ROWS:].reshape(LATS, ROWS, 4),
        ],
        axis=1,
    ).reshape(LATS, SIDE)
    at_lat = jnp.arange(LATS)[:, None]
    band = jnp.where(at_lat == 0, window[:1], jnp.where(at_lat == LATS - 1, window[1:], -1))
    wanted = jnp.concatenate([band, side], axis=1)
    holder = jnp.where(wanted >= 0, wanted // row_slots, -1)
    local = wanted - late_lat * row_slots
    spot = local // SLOTS * (WIDE // 2) + local % SLOTS
    (send,) = call(
        send_kernel, [((DEPTH, DEPTH), bf16)], place, holder, spot, smem=1, limit=16
    )
    chunk = ((PEERS, 16, WIDE), f32)
    first_got = got
    chunks, north = call(
        widen_kernel, [chunk, ((pairs, 8, WIDE), f32)], place, got, send, north, west, smem=1
    )
    north = shift(north, 1, 0)
    late_holder, _ = lax.optimization_barrier((holder, chunks))
    take, coef = call(
        take_kernel,
        [((DEPTH, CHUNK), bf16), ((5, TALL, WIDE), f32)],
        place,
        late_holder,
        smem=1,
    )

    def to_blocks(chunks):
        return lax.all_to_all(chunks, "lat", 0, 0, tiled=True)

    def section_one(got):
        return call(
            first_kernel,
            [((PLANES, MID, WIDE), f32), message],
            place,
            diffusion,
            wide,
            north,
            west,
            got,
            take,
            coef,
            pick,
            mix,
            spin,
            flag,
            smem=2,
            scratch=[pltpu.VMEM((PLANES, TALL, WIDE), f32), pltpu.VMEM((PLANES, MID, WIDE), f32)],
        )

    def section_two(middle, got):
        return call(
            second_kernel,
            [(fields.shape, f32), (fields.shape, f32)],
            place,
            diffusion,
            middle,
            got,
            take,
            coef,
            fields,
            smem=2,
            scratch=[pltpu.VMEM((PLANES, MID, WIDE), f32)],
        )

    middle, sent = section_one(to_blocks(chunks))
    got = to_holders(sent)
    (chunks,) = call(choice_kernel, [chunk], place, got, send, smem=1)
    fitting = section_two(middle, to_blocks(chunks))

    def with_room():
        def dense(got):
            chunks = call(
                dense_kernel,
                [((PEERS, PLANES, CHUNK), f32)],
                place,
                got,
                holder,
                spot,
                smem=1,
                limit=16,
            )
            return to_blocks(chunks[0]).sum(axis=0)

        middle, sent = section_one(dense(first_got))
        return section_two(middle, dense(to_holders(sent)))

    accumulated, section_three = lax.cond(crowded, with_room, lambda: fitting)
    return (accumulated[None], section_three[None])


def solution(mesh):
    return jax.shard_map(
        shards,
        mesh=mesh,
        in_specs=(
            P("panel", None, None, "lat", "lon"),
            P("panel", "lat", "lon", None),
            P("panel", "lat", "lon", None, None),
            P("panel", "lat", "lon", None),
            P("panel", None),
            P(),
        ),
        out_specs=(P("panel", None, None, "lat", "lon"), P("panel", None, None, "lat", "lon")),
        check_vma=False,
    )
```

```python
import math

import jax
import jax.numpy as jnp
from jax import lax
from jax.experimental import pallas as pl
from jax.experimental.pallas import tpu as pltpu
from jax.sharding import PartitionSpec as P

GAMMA = 5.0 / 3.0
RADIAL_STEP = 0.65 / 32.0
FIELDS = 8
LEVELS = 4
PLANES = FIELDS * LEVELS
PAIRS = PLANES // 2
LOW_LEVEL = (0, 1)
HIGH_LEVEL = (3, 2)
ROWS = 16
COLS = 48
SLOTS = 33
LATS = 16
LONS = 16
ROOM = 63
FLAG_LANE = 63
WIDE = 128
HALF = 64
TALL = ROWS + 16
MID = ROWS + 8
BAND = 4 * HALF
SIDE = 4 * TALL
CHUNK = BAND + SIDE
PEERS = 16
THIRD = 42
CHOICE_TILES = -(-PEERS // 3)
CHOICE_DEPTH = CHOICE_TILES * WIDE
DEPTH = PEERS * HALF
PANEL_ROWS = ROWS * LATS
PANEL_COLS = COLS * LONS
DTHETA = 0.5 * math.pi / PANEL_ROWS
DPHI = 1.5 * math.pi / PANEL_COLS
FINEST = min(DTHETA, DPHI)
TIME_STEP = 0.1 * FINEST
RADII = [0.35 + 0.65 * (k + 16 - LEVELS // 2 + 0.5) / 32.0 for k in range(LEVELS)]
VMEM = pl.BlockSpec(memory_space=pltpu.VMEM)
SMEM = pl.BlockSpec(memory_space=pltpu.SMEM)
MIB = 1024 * 1024


def iota(shape, axis):
    return lax.broadcasted_iota(jnp.int32, shape, axis)


def column_of(shape):
    return iota(shape, len(shape) - 1) & (HALF - 1)


def turn(value, lanes):
    return pltpu.roll(value, lanes % WIDE, 1) if lanes % WIDE else value


def split_dot(left, right):
    total = None
    for _ in range(3):
        part = left.astype(jnp.bfloat16)
        left = left - part.astype(jnp.float32)
        term = jnp.dot(part, right, preferred_element_type=jnp.float32)
        total = term if total is None else total + term
    return total


def donor_message(planes, pick, mix, spin):
    chosen = split_dot(planes, pick).reshape(PAIRS, MID, 2 * WIDE)
    both = jnp.sum(chosen * mix[None], axis=1)
    both = jnp.concatenate([both[:, :WIDE], both[:, WIDE:]], axis=0)
    mixed = both + pltpu.roll(both, HALF, 1)
    cosine = spin[0:1]
    sine = spin[1:2]
    at = (iota((PLANES, WIDE), 0) & (PAIRS - 1)) // 2
    theta = (at == 2) | (at == 5)
    phi = (at == 3) | (at == 6)
    other = jnp.where(theta, pltpu.roll(mixed, PLANES - 2, 0), -pltpu.roll(mixed, 2, 0))
    turned = jnp.where(theta | phi, cosine * mixed + sine * other, mixed)
    return jnp.where(iota((PAIRS, WIDE), 1) < HALF, turned[:PAIRS], turned[PAIRS:])


def post_message(place_ref, packed, flag, out_ref):
    panel = place_ref[0]
    spot = (iota((16, WIDE), 0) == 0) & (iota((16, WIDE), 1) == FLAG_LANE)
    blank = jnp.where(spot, flag[0:1], 0.0)
    packed = jnp.where(spot, blank, packed)
    out_ref[pl.ds((1 - panel) * PEERS, PEERS)] = jnp.broadcast_to(packed[None], (PEERS, 16, WIDE))
    out_ref[pl.ds(panel * PEERS, PEERS)] = jnp.broadcast_to(blank[None], (PEERS, 16, WIDE))


def cut_kernel(state_ref, held_ref, south_ref, east_ref, corner_ref, plane_ref):
    for plane in range(PLANES):
        plane_ref[plane, :, :COLS] = state_ref[plane // LEVELS, plane % LEVELS]
    lane = iota((ROWS, WIDE), 1)
    column = column_of((ROWS, WIDE))
    own = (column >= 8) & (column < 8 + COLS)
    for pair in range(PAIRS):
        field, which = pair // 2, pair % 2
        low = turn(plane_ref[field * LEVELS + LOW_LEVEL[which]], 8)
        high = turn(plane_ref[field * LEVELS + HIGH_LEVEL[which]], HALF + 8)
        tile = jnp.where(own, jnp.where(lane < HALF, low, high), 0.0)
        held_ref[pair] = tile
        south_ref[pair] = tile[:8]
    for group in range(2):
        columns = jnp.zeros((ROWS, WIDE), jnp.float32)
        for which in range(8):
            moved = turn(held_ref[8 * group + which], 8 * which - 8)
            columns = jnp.where(column // 8 == which, moved, columns)
        east_ref[group] = columns
        corner_ref[group] = columns[:8]


def donor_tables(donor_ref, pick_ref, mix_ref, spin_ref, line_ref):
    late = iota((1, WIDE), 1) >= HALF

    def twice(value, fill):
        line_ref[...] = jnp.full((1, WIDE), fill, jnp.float32)
        line_ref[:, :SLOTS] = value
        line = line_ref[...]
        return jnp.where(late, pltpu.roll(line, HALF, 1), line)

    cell = twice(donor_ref[0:1], -10.0 * COLS)
    row_at = jnp.floor((cell + 0.5) * (1.0 / COLS))
    col_at = cell - row_at * COLS + jnp.where(late, 1.0, 0.0)
    upper = jnp.where(late, twice(donor_ref[2:3], 0.0), twice(donor_ref[1:2], 0.0))
    lower = jnp.where(late, twice(donor_ref[4:5], 0.0), twice(donor_ref[3:4], 0.0))
    angle = twice(donor_ref[5:6], 0.0)
    spin_ref[0:1] = jnp.cos(angle)
    spin_ref[1:2] = jnp.sin(angle)
    lane = iota((WIDE, WIDE), 0).astype(jnp.float32)
    real = jnp.where(row_at >= 0, col_at + 8.0, -1000.0)
    pick_ref[:, :WIDE] = jnp.where(lane == real, 1.0, 0.0).astype(jnp.bfloat16)
    pick_ref[:, WIDE:] = jnp.where(lane == real + HALF, 1.0, 0.0).astype(jnp.bfloat16)
    row = iota((MID, WIDE), 0).astype(jnp.float32)
    mix = jnp.where(row == row_at, upper, 0.0) + jnp.where(row == row_at + 1.0, lower, 0.0)
    mix_ref[:, :WIDE] = mix
    mix_ref[:, WIDE:] = mix


def prepare_kernel(
    donor_ref, bands_ref, sides_ref, pick_ref, mix_ref, spin_ref, flag_ref, line_ref
):
    donor_tables(donor_ref, pick_ref, mix_ref, spin_ref, line_ref)
    width = bands_ref.shape[1]
    column = iota((width, WIDE), 0) - 4
    start = iota((width, WIDE), 1) * COLS - 8
    within = (column >= start) & (column < start + 64) & (start < PANEL_COLS)
    columns = jnp.where(within, 1.0, 0.0).astype(jnp.bfloat16)
    row = iota((PANEL_ROWS, WIDE), 0)
    start = iota((PANEL_ROWS, WIDE), 1) * ROWS - 8
    within = (row >= start) & (row < start + TALL) & (start < PANEL_ROWS)
    rows = jnp.where(within, 1.0, 0.0).astype(jnp.bfloat16)

    def most(slots, windows):
        ones = []
        for which in range(LATS):
            first = which * LONS * SLOTS
            inside = (slots >= first) & (slots < first + LONS * SLOTS)
            ones.append(jnp.where(inside, 1.0, 0.0))
        ones = jnp.concatenate(ones, axis=0).astype(jnp.bfloat16)
        counts = jnp.dot(ones, windows, preferred_element_type=jnp.float32)
        return jnp.max(jnp.sum(counts.reshape(2 * LATS, 4, WIDE), axis=1))

    total = most(bands_ref[...], columns) + most(sides_ref[...], rows)
    flag_ref[...] = jnp.full(flag_ref.shape, total, jnp.float32)


def donor_kernel(
    place_ref, held_ref, south_ref, east_ref, corner_ref, pick_ref, mix_ref, spin_ref, flag_ref,
    lower_ref, out_ref
):
    column = column_of((ROWS, WIDE))
    beyond = column >= 8 + COLS
    for pair in range(PAIRS):
        group, which = pair // 8, pair % 8
        east = turn(east_ref[group], 8 + COLS - 8 * which)
        corner = turn(corner_ref[group], 8 + COLS - 8 * which)
        lower_ref[pair, :ROWS] = jnp.where(beyond, east, held_ref[pair])
        lower_ref[pair, ROWS:] = jnp.where(beyond[:8], corner, south_ref[pair])
    planes = lower_ref[...].reshape(PAIRS * MID, WIDE)
    packed = donor_message(planes, pick_ref[...], mix_ref[...], spin_ref[...])
    post_message(place_ref, packed, flag_ref[...], out_ref)


def last_kernel(lower_ref, west_ref):
    column = column_of((MID, WIDE))
    for group in range(2):
        columns = jnp.zeros((MID, WIDE), jnp.float32)
        for which in range(8):
            moved = turn(lower_ref[8 * group + which], 8 * which - COLS)
            columns = jnp.where(column // 8 == which, moved, columns)
        west_ref[group] = columns


def split_parts(held):
    parts = []
    for _ in range(3):
        part = held.astype(jnp.bfloat16)
        held = held - part.astype(jnp.float32)
        parts.append(part)
    return jnp.concatenate(parts, axis=0)


def join_parts(terms):
    return terms[:PLANES] + terms[PLANES : 2 * PLANES] + terms[2 * PLANES :]


def from_row(place_ref, got_ref):
    base = (1 - place_ref[0]) * PEERS
    third = iota((16, WIDE), 1) // THIRD
    tiles = []
    for tile in range(CHOICE_TILES):
        top = jnp.zeros((16, WIDE), jnp.float32)
        end = top
        for which in range(min(3, PEERS - 3 * tile)):
            message = got_ref[base + 3 * tile + which]
            top = jnp.where(third == which, turn(message, THIRD * which), top)
            end = jnp.where(third == which, turn(message, THIRD * which - HALF), end)
        tiles.append(jnp.concatenate([top, end], axis=0))
    return split_parts(jnp.concatenate(tiles, axis=1))


def rank_of(chosen):
    order = iota((CHUNK, CHUNK), 0) < iota((CHUNK, CHUNK), 1)
    order = jnp.where(order, 1.0, 0.0).astype(jnp.bfloat16)
    ones = jnp.where(chosen, 1.0, 0.0).astype(jnp.bfloat16)
    return jnp.dot(ones, order, preferred_element_type=jnp.float32)


def send_kernel(place_ref, holder_ref, spot_ref, send_ref):
    mine = holder_ref[...] == place_ref[1]
    spot = spot_ref[...].astype(jnp.float32)
    rank = rank_of(mine)
    key = jnp.where(mine & (rank < ROOM), rank, -1.0)
    place_at = iota((HALF, CHUNK), 0).astype(jnp.float32)
    eye = iota((WIDE, WIDE), 0) == iota((WIDE, WIDE), 1)
    depth = iota((CHOICE_DEPTH, WIDE), 0).astype(jnp.float32) + 1.0
    for pair in range(LATS // 2):
        tables = []
        for block in (2 * pair, 2 * pair + 1):
            found = place_at == key[block : block + 1]
            tables.append(
                jnp.sum(jnp.where(found, spot[block : block + 1] + 1.0, 0.0), axis=1, keepdims=True)
            )
        table = jnp.concatenate(tables, axis=0)
        line = jnp.sum(jnp.where(eye, table, 0.0), axis=0, keepdims=True)
        hot = jnp.where(depth == line, 1.0, 0.0).astype(jnp.bfloat16)
        send_ref[:, pair * WIDE : (pair + 1) * WIDE] = hot


def take_kernel(place_ref, holder_ref, take_ref, coef_ref):
    lat = place_ref[1]
    own = holder_ref[pl.ds(lat, 1)]
    masks = iota((PEERS, CHUNK), 0) == own
    rank = jnp.sum(jnp.where(masks, rank_of(masks), 0.0), axis=0, keepdims=True)
    fits = (own >= 0) & (rank < ROOM)
    index = jnp.where(fits, own.astype(jnp.float32) * HALF + rank, -1.0)
    hot = iota((DEPTH, CHUNK), 0).astype(jnp.float32) == index
    take_ref[...] = jnp.where(hot, 1.0, 0.0).astype(jnp.bfloat16)
    row = (lat * ROWS - 8 + iota((TALL, WIDE), 0)).astype(jnp.float32)
    column = (place_ref[2] * COLS - 8 + column_of((TALL, WIDE))).astype(jnp.float32)
    colatitude = 0.25 * math.pi + (row + 0.5) * DTHETA
    longitude = -0.75 * math.pi + (column + 0.5) * DPHI
    sine, cosine = jnp.sin(colatitude), jnp.cos(colatitude)
    twirl = 2.0 * 0.25 / TIME_STEP
    yang = place_ref[0] == 1
    coef_ref[0] = sine
    coef_ref[1] = 1.0 / sine
    coef_ref[2] = twirl * jnp.where(yang, sine * jnp.sin(longitude), cosine)
    coef_ref[3] = twirl * jnp.where(yang, cosine * jnp.sin(longitude), -sine)
    coef_ref[4] = twirl * jnp.where(yang, jnp.cos(longitude), 0.0)


def widen_kernel(place_ref, got_ref, send_ref, lower_ref, west_ref, out_ref, edge_ref):
    column = column_of((8, WIDE))
    for pair in range(PAIRS):
        group, which = pair // 8, pair % 8
        west = turn(west_ref[group, 8:16], -8 * which)
        edge_ref[pair] = jnp.where(column < 8, west, lower_ref[pair, 8:16])
    choice_kernel(place_ref, got_ref, send_ref, out_ref)


def choice_kernel(place_ref, got_ref, send_ref, out_ref):
    parts = from_row(place_ref, got_ref)
    terms = jnp.dot(parts, send_ref[...], preferred_element_type=jnp.float32)
    chosen = join_parts(terms)
    low = iota((16, WIDE), 1) < HALF
    for pair in range(PEERS // 2):
        tile = chosen[:, pair * WIDE : (pair + 1) * WIDE]
        top, end = tile[:16], tile[16:]
        out_ref[2 * pair] = jnp.where(low, top, pltpu.roll(end, HALF, 1))
        out_ref[2 * pair + 1] = jnp.where(low, pltpu.roll(top, HALF, 1), end)


def dense_kernel(place_ref, got_ref, holder_ref, spot_ref, out_ref):
    parts = from_row(place_ref, got_ref)
    index = jnp.where(holder_ref[...] == place_ref[1], spot_ref[...], -1)
    at = iota((CHOICE_DEPTH, CHUNK), 0)
    for block in range(LATS):
        hot = jnp.where(at == index[block : block + 1], 1.0, 0.0).astype(jnp.bfloat16)
        out_ref[block] = join_parts(jnp.dot(parts, hot, preferred_element_type=jnp.float32))


def ghost_values(got_ref, take_ref):
    if len(got_ref.shape) == 2:
        return got_ref[...]
    low = iota((16, WIDE), 1) < HALF
    tiles = []
    for pair in range(PEERS // 2):
        one = got_ref[2 * pair]
        two = got_ref[2 * pair + 1]
        top = jnp.where(low, one, pltpu.roll(two, HALF, 1))
        end = jnp.where(low, pltpu.roll(one, HALF, 1), two)
        tiles.append(jnp.concatenate([top, end], axis=0))
    parts = split_parts(jnp.concatenate(tiles, axis=1))
    return join_parts(jnp.dot(parts, take_ref[...], preferred_element_type=jnp.float32))


def fill_ghosts(place_ref, ghosts, work_ref, rows):
    lat, lon = place_ref[1], place_ref[2]
    trim = (TALL - rows) // 2
    top = 8 - trim
    half = PLANES // 2

    @pl.when((lon == 0) | (lon == LONS - 1))
    def _():
        side = ghosts[:, BAND:]
        first = jnp.where(lon == 0, 4, 8 + COLS)
        own = iota((rows, WIDE), 1) // 4 == iota((rows, WIDE), 0) + trim

        def spread(part):
            return jnp.where(own[None], part[:, None, :], 0.0).reshape(PAIRS * rows, WIDE)

        both = jnp.concatenate([spread(side[:half]), spread(side[half:])], axis=1)
        source = iota((2 * WIDE, WIDE), 0)
        target = first + (source & 3) + jnp.where(source >= WIDE, HALF, 0)
        hot = jnp.where(target == iota((2 * WIDE, WIDE), 1), 1.0, 0.0).astype(jnp.bfloat16)
        moved = split_dot(both, hot).reshape(PAIRS, rows, WIDE)
        column = column_of((rows, WIDE))
        ghost = (column >= first) & (column < first + 4)
        work_ref[...] = jnp.where(ghost[None], moved, work_ref[...])

    @pl.when((lat == 0) | (lat == LATS - 1))
    def _():
        low = iota((half, WIDE), 1) < HALF
        lines = []
        for which in range(2):
            piece = ghosts[:, which * WIDE : (which + 1) * WIDE]
            one, two = piece[:half], piece[half:]
            lines.append(jnp.where(low, one, pltpu.roll(two, HALF, 1)))
            lines.append(jnp.where(low, pltpu.roll(one, HALF, 1), two))

        @pl.when(lat == 0)
        def _():
            for row in range(4):
                work_ref[:, top - 4 + row, :] = lines[row]

        @pl.when(lat == LATS - 1)
        def _():
            for row in range(4):
                work_ref[:, top + ROWS + row, :] = lines[row]


def rates(load, rows, coef_ref, diffusion_ref):
    low = iota((rows, WIDE), 1) < HALF

    def levels(values):
        halves = [
            jnp.where(low, values[LOW_LEVEL[k]], values[HIGH_LEVEL[k]]).astype(jnp.float32)
            for k in range(2)
        ]
        return jnp.concatenate(halves, axis=0)

    def whole(which):
        value = coef_ref[which]
        if rows < TALL:
            value = pltpu.roll(value, TALL - (TALL - rows) // 2, 0)[:rows]
        return jnp.concatenate([value] * 2, axis=0)

    sine = whole(0)
    per_sine = whole(1)
    radius = levels(RADII)
    inverse = levels([1.0 / r for r in RADII])
    square = levels([r * r for r in RADII])
    per_square = levels([1.0 / (r * r) for r in RADII])
    sign = jnp.where(low, 1.0, -1.0)
    ends = sign * (1.0 / RADIAL_STEP)
    inner = sign * (1.0 / (2.0 * RADIAL_STEP))
    viscosity = diffusion_ref[0] * (FINEST * FINEST / TIME_STEP)
    resistivity = diffusion_ref[1] * (FINEST * FINEST / TIME_STEP)

    def slope(value, axis, step):
        size = value.shape[axis]
        near = pltpu.roll(value, size - 1, axis) - pltpu.roll(value, 1, axis)
        far = pltpu.roll(value, size - 2, axis) - pltpu.roll(value, 2, axis)
        return near * (8.0 / (12.0 * step)) - far * (1.0 / (12.0 * step))

    def d_theta(value):
        return slope(value, 0, DTHETA)

    def d_phi(value):
        return slope(value, 1, DPHI)

    def d_radius(value):
        one, two = value[:rows], value[rows:]
        return jnp.concatenate(
            [(two - one) * ends, (pltpu.roll(two, HALF, 1) - one) * inner], axis=0
        )

    def by_radius(value):
        return value * radius

    def per_radius(value):
        return value * inverse

    def curl(vector):
        part_r, part_t, part_p = vector
        return (
            per_radius((d_theta(sine * part_p) - d_phi(part_t)) * per_sine),
            per_radius(d_phi(part_r) * per_sine - d_radius(by_radius(part_p))),
            per_radius(d_radius(by_radius(part_t)) - d_theta(part_r)),
        )

    def gradient(value):
        return (
            d_radius(value),
            per_radius(d_theta(value)),
            per_radius(d_phi(value) * per_sine),
        )

    def cross(left, right):
        return (
            left[1] * right[2] - left[2] * right[1],
            left[2] * right[0] - left[0] * right[2],
            left[0] * right[1] - left[1] * right[0],
        )

    def advect(vector, slopes):
        return vector[0] * slopes[0] + vector[1] * slopes[1] + vector[2] * slopes[2]

    velocity = [load(which) for which in (1, 2, 3)]
    magnetic = [load(which) for which in (4, 5, 6)]
    vorticity = curl(velocity)
    current = curl(magnetic)
    spread = d_radius(square * velocity[0]) * per_square + per_radius(
        (d_theta(sine * velocity[1]) + d_phi(velocity[2])) * per_sine
    )
    induced = cross(velocity, magnetic)
    electric = [induced[k] - resistivity * current[k] for k in range(3)]
    kinetic = 0.5 * (
        velocity[0] * velocity[0] + velocity[1] * velocity[1] + velocity[2] * velocity[2]
    )
    curl_electric = curl(electric)
    log_rho = load(0)
    rho_rate = -advect(velocity, gradient(log_rho)) - spread
    pressure = load(7)
    slope_pressure = gradient(pressure)
    pressure_rate = -advect(velocity, slope_pressure) - GAMMA * pressure * spread
    lorentz = cross(current, magnetic)
    per_rho = jnp.exp(-log_rho)
    slope_kinetic = gradient(kinetic)
    curl_vorticity = curl(vorticity)
    lamb = cross(velocity, vorticity)
    turning = cross((whole(2), whole(3), whole(4)), velocity)
    momentum = [
        lamb[k]
        - slope_kinetic[k]
        + per_rho * (lorentz[k] - slope_pressure[k])
        - turning[k]
        - viscosity * curl_vorticity[k]
        for k in range(3)
    ]
    return [rho_rate, *momentum, *curl_electric, pressure_rate]


def first_kernel(
    place_ref,
    diffusion_ref,
    lower_ref,
    north_ref,
    west_ref,
    got_ref,
    take_ref,
    coef_ref,
    pick_ref,
    mix_ref,
    spin_ref,
    flag_ref,
    middle_ref,
    out_ref,
    work_ref,
    next_ref,
):
    column = column_of((TALL, WIDE))
    for pair in range(PAIRS):
        group, which = pair // 8, pair % 8
        west = turn(west_ref[group], -8 * which)
        work_ref[pair, :8] = north_ref[pair]
        work_ref[pair, 8:] = jnp.where(column[8:] < 8, west, lower_ref[pair])
    ghosts = ghost_values(got_ref, take_ref)
    fill_ghosts(place_ref, ghosts, work_ref, TALL)

    def load(which):
        return work_ref[2 * which : 2 * which + 2].reshape(2 * TALL, WIDE)

    found = rates(load, TALL, coef_ref, diffusion_ref)
    row = iota((TALL, WIDE), 0)
    inside = (column >= 4) & (column < 12 + COLS) & (row >= 4) & (row < 12 + ROWS)
    for which in range(FIELDS):
        value = load(which) + (0.5 * TIME_STEP) * found[which]
        for half in range(2):
            part = jnp.where(inside, value[half * TALL : (half + 1) * TALL], 0.0)
            next_ref[2 * which + half] = part[8:]
            middle_ref[2 * which + half] = pltpu.roll(part, TALL - 4, 0)[:MID]
    planes = next_ref[...].reshape(PAIRS * MID, WIDE)
    packed = donor_message(planes, pick_ref[...], mix_ref[...], spin_ref[...])
    post_message(place_ref, packed, flag_ref[...], out_ref)


def second_kernel(
    place_ref,
    diffusion_ref,
    middle_ref,
    got_ref,
    take_ref,
    coef_ref,
    held_ref,
    whole_ref,
    third_ref,
    work_ref,
):
    work_ref[...] = middle_ref[...]
    ghosts = ghost_values(got_ref, take_ref)
    fill_ghosts(place_ref, ghosts, work_ref, MID)

    def load(which):
        return work_ref[2 * which : 2 * which + 2].reshape(2 * MID, WIDE)

    found = rates(load, MID, coef_ref, diffusion_ref)

    def centre(value):
        return pltpu.roll(value, MID - 4, 0)[:ROWS]

    def place(out_ref, pair, value):
        field, half = pair // 2, pair % 2
        out_ref[field, LOW_LEVEL[half]] = turn(value, -8)[:, :COLS]
        out_ref[field, HIGH_LEVEL[half]] = turn(value, -8 - HALF)[:, :COLS]

    for pair in range(PAIRS):
        field, half = pair // 2, pair % 2
        rate = found[field][half * MID : (half + 1) * MID]
        held = held_ref[pair]
        step = centre(rate) * (0.5 * TIME_STEP)
        middle = centre(middle_ref[pair])
        place(third_ref, pair, held + step)
        place(whole_ref, pair, held + ((middle - held) + 2.0 * step) * (1.0 / 3.0))


def shift(value, move_lat, move_lon):
    pairs = []
    for a in range(LATS):
        for b in range(LONS):
            goal_a, goal_b = a + move_lat, b + move_lon
            if 0 <= goal_a < LATS and 0 <= goal_b < LONS:
                pairs.append((a * LONS + b, goal_a * LONS + goal_b))
    return lax.ppermute(value, ("lat", "lon"), pairs)


def shards(state, donor_cell, donor_weights, donor_turn, border_source, diffusion):
    fields = state[0]
    panel = lax.axis_index("panel")
    lat = lax.axis_index("lat")
    lon = lax.axis_index("lon")
    place = jnp.stack([panel, lat, lon]).astype(jnp.int32)
    f32 = jnp.float32

    def call(kernel, outs, *args, smem=0, specs=None, scratch=(), limit=10):
        shapes = [jax.ShapeDtypeStruct(shape, dtype) for shape, dtype in outs]
        return pl.pallas_call(
            kernel,
            out_shape=shapes,
            in_specs=specs or [SMEM] * smem + [VMEM] * (len(args) - smem),
            out_specs=[VMEM] * len(outs),
            scratch_shapes=scratch,
            compiler_params=pltpu.CompilerParams(vmem_limit_bytes=limit * MIB),
        )(*args)

    bf16 = jnp.bfloat16
    held, south, east, corner = call(
        cut_kernel,
        [
            ((PAIRS, ROWS, WIDE), f32),
            ((PAIRS, 8, WIDE), f32),
            ((2, ROWS, WIDE), f32),
            ((2, 8, WIDE), f32),
        ],
        fields,
        scratch=[pltpu.VMEM((PLANES, ROWS, WIDE), f32)],
    )
    south = shift(south, -1, 0)
    east = shift(east, 0, -1)
    corner = shift(corner, -1, -1)

    ring = PANEL_COLS + 8
    row_slots = LONS * SLOTS
    border = border_source[0]
    bands = border[: 8 * ring].reshape(8, ring)
    sides = border[8 * ring :].reshape(PANEL_ROWS, 8)
    donor = jnp.concatenate(
        [donor_cell[0, 0].astype(f32), donor_weights[0, 0, 0], donor_turn[0, 0]], axis=0
    )
    pick, mix, spin, flag = call(
        prepare_kernel,
        [((WIDE, 2 * WIDE), bf16), ((MID, 2 * WIDE), f32), ((2, WIDE), f32), ((8, WIDE), f32)],
        donor,
        jnp.pad(bands, ((0, 0), (0, 7 * WIDE - ring)), constant_values=-1),
        sides.T,
        scratch=[pltpu.VMEM((1, WIDE), f32)],
    )
    message = ((2 * PEERS, 16, WIDE), f32)
    lower, sent = call(
        donor_kernel,
        [((PAIRS, MID, WIDE), f32), message],
        place,
        held,
        south,
        east,
        corner,
        pick,
        mix,
        spin,
        flag,
        smem=1,
    )

    def to_holders(sent):
        return lax.all_to_all(sent, ("panel", "lon"), 0, 0, tiled=True)

    got = to_holders(sent)

    crowded = jnp.maximum(got[0, 0, FLAG_LANE], got[PEERS, 0, FLAG_LANE]) > ROOM

    late_lat, late_lon, bands, sides, late_lower, _ = lax.optimization_barrier(
        (lat, lon, bands, sides, lower, sent)
    )
    (west,) = call(last_kernel, [((2, MID, WIDE), f32)], late_lower)
    west = shift(west, 0, 1)

    window = jnp.pad(bands, ((0, 0), (4, 4)), constant_values=-1)
    window = lax.dynamic_slice(window, (0, late_lon * COLS), (8, 64)).reshape(2, BAND)
    side = jnp.where(late_lon == 0, sides[:, :4], sides[:, 4:])
    side = jnp.where((late_lon == 0) | (late_lon == LONS - 1), side, -1)
    side = jnp.pad(side, ((8, 8), (0, 0)), constant_values=-1)
    side = jnp.concatenate(
        [
            side[:PANEL_ROWS].reshape(LATS, ROWS, 4),
            side[ROWS:].reshape(LATS, ROWS, 4),
        ],
        axis=1,
    ).reshape(LATS, SIDE)
    at_lat = jnp.arange(LATS)[:, None]
    band = jnp.where(at_lat == 0, window[:1], jnp.where(at_lat == LATS - 1, window[1:], -1))
    wanted = jnp.concatenate([band, side], axis=1)
    holder = jnp.where(wanted >= 0, wanted // row_slots, -1)
    local = wanted - late_lat * row_slots
    block = local // SLOTS
    spot = block // 3 * WIDE + block % 3 * THIRD + local % SLOTS
    (send,) = call(
        send_kernel, [((CHOICE_DEPTH, DEPTH), bf16)], place, holder, spot, smem=1, limit=16
    )
    chunk = ((PEERS, 16, WIDE), f32)
    first_got = got
    chunks, north = call(
        widen_kernel, [chunk, ((PAIRS, 8, WIDE), f32)], place, got, send, lower, west, smem=1
    )
    north = shift(north, 1, 0)
    late_holder, _ = lax.optimization_barrier((holder, chunks))
    take, coef = call(
        take_kernel,
        [((DEPTH, CHUNK), bf16), ((5, TALL, WIDE), f32)],
        place,
        late_holder,
        smem=1,
    )

    def to_blocks(chunks):
        return lax.all_to_all(chunks, "lat", 0, 0, tiled=True)

    def section_one(got):
        return call(
            first_kernel,
            [((PAIRS, MID, WIDE), f32), message],
            place,
            diffusion,
            lower,
            north,
            west,
            got,
            take,
            coef,
            pick,
            mix,
            spin,
            flag,
            smem=2,
            scratch=[pltpu.VMEM((PAIRS, TALL, WIDE), f32), pltpu.VMEM((PAIRS, MID, WIDE), f32)],
        )

    def section_two(middle, got):
        return call(
            second_kernel,
            [(fields.shape, f32), (fields.shape, f32)],
            place,
            diffusion,
            middle,
            got,
            take,
            coef,
            held,
            smem=2,
            scratch=[pltpu.VMEM((PAIRS, MID, WIDE), f32)],
        )

    middle, sent = section_one(to_blocks(chunks))
    got = to_holders(sent)
    (chunks,) = call(choice_kernel, [chunk], place, got, send, smem=1)
    fitting = section_two(middle, to_blocks(chunks))

    def with_room():
        def dense(got):
            chunks = call(
                dense_kernel,
                [((PEERS, PLANES, CHUNK), f32)],
                place,
                got,
                holder,
                spot,
                smem=1,
                limit=16,
            )
            return to_blocks(chunks[0]).sum(axis=0)

        middle, sent = section_one(dense(first_got))
        return section_two(middle, dense(to_holders(sent)))

    accumulated, section_three = lax.cond(crowded, with_room, lambda: fitting)
    return (accumulated[None], section_three[None])


def solution(mesh):
    return jax.shard_map(
        shards,
        mesh=mesh,
        in_specs=(
            P("panel", None, None, "lat", "lon"),
            P("panel", "lat", "lon", None),
            P("panel", "lat", "lon", None, None),
            P("panel", "lat", "lon", None),
            P("panel", None),
            P(),
        ),
        out_specs=(P("panel", None, None, "lat", "lon"), P("panel", None, None, "lat", "lon")),
        check_vma=False,
    )
```

```python
import math

import jax
import jax.numpy as jnp
from jax import lax
from jax.experimental import pallas as pl
from jax.experimental.pallas import tpu as pltpu
from jax.sharding import PartitionSpec as P

GAMMA = 5.0 / 3.0
RADIAL_STEP = 0.65 / 32.0
FIELDS = 8
LEVELS = 4
PLANES = FIELDS * LEVELS
PAIRS = PLANES // 2
LOW_LEVEL = (0, 1)
HIGH_LEVEL = (3, 2)
ROWS = 16
COLS = 48
SLOTS = 33
LATS = 16
LONS = 16
ROOM = 63
WIDE = 128
HALF = 64
TALL = ROWS + 16
MID = ROWS + 8
BAND = 4 * HALF
SIDE = 4 * TALL
CHUNK = BAND + SIDE
PEERS = 16
PACKED = 32
MESSAGE = 9 * WIDE
TAIL = 8 * WIDE
FLAG = TAIL + HALF - 1
CHOICE_TILES = PEERS * PACKED // WIDE
CHOICE_DEPTH = (CHOICE_TILES + 1) * WIDE
DEPTH = PEERS * HALF
PANEL_ROWS = ROWS * LATS
PANEL_COLS = COLS * LONS
DTHETA = 0.5 * math.pi / PANEL_ROWS
DPHI = 1.5 * math.pi / PANEL_COLS
FINEST = min(DTHETA, DPHI)
TIME_STEP = 0.1 * FINEST
RADII = [0.35 + 0.65 * (k + 16 - LEVELS // 2 + 0.5) / 32.0 for k in range(LEVELS)]
VMEM = pl.BlockSpec(memory_space=pltpu.VMEM)
SMEM = pl.BlockSpec(memory_space=pltpu.SMEM)
MIB = 1024 * 1024


def iota(shape, axis):
    return lax.broadcasted_iota(jnp.int32, shape, axis)


def column_of(shape):
    return iota(shape, len(shape) - 1) & (HALF - 1)


def turn(value, lanes):
    return pltpu.roll(value, lanes % WIDE, 1) if lanes % WIDE else value


def split_dot(left, right):
    total = None
    for _ in range(3):
        part = left.astype(jnp.bfloat16)
        left = left - part.astype(jnp.float32)
        term = jnp.dot(part, right, preferred_element_type=jnp.float32)
        total = term if total is None else total + term
    return total


def donor_message(planes, pick, mix, spin):
    chosen = split_dot(planes, pick).reshape(PAIRS, MID, 2 * WIDE)
    both = jnp.sum(chosen * mix[None], axis=1)
    both = jnp.concatenate([both[:, :WIDE], both[:, WIDE:]], axis=0)
    mixed = both + pltpu.roll(both, HALF, 1)
    cosine = spin[0:1]
    sine = spin[1:2]
    at = (iota((PLANES, WIDE), 0) & (PAIRS - 1)) // 2
    theta = (at == 2) | (at == 5)
    phi = (at == 3) | (at == 6)
    other = jnp.where(theta, pltpu.roll(mixed, PLANES - 2, 0), -pltpu.roll(mixed, 2, 0))
    turned = jnp.where(theta | phi, cosine * mixed + sine * other, mixed)
    return jnp.where(iota((PAIRS, WIDE), 1) < HALF, turned[:PAIRS], turned[PAIRS:])


def post_message(place_ref, packed, flag, out_ref):
    panel = place_ref[0]
    lane = iota((16, WIDE), 1)
    column = lane & (HALF - 1)
    dense = jnp.where(column[:8] < PACKED, packed[:8], turn(packed[8:], PACKED))
    last = jnp.where(
        lane < HALF, packed[:, PACKED : PACKED + 1], packed[:, HALF + PACKED : HALF + PACKED + 1]
    )
    tail = jnp.sum(jnp.where(column == iota((16, WIDE), 0), last, 0.0), axis=0, keepdims=True)
    blank = jnp.where(lane[:1] == FLAG - TAIL, flag, 0.0)
    tail = jnp.where(lane[:1] == FLAG - TAIL, flag, tail)
    zero = jnp.zeros((1, WIDE), jnp.float32)
    for row in range(9):
        full = dense[row : row + 1] if row < 8 else tail
        empty = zero if row < 8 else blank
        at = slice(row * WIDE, (row + 1) * WIDE)
        out_ref[pl.ds((1 - panel) * PEERS, PEERS), :, at] = jnp.broadcast_to(
            full[None], (PEERS, 1, WIDE)
        )
        out_ref[pl.ds(panel * PEERS, PEERS), :, at] = jnp.broadcast_to(
            empty[None], (PEERS, 1, WIDE)
        )


def cut_kernel(state_ref, held_ref, south_ref, east_ref, corner_ref, plane_ref):
    for plane in range(PLANES):
        plane_ref[plane, :, :COLS] = state_ref[plane // LEVELS, plane % LEVELS]
    lane = iota((ROWS, WIDE), 1)
    column = column_of((ROWS, WIDE))
    own = (column >= 8) & (column < 8 + COLS)
    for pair in range(PAIRS):
        field, which = pair // 2, pair % 2
        low = turn(plane_ref[field * LEVELS + LOW_LEVEL[which]], 8)
        high = turn(plane_ref[field * LEVELS + HIGH_LEVEL[which]], HALF + 8)
        tile = jnp.where(own, jnp.where(lane < HALF, low, high), 0.0)
        held_ref[pair] = tile
        south_ref[pair] = tile[:8]
    for group in range(2):
        columns = jnp.zeros((ROWS, WIDE), jnp.float32)
        for which in range(8):
            moved = turn(held_ref[8 * group + which], 8 * which - 8)
            columns = jnp.where(column // 8 == which, moved, columns)
        east_ref[group] = columns
        corner_ref[group] = columns[:8]


def donor_tables(donor_ref, pick_ref, mix_ref, spin_ref, line_ref):
    late = iota((1, WIDE), 1) >= HALF

    def twice(value, fill):
        line_ref[...] = jnp.full((1, WIDE), fill, jnp.float32)
        line_ref[:, :SLOTS] = value
        line = line_ref[...]
        return jnp.where(late, pltpu.roll(line, HALF, 1), line)

    cell = twice(donor_ref[0:1], -10.0 * COLS)
    row_at = jnp.floor((cell + 0.5) * (1.0 / COLS))
    col_at = cell - row_at * COLS + jnp.where(late, 1.0, 0.0)
    upper = jnp.where(late, twice(donor_ref[2:3], 0.0), twice(donor_ref[1:2], 0.0))
    lower = jnp.where(late, twice(donor_ref[4:5], 0.0), twice(donor_ref[3:4], 0.0))
    angle = twice(donor_ref[5:6], 0.0)
    spin_ref[0:1] = jnp.cos(angle)
    spin_ref[1:2] = jnp.sin(angle)
    lane = iota((WIDE, WIDE), 0).astype(jnp.float32)
    real = jnp.where(row_at >= 0, col_at + 8.0, -1000.0)
    pick_ref[:, :WIDE] = jnp.where(lane == real, 1.0, 0.0).astype(jnp.bfloat16)
    pick_ref[:, WIDE:] = jnp.where(lane == real + HALF, 1.0, 0.0).astype(jnp.bfloat16)
    row = iota((MID, WIDE), 0).astype(jnp.float32)
    mix = jnp.where(row == row_at, upper, 0.0) + jnp.where(row == row_at + 1.0, lower, 0.0)
    mix_ref[:, :WIDE] = mix
    mix_ref[:, WIDE:] = mix


def count_kernel(bands_ref, sides_ref, flag_ref):
    width = bands_ref.shape[1]
    column = iota((width, WIDE), 0) - 4
    start = iota((width, WIDE), 1) * COLS - 8
    within = (column >= start) & (column < start + 64) & (start < PANEL_COLS)
    columns = jnp.where(within, 1.0, 0.0).astype(jnp.bfloat16)
    row = iota((PANEL_ROWS, WIDE), 0)
    start = iota((PANEL_ROWS, WIDE), 1) * ROWS - 8
    within = (row >= start) & (row < start + TALL) & (start < PANEL_ROWS)
    rows = jnp.where(within, 1.0, 0.0).astype(jnp.bfloat16)

    def most(slots, windows):
        ones = []
        for which in range(LATS):
            first = which * LONS * SLOTS
            inside = (slots >= first) & (slots < first + LONS * SLOTS)
            ones.append(jnp.where(inside, 1.0, 0.0))
        ones = jnp.concatenate(ones, axis=0).astype(jnp.bfloat16)
        counts = jnp.dot(ones, windows, preferred_element_type=jnp.float32)
        return jnp.max(jnp.sum(counts.reshape(2 * LATS, 4, WIDE), axis=1))

    total = most(bands_ref[...], columns) + most(sides_ref[...], rows)
    flag_ref[...] = jnp.full(flag_ref.shape, total, jnp.float32)


def donor_kernel(
    place_ref, held_ref, south_ref, east_ref, corner_ref, pick_ref, mix_ref, spin_ref,
    lower_ref, out_ref
):
    column = column_of((ROWS, WIDE))
    beyond = column >= 8 + COLS
    for pair in range(PAIRS):
        group, which = pair // 8, pair % 8
        east = turn(east_ref[group], 8 + COLS - 8 * which)
        corner = turn(corner_ref[group], 8 + COLS - 8 * which)
        lower_ref[pair, :ROWS] = jnp.where(beyond, east, held_ref[pair])
        lower_ref[pair, ROWS:] = jnp.where(beyond[:8], corner, south_ref[pair])
    planes = lower_ref[...].reshape(PAIRS * MID, WIDE)
    packed = donor_message(planes, pick_ref[...], mix_ref[...], spin_ref[...])
    post_message(place_ref, packed, jnp.zeros((1, WIDE), jnp.float32), out_ref)


def last_kernel(lower_ref, west_ref):
    column = column_of((MID, WIDE))
    for group in range(2):
        columns = jnp.zeros((MID, WIDE), jnp.float32)
        for which in range(8):
            moved = turn(lower_ref[8 * group + which], 8 * which - COLS)
            columns = jnp.where(column // 8 == which, moved, columns)
        west_ref[group] = columns


def split_parts(held):
    parts = []
    for _ in range(3):
        part = held.astype(jnp.bfloat16)
        held = held - part.astype(jnp.float32)
        parts.append(part)
    return jnp.concatenate(parts, axis=0)


def join_parts(terms):
    return terms[:PLANES] + terms[PLANES : 2 * PLANES] + terms[2 * PLANES :]


def from_row(place_ref, got_ref):
    base = (1 - place_ref[0]) * PEERS
    part = iota((8, WIDE), 1) // PACKED
    tiles = []
    tails = []
    for tile in range(CHOICE_TILES):
        rows = [jnp.zeros((8, WIDE), jnp.float32)] * 4
        for which in range(4):
            at = base + 4 * tile + which
            message = jnp.concatenate(
                [got_ref[at, :, row * WIDE : (row + 1) * WIDE] for row in range(8)], axis=0
            )
            tails.append(got_ref[at, :, TAIL:])
            for group in range(4):
                moved = turn(message, PACKED * (which - group))
                rows[group] = jnp.where(part == which, moved, rows[group])
        tiles.append(jnp.concatenate(rows, axis=0))
    tails.append(jnp.zeros((WIDE - PEERS, WIDE), jnp.float32))
    tails = jnp.concatenate(tails, axis=0).T
    tiles.append(jnp.concatenate([tails[:PAIRS], tails[HALF : HALF + PAIRS]], axis=0))
    return split_parts(jnp.concatenate(tiles, axis=1))


def rank_of(chosen):
    order = iota((CHUNK, CHUNK), 0) < iota((CHUNK, CHUNK), 1)
    order = jnp.where(order, 1.0, 0.0).astype(jnp.bfloat16)
    ones = jnp.where(chosen, 1.0, 0.0).astype(jnp.bfloat16)
    return jnp.dot(ones, order, preferred_element_type=jnp.float32)


def send_kernel(place_ref, holder_ref, spot_ref, send_ref):
    mine = holder_ref[...] == place_ref[1]
    spot = spot_ref[...].astype(jnp.float32)
    rank = rank_of(mine)
    key = jnp.where(mine & (rank < ROOM), rank, -1.0)
    place_at = iota((HALF, CHUNK), 0).astype(jnp.float32)
    eye = iota((WIDE, WIDE), 0) == iota((WIDE, WIDE), 1)
    depth = iota((CHOICE_DEPTH, WIDE), 0).astype(jnp.float32) + 1.0
    for pair in range(LATS // 2):
        tables = []
        for block in (2 * pair, 2 * pair + 1):
            found = place_at == key[block : block + 1]
            tables.append(
                jnp.sum(jnp.where(found, spot[block : block + 1] + 1.0, 0.0), axis=1, keepdims=True)
            )
        table = jnp.concatenate(tables, axis=0)
        line = jnp.sum(jnp.where(eye, table, 0.0), axis=0, keepdims=True)
        hot = jnp.where(depth == line, 1.0, 0.0).astype(jnp.bfloat16)
        send_ref[:, pair * WIDE : (pair + 1) * WIDE] = hot


def take_kernel(place_ref, holder_ref, take_ref, coef_ref):
    lat = place_ref[1]
    own = holder_ref[pl.ds(lat, 1)]
    masks = iota((PEERS, CHUNK), 0) == own
    rank = jnp.sum(jnp.where(masks, rank_of(masks), 0.0), axis=0, keepdims=True)
    fits = (own >= 0) & (rank < ROOM)
    index = jnp.where(fits, own.astype(jnp.float32) * HALF + rank, -1.0)
    hot = iota((DEPTH, CHUNK), 0).astype(jnp.float32) == index
    take_ref[...] = jnp.where(hot, 1.0, 0.0).astype(jnp.bfloat16)
    row = (lat * ROWS - 8 + iota((TALL, WIDE), 0)).astype(jnp.float32)
    column = (place_ref[2] * COLS - 8 + column_of((TALL, WIDE))).astype(jnp.float32)
    colatitude = 0.25 * math.pi + (row + 0.5) * DTHETA
    longitude = -0.75 * math.pi + (column + 0.5) * DPHI
    sine, cosine = jnp.sin(colatitude), jnp.cos(colatitude)
    twirl = 2.0 * 0.25 / TIME_STEP
    yang = place_ref[0] == 1
    coef_ref[0] = sine
    coef_ref[1] = 1.0 / sine
    coef_ref[2] = twirl * jnp.where(yang, sine * jnp.sin(longitude), cosine)
    coef_ref[3] = twirl * jnp.where(yang, cosine * jnp.sin(longitude), -sine)
    coef_ref[4] = twirl * jnp.where(yang, jnp.cos(longitude), 0.0)


def widen_kernel(place_ref, got_ref, send_ref, lower_ref, west_ref, out_ref, edge_ref):
    column = column_of((8, WIDE))
    for pair in range(PAIRS):
        group, which = pair // 8, pair % 8
        west = turn(west_ref[group, 8:16], -8 * which)
        edge_ref[pair] = jnp.where(column < 8, west, lower_ref[pair, 8:16])
    choice_kernel(place_ref, got_ref, send_ref, out_ref)


def choice_kernel(place_ref, got_ref, send_ref, out_ref):
    parts = from_row(place_ref, got_ref)
    terms = jnp.dot(parts, send_ref[...], preferred_element_type=jnp.float32)
    chosen = join_parts(terms)
    low = iota((16, WIDE), 1) < HALF
    for pair in range(PEERS // 2):
        tile = chosen[:, pair * WIDE : (pair + 1) * WIDE]
        top, end = tile[:16], tile[16:]
        out_ref[2 * pair] = jnp.where(low, top, pltpu.roll(end, HALF, 1))
        out_ref[2 * pair + 1] = jnp.where(low, pltpu.roll(top, HALF, 1), end)


def dense_kernel(place_ref, got_ref, holder_ref, spot_ref, out_ref):
    parts = from_row(place_ref, got_ref)
    index = jnp.where(holder_ref[...] == place_ref[1], spot_ref[...], -1)
    at = iota((CHOICE_DEPTH, CHUNK), 0)
    for block in range(LATS):
        hot = jnp.where(at == index[block : block + 1], 1.0, 0.0).astype(jnp.bfloat16)
        out_ref[block] = join_parts(jnp.dot(parts, hot, preferred_element_type=jnp.float32))


def ghost_values(got_ref, take_ref):
    if len(got_ref.shape) == 2:
        return got_ref[...]
    low = iota((16, WIDE), 1) < HALF
    tiles = []
    for pair in range(PEERS // 2):
        one = got_ref[2 * pair]
        two = got_ref[2 * pair + 1]
        top = jnp.where(low, one, pltpu.roll(two, HALF, 1))
        end = jnp.where(low, pltpu.roll(one, HALF, 1), two)
        tiles.append(jnp.concatenate([top, end], axis=0))
    parts = split_parts(jnp.concatenate(tiles, axis=1))
    return join_parts(jnp.dot(parts, take_ref[...], preferred_element_type=jnp.float32))


def fill_ghosts(place_ref, ghosts, work_ref, rows):
    lat, lon = place_ref[1], place_ref[2]
    trim = (TALL - rows) // 2
    top = 8 - trim
    half = PLANES // 2

    @pl.when((lon == 0) | (lon == LONS - 1))
    def _():
        side = ghosts[:, BAND:]
        first = jnp.where(lon == 0, 4, 8 + COLS)
        own = iota((rows, WIDE), 1) // 4 == iota((rows, WIDE), 0) + trim

        def spread(part):
            return jnp.where(own[None], part[:, None, :], 0.0).reshape(PAIRS * rows, WIDE)

        both = jnp.concatenate([spread(side[:half]), spread(side[half:])], axis=1)
        source = iota((2 * WIDE, WIDE), 0)
        target = first + (source & 3) + jnp.where(source >= WIDE, HALF, 0)
        hot = jnp.where(target == iota((2 * WIDE, WIDE), 1), 1.0, 0.0).astype(jnp.bfloat16)
        moved = split_dot(both, hot).reshape(PAIRS, rows, WIDE)
        column = column_of((rows, WIDE))
        ghost = (column >= first) & (column < first + 4)
        work_ref[...] = jnp.where(ghost[None], moved, work_ref[...])

    @pl.when((lat == 0) | (lat == LATS - 1))
    def _():
        low = iota((half, WIDE), 1) < HALF
        lines = []
        for which in range(2):
            piece = ghosts[:, which * WIDE : (which + 1) * WIDE]
            one, two = piece[:half], piece[half:]
            lines.append(jnp.where(low, one, pltpu.roll(two, HALF, 1)))
            lines.append(jnp.where(low, pltpu.roll(one, HALF, 1), two))

        @pl.when(lat == 0)
        def _():
            for row in range(4):
                work_ref[:, top - 4 + row, :] = lines[row]

        @pl.when(lat == LATS - 1)
        def _():
            for row in range(4):
                work_ref[:, top + ROWS + row, :] = lines[row]


def rates(load, rows, coef_ref, diffusion_ref):
    low = iota((rows, WIDE), 1) < HALF

    def levels(values):
        halves = [
            jnp.where(low, values[LOW_LEVEL[k]], values[HIGH_LEVEL[k]]).astype(jnp.float32)
            for k in range(2)
        ]
        return jnp.concatenate(halves, axis=0)

    def whole(which):
        value = coef_ref[which]
        if rows < TALL:
            value = pltpu.roll(value, TALL - (TALL - rows) // 2, 0)[:rows]
        return jnp.concatenate([value] * 2, axis=0)

    sine = whole(0)
    per_sine = whole(1)
    radius = levels(RADII)
    inverse = levels([1.0 / r for r in RADII])
    square = levels([r * r for r in RADII])
    per_square = levels([1.0 / (r * r) for r in RADII])
    sign = jnp.where(low, 1.0, -1.0)
    ends = sign * (1.0 / RADIAL_STEP)
    inner = sign * (1.0 / (2.0 * RADIAL_STEP))
    viscosity = diffusion_ref[0] * (FINEST * FINEST / TIME_STEP)
    resistivity = diffusion_ref[1] * (FINEST * FINEST / TIME_STEP)

    def slope(value, axis, step):
        size = value.shape[axis]
        near = pltpu.roll(value, size - 1, axis) - pltpu.roll(value, 1, axis)
        far = pltpu.roll(value, size - 2, axis) - pltpu.roll(value, 2, axis)
        return near * (8.0 / (12.0 * step)) - far * (1.0 / (12.0 * step))

    def d_theta(value):
        return slope(value, 0, DTHETA)

    def d_phi(value):
        return slope(value, 1, DPHI)

    def d_radius(value):
        one, two = value[:rows], value[rows:]
        return jnp.concatenate(
            [(two - one) * ends, (pltpu.roll(two, HALF, 1) - one) * inner], axis=0
        )

    def by_radius(value):
        return value * radius

    def per_radius(value):
        return value * inverse

    def curl(vector):
        part_r, part_t, part_p = vector
        return (
            per_radius((d_theta(sine * part_p) - d_phi(part_t)) * per_sine),
            per_radius(d_phi(part_r) * per_sine - d_radius(by_radius(part_p))),
            per_radius(d_radius(by_radius(part_t)) - d_theta(part_r)),
        )

    def gradient(value):
        return (
            d_radius(value),
            per_radius(d_theta(value)),
            per_radius(d_phi(value) * per_sine),
        )

    def cross(left, right):
        return (
            left[1] * right[2] - left[2] * right[1],
            left[2] * right[0] - left[0] * right[2],
            left[0] * right[1] - left[1] * right[0],
        )

    def advect(vector, slopes):
        return vector[0] * slopes[0] + vector[1] * slopes[1] + vector[2] * slopes[2]

    velocity = [load(which) for which in (1, 2, 3)]
    magnetic = [load(which) for which in (4, 5, 6)]
    vorticity = curl(velocity)
    current = curl(magnetic)
    spread = d_radius(square * velocity[0]) * per_square + per_radius(
        (d_theta(sine * velocity[1]) + d_phi(velocity[2])) * per_sine
    )
    induced = cross(velocity, magnetic)
    electric = [induced[k] - resistivity * current[k] for k in range(3)]
    kinetic = 0.5 * (
        velocity[0] * velocity[0] + velocity[1] * velocity[1] + velocity[2] * velocity[2]
    )
    curl_electric = curl(electric)
    log_rho = load(0)
    rho_rate = -advect(velocity, gradient(log_rho)) - spread
    pressure = load(7)
    slope_pressure = gradient(pressure)
    pressure_rate = -advect(velocity, slope_pressure) - GAMMA * pressure * spread
    lorentz = cross(current, magnetic)
    per_rho = jnp.exp(-log_rho)
    slope_kinetic = gradient(kinetic)
    curl_vorticity = curl(vorticity)
    lamb = cross(velocity, vorticity)
    turning = cross((whole(2), whole(3), whole(4)), velocity)
    momentum = [
        lamb[k]
        - slope_kinetic[k]
        + per_rho * (lorentz[k] - slope_pressure[k])
        - turning[k]
        - viscosity * curl_vorticity[k]
        for k in range(3)
    ]
    return [rho_rate, *momentum, *curl_electric, pressure_rate]


def first_kernel(
    place_ref,
    diffusion_ref,
    lower_ref,
    north_ref,
    west_ref,
    got_ref,
    take_ref,
    coef_ref,
    pick_ref,
    mix_ref,
    spin_ref,
    flag_ref,
    middle_ref,
    out_ref,
    work_ref,
    next_ref,
):
    column = column_of((TALL, WIDE))
    for pair in range(PAIRS):
        group, which = pair // 8, pair % 8
        west = turn(west_ref[group], -8 * which)
        work_ref[pair, :8] = north_ref[pair]
        work_ref[pair, 8:] = jnp.where(column[8:] < 8, west, lower_ref[pair])
    ghosts = ghost_values(got_ref, take_ref)
    fill_ghosts(place_ref, ghosts, work_ref, TALL)

    def load(which):
        return work_ref[2 * which : 2 * which + 2].reshape(2 * TALL, WIDE)

    found = rates(load, TALL, coef_ref, diffusion_ref)
    row = iota((TALL, WIDE), 0)
    inside = (column >= 4) & (column < 12 + COLS) & (row >= 4) & (row < 12 + ROWS)
    for which in range(FIELDS):
        value = load(which) + (0.5 * TIME_STEP) * found[which]
        for half in range(2):
            part = jnp.where(inside, value[half * TALL : (half + 1) * TALL], 0.0)
            next_ref[2 * which + half] = part[8:]
            middle_ref[2 * which + half] = pltpu.roll(part, TALL - 4, 0)[:MID]
    planes = next_ref[...].reshape(PAIRS * MID, WIDE)
    packed = donor_message(planes, pick_ref[...], mix_ref[...], spin_ref[...])
    post_message(place_ref, packed, flag_ref[0:1], out_ref)


def second_kernel(
    place_ref,
    diffusion_ref,
    middle_ref,
    got_ref,
    take_ref,
    coef_ref,
    held_ref,
    whole_ref,
    third_ref,
    work_ref,
):
    work_ref[...] = middle_ref[...]
    ghosts = ghost_values(got_ref, take_ref)
    fill_ghosts(place_ref, ghosts, work_ref, MID)

    def load(which):
        return work_ref[2 * which : 2 * which + 2].reshape(2 * MID, WIDE)

    found = rates(load, MID, coef_ref, diffusion_ref)

    def centre(value):
        return pltpu.roll(value, MID - 4, 0)[:ROWS]

    def place(out_ref, pair, value):
        field, half = pair // 2, pair % 2
        out_ref[field, LOW_LEVEL[half]] = turn(value, -8)[:, :COLS]
        out_ref[field, HIGH_LEVEL[half]] = turn(value, -8 - HALF)[:, :COLS]

    for pair in range(PAIRS):
        field, half = pair // 2, pair % 2
        rate = found[field][half * MID : (half + 1) * MID]
        held = held_ref[pair]
        step = centre(rate) * (0.5 * TIME_STEP)
        middle = centre(middle_ref[pair])
        place(third_ref, pair, held + step)
        place(whole_ref, pair, held + ((middle - held) + 2.0 * step) * (1.0 / 3.0))


def shift(value, move_lat, move_lon):
    pairs = []
    for a in range(LATS):
        for b in range(LONS):
            goal_a, goal_b = a + move_lat, b + move_lon
            if 0 <= goal_a < LATS and 0 <= goal_b < LONS:
                pairs.append((a * LONS + b, goal_a * LONS + goal_b))
    return lax.ppermute(value, ("lat", "lon"), pairs)


def shards(state, donor_cell, donor_weights, donor_turn, border_source, diffusion):
    fields = state[0]
    panel = lax.axis_index("panel")
    lat = lax.axis_index("lat")
    lon = lax.axis_index("lon")
    place = jnp.stack([panel, lat, lon]).astype(jnp.int32)
    f32 = jnp.float32

    def call(kernel, outs, *args, smem=0, specs=None, scratch=(), limit=10):
        shapes = [jax.ShapeDtypeStruct(shape, dtype) for shape, dtype in outs]
        return pl.pallas_call(
            kernel,
            out_shape=shapes,
            in_specs=specs or [SMEM] * smem + [VMEM] * (len(args) - smem),
            out_specs=[VMEM] * len(outs),
            scratch_shapes=scratch,
            compiler_params=pltpu.CompilerParams(vmem_limit_bytes=limit * MIB),
        )(*args)

    bf16 = jnp.bfloat16
    held, south, east, corner = call(
        cut_kernel,
        [
            ((PAIRS, ROWS, WIDE), f32),
            ((PAIRS, 8, WIDE), f32),
            ((2, ROWS, WIDE), f32),
            ((2, 8, WIDE), f32),
        ],
        fields,
        scratch=[pltpu.VMEM((PLANES, ROWS, WIDE), f32)],
    )
    south = shift(south, -1, 0)
    east = shift(east, 0, -1)
    corner = shift(corner, -1, -1)

    donor = jnp.concatenate(
        [donor_cell[0, 0].astype(f32), donor_weights[0, 0, 0], donor_turn[0, 0]], axis=0
    )
    pick, mix, spin = call(
        donor_tables,
        [((WIDE, 2 * WIDE), bf16), ((MID, 2 * WIDE), f32), ((2, WIDE), f32)],
        donor,
        scratch=[pltpu.VMEM((1, WIDE), f32)],
    )
    message = ((2 * PEERS, 1, MESSAGE), f32)
    lower, sent = call(
        donor_kernel,
        [((PAIRS, MID, WIDE), f32), message],
        place,
        held,
        south,
        east,
        corner,
        pick,
        mix,
        spin,
        smem=1,
    )

    def to_holders(sent):
        return lax.all_to_all(sent, ("panel", "lon"), 0, 0, tiled=True)

    got = to_holders(sent)

    late_lat, late_lon, border, late_lower, _ = lax.optimization_barrier(
        (lat, lon, border_source[0], lower, sent)
    )
    (west,) = call(last_kernel, [((2, MID, WIDE), f32)], late_lower)
    west = shift(west, 0, 1)

    ring = PANEL_COLS + 8
    row_slots = LONS * SLOTS
    bands = border[: 8 * ring].reshape(8, ring)
    sides = border[8 * ring :].reshape(PANEL_ROWS, 8)
    window = jnp.pad(bands, ((0, 0), (4, 4)), constant_values=-1)
    window = lax.dynamic_slice(window, (0, late_lon * COLS), (8, 64)).reshape(2, BAND)
    side = jnp.where(late_lon == 0, sides[:, :4], sides[:, 4:])
    side = jnp.where((late_lon == 0) | (late_lon == LONS - 1), side, -1)
    side = jnp.pad(side, ((8, 8), (0, 0)), constant_values=-1)
    side = jnp.concatenate(
        [
            side[:PANEL_ROWS].reshape(LATS, ROWS, 4),
            side[ROWS:].reshape(LATS, ROWS, 4),
        ],
        axis=1,
    ).reshape(LATS, SIDE)
    at_lat = jnp.arange(LATS)[:, None]
    band = jnp.where(at_lat == 0, window[:1], jnp.where(at_lat == LATS - 1, window[1:], -1))
    wanted = jnp.concatenate([band, side], axis=1)
    holder = jnp.where(wanted >= 0, wanted // row_slots, -1)
    local = wanted - late_lat * row_slots
    block = local // SLOTS
    slot = local % SLOTS
    spot = jnp.where(slot < PACKED, block * PACKED + slot, PEERS * PACKED + block)
    (send,) = call(
        send_kernel, [((CHOICE_DEPTH, DEPTH), bf16)], place, holder, spot, smem=1, limit=16
    )
    chunk = ((PEERS, 16, WIDE), f32)
    first_got = got
    chunks, north = call(
        widen_kernel, [chunk, ((PAIRS, 8, WIDE), f32)], place, got, send, lower, west, smem=1
    )
    north = shift(north, 1, 0)
    late_holder, bands, sides, _ = lax.optimization_barrier((holder, bands, sides, chunks))
    take, coef = call(
        take_kernel,
        [((DEPTH, CHUNK), bf16), ((5, TALL, WIDE), f32)],
        place,
        late_holder,
        smem=1,
    )

    (flag,) = call(
        count_kernel,
        [((8, WIDE), f32)],
        jnp.pad(bands, ((0, 0), (0, 7 * WIDE - ring)), constant_values=-1),
        sides.T,
    )

    def to_blocks(chunks):
        return lax.all_to_all(chunks, "lat", 0, 0, tiled=True)

    def section_one(got):
        return call(
            first_kernel,
            [((PAIRS, MID, WIDE), f32), message],
            place,
            diffusion,
            lower,
            north,
            west,
            got,
            take,
            coef,
            pick,
            mix,
            spin,
            flag,
            smem=2,
            scratch=[pltpu.VMEM((PAIRS, TALL, WIDE), f32), pltpu.VMEM((PAIRS, MID, WIDE), f32)],
        )

    def section_two(middle, got):
        return call(
            second_kernel,
            [(fields.shape, f32), (fields.shape, f32)],
            place,
            diffusion,
            middle,
            got,
            take,
            coef,
            held,
            smem=2,
            scratch=[pltpu.VMEM((PAIRS, MID, WIDE), f32)],
        )

    middle, sent = section_one(to_blocks(chunks))
    got = to_holders(sent)
    crowded = jnp.maximum(got[0, 0, FLAG], got[PEERS, 0, FLAG]) > ROOM
    (chunks,) = call(choice_kernel, [chunk], place, got, send, smem=1)
    fitting = section_two(middle, to_blocks(chunks))

    def with_room():
        def dense(got):
            chunks = call(
                dense_kernel,
                [((PEERS, PLANES, CHUNK), f32)],
                place,
                got,
                holder,
                spot,
                smem=1,
                limit=16,
            )
            return to_blocks(chunks[0]).sum(axis=0)

        middle, sent = section_one(dense(first_got))
        return section_two(middle, dense(to_holders(sent)))

    accumulated, section_three = lax.cond(crowded, with_room, lambda: fitting)
    return (accumulated[None], section_three[None])


def solution(mesh):
    return jax.shard_map(
        shards,
        mesh=mesh,
        in_specs=(
            P("panel", None, None, "lat", "lon"),
            P("panel", "lat", "lon", None),
            P("panel", "lat", "lon", None, None),
            P("panel", "lat", "lon", None),
            P("panel", None),
            P(),
        ),
        out_specs=(P("panel", None, None, "lat", "lon"), P("panel", None, None, "lat", "lon")),
        check_vma=False,
    )
```

```python
import math

import jax
import jax.numpy as jnp
from jax import lax
from jax.experimental import pallas as pl
from jax.experimental.pallas import tpu as pltpu
from jax.sharding import PartitionSpec as P

GAMMA = 5.0 / 3.0
RADIAL_STEP = 0.65 / 32.0
FIELDS = 8
LEVELS = 4
PLANES = FIELDS * LEVELS
PAIRS = PLANES // 2
LOW_LEVEL = (0, 1)
HIGH_LEVEL = (3, 2)
ROWS = 16
COLS = 48
SLOTS = 33
LATS = 16
LONS = 16
ROOM = 63
WIDE = 128
HALF = 64
TALL = ROWS + 16
MID = ROWS + 8
BAND = 4 * HALF
SIDE = 4 * TALL
CHUNK = BAND + SIDE
PEERS = 16
PACKED = 32
MESSAGE = 9 * WIDE
TAIL = 8 * WIDE
FLAG = TAIL + HALF - 1
CHOICE_TILES = PEERS * PACKED // WIDE
CHOICE_DEPTH = (CHOICE_TILES + 1) * WIDE
DEPTH = PEERS * HALF
PANEL_ROWS = ROWS * LATS
PANEL_COLS = COLS * LONS
DTHETA = 0.5 * math.pi / PANEL_ROWS
DPHI = 1.5 * math.pi / PANEL_COLS
FINEST = min(DTHETA, DPHI)
TIME_STEP = 0.1 * FINEST
RADII = [0.35 + 0.65 * (k + 16 - LEVELS // 2 + 0.5) / 32.0 for k in range(LEVELS)]
VMEM = pl.BlockSpec(memory_space=pltpu.VMEM)
SMEM = pl.BlockSpec(memory_space=pltpu.SMEM)
MIB = 1024 * 1024


def iota(shape, axis):
    return lax.broadcasted_iota(jnp.int32, shape, axis)


def column_of(shape):
    return iota(shape, len(shape) - 1) & (HALF - 1)


def turn(value, lanes):
    return pltpu.roll(value, lanes % WIDE, 1) if lanes % WIDE else value


def three_parts(value):
    parts = []
    for _ in range(3):
        part = value.astype(jnp.bfloat16)
        value = value - part.astype(jnp.float32)
        parts.append(part)
    return parts


def donor_message(planes, pick, mix, spin):
    parts = jnp.concatenate(three_parts(planes), axis=1)
    chosen = jnp.dot(parts, pick, preferred_element_type=jnp.float32)
    chosen = chosen.reshape(PAIRS, MID, 2 * WIDE)
    both = jnp.sum(chosen * mix[None], axis=1)
    both = jnp.concatenate([both[:, :WIDE], both[:, WIDE:]], axis=0)
    mixed = both + pltpu.roll(both, HALF, 1)
    cosine = spin[0:1]
    sine = spin[1:2]
    at = (iota((PLANES, WIDE), 0) & (PAIRS - 1)) // 2
    theta = (at == 2) | (at == 5)
    phi = (at == 3) | (at == 6)
    other = jnp.where(theta, pltpu.roll(mixed, PLANES - 2, 0), -pltpu.roll(mixed, 2, 0))
    turned = jnp.where(theta | phi, cosine * mixed + sine * other, mixed)
    return jnp.where(iota((PAIRS, WIDE), 1) < HALF, turned[:PAIRS], turned[PAIRS:])


def post_message(place_ref, packed, flag, out_ref):
    panel = place_ref[0]
    lane = iota((16, WIDE), 1)
    column = lane & (HALF - 1)
    dense = jnp.where(column[:8] < PACKED, packed[:8], turn(packed[8:], PACKED))
    last = jnp.where(
        lane < HALF, packed[:, PACKED : PACKED + 1], packed[:, HALF + PACKED : HALF + PACKED + 1]
    )
    tail = jnp.sum(jnp.where(column == iota((16, WIDE), 0), last, 0.0), axis=0, keepdims=True)
    blank = jnp.where(lane[:1] == FLAG - TAIL, flag, 0.0)
    tail = jnp.where(lane[:1] == FLAG - TAIL, flag, tail)
    zero = jnp.zeros((1, WIDE), jnp.float32)
    for row in range(9):
        full = dense[row : row + 1] if row < 8 else tail
        empty = zero if row < 8 else blank
        at = slice(row * WIDE, (row + 1) * WIDE)
        out_ref[pl.ds((1 - panel) * PEERS, PEERS), :, at] = jnp.broadcast_to(
            full[None], (PEERS, 1, WIDE)
        )
        out_ref[pl.ds(panel * PEERS, PEERS), :, at] = jnp.broadcast_to(
            empty[None], (PEERS, 1, WIDE)
        )


def cut_kernel(state_ref, held_ref, south_ref, east_ref, corner_ref, plane_ref):
    for plane in range(PLANES):
        plane_ref[plane, :, :COLS] = state_ref[plane // LEVELS, plane % LEVELS]
    lane = iota((ROWS, WIDE), 1)
    column = column_of((ROWS, WIDE))
    own = (column >= 8) & (column < 8 + COLS)
    for pair in range(PAIRS):
        field, which = pair // 2, pair % 2
        low = turn(plane_ref[field * LEVELS + LOW_LEVEL[which]], 8)
        high = turn(plane_ref[field * LEVELS + HIGH_LEVEL[which]], HALF + 8)
        tile = jnp.where(own, jnp.where(lane < HALF, low, high), 0.0)
        held_ref[pair] = tile
        south_ref[pair] = tile[:8]
    for group in range(2):
        columns = jnp.zeros((ROWS, WIDE), jnp.float32)
        for which in range(8):
            moved = turn(held_ref[8 * group + which], 8 * which - 8)
            columns = jnp.where(column // 8 == which, moved, columns)
        east_ref[group] = columns
        corner_ref[group] = columns[:8]


def donor_tables(donor_ref, pick_ref, mix_ref, spin_ref, line_ref):
    late = iota((1, WIDE), 1) >= HALF

    def twice(value, fill):
        line_ref[...] = jnp.full((1, WIDE), fill, jnp.float32)
        line_ref[:, :SLOTS] = value
        line = line_ref[...]
        return jnp.where(late, pltpu.roll(line, HALF, 1), line)

    cell = twice(donor_ref[0:1], -10.0 * COLS)
    row_at = jnp.floor((cell + 0.5) * (1.0 / COLS))
    col_at = cell - row_at * COLS + jnp.where(late, 1.0, 0.0)
    upper = jnp.where(late, twice(donor_ref[2:3], 0.0), twice(donor_ref[1:2], 0.0))
    lower = jnp.where(late, twice(donor_ref[4:5], 0.0), twice(donor_ref[3:4], 0.0))
    angle = twice(donor_ref[5:6], 0.0)
    spin_ref[0:1] = jnp.cos(angle)
    spin_ref[1:2] = jnp.sin(angle)
    lane = iota((WIDE, WIDE), 0).astype(jnp.float32)
    real = jnp.where(row_at >= 0, col_at + 8.0, -1000.0)
    low = jnp.where(lane == real, 1.0, 0.0).astype(jnp.bfloat16)
    high = jnp.where(lane == real + HALF, 1.0, 0.0).astype(jnp.bfloat16)
    for part in range(3):
        pick_ref[part * WIDE : (part + 1) * WIDE, :WIDE] = low
        pick_ref[part * WIDE : (part + 1) * WIDE, WIDE:] = high
    row = iota((MID, WIDE), 0).astype(jnp.float32)
    mix = jnp.where(row == row_at, upper, 0.0) + jnp.where(row == row_at + 1.0, lower, 0.0)
    mix_ref[:, :WIDE] = mix
    mix_ref[:, WIDE:] = mix


def count_kernel(bands_ref, sides_ref, flag_ref):
    width = bands_ref.shape[1]
    column = iota((width, WIDE), 0) - 4
    start = iota((width, WIDE), 1) * COLS - 8
    within = (column >= start) & (column < start + 64) & (start < PANEL_COLS)
    columns = jnp.where(within, 1.0, 0.0).astype(jnp.bfloat16)
    row = iota((PANEL_ROWS, WIDE), 0)
    start = iota((PANEL_ROWS, WIDE), 1) * ROWS - 8
    within = (row >= start) & (row < start + TALL) & (start < PANEL_ROWS)
    rows = jnp.where(within, 1.0, 0.0).astype(jnp.bfloat16)

    def most(slots, windows):
        ones = []
        for which in range(LATS):
            first = which * LONS * SLOTS
            inside = (slots >= first) & (slots < first + LONS * SLOTS)
            ones.append(jnp.where(inside, 1.0, 0.0))
        ones = jnp.concatenate(ones, axis=0).astype(jnp.bfloat16)
        counts = jnp.dot(ones, windows, preferred_element_type=jnp.float32)
        return jnp.max(jnp.sum(counts.reshape(2 * LATS, 4, WIDE), axis=1))

    total = most(bands_ref[...], columns) + most(sides_ref[...], rows)
    flag_ref[...] = jnp.full(flag_ref.shape, total, jnp.float32)


def donor_kernel(
    place_ref, held_ref, south_ref, east_ref, corner_ref, pick_ref, mix_ref, spin_ref,
    lower_ref, out_ref
):
    column = column_of((ROWS, WIDE))
    beyond = column >= 8 + COLS
    for pair in range(PAIRS):
        group, which = pair // 8, pair % 8
        east = turn(east_ref[group], 8 + COLS - 8 * which)
        corner = turn(corner_ref[group], 8 + COLS - 8 * which)
        lower_ref[pair, :ROWS] = jnp.where(beyond, east, held_ref[pair])
        lower_ref[pair, ROWS:] = jnp.where(beyond[:8], corner, south_ref[pair])
    planes = lower_ref[...].reshape(PAIRS * MID, WIDE)
    packed = donor_message(planes, pick_ref[...], mix_ref[...], spin_ref[...])
    post_message(place_ref, packed, jnp.zeros((1, WIDE), jnp.float32), out_ref)


def last_kernel(lower_ref, west_ref):
    column = column_of((MID, WIDE))
    for group in range(2):
        columns = jnp.zeros((MID, WIDE), jnp.float32)
        for which in range(8):
            moved = turn(lower_ref[8 * group + which], 8 * which - COLS)
            columns = jnp.where(column // 8 == which, moved, columns)
        west_ref[group] = columns


def split_parts(held):
    return jnp.concatenate(three_parts(held), axis=0)


def join_parts(terms):
    return terms[:PLANES] + terms[PLANES : 2 * PLANES] + terms[2 * PLANES :]


def from_row(place_ref, got_ref):
    base = (1 - place_ref[0]) * PEERS
    part = iota((8, WIDE), 1) // PACKED
    tiles = []
    tails = []
    for tile in range(CHOICE_TILES):
        rows = [jnp.zeros((8, WIDE), jnp.float32)] * 4
        for which in range(4):
            at = base + 4 * tile + which
            message = jnp.concatenate(
                [got_ref[at, :, row * WIDE : (row + 1) * WIDE] for row in range(8)], axis=0
            )
            tails.append(got_ref[at, :, TAIL:])
            for group in range(4):
                moved = turn(message, PACKED * (which - group))
                rows[group] = jnp.where(part == which, moved, rows[group])
        tiles.append(jnp.concatenate(rows, axis=0))
    tails.append(jnp.zeros((WIDE - PEERS, WIDE), jnp.float32))
    tails = jnp.concatenate(tails, axis=0).T
    tiles.append(jnp.concatenate([tails[:PAIRS], tails[HALF : HALF + PAIRS]], axis=0))
    return split_parts(jnp.concatenate(tiles, axis=1))


def rank_of(chosen):
    order = iota((CHUNK, CHUNK), 0) < iota((CHUNK, CHUNK), 1)
    order = jnp.where(order, 1.0, 0.0).astype(jnp.bfloat16)
    ones = jnp.where(chosen, 1.0, 0.0).astype(jnp.bfloat16)
    return jnp.dot(ones, order, preferred_element_type=jnp.float32)


def send_kernel(place_ref, holder_ref, spot_ref, send_ref):
    mine = holder_ref[...] == place_ref[1]
    spot = spot_ref[...].astype(jnp.float32)
    rank = rank_of(mine)
    key = jnp.where(mine & (rank < ROOM), rank, -1.0)
    place_at = iota((HALF, CHUNK), 0).astype(jnp.float32)
    eye = iota((WIDE, WIDE), 0) == iota((WIDE, WIDE), 1)
    depth = iota((CHOICE_DEPTH, WIDE), 0).astype(jnp.float32) + 1.0
    for pair in range(LATS // 2):
        tables = []
        for block in (2 * pair, 2 * pair + 1):
            found = place_at == key[block : block + 1]
            tables.append(
                jnp.sum(jnp.where(found, spot[block : block + 1] + 1.0, 0.0), axis=1, keepdims=True)
            )
        table = jnp.concatenate(tables, axis=0)
        line = jnp.sum(jnp.where(eye, table, 0.0), axis=0, keepdims=True)
        hot = jnp.where(depth == line, 1.0, 0.0).astype(jnp.bfloat16)
        send_ref[:, pair * WIDE : (pair + 1) * WIDE] = hot


def take_kernel(place_ref, holder_ref, take_ref, coef_ref):
    lat = place_ref[1]
    own = holder_ref[pl.ds(lat, 1)]
    masks = iota((PEERS, CHUNK), 0) == own
    rank = jnp.sum(jnp.where(masks, rank_of(masks), 0.0), axis=0, keepdims=True)
    fits = (own >= 0) & (rank < ROOM)
    index = jnp.where(fits, own.astype(jnp.float32) * HALF + rank, -1.0)
    hot = iota((DEPTH, CHUNK), 0).astype(jnp.float32) == index
    take_ref[...] = jnp.where(hot, 1.0, 0.0).astype(jnp.bfloat16)
    row = (lat * ROWS - 8 + iota((TALL, WIDE), 0)).astype(jnp.float32)
    column = (place_ref[2] * COLS - 8 + column_of((TALL, WIDE))).astype(jnp.float32)
    colatitude = 0.25 * math.pi + (row + 0.5) * DTHETA
    longitude = -0.75 * math.pi + (column + 0.5) * DPHI
    sine, cosine = jnp.sin(colatitude), jnp.cos(colatitude)
    twirl = 2.0 * 0.25 / TIME_STEP
    yang = place_ref[0] == 1
    coef_ref[0] = sine
    coef_ref[1] = 1.0 / sine
    coef_ref[2] = twirl * jnp.where(yang, sine * jnp.sin(longitude), cosine)
    coef_ref[3] = twirl * jnp.where(yang, cosine * jnp.sin(longitude), -sine)
    coef_ref[4] = twirl * jnp.where(yang, jnp.cos(longitude), 0.0)


def widen_kernel(place_ref, got_ref, send_ref, lower_ref, west_ref, out_ref, edge_ref):
    column = column_of((8, WIDE))
    for pair in range(PAIRS):
        group, which = pair // 8, pair % 8
        west = turn(west_ref[group, 8:16], -8 * which)
        edge_ref[pair] = jnp.where(column < 8, west, lower_ref[pair, 8:16])
    choice_kernel(place_ref, got_ref, send_ref, out_ref)


def choice_kernel(place_ref, got_ref, send_ref, out_ref):
    parts = from_row(place_ref, got_ref)
    terms = jnp.dot(parts, send_ref[...], preferred_element_type=jnp.float32)
    chosen = join_parts(terms)
    low = iota((16, WIDE), 1) < HALF
    for pair in range(PEERS // 2):
        tile = chosen[:, pair * WIDE : (pair + 1) * WIDE]
        top, end = tile[:16], tile[16:]
        out_ref[2 * pair] = jnp.where(low, top, pltpu.roll(end, HALF, 1))
        out_ref[2 * pair + 1] = jnp.where(low, pltpu.roll(top, HALF, 1), end)


def dense_kernel(place_ref, got_ref, holder_ref, spot_ref, out_ref):
    parts = from_row(place_ref, got_ref)
    index = jnp.where(holder_ref[...] == place_ref[1], spot_ref[...], -1)
    at = iota((CHOICE_DEPTH, CHUNK), 0)
    for block in range(LATS):
        hot = jnp.where(at == index[block : block + 1], 1.0, 0.0).astype(jnp.bfloat16)
        out_ref[block] = join_parts(jnp.dot(parts, hot, preferred_element_type=jnp.float32))


def ghost_values(got_ref, take_ref):
    if len(got_ref.shape) == 2:
        return got_ref[...]
    low = iota((16, WIDE), 1) < HALF
    tiles = []
    for pair in range(PEERS // 2):
        one = got_ref[2 * pair]
        two = got_ref[2 * pair + 1]
        top = jnp.where(low, one, pltpu.roll(two, HALF, 1))
        end = jnp.where(low, pltpu.roll(one, HALF, 1), two)
        tiles.append(jnp.concatenate([top, end], axis=0))
    parts = split_parts(jnp.concatenate(tiles, axis=1))
    return join_parts(jnp.dot(parts, take_ref[...], preferred_element_type=jnp.float32))


def fill_ghosts(place_ref, ghosts, work_ref, rows):
    lat, lon = place_ref[1], place_ref[2]
    trim = (TALL - rows) // 2
    top = 8 - trim
    half = PLANES // 2

    @pl.when((lon == 0) | (lon == LONS - 1))
    def _():
        side = ghosts[:, BAND:]
        first = jnp.where(lon == 0, 4, 8 + COLS)
        own = iota((rows, WIDE), 1) // 4 == iota((rows, WIDE), 0) + trim

        def spread(part):
            part = part.astype(jnp.float32)[:, None, :]
            return jnp.where(own[None], part, 0.0).astype(jnp.bfloat16).reshape(PAIRS * rows, WIDE)

        pieces = []
        for part in three_parts(side):
            pieces += [spread(part[:half]), spread(part[half:])]
        both = jnp.concatenate(pieces, axis=1)
        source = iota((6 * WIDE, WIDE), 0)
        target = first + (source & 3) + jnp.where((source & WIDE) != 0, HALF, 0)
        hot = jnp.where(target == iota((6 * WIDE, WIDE), 1), 1.0, 0.0).astype(jnp.bfloat16)
        moved = jnp.dot(both, hot, preferred_element_type=jnp.float32)
        moved = moved.reshape(PAIRS, rows, WIDE)
        column = column_of((rows, WIDE))
        ghost = (column >= first) & (column < first + 4)
        work_ref[...] = jnp.where(ghost[None], moved, work_ref[...])

    @pl.when((lat == 0) | (lat == LATS - 1))
    def _():
        low = iota((half, WIDE), 1) < HALF
        lines = []
        for which in range(2):
            piece = ghosts[:, which * WIDE : (which + 1) * WIDE]
            one, two = piece[:half], piece[half:]
            lines.append(jnp.where(low, one, pltpu.roll(two, HALF, 1)))
            lines.append(jnp.where(low, pltpu.roll(one, HALF, 1), two))

        @pl.when(lat == 0)
        def _():
            for row in range(4):
                work_ref[:, top - 4 + row, :] = lines[row]

        @pl.when(lat == LATS - 1)
        def _():
            for row in range(4):
                work_ref[:, top + ROWS + row, :] = lines[row]


def rates(load, rows, coef_ref, diffusion_ref):
    low = iota((rows, WIDE), 1) < HALF

    def levels(values):
        halves = [
            jnp.where(low, values[LOW_LEVEL[k]], values[HIGH_LEVEL[k]]).astype(jnp.float32)
            for k in range(2)
        ]
        return jnp.concatenate(halves, axis=0)

    def whole(which):
        value = coef_ref[which]
        if rows < TALL:
            value = pltpu.roll(value, TALL - (TALL - rows) // 2, 0)[:rows]
        return jnp.concatenate([value] * 2, axis=0)

    sine = whole(0)
    per_sine = whole(1)
    radius = levels(RADII)
    inverse = levels([1.0 / r for r in RADII])
    square = levels([r * r for r in RADII])
    per_square = levels([1.0 / (r * r) for r in RADII])
    sign = jnp.where(low, 1.0, -1.0)
    ends = sign * (1.0 / RADIAL_STEP)
    inner = sign * (1.0 / (2.0 * RADIAL_STEP))
    viscosity = diffusion_ref[0] * (FINEST * FINEST / TIME_STEP)
    resistivity = diffusion_ref[1] * (FINEST * FINEST / TIME_STEP)

    def slope(value, axis, step):
        size = value.shape[axis]
        near = pltpu.roll(value, size - 1, axis) - pltpu.roll(value, 1, axis)
        far = pltpu.roll(value, size - 2, axis) - pltpu.roll(value, 2, axis)
        return near * (8.0 / (12.0 * step)) - far * (1.0 / (12.0 * step))

    def d_theta(value):
        return slope(value, 0, DTHETA)

    def d_phi(value):
        return slope(value, 1, DPHI)

    def d_radius(value):
        one, two = value[:rows], value[rows:]
        return jnp.concatenate(
            [(two - one) * ends, (pltpu.roll(two, HALF, 1) - one) * inner], axis=0
        )

    def by_radius(value):
        return value * radius

    def per_radius(value):
        return value * inverse

    def curl(vector):
        part_r, part_t, part_p = vector
        return (
            per_radius((d_theta(sine * part_p) - d_phi(part_t)) * per_sine),
            per_radius(d_phi(part_r) * per_sine - d_radius(by_radius(part_p))),
            per_radius(d_radius(by_radius(part_t)) - d_theta(part_r)),
        )

    def gradient(value):
        return (
            d_radius(value),
            per_radius(d_theta(value)),
            per_radius(d_phi(value) * per_sine),
        )

    def cross(left, right):
        return (
            left[1] * right[2] - left[2] * right[1],
            left[2] * right[0] - left[0] * right[2],
            left[0] * right[1] - left[1] * right[0],
        )

    def advect(vector, slopes):
        return vector[0] * slopes[0] + vector[1] * slopes[1] + vector[2] * slopes[2]

    velocity = [load(which) for which in (1, 2, 3)]
    magnetic = [load(which) for which in (4, 5, 6)]
    vorticity = curl(velocity)
    current = curl(magnetic)
    spread = d_radius(square * velocity[0]) * per_square + per_radius(
        (d_theta(sine * velocity[1]) + d_phi(velocity[2])) * per_sine
    )
    induced = cross(velocity, magnetic)
    electric = [induced[k] - resistivity * current[k] for k in range(3)]
    kinetic = 0.5 * (
        velocity[0] * velocity[0] + velocity[1] * velocity[1] + velocity[2] * velocity[2]
    )
    curl_electric = curl(electric)
    log_rho = load(0)
    rho_rate = -advect(velocity, gradient(log_rho)) - spread
    pressure = load(7)
    slope_pressure = gradient(pressure)
    pressure_rate = -advect(velocity, slope_pressure) - GAMMA * pressure * spread
    lorentz = cross(current, magnetic)
    per_rho = jnp.exp(-log_rho)
    slope_kinetic = gradient(kinetic)
    curl_vorticity = curl(vorticity)
    lamb = cross(velocity, vorticity)
    turning = cross((whole(2), whole(3), whole(4)), velocity)
    momentum = [
        lamb[k]
        - slope_kinetic[k]
        + per_rho * (lorentz[k] - slope_pressure[k])
        - turning[k]
        - viscosity * curl_vorticity[k]
        for k in range(3)
    ]
    return [rho_rate, *momentum, *curl_electric, pressure_rate]


def first_kernel(
    place_ref,
    diffusion_ref,
    lower_ref,
    north_ref,
    west_ref,
    got_ref,
    take_ref,
    coef_ref,
    pick_ref,
    mix_ref,
    spin_ref,
    flag_ref,
    middle_ref,
    out_ref,
    work_ref,
    next_ref,
):
    column = column_of((TALL, WIDE))
    for pair in range(PAIRS):
        group, which = pair // 8, pair % 8
        west = turn(west_ref[group], -8 * which)
        work_ref[pair, :8] = north_ref[pair]
        work_ref[pair, 8:] = jnp.where(column[8:] < 8, west, lower_ref[pair])
    ghosts = ghost_values(got_ref, take_ref)
    fill_ghosts(place_ref, ghosts, work_ref, TALL)

    def load(which):
        return work_ref[2 * which : 2 * which + 2].reshape(2 * TALL, WIDE)

    found = rates(load, TALL, coef_ref, diffusion_ref)
    row = iota((TALL, WIDE), 0)
    inside = (column >= 4) & (column < 12 + COLS) & (row >= 4) & (row < 12 + ROWS)
    for which in range(FIELDS):
        value = load(which) + (0.5 * TIME_STEP) * found[which]
        for half in range(2):
            part = jnp.where(inside, value[half * TALL : (half + 1) * TALL], 0.0)
            next_ref[2 * which + half] = part[8:]
            middle_ref[2 * which + half] = pltpu.roll(part, TALL - 4, 0)[:MID]
    planes = next_ref[...].reshape(PAIRS * MID, WIDE)
    packed = donor_message(planes, pick_ref[...], mix_ref[...], spin_ref[...])
    post_message(place_ref, packed, flag_ref[0:1], out_ref)


def second_kernel(
    place_ref,
    diffusion_ref,
    middle_ref,
    got_ref,
    take_ref,
    coef_ref,
    held_ref,
    whole_ref,
    third_ref,
    work_ref,
):
    work_ref[...] = middle_ref[...]
    ghosts = ghost_values(got_ref, take_ref)
    fill_ghosts(place_ref, ghosts, work_ref, MID)

    def load(which):
        return work_ref[2 * which : 2 * which + 2].reshape(2 * MID, WIDE)

    found = rates(load, MID, coef_ref, diffusion_ref)

    def centre(value):
        return pltpu.roll(value, MID - 4, 0)[:ROWS]

    def place(out_ref, pair, value):
        field, half = pair // 2, pair % 2
        out_ref[field, LOW_LEVEL[half]] = turn(value, -8)[:, :COLS]
        out_ref[field, HIGH_LEVEL[half]] = turn(value, -8 - HALF)[:, :COLS]

    for pair in range(PAIRS):
        field, half = pair // 2, pair % 2
        rate = found[field][half * MID : (half + 1) * MID]
        held = held_ref[pair]
        step = centre(rate) * (0.5 * TIME_STEP)
        middle = centre(middle_ref[pair])
        place(third_ref, pair, held + step)
        place(whole_ref, pair, held + ((middle - held) + 2.0 * step) * (1.0 / 3.0))


def shift(value, move_lat, move_lon):
    pairs = []
    for a in range(LATS):
        for b in range(LONS):
            goal_a, goal_b = a + move_lat, b + move_lon
            if 0 <= goal_a < LATS and 0 <= goal_b < LONS:
                pairs.append((a * LONS + b, goal_a * LONS + goal_b))
    return lax.ppermute(value, ("lat", "lon"), pairs)


def shards(state, donor_cell, donor_weights, donor_turn, border_source, diffusion):
    fields = state[0]
    panel = lax.axis_index("panel")
    lat = lax.axis_index("lat")
    lon = lax.axis_index("lon")
    place = jnp.stack([panel, lat, lon]).astype(jnp.int32)
    f32 = jnp.float32

    def call(kernel, outs, *args, smem=0, specs=None, scratch=(), limit=10):
        shapes = [jax.ShapeDtypeStruct(shape, dtype) for shape, dtype in outs]
        return pl.pallas_call(
            kernel,
            out_shape=shapes,
            in_specs=specs or [SMEM] * smem + [VMEM] * (len(args) - smem),
            out_specs=[VMEM] * len(outs),
            scratch_shapes=scratch,
            compiler_params=pltpu.CompilerParams(vmem_limit_bytes=limit * MIB),
        )(*args)

    bf16 = jnp.bfloat16
    held, south, east, corner = call(
        cut_kernel,
        [
            ((PAIRS, ROWS, WIDE), f32),
            ((PAIRS, 8, WIDE), f32),
            ((2, ROWS, WIDE), f32),
            ((2, 8, WIDE), f32),
        ],
        fields,
        scratch=[pltpu.VMEM((PLANES, ROWS, WIDE), f32)],
    )
    south = shift(south, -1, 0)
    east = shift(east, 0, -1)
    corner = shift(corner, -1, -1)

    donor = jnp.concatenate(
        [donor_cell[0, 0].astype(f32), donor_weights[0, 0, 0], donor_turn[0, 0]], axis=0
    )
    pick, mix, spin = call(
        donor_tables,
        [((3 * WIDE, 2 * WIDE), bf16), ((MID, 2 * WIDE), f32), ((2, WIDE), f32)],
        donor,
        scratch=[pltpu.VMEM((1, WIDE), f32)],
    )
    message = ((2 * PEERS, 1, MESSAGE), f32)
    lower, sent = call(
        donor_kernel,
        [((PAIRS, MID, WIDE), f32), message],
        place,
        held,
        south,
        east,
        corner,
        pick,
        mix,
        spin,
        smem=1,
    )

    def to_holders(sent):
        return lax.all_to_all(sent, ("panel", "lon"), 0, 0, tiled=True)

    got = to_holders(sent)

    late_lat, late_lon, border, late_lower, _ = lax.optimization_barrier(
        (lat, lon, border_source, lower, sent)
    )
    border = border[0]
    (west,) = call(last_kernel, [((2, MID, WIDE), f32)], late_lower)
    west = shift(west, 0, 1)

    ring = PANEL_COLS + 8
    row_slots = LONS * SLOTS
    bands = border[: 8 * ring].reshape(8, ring)
    sides = border[8 * ring :].reshape(PANEL_ROWS, 8)
    window = jnp.pad(bands, ((0, 0), (4, 4)), constant_values=-1)
    window = lax.dynamic_slice(window, (0, late_lon * COLS), (8, 64)).reshape(2, BAND)
    side = jnp.where(late_lon == 0, sides[:, :4], sides[:, 4:])
    side = jnp.where((late_lon == 0) | (late_lon == LONS - 1), side, -1)
    side = jnp.pad(side, ((8, 8), (0, 0)), constant_values=-1)
    side = jnp.concatenate(
        [
            side[:PANEL_ROWS].reshape(LATS, ROWS, 4),
            side[ROWS:].reshape(LATS, ROWS, 4),
        ],
        axis=1,
    ).reshape(LATS, SIDE)
    at_lat = jnp.arange(LATS)[:, None]
    band = jnp.where(at_lat == 0, window[:1], jnp.where(at_lat == LATS - 1, window[1:], -1))
    wanted = jnp.concatenate([band, side], axis=1)
    holder = jnp.where(wanted >= 0, wanted // row_slots, -1)
    local = wanted - late_lat * row_slots
    block = local // SLOTS
    slot = local % SLOTS
    spot = jnp.where(slot < PACKED, block * PACKED + slot, PEERS * PACKED + block)
    (send,) = call(
        send_kernel, [((CHOICE_DEPTH, DEPTH), bf16)], place, holder, spot, smem=1, limit=16
    )
    chunk = ((PEERS, 16, WIDE), f32)
    first_got = got
    chunks, north = call(
        widen_kernel, [chunk, ((PAIRS, 8, WIDE), f32)], place, got, send, lower, west, smem=1
    )
    north = shift(north, 1, 0)
    late_holder, bands, sides, _ = lax.optimization_barrier((holder, bands, sides, chunks))
    take, coef = call(
        take_kernel,
        [((DEPTH, CHUNK), bf16), ((5, TALL, WIDE), f32)],
        place,
        late_holder,
        smem=1,
    )

    (flag,) = call(
        count_kernel,
        [((8, WIDE), f32)],
        jnp.pad(bands, ((0, 0), (0, 7 * WIDE - ring)), constant_values=-1),
        sides.T,
    )

    def to_blocks(chunks):
        return lax.all_to_all(chunks, "lat", 0, 0, tiled=True)

    def section_one(got):
        return call(
            first_kernel,
            [((PAIRS, MID, WIDE), f32), message],
            place,
            diffusion,
            lower,
            north,
            west,
            got,
            take,
            coef,
            pick,
            mix,
            spin,
            flag,
            smem=2,
            scratch=[pltpu.VMEM((PAIRS, TALL, WIDE), f32), pltpu.VMEM((PAIRS, MID, WIDE), f32)],
        )

    def section_two(middle, got):
        return call(
            second_kernel,
            [(fields.shape, f32), (fields.shape, f32)],
            place,
            diffusion,
            middle,
            got,
            take,
            coef,
            held,
            smem=2,
            scratch=[pltpu.VMEM((PAIRS, MID, WIDE), f32)],
        )

    middle, sent = section_one(to_blocks(chunks))
    got = to_holders(sent)
    crowded = jnp.maximum(got[0, 0, FLAG], got[PEERS, 0, FLAG]) > ROOM
    (chunks,) = call(choice_kernel, [chunk], place, got, send, smem=1)
    fitting = section_two(middle, to_blocks(chunks))

    def with_room():
        def dense(got):
            chunks = call(
                dense_kernel,
                [((PEERS, PLANES, CHUNK), f32)],
                place,
                got,
                holder,
                spot,
                smem=1,
                limit=16,
            )
            return to_blocks(chunks[0]).sum(axis=0)

        middle, sent = section_one(dense(first_got))
        return section_two(middle, dense(to_holders(sent)))

    accumulated, section_three = lax.cond(crowded, with_room, lambda: fitting)
    return (accumulated[None], section_three[None])


def solution(mesh):
    return jax.shard_map(
        shards,
        mesh=mesh,
        in_specs=(
            P("panel", None, None, "lat", "lon"),
            P("panel", "lat", "lon", None),
            P("panel", "lat", "lon", None, None),
            P("panel", "lat", "lon", None),
            P("panel", None),
            P(),
        ),
        out_specs=(P("panel", None, None, "lat", "lon"), P("panel", None, None, "lat", "lon")),
        check_vma=False,
    )
```

```python
import math

import jax
import jax.numpy as jnp
from jax import lax
from jax.experimental import pallas as pl
from jax.experimental.pallas import tpu as pltpu
from jax.sharding import PartitionSpec as P

GAMMA = 5.0 / 3.0
RADIAL_STEP = 0.65 / 32.0
FIELDS = 8
LEVELS = 4
PLANES = FIELDS * LEVELS
PAIRS = PLANES // 2
LOW_LEVEL = (0, 1)
HIGH_LEVEL = (3, 2)
ROWS = 16
COLS = 48
SLOTS = 33
LATS = 16
LONS = 16
ROOM = 63
WIDE = 128
HALF = 64
TALL = ROWS + 16
MID = ROWS + 8
BAND = 4 * HALF
SIDE = 4 * TALL
CHUNK = BAND + SIDE
PEERS = 16
PACKED = 32
MESSAGE = 9 * WIDE
TAIL = 8 * WIDE
FLAG = TAIL + HALF - 1
CHOICE_TILES = PEERS * PACKED // WIDE
CHOICE_DEPTH = (CHOICE_TILES + 1) * WIDE
DEPTH = PEERS * HALF
PANEL_ROWS = ROWS * LATS
PANEL_COLS = COLS * LONS
DTHETA = 0.5 * math.pi / PANEL_ROWS
DPHI = 1.5 * math.pi / PANEL_COLS
FINEST = min(DTHETA, DPHI)
TIME_STEP = 0.1 * FINEST
RADII = [0.35 + 0.65 * (k + 16 - LEVELS // 2 + 0.5) / 32.0 for k in range(LEVELS)]
VMEM = pl.BlockSpec(memory_space=pltpu.VMEM)
SMEM = pl.BlockSpec(memory_space=pltpu.SMEM)
MIB = 1024 * 1024


def iota(shape, axis):
    return lax.broadcasted_iota(jnp.int32, shape, axis)


def column_of(shape):
    return iota(shape, len(shape) - 1) & (HALF - 1)


def turn(value, lanes):
    return pltpu.roll(value, lanes % WIDE, 1) if lanes % WIDE else value


def three_parts(value):
    parts = []
    for _ in range(3):
        part = value.astype(jnp.bfloat16)
        value = value - part.astype(jnp.float32)
        parts.append(part)
    return parts


def donor_message(planes, pick, mix, spin):
    parts = jnp.concatenate(three_parts(planes), axis=1)
    chosen = jnp.dot(parts, pick, preferred_element_type=jnp.float32)
    chosen = chosen.reshape(PAIRS, MID, 2 * WIDE)
    both = jnp.sum(chosen * mix[None], axis=1)
    both = jnp.concatenate([both[:, :WIDE], both[:, WIDE:]], axis=0)
    mixed = both + pltpu.roll(both, HALF, 1)
    cosine = spin[0:1]
    sine = spin[1:2]
    at = (iota((PLANES, WIDE), 0) & (PAIRS - 1)) // 2
    theta = (at == 2) | (at == 5)
    phi = (at == 3) | (at == 6)
    other = jnp.where(theta, pltpu.roll(mixed, PLANES - 2, 0), -pltpu.roll(mixed, 2, 0))
    turned = jnp.where(theta | phi, cosine * mixed + sine * other, mixed)
    return jnp.where(iota((PAIRS, WIDE), 1) < HALF, turned[:PAIRS], turned[PAIRS:])


def post_message(place_ref, packed, flag, out_ref):
    panel = place_ref[0]
    lane = iota((16, WIDE), 1)
    column = lane & (HALF - 1)
    dense = jnp.where(column[:8] < PACKED, packed[:8], turn(packed[8:], PACKED))
    last = jnp.where(
        lane < HALF, packed[:, PACKED : PACKED + 1], packed[:, HALF + PACKED : HALF + PACKED + 1]
    )
    tail = jnp.sum(jnp.where(column == iota((16, WIDE), 0), last, 0.0), axis=0, keepdims=True)
    blank = jnp.where(lane[:1] == FLAG - TAIL, flag, 0.0)
    tail = jnp.where(lane[:1] == FLAG - TAIL, flag, tail)
    zero = jnp.zeros((1, WIDE), jnp.float32)
    for row in range(9):
        full = dense[row : row + 1] if row < 8 else tail
        empty = zero if row < 8 else blank
        at = slice(row * WIDE, (row + 1) * WIDE)
        out_ref[pl.ds((1 - panel) * PEERS, PEERS), :, at] = jnp.broadcast_to(
            full[None], (PEERS, 1, WIDE)
        )
        out_ref[pl.ds(panel * PEERS, PEERS), :, at] = jnp.broadcast_to(
            empty[None], (PEERS, 1, WIDE)
        )


def cut_kernel(state_ref, held_ref, south_ref, east_ref, corner_ref, plane_ref):
    for plane in range(PLANES):
        plane_ref[plane, :, :COLS] = state_ref[plane // LEVELS, plane % LEVELS]
    lane = iota((ROWS, WIDE), 1)
    column = column_of((ROWS, WIDE))
    own = (column >= 8) & (column < 8 + COLS)
    for pair in range(PAIRS):
        field, which = pair // 2, pair % 2
        low = turn(plane_ref[field * LEVELS + LOW_LEVEL[which]], 8)
        high = turn(plane_ref[field * LEVELS + HIGH_LEVEL[which]], HALF + 8)
        tile = jnp.where(own, jnp.where(lane < HALF, low, high), 0.0)
        held_ref[pair] = tile
        south_ref[pair] = tile[:8]
    for group in range(2):
        columns = jnp.zeros((ROWS, WIDE), jnp.float32)
        for which in range(8):
            moved = turn(held_ref[8 * group + which], 8 * which - 8)
            columns = jnp.where(column // 8 == which, moved, columns)
        east_ref[group] = columns
        corner_ref[group] = columns[:8]


def donor_tables(donor_ref, pick_ref, mix_ref, spin_ref, line_ref):
    late = iota((1, WIDE), 1) >= HALF

    def twice(value, fill):
        line_ref[...] = jnp.full((1, WIDE), fill, jnp.float32)
        line_ref[:, :SLOTS] = value
        line = line_ref[...]
        return jnp.where(late, pltpu.roll(line, HALF, 1), line)

    cell = twice(donor_ref[0:1], -10.0 * COLS)
    row_at = jnp.floor((cell + 0.5) * (1.0 / COLS))
    col_at = cell - row_at * COLS + jnp.where(late, 1.0, 0.0)
    upper = jnp.where(late, twice(donor_ref[2:3], 0.0), twice(donor_ref[1:2], 0.0))
    lower = jnp.where(late, twice(donor_ref[4:5], 0.0), twice(donor_ref[3:4], 0.0))
    angle = twice(donor_ref[5:6], 0.0)
    spin_ref[0:1] = jnp.cos(angle)
    spin_ref[1:2] = jnp.sin(angle)
    lane = iota((WIDE, WIDE), 0).astype(jnp.float32)
    real = jnp.where(row_at >= 0, col_at + 8.0, -1000.0)
    low = jnp.where(lane == real, 1.0, 0.0).astype(jnp.bfloat16)
    high = jnp.where(lane == real + HALF, 1.0, 0.0).astype(jnp.bfloat16)
    for part in range(3):
        pick_ref[part * WIDE : (part + 1) * WIDE, :WIDE] = low
        pick_ref[part * WIDE : (part + 1) * WIDE, WIDE:] = high
    row = iota((MID, WIDE), 0).astype(jnp.float32)
    mix = jnp.where(row == row_at, upper, 0.0) + jnp.where(row == row_at + 1.0, lower, 0.0)
    mix_ref[:, :WIDE] = mix
    mix_ref[:, WIDE:] = mix


def count_kernel(bands_ref, sides_ref, flag_ref):
    width = bands_ref.shape[1]
    column = iota((width, WIDE), 0) - 4
    start = iota((width, WIDE), 1) * COLS - 8
    within = (column >= start) & (column < start + 64) & (start < PANEL_COLS)
    columns = jnp.where(within, 1.0, 0.0).astype(jnp.bfloat16)
    row = iota((PANEL_ROWS, WIDE), 0)
    start = iota((PANEL_ROWS, WIDE), 1) * ROWS - 8
    within = (row >= start) & (row < start + TALL) & (start < PANEL_ROWS)
    rows = jnp.where(within, 1.0, 0.0).astype(jnp.bfloat16)

    def most(slots, windows):
        ones = []
        for which in range(LATS):
            first = which * LONS * SLOTS
            inside = (slots >= first) & (slots < first + LONS * SLOTS)
            ones.append(jnp.where(inside, 1.0, 0.0))
        ones = jnp.concatenate(ones, axis=0).astype(jnp.bfloat16)
        counts = jnp.dot(ones, windows, preferred_element_type=jnp.float32)
        return jnp.max(jnp.sum(counts.reshape(2 * LATS, 4, WIDE), axis=1))

    total = most(bands_ref[...], columns) + most(sides_ref[...], rows)
    flag_ref[...] = jnp.full(flag_ref.shape, total, jnp.float32)


def donor_kernel(
    place_ref, held_ref, south_ref, east_ref, corner_ref, pick_ref, mix_ref, spin_ref,
    lower_ref, north_ref, out_ref
):
    column = column_of((ROWS, WIDE))
    beyond = column >= 8 + COLS
    for pair in range(PAIRS):
        group, which = pair // 8, pair % 8
        east = turn(east_ref[group], 8 + COLS - 8 * which)
        corner = turn(corner_ref[group], 8 + COLS - 8 * which)
        lower_ref[pair, :ROWS] = jnp.where(beyond, east, held_ref[pair])
        lower_ref[pair, ROWS:] = jnp.where(beyond[:8], corner, south_ref[pair])
        north_ref[pair] = lower_ref[pair, 8:16]
    planes = lower_ref[...].reshape(PAIRS * MID, WIDE)
    packed = donor_message(planes, pick_ref[...], mix_ref[...], spin_ref[...])
    post_message(place_ref, packed, jnp.zeros((1, WIDE), jnp.float32), out_ref)


def split_parts(held):
    return jnp.concatenate(three_parts(held), axis=0)


def join_parts(terms):
    return terms[:PLANES] + terms[PLANES : 2 * PLANES] + terms[2 * PLANES :]


def from_row(place_ref, got_ref):
    base = (1 - place_ref[0]) * PEERS
    part = iota((8, WIDE), 1) // PACKED
    tiles = []
    tails = []
    for tile in range(CHOICE_TILES):
        rows = [jnp.zeros((8, WIDE), jnp.float32)] * 4
        for which in range(4):
            at = base + 4 * tile + which
            message = jnp.concatenate(
                [got_ref[at, :, row * WIDE : (row + 1) * WIDE] for row in range(8)], axis=0
            )
            tails.append(got_ref[at, :, TAIL:])
            for group in range(4):
                moved = turn(message, PACKED * (which - group))
                rows[group] = jnp.where(part == which, moved, rows[group])
        tiles.append(jnp.concatenate(rows, axis=0))
    tails.append(jnp.zeros((WIDE - PEERS, WIDE), jnp.float32))
    tails = jnp.concatenate(tails, axis=0).T
    tiles.append(jnp.concatenate([tails[:PAIRS], tails[HALF : HALF + PAIRS]], axis=0))
    return split_parts(jnp.concatenate(tiles, axis=1))


def rank_of(chosen):
    order = iota((CHUNK, CHUNK), 0) < iota((CHUNK, CHUNK), 1)
    order = jnp.where(order, 1.0, 0.0).astype(jnp.bfloat16)
    ones = jnp.where(chosen, 1.0, 0.0).astype(jnp.bfloat16)
    return jnp.dot(ones, order, preferred_element_type=jnp.float32)


def send_kernel(place_ref, holder_ref, spot_ref, send_ref):
    mine = holder_ref[...] == place_ref[1]
    spot = spot_ref[...].astype(jnp.float32)
    rank = rank_of(mine)
    key = jnp.where(mine & (rank < ROOM), rank, -1.0)
    place_at = iota((HALF, CHUNK), 0).astype(jnp.float32)
    eye = iota((WIDE, WIDE), 0) == iota((WIDE, WIDE), 1)
    depth = iota((CHOICE_DEPTH, WIDE), 0).astype(jnp.float32) + 1.0
    for pair in range(LATS // 2):
        tables = []
        for block in (2 * pair, 2 * pair + 1):
            found = place_at == key[block : block + 1]
            tables.append(
                jnp.sum(jnp.where(found, spot[block : block + 1] + 1.0, 0.0), axis=1, keepdims=True)
            )
        table = jnp.concatenate(tables, axis=0)
        line = jnp.sum(jnp.where(eye, table, 0.0), axis=0, keepdims=True)
        hot = jnp.where(depth == line, 1.0, 0.0).astype(jnp.bfloat16)
        send_ref[:, pair * WIDE : (pair + 1) * WIDE] = hot


def take_kernel(place_ref, holder_ref, take_ref, coef_ref):
    lat = place_ref[1]
    own = holder_ref[pl.ds(lat, 1)]
    masks = iota((PEERS, CHUNK), 0) == own
    rank = jnp.sum(jnp.where(masks, rank_of(masks), 0.0), axis=0, keepdims=True)
    fits = (own >= 0) & (rank < ROOM)
    index = jnp.where(fits, own.astype(jnp.float32) * HALF + rank, -1.0)
    hot = iota((DEPTH, CHUNK), 0).astype(jnp.float32) == index
    take_ref[...] = jnp.where(hot, 1.0, 0.0).astype(jnp.bfloat16)
    row = (lat * ROWS - 8 + iota((TALL, WIDE), 0)).astype(jnp.float32)
    column = (place_ref[2] * COLS - 8 + column_of((TALL, WIDE))).astype(jnp.float32)
    colatitude = 0.25 * math.pi + (row + 0.5) * DTHETA
    longitude = -0.75 * math.pi + (column + 0.5) * DPHI
    sine, cosine = jnp.sin(colatitude), jnp.cos(colatitude)
    twirl = 2.0 * 0.25 / TIME_STEP
    yang = place_ref[0] == 1
    coef_ref[0] = sine
    coef_ref[1] = 1.0 / sine
    coef_ref[2] = twirl * jnp.where(yang, sine * jnp.sin(longitude), cosine)
    coef_ref[3] = twirl * jnp.where(yang, cosine * jnp.sin(longitude), -sine)
    coef_ref[4] = twirl * jnp.where(yang, jnp.cos(longitude), 0.0)


def widen_kernel(place_ref, got_ref, send_ref, lower_ref, north_ref, out_ref, west_ref):
    column = column_of((TALL, WIDE))
    for group in range(2):
        columns = jnp.zeros((TALL, WIDE), jnp.float32)
        for which in range(8):
            pair = 8 * group + which
            rows = jnp.concatenate([north_ref[pair], lower_ref[pair]], axis=0)
            moved = turn(rows, 8 * which - COLS)
            columns = jnp.where(column // 8 == which, moved, columns)
        west_ref[group] = columns
    choice_kernel(place_ref, got_ref, send_ref, out_ref)


def choice_kernel(place_ref, got_ref, send_ref, out_ref):
    parts = from_row(place_ref, got_ref)
    terms = jnp.dot(parts, send_ref[...], preferred_element_type=jnp.float32)
    chosen = join_parts(terms)
    low = iota((16, WIDE), 1) < HALF
    for pair in range(PEERS // 2):
        tile = chosen[:, pair * WIDE : (pair + 1) * WIDE]
        top, end = tile[:16], tile[16:]
        out_ref[2 * pair] = jnp.where(low, top, pltpu.roll(end, HALF, 1))
        out_ref[2 * pair + 1] = jnp.where(low, pltpu.roll(top, HALF, 1), end)


def dense_kernel(place_ref, got_ref, holder_ref, spot_ref, out_ref):
    parts = from_row(place_ref, got_ref)
    index = jnp.where(holder_ref[...] == place_ref[1], spot_ref[...], -1)
    at = iota((CHOICE_DEPTH, CHUNK), 0)
    for block in range(LATS):
        hot = jnp.where(at == index[block : block + 1], 1.0, 0.0).astype(jnp.bfloat16)
        out_ref[block] = join_parts(jnp.dot(parts, hot, preferred_element_type=jnp.float32))


def ghost_values(got_ref, take_ref):
    if len(got_ref.shape) == 2:
        return got_ref[...]
    low = iota((16, WIDE), 1) < HALF
    tiles = []
    for pair in range(PEERS // 2):
        one = got_ref[2 * pair]
        two = got_ref[2 * pair + 1]
        top = jnp.where(low, one, pltpu.roll(two, HALF, 1))
        end = jnp.where(low, pltpu.roll(one, HALF, 1), two)
        tiles.append(jnp.concatenate([top, end], axis=0))
    parts = split_parts(jnp.concatenate(tiles, axis=1))
    return join_parts(jnp.dot(parts, take_ref[...], preferred_element_type=jnp.float32))


def fill_ghosts(place_ref, ghosts, work_ref, rows):
    lat, lon = place_ref[1], place_ref[2]
    trim = (TALL - rows) // 2
    top = 8 - trim
    half = PLANES // 2

    @pl.when((lon == 0) | (lon == LONS - 1))
    def _():
        side = ghosts[:, BAND:]
        first = jnp.where(lon == 0, 4, 8 + COLS)
        own = iota((rows, WIDE), 1) // 4 == iota((rows, WIDE), 0) + trim

        def spread(part):
            part = part.astype(jnp.float32)[:, None, :]
            return jnp.where(own[None], part, 0.0).astype(jnp.bfloat16).reshape(PAIRS * rows, WIDE)

        pieces = []
        for part in three_parts(side):
            pieces += [spread(part[:half]), spread(part[half:])]
        both = jnp.concatenate(pieces, axis=1)
        source = iota((6 * WIDE, WIDE), 0)
        target = first + (source & 3) + jnp.where((source & WIDE) != 0, HALF, 0)
        hot = jnp.where(target == iota((6 * WIDE, WIDE), 1), 1.0, 0.0).astype(jnp.bfloat16)
        moved = jnp.dot(both, hot, preferred_element_type=jnp.float32)
        moved = moved.reshape(PAIRS, rows, WIDE)
        column = column_of((rows, WIDE))
        ghost = (column >= first) & (column < first + 4)
        work_ref[...] = jnp.where(ghost[None], moved, work_ref[...])

    @pl.when((lat == 0) | (lat == LATS - 1))
    def _():
        low = iota((half, WIDE), 1) < HALF
        lines = []
        for which in range(2):
            piece = ghosts[:, which * WIDE : (which + 1) * WIDE]
            one, two = piece[:half], piece[half:]
            lines.append(jnp.where(low, one, pltpu.roll(two, HALF, 1)))
            lines.append(jnp.where(low, pltpu.roll(one, HALF, 1), two))

        @pl.when(lat == 0)
        def _():
            for row in range(4):
                work_ref[:, top - 4 + row, :] = lines[row]

        @pl.when(lat == LATS - 1)
        def _():
            for row in range(4):
                work_ref[:, top + ROWS + row, :] = lines[row]


def rates(load, rows, coef_ref, diffusion_ref):
    low = iota((rows, WIDE), 1) < HALF

    def levels(values):
        halves = [
            jnp.where(low, values[LOW_LEVEL[k]], values[HIGH_LEVEL[k]]).astype(jnp.float32)
            for k in range(2)
        ]
        return jnp.concatenate(halves, axis=0)

    def whole(which):
        value = coef_ref[which]
        if rows < TALL:
            value = pltpu.roll(value, TALL - (TALL - rows) // 2, 0)[:rows]
        return jnp.concatenate([value] * 2, axis=0)

    sine = whole(0)
    per_sine = whole(1)
    radius = levels(RADII)
    inverse = levels([1.0 / r for r in RADII])
    square = levels([r * r for r in RADII])
    per_square = levels([1.0 / (r * r) for r in RADII])
    sign = jnp.where(low, 1.0, -1.0)
    ends = sign * (1.0 / RADIAL_STEP)
    inner = sign * (1.0 / (2.0 * RADIAL_STEP))
    viscosity = diffusion_ref[0] * (FINEST * FINEST / TIME_STEP)
    resistivity = diffusion_ref[1] * (FINEST * FINEST / TIME_STEP)

    def slope(value, axis, step):
        size = value.shape[axis]
        near = pltpu.roll(value, size - 1, axis) - pltpu.roll(value, 1, axis)
        far = pltpu.roll(value, size - 2, axis) - pltpu.roll(value, 2, axis)
        return near * (8.0 / (12.0 * step)) - far * (1.0 / (12.0 * step))

    def d_theta(value):
        return slope(value, 0, DTHETA)

    def d_phi(value):
        return slope(value, 1, DPHI)

    def d_radius(value):
        one, two = value[:rows], value[rows:]
        return jnp.concatenate(
            [(two - one) * ends, (pltpu.roll(two, HALF, 1) - one) * inner], axis=0
        )

    def by_radius(value):
        return value * radius

    def per_radius(value):
        return value * inverse

    def curl(vector):
        part_r, part_t, part_p = vector
        return (
            per_radius((d_theta(sine * part_p) - d_phi(part_t)) * per_sine),
            per_radius(d_phi(part_r) * per_sine - d_radius(by_radius(part_p))),
            per_radius(d_radius(by_radius(part_t)) - d_theta(part_r)),
        )

    def gradient(value):
        return (
            d_radius(value),
            per_radius(d_theta(value)),
            per_radius(d_phi(value) * per_sine),
        )

    def cross(left, right):
        return (
            left[1] * right[2] - left[2] * right[1],
            left[2] * right[0] - left[0] * right[2],
            left[0] * right[1] - left[1] * right[0],
        )

    def advect(vector, slopes):
        return vector[0] * slopes[0] + vector[1] * slopes[1] + vector[2] * slopes[2]

    velocity = [load(which) for which in (1, 2, 3)]
    magnetic = [load(which) for which in (4, 5, 6)]
    vorticity = curl(velocity)
    current = curl(magnetic)
    spread = d_radius(square * velocity[0]) * per_square + per_radius(
        (d_theta(sine * velocity[1]) + d_phi(velocity[2])) * per_sine
    )
    induced = cross(velocity, magnetic)
    electric = [induced[k] - resistivity * current[k] for k in range(3)]
    kinetic = 0.5 * (
        velocity[0] * velocity[0] + velocity[1] * velocity[1] + velocity[2] * velocity[2]
    )
    curl_electric = curl(electric)
    log_rho = load(0)
    rho_rate = -advect(velocity, gradient(log_rho)) - spread
    pressure = load(7)
    slope_pressure = gradient(pressure)
    pressure_rate = -advect(velocity, slope_pressure) - GAMMA * pressure * spread
    lorentz = cross(current, magnetic)
    per_rho = jnp.exp(-log_rho)
    slope_kinetic = gradient(kinetic)
    curl_vorticity = curl(vorticity)
    lamb = cross(velocity, vorticity)
    turning = cross((whole(2), whole(3), whole(4)), velocity)
    momentum = [
        lamb[k]
        - slope_kinetic[k]
        + per_rho * (lorentz[k] - slope_pressure[k])
        - turning[k]
        - viscosity * curl_vorticity[k]
        for k in range(3)
    ]
    return [rho_rate, *momentum, *curl_electric, pressure_rate]


def first_kernel(
    place_ref,
    diffusion_ref,
    lower_ref,
    north_ref,
    west_ref,
    got_ref,
    take_ref,
    coef_ref,
    pick_ref,
    mix_ref,
    spin_ref,
    flag_ref,
    middle_ref,
    out_ref,
    work_ref,
    next_ref,
):
    column = column_of((TALL, WIDE))
    for pair in range(PAIRS):
        group, which = pair // 8, pair % 8
        west = turn(west_ref[group], -8 * which)
        rows = jnp.concatenate([north_ref[pair], lower_ref[pair]], axis=0)
        work_ref[pair] = jnp.where(column < 8, west, rows)
    ghosts = ghost_values(got_ref, take_ref)
    fill_ghosts(place_ref, ghosts, work_ref, TALL)

    def load(which):
        return work_ref[2 * which : 2 * which + 2].reshape(2 * TALL, WIDE)

    found = rates(load, TALL, coef_ref, diffusion_ref)
    row = iota((TALL, WIDE), 0)
    inside = (column >= 4) & (column < 12 + COLS) & (row >= 4) & (row < 12 + ROWS)
    for which in range(FIELDS):
        value = load(which) + (0.5 * TIME_STEP) * found[which]
        for half in range(2):
            part = jnp.where(inside, value[half * TALL : (half + 1) * TALL], 0.0)
            next_ref[2 * which + half] = part[8:]
            middle_ref[2 * which + half] = pltpu.roll(part, TALL - 4, 0)[:MID]
    planes = next_ref[...].reshape(PAIRS * MID, WIDE)
    packed = donor_message(planes, pick_ref[...], mix_ref[...], spin_ref[...])
    post_message(place_ref, packed, flag_ref[0:1], out_ref)


def second_kernel(
    place_ref,
    diffusion_ref,
    middle_ref,
    got_ref,
    take_ref,
    coef_ref,
    held_ref,
    whole_ref,
    third_ref,
    work_ref,
):
    work_ref[...] = middle_ref[...]
    ghosts = ghost_values(got_ref, take_ref)
    fill_ghosts(place_ref, ghosts, work_ref, MID)

    def load(which):
        return work_ref[2 * which : 2 * which + 2].reshape(2 * MID, WIDE)

    found = rates(load, MID, coef_ref, diffusion_ref)

    def centre(value):
        return pltpu.roll(value, MID - 4, 0)[:ROWS]

    def place(out_ref, pair, value):
        field, half = pair // 2, pair % 2
        out_ref[field, LOW_LEVEL[half]] = turn(value, -8)[:, :COLS]
        out_ref[field, HIGH_LEVEL[half]] = turn(value, -8 - HALF)[:, :COLS]

    for pair in range(PAIRS):
        field, half = pair // 2, pair % 2
        rate = found[field][half * MID : (half + 1) * MID]
        held = held_ref[pair]
        step = centre(rate) * (0.5 * TIME_STEP)
        middle = centre(middle_ref[pair])
        place(third_ref, pair, held + step)
        place(whole_ref, pair, held + ((middle - held) + 2.0 * step) * (1.0 / 3.0))


def shift(value, move_lat, move_lon):
    pairs = []
    for a in range(LATS):
        for b in range(LONS):
            goal_a, goal_b = a + move_lat, b + move_lon
            if 0 <= goal_a < LATS and 0 <= goal_b < LONS:
                pairs.append((a * LONS + b, goal_a * LONS + goal_b))
    return lax.ppermute(value, ("lat", "lon"), pairs)


def shards(state, donor_cell, donor_weights, donor_turn, border_source, diffusion):
    fields = state[0]
    panel = lax.axis_index("panel")
    lat = lax.axis_index("lat")
    lon = lax.axis_index("lon")
    place = jnp.stack([panel, lat, lon]).astype(jnp.int32)
    f32 = jnp.float32

    def call(kernel, outs, *args, smem=0, specs=None, scratch=(), limit=10):
        shapes = [jax.ShapeDtypeStruct(shape, dtype) for shape, dtype in outs]
        return pl.pallas_call(
            kernel,
            out_shape=shapes,
            in_specs=specs or [SMEM] * smem + [VMEM] * (len(args) - smem),
            out_specs=[VMEM] * len(outs),
            scratch_shapes=scratch,
            compiler_params=pltpu.CompilerParams(vmem_limit_bytes=limit * MIB),
        )(*args)

    bf16 = jnp.bfloat16
    held, south, east, corner = call(
        cut_kernel,
        [
            ((PAIRS, ROWS, WIDE), f32),
            ((PAIRS, 8, WIDE), f32),
            ((2, ROWS, WIDE), f32),
            ((2, 8, WIDE), f32),
        ],
        fields,
        scratch=[pltpu.VMEM((PLANES, ROWS, WIDE), f32)],
    )
    south = shift(south, -1, 0)
    east = shift(east, 0, -1)
    corner = shift(corner, -1, -1)

    donor = jnp.concatenate(
        [donor_cell[0, 0].astype(f32), donor_weights[0, 0, 0], donor_turn[0, 0]], axis=0
    )
    pick, mix, spin = call(
        donor_tables,
        [((3 * WIDE, 2 * WIDE), bf16), ((MID, 2 * WIDE), f32), ((2, WIDE), f32)],
        donor,
        scratch=[pltpu.VMEM((1, WIDE), f32)],
    )
    message = ((2 * PEERS, 1, MESSAGE), f32)
    lower, north, sent = call(
        donor_kernel,
        [((PAIRS, MID, WIDE), f32), ((PAIRS, 8, WIDE), f32), message],
        place,
        held,
        south,
        east,
        corner,
        pick,
        mix,
        spin,
        smem=1,
    )

    def to_holders(sent):
        return lax.all_to_all(sent, ("panel", "lon"), 0, 0, tiled=True)

    got = to_holders(sent)

    north, late_lat, late_lon, border, _ = lax.optimization_barrier(
        (north, lat, lon, border_source[0], sent)
    )
    north = shift(north, 1, 0)

    ring = PANEL_COLS + 8
    row_slots = LONS * SLOTS
    bands = border[: 8 * ring].reshape(8, ring)
    sides = border[8 * ring :].reshape(PANEL_ROWS, 8)
    window = jnp.pad(bands, ((0, 0), (4, 4)), constant_values=-1)
    window = lax.dynamic_slice(window, (0, late_lon * COLS), (8, 64)).reshape(2, BAND)
    side = jnp.where(late_lon == 0, sides[:, :4], sides[:, 4:])
    side = jnp.where((late_lon == 0) | (late_lon == LONS - 1), side, -1)
    side = jnp.pad(side, ((8, 8), (0, 0)), constant_values=-1)
    side = jnp.concatenate(
        [
            side[:PANEL_ROWS].reshape(LATS, ROWS, 4),
            side[ROWS:].reshape(LATS, ROWS, 4),
        ],
        axis=1,
    ).reshape(LATS, SIDE)
    at_lat = jnp.arange(LATS)[:, None]
    band = jnp.where(at_lat == 0, window[:1], jnp.where(at_lat == LATS - 1, window[1:], -1))
    wanted = jnp.concatenate([band, side], axis=1)
    holder = jnp.where(wanted >= 0, wanted // row_slots, -1)
    local = wanted - late_lat * row_slots
    block = local // SLOTS
    slot = local % SLOTS
    spot = jnp.where(slot < PACKED, block * PACKED + slot, PEERS * PACKED + block)
    (send,) = call(
        send_kernel, [((CHOICE_DEPTH, DEPTH), bf16)], place, holder, spot, smem=1, limit=16
    )
    chunk = ((PEERS, 16, WIDE), f32)
    first_got = got
    chunks, west = call(
        widen_kernel, [chunk, ((2, TALL, WIDE), f32)], place, got, send, lower, north, smem=1
    )
    west = shift(west, 0, 1)
    late_holder, bands, sides, _ = lax.optimization_barrier((holder, bands, sides, chunks))
    take, coef = call(
        take_kernel,
        [((DEPTH, CHUNK), bf16), ((5, TALL, WIDE), f32)],
        place,
        late_holder,
        smem=1,
    )

    (flag,) = call(
        count_kernel,
        [((8, WIDE), f32)],
        jnp.pad(bands, ((0, 0), (0, 7 * WIDE - ring)), constant_values=-1),
        sides.T,
    )

    def to_blocks(chunks):
        return lax.all_to_all(chunks, "lat", 0, 0, tiled=True)

    def section_one(got):
        return call(
            first_kernel,
            [((PAIRS, MID, WIDE), f32), message],
            place,
            diffusion,
            lower,
            north,
            west,
            got,
            take,
            coef,
            pick,
            mix,
            spin,
            flag,
            smem=2,
            scratch=[pltpu.VMEM((PAIRS, TALL, WIDE), f32), pltpu.VMEM((PAIRS, MID, WIDE), f32)],
        )

    def section_two(middle, got):
        return call(
            second_kernel,
            [(fields.shape, f32), (fields.shape, f32)],
            place,
            diffusion,
            middle,
            got,
            take,
            coef,
            held,
            smem=2,
            scratch=[pltpu.VMEM((PAIRS, MID, WIDE), f32)],
        )

    middle, sent = section_one(to_blocks(chunks))
    got = to_holders(sent)
    crowded = jnp.maximum(got[0, 0, FLAG], got[PEERS, 0, FLAG]) > ROOM
    (chunks,) = call(choice_kernel, [chunk], place, got, send, smem=1)
    fitting = section_two(middle, to_blocks(chunks))

    def with_room():
        def dense(got):
            chunks = call(
                dense_kernel,
                [((PEERS, PLANES, CHUNK), f32)],
                place,
                got,
                holder,
                spot,
                smem=1,
                limit=16,
            )
            return to_blocks(chunks[0]).sum(axis=0)

        middle, sent = section_one(dense(first_got))
        return section_two(middle, dense(to_holders(sent)))

    accumulated, section_three = lax.cond(crowded, with_room, lambda: fitting)
    return (accumulated[None], section_three[None])


def solution(mesh):
    return jax.shard_map(
        shards,
        mesh=mesh,
        in_specs=(
            P("panel", None, None, "lat", "lon"),
            P("panel", "lat", "lon", None),
            P("panel", "lat", "lon", None, None),
            P("panel", "lat", "lon", None),
            P("panel", None),
            P(),
        ),
        out_specs=(P("panel", None, None, "lat", "lon"), P("panel", None, None, "lat", "lon")),
        check_vma=False,
    )
```

```python
import math

import jax
import jax.numpy as jnp
from jax import lax
from jax.experimental import pallas as pl
from jax.experimental.pallas import tpu as pltpu
from jax.sharding import PartitionSpec as P

GAMMA = 5.0 / 3.0
RADIAL_STEP = 0.65 / 32.0
FIELDS = 8
LEVELS = 4
PLANES = FIELDS * LEVELS
PAIRS = PLANES // 2
LOW_LEVEL = (0, 1)
HIGH_LEVEL = (3, 2)
ROWS = 16
COLS = 48
SLOTS = 33
LATS = 16
LONS = 16
ROOM = 63
WIDE = 128
HALF = 64
TALL = ROWS + 16
MID = ROWS + 8
BAND = 4 * HALF
SIDE = 4 * TALL
CHUNK = BAND + SIDE
PEERS = 16
PACKED = 32
MESSAGE = 9 * WIDE
TAIL = 8 * WIDE
FLAG = TAIL + HALF - 1
CHOICE_TILES = PEERS * PACKED // WIDE
CHOICE_DEPTH = (CHOICE_TILES + 1) * WIDE
DEPTH = PEERS * HALF
PANEL_ROWS = ROWS * LATS
PANEL_COLS = COLS * LONS
DTHETA = 0.5 * math.pi / PANEL_ROWS
DPHI = 1.5 * math.pi / PANEL_COLS
FINEST = min(DTHETA, DPHI)
TIME_STEP = 0.1 * FINEST
RADII = [0.35 + 0.65 * (k + 16 - LEVELS // 2 + 0.5) / 32.0 for k in range(LEVELS)]
VMEM = pl.BlockSpec(memory_space=pltpu.VMEM)
SMEM = pl.BlockSpec(memory_space=pltpu.SMEM)
MIB = 1024 * 1024


def iota(shape, axis):
    return lax.broadcasted_iota(jnp.int32, shape, axis)


def column_of(shape):
    return iota(shape, len(shape) - 1) & (HALF - 1)


def turn(value, lanes):
    return pltpu.roll(value, lanes % WIDE, 1) if lanes % WIDE else value


def three_parts(value):
    parts = []
    for _ in range(3):
        part = value.astype(jnp.bfloat16)
        value = value - part.astype(jnp.float32)
        parts.append(part)
    return parts


def donor_message(planes, pick, mix, spin):
    parts = jnp.concatenate(three_parts(planes), axis=1)
    chosen = jnp.dot(parts, pick, preferred_element_type=jnp.float32)
    chosen = chosen.reshape(PAIRS, MID, 2 * WIDE)
    both = jnp.sum(chosen * mix[None], axis=1)
    both = jnp.concatenate([both[:, :WIDE], both[:, WIDE:]], axis=0)
    mixed = both + pltpu.roll(both, HALF, 1)
    cosine = spin[0:1]
    sine = spin[1:2]
    at = (iota((PLANES, WIDE), 0) & (PAIRS - 1)) // 2
    theta = (at == 2) | (at == 5)
    phi = (at == 3) | (at == 6)
    other = jnp.where(theta, pltpu.roll(mixed, PLANES - 2, 0), -pltpu.roll(mixed, 2, 0))
    turned = jnp.where(theta | phi, cosine * mixed + sine * other, mixed)
    return jnp.where(iota((PAIRS, WIDE), 1) < HALF, turned[:PAIRS], turned[PAIRS:])


def post_message(place_ref, packed, flag, out_ref):
    panel = place_ref[0]
    lane = iota((16, WIDE), 1)
    column = lane & (HALF - 1)
    dense = jnp.where(column[:8] < PACKED, packed[:8], turn(packed[8:], PACKED))
    last = jnp.where(
        lane < HALF, packed[:, PACKED : PACKED + 1], packed[:, HALF + PACKED : HALF + PACKED + 1]
    )
    tail = jnp.sum(jnp.where(column == iota((16, WIDE), 0), last, 0.0), axis=0, keepdims=True)
    blank = jnp.where(lane[:1] == FLAG - TAIL, flag, 0.0)
    tail = jnp.where(lane[:1] == FLAG - TAIL, flag, tail)
    zero = jnp.zeros((1, WIDE), jnp.float32)
    for row in range(9):
        full = dense[row : row + 1] if row < 8 else tail
        empty = zero if row < 8 else blank
        at = slice(row * WIDE, (row + 1) * WIDE)
        out_ref[pl.ds((1 - panel) * PEERS, PEERS), :, at] = jnp.broadcast_to(
            full[None], (PEERS, 1, WIDE)
        )
        out_ref[pl.ds(panel * PEERS, PEERS), :, at] = jnp.broadcast_to(
            empty[None], (PEERS, 1, WIDE)
        )


def pair_tile(state_ref, plane_ref, pair, rows):
    field, which = pair // 2, pair % 2
    plane_ref[2 * pair, :, :COLS] = state_ref[field, LOW_LEVEL[which], :rows]
    plane_ref[2 * pair + 1, :, :COLS] = state_ref[field, HIGH_LEVEL[which], :rows]
    column = column_of((rows, WIDE))
    low = turn(plane_ref[2 * pair], 8)
    high = turn(plane_ref[2 * pair + 1], HALF + 8)
    tile = jnp.where(iota((rows, WIDE), 1) < HALF, low, high)
    return jnp.where((column >= 8) & (column < 8 + COLS), tile, 0.0)


def cut_kernel(state_ref, held_ref, east_ref, corner_ref, plane_ref):
    column = column_of((ROWS, WIDE))
    for pair in range(PAIRS):
        held_ref[pair] = pair_tile(state_ref, plane_ref, pair, ROWS)
    for group in range(2):
        columns = jnp.zeros((ROWS, WIDE), jnp.float32)
        for which in range(8):
            moved = turn(held_ref[8 * group + which], 8 * which - 8)
            columns = jnp.where(column // 8 == which, moved, columns)
        east_ref[group] = columns
        corner_ref[group] = columns[:8]


def donor_tables(donor_ref, pick_ref, mix_ref, spin_ref, line_ref):
    late = iota((1, WIDE), 1) >= HALF

    def twice(value, fill):
        line_ref[...] = jnp.full((1, WIDE), fill, jnp.float32)
        line_ref[:, :SLOTS] = value
        line = line_ref[...]
        return jnp.where(late, pltpu.roll(line, HALF, 1), line)

    cell = twice(donor_ref[0:1], -10.0 * COLS)
    row_at = jnp.floor((cell + 0.5) * (1.0 / COLS))
    col_at = cell - row_at * COLS + jnp.where(late, 1.0, 0.0)
    upper = jnp.where(late, twice(donor_ref[2:3], 0.0), twice(donor_ref[1:2], 0.0))
    lower = jnp.where(late, twice(donor_ref[4:5], 0.0), twice(donor_ref[3:4], 0.0))
    angle = twice(donor_ref[5:6], 0.0)
    spin_ref[0:1] = jnp.cos(angle)
    spin_ref[1:2] = jnp.sin(angle)
    lane = iota((WIDE, WIDE), 0).astype(jnp.float32)
    real = jnp.where(row_at >= 0, col_at + 8.0, -1000.0)
    low = jnp.where(lane == real, 1.0, 0.0).astype(jnp.bfloat16)
    high = jnp.where(lane == real + HALF, 1.0, 0.0).astype(jnp.bfloat16)
    for part in range(3):
        pick_ref[part * WIDE : (part + 1) * WIDE, :WIDE] = low
        pick_ref[part * WIDE : (part + 1) * WIDE, WIDE:] = high
    row = iota((MID, WIDE), 0).astype(jnp.float32)
    mix = jnp.where(row == row_at, upper, 0.0) + jnp.where(row == row_at + 1.0, lower, 0.0)
    mix_ref[:, :WIDE] = mix
    mix_ref[:, WIDE:] = mix


def count_kernel(bands_ref, sides_ref, flag_ref):
    width = bands_ref.shape[1]
    column = iota((width, WIDE), 0) - 4
    start = iota((width, WIDE), 1) * COLS - 8
    within = (column >= start) & (column < start + 64) & (start < PANEL_COLS)
    columns = jnp.where(within, 1.0, 0.0).astype(jnp.bfloat16)
    row = iota((PANEL_ROWS, WIDE), 0)
    start = iota((PANEL_ROWS, WIDE), 1) * ROWS - 8
    within = (row >= start) & (row < start + TALL) & (start < PANEL_ROWS)
    rows = jnp.where(within, 1.0, 0.0).astype(jnp.bfloat16)

    def most(slots, windows):
        ones = []
        for which in range(LATS):
            first = which * LONS * SLOTS
            inside = (slots >= first) & (slots < first + LONS * SLOTS)
            ones.append(jnp.where(inside, 1.0, 0.0))
        ones = jnp.concatenate(ones, axis=0).astype(jnp.bfloat16)
        counts = jnp.dot(ones, windows, preferred_element_type=jnp.float32)
        return jnp.max(jnp.sum(counts.reshape(2 * LATS, 4, WIDE), axis=1))

    total = most(bands_ref[...], columns) + most(sides_ref[...], rows)
    flag_ref[...] = jnp.full(flag_ref.shape, total, jnp.float32)


def donor_kernel(
    place_ref, held_ref, south_ref, east_ref, corner_ref, pick_ref, mix_ref, spin_ref,
    lower_ref, north_ref, out_ref, plane_ref
):
    column = column_of((ROWS, WIDE))
    beyond = column >= 8 + COLS
    for pair in range(PAIRS):
        group, which = pair // 8, pair % 8
        east = turn(east_ref[group], 8 + COLS - 8 * which)
        corner = turn(corner_ref[group], 8 + COLS - 8 * which)
        lower_ref[pair, :ROWS] = jnp.where(beyond, east, held_ref[pair])
        south = pair_tile(south_ref, plane_ref, pair, 8)
        lower_ref[pair, ROWS:] = jnp.where(beyond[:8], corner, south)
        north_ref[pair] = lower_ref[pair, 8:16]
    planes = lower_ref[...].reshape(PAIRS * MID, WIDE)
    packed = donor_message(planes, pick_ref[...], mix_ref[...], spin_ref[...])
    post_message(place_ref, packed, jnp.zeros((1, WIDE), jnp.float32), out_ref)


def split_parts(held):
    return jnp.concatenate(three_parts(held), axis=0)


def join_parts(terms):
    return terms[:PLANES] + terms[PLANES : 2 * PLANES] + terms[2 * PLANES :]


def from_row(place_ref, got_ref):
    base = (1 - place_ref[0]) * PEERS
    part = iota((8, WIDE), 1) // PACKED
    tiles = []
    tails = []
    for tile in range(CHOICE_TILES):
        rows = [jnp.zeros((8, WIDE), jnp.float32)] * 4
        for which in range(4):
            at = base + 4 * tile + which
            message = jnp.concatenate(
                [got_ref[at, :, row * WIDE : (row + 1) * WIDE] for row in range(8)], axis=0
            )
            tails.append(got_ref[at, :, TAIL:])
            for group in range(4):
                moved = turn(message, PACKED * (which - group))
                rows[group] = jnp.where(part == which, moved, rows[group])
        tiles.append(jnp.concatenate(rows, axis=0))
    tails.append(jnp.zeros((WIDE - PEERS, WIDE), jnp.float32))
    tails = jnp.concatenate(tails, axis=0).T
    tiles.append(jnp.concatenate([tails[:PAIRS], tails[HALF : HALF + PAIRS]], axis=0))
    return split_parts(jnp.concatenate(tiles, axis=1))


def rank_of(chosen):
    order = iota((CHUNK, CHUNK), 0) < iota((CHUNK, CHUNK), 1)
    order = jnp.where(order, 1.0, 0.0).astype(jnp.bfloat16)
    ones = jnp.where(chosen, 1.0, 0.0).astype(jnp.bfloat16)
    return jnp.dot(ones, order, preferred_element_type=jnp.float32)


def send_kernel(place_ref, holder_ref, spot_ref, send_ref):
    mine = holder_ref[...] == place_ref[1]
    spot = spot_ref[...].astype(jnp.float32)
    rank = rank_of(mine)
    key = jnp.where(mine & (rank < ROOM), rank, -1.0)
    place_at = iota((HALF, CHUNK), 0).astype(jnp.float32)
    eye = iota((WIDE, WIDE), 0) == iota((WIDE, WIDE), 1)
    depth = iota((CHOICE_DEPTH, WIDE), 0).astype(jnp.float32) + 1.0
    for pair in range(LATS // 2):
        tables = []
        for block in (2 * pair, 2 * pair + 1):
            found = place_at == key[block : block + 1]
            tables.append(
                jnp.sum(jnp.where(found, spot[block : block + 1] + 1.0, 0.0), axis=1, keepdims=True)
            )
        table = jnp.concatenate(tables, axis=0)
        line = jnp.sum(jnp.where(eye, table, 0.0), axis=0, keepdims=True)
        hot = jnp.where(depth == line, 1.0, 0.0).astype(jnp.bfloat16)
        send_ref[:, pair * WIDE : (pair + 1) * WIDE] = hot


def take_kernel(place_ref, holder_ref, take_ref, coef_ref):
    lat = place_ref[1]
    own = holder_ref[pl.ds(lat, 1)]
    masks = iota((PEERS, CHUNK), 0) == own
    rank = jnp.sum(jnp.where(masks, rank_of(masks), 0.0), axis=0, keepdims=True)
    fits = (own >= 0) & (rank < ROOM)
    index = jnp.where(fits, own.astype(jnp.float32) * HALF + rank, -1.0)
    hot = iota((DEPTH, CHUNK), 0).astype(jnp.float32) == index
    take_ref[...] = jnp.where(hot, 1.0, 0.0).astype(jnp.bfloat16)
    row = (lat * ROWS - 8 + iota((TALL, WIDE), 0)).astype(jnp.float32)
    column = (place_ref[2] * COLS - 8 + column_of((TALL, WIDE))).astype(jnp.float32)
    colatitude = 0.25 * math.pi + (row + 0.5) * DTHETA
    longitude = -0.75 * math.pi + (column + 0.5) * DPHI
    sine, cosine = jnp.sin(colatitude), jnp.cos(colatitude)
    twirl = 2.0 * 0.25 / TIME_STEP
    yang = place_ref[0] == 1
    coef_ref[0] = sine
    coef_ref[1] = 1.0 / sine
    coef_ref[2] = twirl * jnp.where(yang, sine * jnp.sin(longitude), cosine)
    coef_ref[3] = twirl * jnp.where(yang, cosine * jnp.sin(longitude), -sine)
    coef_ref[4] = twirl * jnp.where(yang, jnp.cos(longitude), 0.0)


def widen_kernel(place_ref, got_ref, send_ref, lower_ref, north_ref, out_ref, west_ref):
    column = column_of((TALL, WIDE))
    for group in range(2):
        columns = jnp.zeros((TALL, WIDE), jnp.float32)
        for which in range(8):
            pair = 8 * group + which
            rows = jnp.concatenate([north_ref[pair], lower_ref[pair]], axis=0)
            moved = turn(rows, 8 * which - COLS)
            columns = jnp.where(column // 8 == which, moved, columns)
        west_ref[group] = columns
    choice_kernel(place_ref, got_ref, send_ref, out_ref)


def choice_kernel(place_ref, got_ref, send_ref, out_ref):
    parts = from_row(place_ref, got_ref)
    terms = jnp.dot(parts, send_ref[...], preferred_element_type=jnp.float32)
    chosen = join_parts(terms)
    low = iota((16, WIDE), 1) < HALF
    for pair in range(PEERS // 2):
        tile = chosen[:, pair * WIDE : (pair + 1) * WIDE]
        top, end = tile[:16], tile[16:]
        out_ref[2 * pair] = jnp.where(low, top, pltpu.roll(end, HALF, 1))
        out_ref[2 * pair + 1] = jnp.where(low, pltpu.roll(top, HALF, 1), end)


def dense_kernel(place_ref, got_ref, holder_ref, spot_ref, out_ref):
    parts = from_row(place_ref, got_ref)
    index = jnp.where(holder_ref[...] == place_ref[1], spot_ref[...], -1)
    at = iota((CHOICE_DEPTH, CHUNK), 0)
    for block in range(LATS):
        hot = jnp.where(at == index[block : block + 1], 1.0, 0.0).astype(jnp.bfloat16)
        out_ref[block] = join_parts(jnp.dot(parts, hot, preferred_element_type=jnp.float32))


def ghost_values(got_ref, take_ref):
    if len(got_ref.shape) == 2:
        return got_ref[...]
    low = iota((16, WIDE), 1) < HALF
    tiles = []
    for pair in range(PEERS // 2):
        one = got_ref[2 * pair]
        two = got_ref[2 * pair + 1]
        top = jnp.where(low, one, pltpu.roll(two, HALF, 1))
        end = jnp.where(low, pltpu.roll(one, HALF, 1), two)
        tiles.append(jnp.concatenate([top, end], axis=0))
    parts = split_parts(jnp.concatenate(tiles, axis=1))
    return join_parts(jnp.dot(parts, take_ref[...], preferred_element_type=jnp.float32))


def fill_ghosts(place_ref, ghosts, work_ref, rows):
    lat, lon = place_ref[1], place_ref[2]
    trim = (TALL - rows) // 2
    top = 8 - trim
    half = PLANES // 2

    @pl.when((lon == 0) | (lon == LONS - 1))
    def _():
        side = ghosts[:, BAND:]
        first = jnp.where(lon == 0, 4, 8 + COLS)
        own = iota((rows, WIDE), 1) // 4 == iota((rows, WIDE), 0) + trim

        def spread(part):
            part = part.astype(jnp.float32)[:, None, :]
            return jnp.where(own[None], part, 0.0).astype(jnp.bfloat16).reshape(PAIRS * rows, WIDE)

        pieces = []
        for part in three_parts(side):
            pieces += [spread(part[:half]), spread(part[half:])]
        both = jnp.concatenate(pieces, axis=1)
        source = iota((6 * WIDE, WIDE), 0)
        target = first + (source & 3) + jnp.where((source & WIDE) != 0, HALF, 0)
        hot = jnp.where(target == iota((6 * WIDE, WIDE), 1), 1.0, 0.0).astype(jnp.bfloat16)
        moved = jnp.dot(both, hot, preferred_element_type=jnp.float32)
        moved = moved.reshape(PAIRS, rows, WIDE)
        column = column_of((rows, WIDE))
        ghost = (column >= first) & (column < first + 4)
        work_ref[...] = jnp.where(ghost[None], moved, work_ref[...])

    @pl.when((lat == 0) | (lat == LATS - 1))
    def _():
        low = iota((half, WIDE), 1) < HALF
        lines = []
        for which in range(2):
            piece = ghosts[:, which * WIDE : (which + 1) * WIDE]
            one, two = piece[:half], piece[half:]
            lines.append(jnp.where(low, one, pltpu.roll(two, HALF, 1)))
            lines.append(jnp.where(low, pltpu.roll(one, HALF, 1), two))

        @pl.when(lat == 0)
        def _():
            for row in range(4):
                work_ref[:, top - 4 + row, :] = lines[row]

        @pl.when(lat == LATS - 1)
        def _():
            for row in range(4):
                work_ref[:, top + ROWS + row, :] = lines[row]


def rates(load, rows, coef_ref, diffusion_ref):
    low = iota((rows, WIDE), 1) < HALF

    def levels(values):
        halves = [
            jnp.where(low, values[LOW_LEVEL[k]], values[HIGH_LEVEL[k]]).astype(jnp.float32)
            for k in range(2)
        ]
        return jnp.concatenate(halves, axis=0)

    def whole(which):
        value = coef_ref[which]
        if rows < TALL:
            value = pltpu.roll(value, TALL - (TALL - rows) // 2, 0)[:rows]
        return jnp.concatenate([value] * 2, axis=0)

    sine = whole(0)
    per_sine = whole(1)
    radius = levels(RADII)
    inverse = levels([1.0 / r for r in RADII])
    square = levels([r * r for r in RADII])
    per_square = levels([1.0 / (r * r) for r in RADII])
    sign = jnp.where(low, 1.0, -1.0)
    ends = sign * (1.0 / RADIAL_STEP)
    inner = sign * (1.0 / (2.0 * RADIAL_STEP))
    viscosity = diffusion_ref[0] * (FINEST * FINEST / TIME_STEP)
    resistivity = diffusion_ref[1] * (FINEST * FINEST / TIME_STEP)

    def slope(value, axis, step):
        size = value.shape[axis]
        near = pltpu.roll(value, size - 1, axis) - pltpu.roll(value, 1, axis)
        far = pltpu.roll(value, size - 2, axis) - pltpu.roll(value, 2, axis)
        return near * (8.0 / (12.0 * step)) - far * (1.0 / (12.0 * step))

    def d_theta(value):
        return slope(value, 0, DTHETA)

    def d_phi(value):
        return slope(value, 1, DPHI)

    def d_radius(value):
        one, two = value[:rows], value[rows:]
        return jnp.concatenate(
            [(two - one) * ends, (pltpu.roll(two, HALF, 1) - one) * inner], axis=0
        )

    def by_radius(value):
        return value * radius

    def per_radius(value):
        return value * inverse

    def curl(vector):
        part_r, part_t, part_p = vector
        return (
            per_radius((d_theta(sine * part_p) - d_phi(part_t)) * per_sine),
            per_radius(d_phi(part_r) * per_sine - d_radius(by_radius(part_p))),
            per_radius(d_radius(by_radius(part_t)) - d_theta(part_r)),
        )

    def gradient(value):
        return (
            d_radius(value),
            per_radius(d_theta(value)),
            per_radius(d_phi(value) * per_sine),
        )

    def cross(left, right):
        return (
            left[1] * right[2] - left[2] * right[1],
            left[2] * right[0] - left[0] * right[2],
            left[0] * right[1] - left[1] * right[0],
        )

    def advect(vector, slopes):
        return vector[0] * slopes[0] + vector[1] * slopes[1] + vector[2] * slopes[2]

    velocity = [load(which) for which in (1, 2, 3)]
    magnetic = [load(which) for which in (4, 5, 6)]
    vorticity = curl(velocity)
    current = curl(magnetic)
    spread = d_radius(square * velocity[0]) * per_square + per_radius(
        (d_theta(sine * velocity[1]) + d_phi(velocity[2])) * per_sine
    )
    induced = cross(velocity, magnetic)
    electric = [induced[k] - resistivity * current[k] for k in range(3)]
    kinetic = 0.5 * (
        velocity[0] * velocity[0] + velocity[1] * velocity[1] + velocity[2] * velocity[2]
    )
    curl_electric = curl(electric)
    log_rho = load(0)
    rho_rate = -advect(velocity, gradient(log_rho)) - spread
    pressure = load(7)
    slope_pressure = gradient(pressure)
    pressure_rate = -advect(velocity, slope_pressure) - GAMMA * pressure * spread
    lorentz = cross(current, magnetic)
    per_rho = jnp.exp(-log_rho)
    slope_kinetic = gradient(kinetic)
    curl_vorticity = curl(vorticity)
    lamb = cross(velocity, vorticity)
    turning = cross((whole(2), whole(3), whole(4)), velocity)
    momentum = [
        lamb[k]
        - slope_kinetic[k]
        + per_rho * (lorentz[k] - slope_pressure[k])
        - turning[k]
        - viscosity * curl_vorticity[k]
        for k in range(3)
    ]
    return [rho_rate, *momentum, *curl_electric, pressure_rate]


def first_kernel(
    place_ref,
    diffusion_ref,
    lower_ref,
    north_ref,
    west_ref,
    got_ref,
    take_ref,
    coef_ref,
    pick_ref,
    mix_ref,
    spin_ref,
    flag_ref,
    middle_ref,
    out_ref,
    work_ref,
    next_ref,
):
    column = column_of((TALL, WIDE))
    for pair in range(PAIRS):
        group, which = pair // 8, pair % 8
        west = turn(west_ref[group], -8 * which)
        rows = jnp.concatenate([north_ref[pair], lower_ref[pair]], axis=0)
        work_ref[pair] = jnp.where(column < 8, west, rows)
    ghosts = ghost_values(got_ref, take_ref)
    fill_ghosts(place_ref, ghosts, work_ref, TALL)

    def load(which):
        return work_ref[2 * which : 2 * which + 2].reshape(2 * TALL, WIDE)

    found = rates(load, TALL, coef_ref, diffusion_ref)
    row = iota((TALL, WIDE), 0)
    inside = (column >= 4) & (column < 12 + COLS) & (row >= 4) & (row < 12 + ROWS)
    for which in range(FIELDS):
        value = load(which) + (0.5 * TIME_STEP) * found[which]
        for half in range(2):
            part = jnp.where(inside, value[half * TALL : (half + 1) * TALL], 0.0)
            next_ref[2 * which + half] = part[8:]
            middle_ref[2 * which + half] = pltpu.roll(part, TALL - 4, 0)[:MID]
    planes = next_ref[...].reshape(PAIRS * MID, WIDE)
    packed = donor_message(planes, pick_ref[...], mix_ref[...], spin_ref[...])
    post_message(place_ref, packed, flag_ref[0:1], out_ref)


def second_kernel(
    place_ref,
    diffusion_ref,
    middle_ref,
    got_ref,
    take_ref,
    coef_ref,
    held_ref,
    whole_ref,
    third_ref,
    work_ref,
):
    work_ref[...] = middle_ref[...]
    ghosts = ghost_values(got_ref, take_ref)
    fill_ghosts(place_ref, ghosts, work_ref, MID)

    def load(which):
        return work_ref[2 * which : 2 * which + 2].reshape(2 * MID, WIDE)

    found = rates(load, MID, coef_ref, diffusion_ref)

    def centre(value):
        return pltpu.roll(value, MID - 4, 0)[:ROWS]

    def place(out_ref, pair, value):
        field, half = pair // 2, pair % 2
        out_ref[field, LOW_LEVEL[half]] = turn(value, -8)[:, :COLS]
        out_ref[field, HIGH_LEVEL[half]] = turn(value, -8 - HALF)[:, :COLS]

    for pair in range(PAIRS):
        field, half = pair // 2, pair % 2
        rate = found[field][half * MID : (half + 1) * MID]
        held = held_ref[pair]
        step = centre(rate) * (0.5 * TIME_STEP)
        middle = centre(middle_ref[pair])
        place(third_ref, pair, held + step)
        place(whole_ref, pair, held + ((middle - held) + 2.0 * step) * (1.0 / 3.0))


def shift(value, move_lat, move_lon):
    pairs = []
    for a in range(LATS):
        for b in range(LONS):
            goal_a, goal_b = a + move_lat, b + move_lon
            if 0 <= goal_a < LATS and 0 <= goal_b < LONS:
                pairs.append((a * LONS + b, goal_a * LONS + goal_b))
    return lax.ppermute(value, ("lat", "lon"), pairs)


def shards(state, donor_cell, donor_weights, donor_turn, border_source, diffusion):
    fields = state[0]
    panel = lax.axis_index("panel")
    lat = lax.axis_index("lat")
    lon = lax.axis_index("lon")
    place = jnp.stack([panel, lat, lon]).astype(jnp.int32)
    f32 = jnp.float32

    def call(kernel, outs, *args, smem=0, specs=None, scratch=(), limit=10):
        shapes = [jax.ShapeDtypeStruct(shape, dtype) for shape, dtype in outs]
        return pl.pallas_call(
            kernel,
            out_shape=shapes,
            in_specs=specs or [SMEM] * smem + [VMEM] * (len(args) - smem),
            out_specs=[VMEM] * len(outs),
            scratch_shapes=scratch,
            compiler_params=pltpu.CompilerParams(vmem_limit_bytes=limit * MIB),
        )(*args)

    bf16 = jnp.bfloat16
    south = shift(fields, -1, 0)
    held, east, corner = call(
        cut_kernel,
        [
            ((PAIRS, ROWS, WIDE), f32),
            ((2, ROWS, WIDE), f32),
            ((2, 8, WIDE), f32),
        ],
        fields,
        scratch=[pltpu.VMEM((PLANES, ROWS, WIDE), f32)],
    )
    east = shift(east, 0, -1)
    corner = shift(corner, -1, -1)

    donor = jnp.concatenate(
        [donor_cell[0, 0].astype(f32), donor_weights[0, 0, 0], donor_turn[0, 0]], axis=0
    )
    pick, mix, spin = call(
        donor_tables,
        [((3 * WIDE, 2 * WIDE), bf16), ((MID, 2 * WIDE), f32), ((2, WIDE), f32)],
        donor,
        scratch=[pltpu.VMEM((1, WIDE), f32)],
    )
    message = ((2 * PEERS, 1, MESSAGE), f32)
    lower, north, sent = call(
        donor_kernel,
        [((PAIRS, MID, WIDE), f32), ((PAIRS, 8, WIDE), f32), message],
        place,
        held,
        south,
        east,
        corner,
        pick,
        mix,
        spin,
        smem=1,
        scratch=[pltpu.VMEM((PLANES, 8, WIDE), f32)],
    )

    def to_holders(sent):
        return lax.all_to_all(sent, ("panel", "lon"), 0, 0, tiled=True)

    got = to_holders(sent)

    north, late_lat, late_lon, border, _ = lax.optimization_barrier(
        (north, lat, lon, border_source, sent)
    )
    border = lax.optimization_barrier(border[0])
    north = shift(north, 1, 0)

    ring = PANEL_COLS + 8
    row_slots = LONS * SLOTS
    bands = border[: 8 * ring].reshape(8, ring)
    sides = border[8 * ring :].reshape(PANEL_ROWS, 8)
    window = jnp.pad(bands, ((0, 0), (4, 4)), constant_values=-1)
    window = lax.dynamic_slice(window, (0, late_lon * COLS), (8, 64)).reshape(2, BAND)
    side = jnp.where(late_lon == 0, sides[:, :4], sides[:, 4:])
    side = jnp.where((late_lon == 0) | (late_lon == LONS - 1), side, -1)
    side = jnp.pad(side, ((8, 8), (0, 0)), constant_values=-1)
    side = jnp.concatenate(
        [
            side[:PANEL_ROWS].reshape(LATS, ROWS, 4),
            side[ROWS:].reshape(LATS, ROWS, 4),
        ],
        axis=1,
    ).reshape(LATS, SIDE)
    at_lat = jnp.arange(LATS)[:, None]
    band = jnp.where(at_lat == 0, window[:1], jnp.where(at_lat == LATS - 1, window[1:], -1))
    wanted = jnp.concatenate([band, side], axis=1)
    holder = jnp.where(wanted >= 0, wanted // row_slots, -1)
    local = wanted - late_lat * row_slots
    block = local // SLOTS
    slot = local % SLOTS
    spot = jnp.where(slot < PACKED, block * PACKED + slot, PEERS * PACKED + block)
    (send,) = call(
        send_kernel, [((CHOICE_DEPTH, DEPTH), bf16)], place, holder, spot, smem=1, limit=16
    )
    chunk = ((PEERS, 16, WIDE), f32)
    first_got = got
    chunks, west = call(
        widen_kernel, [chunk, ((2, TALL, WIDE), f32)], place, got, send, lower, north, smem=1
    )
    west = shift(west, 0, 1)
    late_holder, bands, sides, _ = lax.optimization_barrier((holder, bands, sides, chunks))
    take, coef = call(
        take_kernel,
        [((DEPTH, CHUNK), bf16), ((5, TALL, WIDE), f32)],
        place,
        late_holder,
        smem=1,
    )

    (flag,) = call(
        count_kernel,
        [((8, WIDE), f32)],
        jnp.pad(bands, ((0, 0), (0, 7 * WIDE - ring)), constant_values=-1),
        sides.T,
    )

    def to_blocks(chunks):
        return lax.all_to_all(chunks, "lat", 0, 0, tiled=True)

    def section_one(got):
        return call(
            first_kernel,
            [((PAIRS, MID, WIDE), f32), message],
            place,
            diffusion,
            lower,
            north,
            west,
            got,
            take,
            coef,
            pick,
            mix,
            spin,
            flag,
            smem=2,
            scratch=[pltpu.VMEM((PAIRS, TALL, WIDE), f32), pltpu.VMEM((PAIRS, MID, WIDE), f32)],
        )

    def section_two(middle, got):
        return call(
            second_kernel,
            [(fields.shape, f32), (fields.shape, f32)],
            place,
            diffusion,
            middle,
            got,
            take,
            coef,
            held,
            smem=2,
            scratch=[pltpu.VMEM((PAIRS, MID, WIDE), f32)],
        )

    middle, sent = section_one(to_blocks(chunks))
    got = to_holders(sent)
    crowded = jnp.maximum(got[0, 0, FLAG], got[PEERS, 0, FLAG]) > ROOM
    (chunks,) = call(choice_kernel, [chunk], place, got, send, smem=1)
    fitting = section_two(middle, to_blocks(chunks))

    def with_room():
        def dense(got):
            chunks = call(
                dense_kernel,
                [((PEERS, PLANES, CHUNK), f32)],
                place,
                got,
                holder,
                spot,
                smem=1,
                limit=16,
            )
            return to_blocks(chunks[0]).sum(axis=0)

        middle, sent = section_one(dense(first_got))
        return section_two(middle, dense(to_holders(sent)))

    accumulated, section_three = lax.cond(crowded, with_room, lambda: fitting)
    return (accumulated[None], section_three[None])


def solution(mesh):
    return jax.shard_map(
        shards,
        mesh=mesh,
        in_specs=(
            P("panel", None, None, "lat", "lon"),
            P("panel", "lat", "lon", None),
            P("panel", "lat", "lon", None, None),
            P("panel", "lat", "lon", None),
            P("panel", None),
            P(),
        ),
        out_specs=(P("panel", None, None, "lat", "lon"), P("panel", None, None, "lat", "lon")),
        check_vma=False,
    )
```

```python
import math

import jax
import jax.numpy as jnp
from jax import lax
from jax.experimental import pallas as pl
from jax.experimental.pallas import tpu as pltpu
from jax.sharding import PartitionSpec as P

GAMMA = 5.0 / 3.0
RADIAL_STEP = 0.65 / 32.0
FIELDS = 8
LEVELS = 4
PLANES = FIELDS * LEVELS
PAIRS = PLANES // 2
LOW_LEVEL = (0, 1)
HIGH_LEVEL = (3, 2)
ROWS = 16
COLS = 48
SLOTS = 33
LATS = 16
LONS = 16
ROOM = 63
WIDE = 128
HALF = 64
TALL = ROWS + 16
MID = ROWS + 8
BAND = 4 * HALF
SIDE = 4 * TALL
CHUNK = BAND + SIDE
PEERS = 16
PACKED = 32
MESSAGE = 9 * WIDE
TAIL = 8 * WIDE
FLAG = TAIL + HALF - 1
CHOICE_TILES = PEERS * PACKED // WIDE
CHOICE_DEPTH = (CHOICE_TILES + 1) * WIDE
DEPTH = PEERS * HALF
PANEL_ROWS = ROWS * LATS
PANEL_COLS = COLS * LONS
DTHETA = 0.5 * math.pi / PANEL_ROWS
DPHI = 1.5 * math.pi / PANEL_COLS
FINEST = min(DTHETA, DPHI)
TIME_STEP = 0.1 * FINEST
RADII = [0.35 + 0.65 * (k + 16 - LEVELS // 2 + 0.5) / 32.0 for k in range(LEVELS)]
VMEM = pl.BlockSpec(memory_space=pltpu.VMEM)
SMEM = pl.BlockSpec(memory_space=pltpu.SMEM)
MIB = 1024 * 1024


def iota(shape, axis):
    return lax.broadcasted_iota(jnp.int32, shape, axis)


def column_of(shape):
    return iota(shape, len(shape) - 1) & (HALF - 1)


def turn(value, lanes):
    return pltpu.roll(value, lanes % WIDE, 1) if lanes % WIDE else value


def three_parts(value):
    parts = []
    for _ in range(3):
        part = value.astype(jnp.bfloat16)
        value = value - part.astype(jnp.float32)
        parts.append(part)
    return parts


def donor_message(planes, pick, mix, spin):
    parts = jnp.concatenate(three_parts(planes), axis=1)
    chosen = jnp.dot(parts, pick, preferred_element_type=jnp.float32)
    chosen = chosen.reshape(PAIRS, MID, 2 * WIDE)
    both = jnp.sum(chosen * mix[None], axis=1)
    both = jnp.concatenate([both[:, :WIDE], both[:, WIDE:]], axis=0)
    mixed = both + pltpu.roll(both, HALF, 1)
    cosine = spin[0:1]
    sine = spin[1:2]
    at = (iota((PLANES, WIDE), 0) & (PAIRS - 1)) // 2
    theta = (at == 2) | (at == 5)
    phi = (at == 3) | (at == 6)
    other = jnp.where(theta, pltpu.roll(mixed, PLANES - 2, 0), -pltpu.roll(mixed, 2, 0))
    turned = jnp.where(theta | phi, cosine * mixed + sine * other, mixed)
    return jnp.where(iota((PAIRS, WIDE), 1) < HALF, turned[:PAIRS], turned[PAIRS:])


def post_message(place_ref, packed, flag, out_ref):
    panel = place_ref[0]
    lane = iota((16, WIDE), 1)
    column = lane & (HALF - 1)
    dense = jnp.where(column[:8] < PACKED, packed[:8], turn(packed[8:], PACKED))
    last = jnp.where(
        lane < HALF, packed[:, PACKED : PACKED + 1], packed[:, HALF + PACKED : HALF + PACKED + 1]
    )
    tail = jnp.sum(jnp.where(column == iota((16, WIDE), 0), last, 0.0), axis=0, keepdims=True)
    blank = jnp.where(lane[:1] == FLAG - TAIL, flag, 0.0)
    tail = jnp.where(lane[:1] == FLAG - TAIL, flag, tail)
    zero = jnp.zeros((1, WIDE), jnp.float32)
    for row in range(9):
        full = dense[row : row + 1] if row < 8 else tail
        empty = zero if row < 8 else blank
        at = slice(row * WIDE, (row + 1) * WIDE)
        out_ref[pl.ds((1 - panel) * PEERS, PEERS), :, at] = jnp.broadcast_to(
            full[None], (PEERS, 1, WIDE)
        )
        out_ref[pl.ds(panel * PEERS, PEERS), :, at] = jnp.broadcast_to(
            empty[None], (PEERS, 1, WIDE)
        )


def cut_kernel(
    state_ref, border_ref, held_ref, south_ref, east_ref, corner_ref, later_ref, plane_ref
):
    later_ref[...] = border_ref[...]
    for plane in range(PLANES):
        plane_ref[plane, :, :COLS] = state_ref[plane // LEVELS, plane % LEVELS]
    lane = iota((ROWS, WIDE), 1)
    column = column_of((ROWS, WIDE))
    own = (column >= 8) & (column < 8 + COLS)
    for pair in range(PAIRS):
        field, which = pair // 2, pair % 2
        low = turn(plane_ref[field * LEVELS + LOW_LEVEL[which]], 8)
        high = turn(plane_ref[field * LEVELS + HIGH_LEVEL[which]], HALF + 8)
        tile = jnp.where(own, jnp.where(lane < HALF, low, high), 0.0)
        held_ref[pair] = tile
        south_ref[pair] = tile[:8]
    for group in range(2):
        columns = jnp.zeros((ROWS, WIDE), jnp.float32)
        for which in range(8):
            moved = turn(held_ref[8 * group + which], 8 * which - 8)
            columns = jnp.where(column // 8 == which, moved, columns)
        east_ref[group] = columns
        corner_ref[group] = columns[:8]


def donor_tables(donor_ref, pick_ref, mix_ref, spin_ref, line_ref):
    late = iota((1, WIDE), 1) >= HALF

    def twice(value, fill):
        line_ref[...] = jnp.full((1, WIDE), fill, jnp.float32)
        line_ref[:, :SLOTS] = value
        line = line_ref[...]
        return jnp.where(late, pltpu.roll(line, HALF, 1), line)

    cell = twice(donor_ref[0:1], -10.0 * COLS)
    row_at = jnp.floor((cell + 0.5) * (1.0 / COLS))
    col_at = cell - row_at * COLS + jnp.where(late, 1.0, 0.0)
    upper = jnp.where(late, twice(donor_ref[2:3], 0.0), twice(donor_ref[1:2], 0.0))
    lower = jnp.where(late, twice(donor_ref[4:5], 0.0), twice(donor_ref[3:4], 0.0))
    angle = twice(donor_ref[5:6], 0.0)
    spin_ref[0:1] = jnp.cos(angle)
    spin_ref[1:2] = jnp.sin(angle)
    lane = iota((WIDE, WIDE), 0).astype(jnp.float32)
    real = jnp.where(row_at >= 0, col_at + 8.0, -1000.0)
    low = jnp.where(lane == real, 1.0, 0.0).astype(jnp.bfloat16)
    high = jnp.where(lane == real + HALF, 1.0, 0.0).astype(jnp.bfloat16)
    for part in range(3):
        pick_ref[part * WIDE : (part + 1) * WIDE, :WIDE] = low
        pick_ref[part * WIDE : (part + 1) * WIDE, WIDE:] = high
    row = iota((MID, WIDE), 0).astype(jnp.float32)
    mix = jnp.where(row == row_at, upper, 0.0) + jnp.where(row == row_at + 1.0, lower, 0.0)
    mix_ref[:, :WIDE] = mix
    mix_ref[:, WIDE:] = mix


def count_kernel(bands_ref, sides_ref, flag_ref):
    width = bands_ref.shape[1]
    column = iota((width, WIDE), 0) - 4
    start = iota((width, WIDE), 1) * COLS - 8
    within = (column >= start) & (column < start + 64) & (start < PANEL_COLS)
    columns = jnp.where(within, 1.0, 0.0).astype(jnp.bfloat16)
    row = iota((PANEL_ROWS, WIDE), 0)
    start = iota((PANEL_ROWS, WIDE), 1) * ROWS - 8
    within = (row >= start) & (row < start + TALL) & (start < PANEL_ROWS)
    rows = jnp.where(within, 1.0, 0.0).astype(jnp.bfloat16)

    def most(slots, windows):
        ones = []
        for which in range(LATS):
            first = which * LONS * SLOTS
            inside = (slots >= first) & (slots < first + LONS * SLOTS)
            ones.append(jnp.where(inside, 1.0, 0.0))
        ones = jnp.concatenate(ones, axis=0).astype(jnp.bfloat16)
        counts = jnp.dot(ones, windows, preferred_element_type=jnp.float32)
        return jnp.max(jnp.sum(counts.reshape(2 * LATS, 4, WIDE), axis=1))

    total = most(bands_ref[...], columns) + most(sides_ref[...], rows)
    flag_ref[...] = jnp.full(flag_ref.shape, total, jnp.float32)


def donor_kernel(
    place_ref, held_ref, south_ref, east_ref, corner_ref, pick_ref, mix_ref, spin_ref,
    lower_ref, north_ref, out_ref
):
    column = column_of((ROWS, WIDE))
    beyond = column >= 8 + COLS
    for pair in range(PAIRS):
        group, which = pair // 8, pair % 8
        east = turn(east_ref[group], 8 + COLS - 8 * which)
        corner = turn(corner_ref[group], 8 + COLS - 8 * which)
        lower_ref[pair, :ROWS] = jnp.where(beyond, east, held_ref[pair])
        lower_ref[pair, ROWS:] = jnp.where(beyond[:8], corner, south_ref[pair])
        north_ref[pair] = lower_ref[pair, 8:16]
    planes = lower_ref[...].reshape(PAIRS * MID, WIDE)
    packed = donor_message(planes, pick_ref[...], mix_ref[...], spin_ref[...])
    post_message(place_ref, packed, jnp.zeros((1, WIDE), jnp.float32), out_ref)


def split_parts(held):
    return jnp.concatenate(three_parts(held), axis=0)


def join_parts(terms):
    return terms[:PLANES] + terms[PLANES : 2 * PLANES] + terms[2 * PLANES :]


def from_row(place_ref, got_ref):
    base = (1 - place_ref[0]) * PEERS
    part = iota((8, WIDE), 1) // PACKED
    tiles = []
    tails = []
    for tile in range(CHOICE_TILES):
        rows = [jnp.zeros((8, WIDE), jnp.float32)] * 4
        for which in range(4):
            at = base + 4 * tile + which
            message = jnp.concatenate(
                [got_ref[at, :, row * WIDE : (row + 1) * WIDE] for row in range(8)], axis=0
            )
            tails.append(got_ref[at, :, TAIL:])
            for group in range(4):
                moved = turn(message, PACKED * (which - group))
                rows[group] = jnp.where(part == which, moved, rows[group])
        tiles.append(jnp.concatenate(rows, axis=0))
    tails.append(jnp.zeros((WIDE - PEERS, WIDE), jnp.float32))
    tails = jnp.concatenate(tails, axis=0).T
    tiles.append(jnp.concatenate([tails[:PAIRS], tails[HALF : HALF + PAIRS]], axis=0))
    return split_parts(jnp.concatenate(tiles, axis=1))


def rank_of(chosen):
    order = iota((CHUNK, CHUNK), 0) < iota((CHUNK, CHUNK), 1)
    order = jnp.where(order, 1.0, 0.0).astype(jnp.bfloat16)
    ones = jnp.where(chosen, 1.0, 0.0).astype(jnp.bfloat16)
    return jnp.dot(ones, order, preferred_element_type=jnp.float32)


def send_kernel(place_ref, holder_ref, spot_ref, send_ref):
    mine = holder_ref[...] == place_ref[1]
    spot = spot_ref[...].astype(jnp.float32)
    rank = rank_of(mine)
    key = jnp.where(mine & (rank < ROOM), rank, -1.0)
    place_at = iota((HALF, CHUNK), 0).astype(jnp.float32)
    eye = iota((WIDE, WIDE), 0) == iota((WIDE, WIDE), 1)
    depth = iota((CHOICE_DEPTH, WIDE), 0).astype(jnp.float32) + 1.0
    for pair in range(LATS // 2):
        tables = []
        for block in (2 * pair, 2 * pair + 1):
            found = place_at == key[block : block + 1]
            tables.append(
                jnp.sum(jnp.where(found, spot[block : block + 1] + 1.0, 0.0), axis=1, keepdims=True)
            )
        table = jnp.concatenate(tables, axis=0)
        line = jnp.sum(jnp.where(eye, table, 0.0), axis=0, keepdims=True)
        hot = jnp.where(depth == line, 1.0, 0.0).astype(jnp.bfloat16)
        send_ref[:, pair * WIDE : (pair + 1) * WIDE] = hot


def take_kernel(place_ref, holder_ref, take_ref, coef_ref):
    lat = place_ref[1]
    own = holder_ref[pl.ds(lat, 1)]
    masks = iota((PEERS, CHUNK), 0) == own
    rank = jnp.sum(jnp.where(masks, rank_of(masks), 0.0), axis=0, keepdims=True)
    fits = (own >= 0) & (rank < ROOM)
    index = jnp.where(fits, own.astype(jnp.float32) * HALF + rank, -1.0)
    hot = iota((DEPTH, CHUNK), 0).astype(jnp.float32) == index
    take_ref[...] = jnp.where(hot, 1.0, 0.0).astype(jnp.bfloat16)
    row = (lat * ROWS - 8 + iota((TALL, WIDE), 0)).astype(jnp.float32)
    column = (place_ref[2] * COLS - 8 + column_of((TALL, WIDE))).astype(jnp.float32)
    colatitude = 0.25 * math.pi + (row + 0.5) * DTHETA
    longitude = -0.75 * math.pi + (column + 0.5) * DPHI
    sine, cosine = jnp.sin(colatitude), jnp.cos(colatitude)
    twirl = 2.0 * 0.25 / TIME_STEP
    yang = place_ref[0] == 1
    coef_ref[0] = sine
    coef_ref[1] = 1.0 / sine
    coef_ref[2] = twirl * jnp.where(yang, sine * jnp.sin(longitude), cosine)
    coef_ref[3] = twirl * jnp.where(yang, cosine * jnp.sin(longitude), -sine)
    coef_ref[4] = twirl * jnp.where(yang, jnp.cos(longitude), 0.0)


def widen_kernel(place_ref, got_ref, send_ref, lower_ref, north_ref, out_ref, west_ref):
    column = column_of((TALL, WIDE))
    for group in range(2):
        columns = jnp.zeros((TALL, WIDE), jnp.float32)
        for which in range(8):
            pair = 8 * group + which
            rows = jnp.concatenate([north_ref[pair], lower_ref[pair]], axis=0)
            moved = turn(rows, 8 * which - COLS)
            columns = jnp.where(column // 8 == which, moved, columns)
        west_ref[group] = columns
    choice_kernel(place_ref, got_ref, send_ref, out_ref)


def choice_kernel(place_ref, got_ref, send_ref, out_ref):
    parts = from_row(place_ref, got_ref)
    terms = jnp.dot(parts, send_ref[...], preferred_element_type=jnp.float32)
    chosen = join_parts(terms)
    low = iota((16, WIDE), 1) < HALF
    for pair in range(PEERS // 2):
        tile = chosen[:, pair * WIDE : (pair + 1) * WIDE]
        top, end = tile[:16], tile[16:]
        out_ref[2 * pair] = jnp.where(low, top, pltpu.roll(end, HALF, 1))
        out_ref[2 * pair + 1] = jnp.where(low, pltpu.roll(top, HALF, 1), end)


def dense_kernel(place_ref, got_ref, holder_ref, spot_ref, out_ref):
    parts = from_row(place_ref, got_ref)
    index = jnp.where(holder_ref[...] == place_ref[1], spot_ref[...], -1)
    at = iota((CHOICE_DEPTH, CHUNK), 0)
    for block in range(LATS):
        hot = jnp.where(at == index[block : block + 1], 1.0, 0.0).astype(jnp.bfloat16)
        out_ref[block] = join_parts(jnp.dot(parts, hot, preferred_element_type=jnp.float32))


def ghost_values(got_ref, take_ref):
    if len(got_ref.shape) == 2:
        return got_ref[...]
    low = iota((16, WIDE), 1) < HALF
    tiles = []
    for pair in range(PEERS // 2):
        one = got_ref[2 * pair]
        two = got_ref[2 * pair + 1]
        top = jnp.where(low, one, pltpu.roll(two, HALF, 1))
        end = jnp.where(low, pltpu.roll(one, HALF, 1), two)
        tiles.append(jnp.concatenate([top, end], axis=0))
    parts = split_parts(jnp.concatenate(tiles, axis=1))
    return join_parts(jnp.dot(parts, take_ref[...], preferred_element_type=jnp.float32))


def fill_ghosts(place_ref, ghosts, work_ref, rows):
    lat, lon = place_ref[1], place_ref[2]
    trim = (TALL - rows) // 2
    top = 8 - trim
    half = PLANES // 2

    @pl.when((lon == 0) | (lon == LONS - 1))
    def _():
        side = ghosts[:, BAND:]
        first = jnp.where(lon == 0, 4, 8 + COLS)
        own = iota((rows, WIDE), 1) // 4 == iota((rows, WIDE), 0) + trim

        def spread(part):
            part = part.astype(jnp.float32)[:, None, :]
            return jnp.where(own[None], part, 0.0).astype(jnp.bfloat16).reshape(PAIRS * rows, WIDE)

        pieces = []
        for part in three_parts(side):
            pieces += [spread(part[:half]), spread(part[half:])]
        both = jnp.concatenate(pieces, axis=1)
        source = iota((6 * WIDE, WIDE), 0)
        target = first + (source & 3) + jnp.where((source & WIDE) != 0, HALF, 0)
        hot = jnp.where(target == iota((6 * WIDE, WIDE), 1), 1.0, 0.0).astype(jnp.bfloat16)
        moved = jnp.dot(both, hot, preferred_element_type=jnp.float32)
        moved = moved.reshape(PAIRS, rows, WIDE)
        column = column_of((rows, WIDE))
        ghost = (column >= first) & (column < first + 4)
        work_ref[...] = jnp.where(ghost[None], moved, work_ref[...])

    @pl.when((lat == 0) | (lat == LATS - 1))
    def _():
        low = iota((half, WIDE), 1) < HALF
        lines = []
        for which in range(2):
            piece = ghosts[:, which * WIDE : (which + 1) * WIDE]
            one, two = piece[:half], piece[half:]
            lines.append(jnp.where(low, one, pltpu.roll(two, HALF, 1)))
            lines.append(jnp.where(low, pltpu.roll(one, HALF, 1), two))

        @pl.when(lat == 0)
        def _():
            for row in range(4):
                work_ref[:, top - 4 + row, :] = lines[row]

        @pl.when(lat == LATS - 1)
        def _():
            for row in range(4):
                work_ref[:, top + ROWS + row, :] = lines[row]


def rates(load, rows, coef_ref, diffusion_ref):
    low = iota((rows, WIDE), 1) < HALF

    def levels(values):
        halves = [
            jnp.where(low, values[LOW_LEVEL[k]], values[HIGH_LEVEL[k]]).astype(jnp.float32)
            for k in range(2)
        ]
        return jnp.concatenate(halves, axis=0)

    def whole(which):
        value = coef_ref[which]
        if rows < TALL:
            value = pltpu.roll(value, TALL - (TALL - rows) // 2, 0)[:rows]
        return jnp.concatenate([value] * 2, axis=0)

    sine = whole(0)
    per_sine = whole(1)
    radius = levels(RADII)
    inverse = levels([1.0 / r for r in RADII])
    square = levels([r * r for r in RADII])
    per_square = levels([1.0 / (r * r) for r in RADII])
    sign = jnp.where(low, 1.0, -1.0)
    ends = sign * (1.0 / RADIAL_STEP)
    inner = sign * (1.0 / (2.0 * RADIAL_STEP))
    viscosity = diffusion_ref[0] * (FINEST * FINEST / TIME_STEP)
    resistivity = diffusion_ref[1] * (FINEST * FINEST / TIME_STEP)

    def slope(value, axis, step):
        size = value.shape[axis]
        near = pltpu.roll(value, size - 1, axis) - pltpu.roll(value, 1, axis)
        far = pltpu.roll(value, size - 2, axis) - pltpu.roll(value, 2, axis)
        return near * (8.0 / (12.0 * step)) - far * (1.0 / (12.0 * step))

    def d_theta(value):
        return slope(value, 0, DTHETA)

    def d_phi(value):
        return slope(value, 1, DPHI)

    def d_radius(value):
        one, two = value[:rows], value[rows:]
        return jnp.concatenate(
            [(two - one) * ends, (pltpu.roll(two, HALF, 1) - one) * inner], axis=0
        )

    def by_radius(value):
        return value * radius

    def per_radius(value):
        return value * inverse

    def curl(vector):
        part_r, part_t, part_p = vector
        return (
            per_radius((d_theta(sine * part_p) - d_phi(part_t)) * per_sine),
            per_radius(d_phi(part_r) * per_sine - d_radius(by_radius(part_p))),
            per_radius(d_radius(by_radius(part_t)) - d_theta(part_r)),
        )

    def gradient(value):
        return (
            d_radius(value),
            per_radius(d_theta(value)),
            per_radius(d_phi(value) * per_sine),
        )

    def cross(left, right):
        return (
            left[1] * right[2] - left[2] * right[1],
            left[2] * right[0] - left[0] * right[2],
            left[0] * right[1] - left[1] * right[0],
        )

    def advect(vector, slopes):
        return vector[0] * slopes[0] + vector[1] * slopes[1] + vector[2] * slopes[2]

    velocity = [load(which) for which in (1, 2, 3)]
    magnetic = [load(which) for which in (4, 5, 6)]
    vorticity = curl(velocity)
    current = curl(magnetic)
    spread = d_radius(square * velocity[0]) * per_square + per_radius(
        (d_theta(sine * velocity[1]) + d_phi(velocity[2])) * per_sine
    )
    induced = cross(velocity, magnetic)
    electric = [induced[k] - resistivity * current[k] for k in range(3)]
    kinetic = 0.5 * (
        velocity[0] * velocity[0] + velocity[1] * velocity[1] + velocity[2] * velocity[2]
    )
    curl_electric = curl(electric)
    log_rho = load(0)
    rho_rate = -advect(velocity, gradient(log_rho)) - spread
    pressure = load(7)
    slope_pressure = gradient(pressure)
    pressure_rate = -advect(velocity, slope_pressure) - GAMMA * pressure * spread
    lorentz = cross(current, magnetic)
    per_rho = jnp.exp(-log_rho)
    slope_kinetic = gradient(kinetic)
    curl_vorticity = curl(vorticity)
    lamb = cross(velocity, vorticity)
    turning = cross((whole(2), whole(3), whole(4)), velocity)
    momentum = [
        lamb[k]
        - slope_kinetic[k]
        + per_rho * (lorentz[k] - slope_pressure[k])
        - turning[k]
        - viscosity * curl_vorticity[k]
        for k in range(3)
    ]
    return [rho_rate, *momentum, *curl_electric, pressure_rate]


def first_kernel(
    place_ref,
    diffusion_ref,
    lower_ref,
    north_ref,
    west_ref,
    got_ref,
    take_ref,
    coef_ref,
    pick_ref,
    mix_ref,
    spin_ref,
    flag_ref,
    middle_ref,
    out_ref,
    work_ref,
    next_ref,
):
    column = column_of((TALL, WIDE))
    for pair in range(PAIRS):
        group, which = pair // 8, pair % 8
        west = turn(west_ref[group], -8 * which)
        rows = jnp.concatenate([north_ref[pair], lower_ref[pair]], axis=0)
        work_ref[pair] = jnp.where(column < 8, west, rows)
    ghosts = ghost_values(got_ref, take_ref)
    fill_ghosts(place_ref, ghosts, work_ref, TALL)

    def load(which):
        return work_ref[2 * which : 2 * which + 2].reshape(2 * TALL, WIDE)

    found = rates(load, TALL, coef_ref, diffusion_ref)
    row = iota((TALL, WIDE), 0)
    inside = (column >= 4) & (column < 12 + COLS) & (row >= 4) & (row < 12 + ROWS)
    for which in range(FIELDS):
        value = load(which) + (0.5 * TIME_STEP) * found[which]
        for half in range(2):
            part = jnp.where(inside, value[half * TALL : (half + 1) * TALL], 0.0)
            next_ref[2 * which + half] = part[8:]
            middle_ref[2 * which + half] = pltpu.roll(part, TALL - 4, 0)[:MID]
    planes = next_ref[...].reshape(PAIRS * MID, WIDE)
    packed = donor_message(planes, pick_ref[...], mix_ref[...], spin_ref[...])
    post_message(place_ref, packed, flag_ref[0:1], out_ref)


def second_kernel(
    place_ref,
    diffusion_ref,
    middle_ref,
    got_ref,
    take_ref,
    coef_ref,
    held_ref,
    whole_ref,
    third_ref,
    work_ref,
):
    work_ref[...] = middle_ref[...]
    ghosts = ghost_values(got_ref, take_ref)
    fill_ghosts(place_ref, ghosts, work_ref, MID)

    def load(which):
        return work_ref[2 * which : 2 * which + 2].reshape(2 * MID, WIDE)

    found = rates(load, MID, coef_ref, diffusion_ref)

    def centre(value):
        return pltpu.roll(value, MID - 4, 0)[:ROWS]

    def place(out_ref, pair, value):
        field, half = pair // 2, pair % 2
        out_ref[field, LOW_LEVEL[half]] = turn(value, -8)[:, :COLS]
        out_ref[field, HIGH_LEVEL[half]] = turn(value, -8 - HALF)[:, :COLS]

    for pair in range(PAIRS):
        field, half = pair // 2, pair % 2
        rate = found[field][half * MID : (half + 1) * MID]
        held = held_ref[pair]
        step = centre(rate) * (0.5 * TIME_STEP)
        middle = centre(middle_ref[pair])
        place(third_ref, pair, held + step)
        place(whole_ref, pair, held + ((middle - held) + 2.0 * step) * (1.0 / 3.0))


def shift(value, move_lat, move_lon):
    pairs = []
    for a in range(LATS):
        for b in range(LONS):
            goal_a, goal_b = a + move_lat, b + move_lon
            if 0 <= goal_a < LATS and 0 <= goal_b < LONS:
                pairs.append((a * LONS + b, goal_a * LONS + goal_b))
    return lax.ppermute(value, ("lat", "lon"), pairs)


def shards(state, donor_cell, donor_weights, donor_turn, border_source, diffusion):
    fields = state[0]
    panel = lax.axis_index("panel")
    lat = lax.axis_index("lat")
    lon = lax.axis_index("lon")
    place = jnp.stack([panel, lat, lon]).astype(jnp.int32)
    f32 = jnp.float32

    def call(kernel, outs, *args, smem=0, specs=None, scratch=(), limit=10):
        shapes = [jax.ShapeDtypeStruct(shape, dtype) for shape, dtype in outs]
        return pl.pallas_call(
            kernel,
            out_shape=shapes,
            in_specs=specs or [SMEM] * smem + [VMEM] * (len(args) - smem),
            out_specs=[VMEM] * len(outs),
            scratch_shapes=scratch,
            compiler_params=pltpu.CompilerParams(vmem_limit_bytes=limit * MIB),
        )(*args)

    bf16 = jnp.bfloat16
    border = border_source[0]
    held, south, east, corner, border = call(
        cut_kernel,
        [
            ((PAIRS, ROWS, WIDE), f32),
            ((PAIRS, 8, WIDE), f32),
            ((2, ROWS, WIDE), f32),
            ((2, 8, WIDE), f32),
            (border.shape, border.dtype),
        ],
        fields,
        border,
        scratch=[pltpu.VMEM((PLANES, ROWS, WIDE), f32)],
    )
    south = shift(south, -1, 0)
    east = shift(east, 0, -1)
    corner = shift(corner, -1, -1)

    donor = jnp.concatenate(
        [donor_cell[0, 0].astype(f32), donor_weights[0, 0, 0], donor_turn[0, 0]], axis=0
    )
    pick, mix, spin = call(
        donor_tables,
        [((3 * WIDE, 2 * WIDE), bf16), ((MID, 2 * WIDE), f32), ((2, WIDE), f32)],
        donor,
        scratch=[pltpu.VMEM((1, WIDE), f32)],
    )
    message = ((2 * PEERS, 1, MESSAGE), f32)
    lower, north, sent = call(
        donor_kernel,
        [((PAIRS, MID, WIDE), f32), ((PAIRS, 8, WIDE), f32), message],
        place,
        held,
        south,
        east,
        corner,
        pick,
        mix,
        spin,
        smem=1,
    )

    def to_holders(sent):
        return lax.all_to_all(sent, ("panel", "lon"), 0, 0, tiled=True)

    got = to_holders(sent)

    north, late_lat, late_lon, border, _ = lax.optimization_barrier(
        (north, lat, lon, border, sent)
    )
    north = shift(north, 1, 0)

    ring = PANEL_COLS + 8
    row_slots = LONS * SLOTS
    bands = border[: 8 * ring].reshape(8, ring)
    sides = border[8 * ring :].reshape(PANEL_ROWS, 8)
    window = jnp.pad(bands, ((0, 0), (4, 4)), constant_values=-1)
    window = lax.dynamic_slice(window, (0, late_lon * COLS), (8, 64)).reshape(2, BAND)
    side = jnp.where(late_lon == 0, sides[:, :4], sides[:, 4:])
    side = jnp.where((late_lon == 0) | (late_lon == LONS - 1), side, -1)
    side = jnp.pad(side, ((8, 8), (0, 0)), constant_values=-1)
    side = jnp.concatenate(
        [
            side[:PANEL_ROWS].reshape(LATS, ROWS, 4),
            side[ROWS:].reshape(LATS, ROWS, 4),
        ],
        axis=1,
    ).reshape(LATS, SIDE)
    at_lat = jnp.arange(LATS)[:, None]
    band = jnp.where(at_lat == 0, window[:1], jnp.where(at_lat == LATS - 1, window[1:], -1))
    wanted = jnp.concatenate([band, side], axis=1)
    holder = jnp.where(wanted >= 0, wanted // row_slots, -1)
    local = wanted - late_lat * row_slots
    block = local // SLOTS
    slot = local % SLOTS
    spot = jnp.where(slot < PACKED, block * PACKED + slot, PEERS * PACKED + block)
    (send,) = call(
        send_kernel, [((CHOICE_DEPTH, DEPTH), bf16)], place, holder, spot, smem=1, limit=16
    )
    chunk = ((PEERS, 16, WIDE), f32)
    first_got = got
    chunks, west = call(
        widen_kernel, [chunk, ((2, TALL, WIDE), f32)], place, got, send, lower, north, smem=1
    )
    west = shift(west, 0, 1)
    late_holder, bands, sides, _ = lax.optimization_barrier((holder, bands, sides, chunks))
    take, coef = call(
        take_kernel,
        [((DEPTH, CHUNK), bf16), ((5, TALL, WIDE), f32)],
        place,
        late_holder,
        smem=1,
    )

    (flag,) = call(
        count_kernel,
        [((8, WIDE), f32)],
        jnp.pad(bands, ((0, 0), (0, 7 * WIDE - ring)), constant_values=-1),
        sides.T,
    )

    def to_blocks(chunks):
        return lax.all_to_all(chunks, "lat", 0, 0, tiled=True)

    def section_one(got):
        return call(
            first_kernel,
            [((PAIRS, MID, WIDE), f32), message],
            place,
            diffusion,
            lower,
            north,
            west,
            got,
            take,
            coef,
            pick,
            mix,
            spin,
            flag,
            smem=2,
            scratch=[pltpu.VMEM((PAIRS, TALL, WIDE), f32), pltpu.VMEM((PAIRS, MID, WIDE), f32)],
        )

    def section_two(middle, got):
        return call(
            second_kernel,
            [(fields.shape, f32), (fields.shape, f32)],
            place,
            diffusion,
            middle,
            got,
            take,
            coef,
            held,
            smem=2,
            scratch=[pltpu.VMEM((PAIRS, MID, WIDE), f32)],
        )

    middle, sent = section_one(to_blocks(chunks))
    got = to_holders(sent)
    crowded = jnp.maximum(got[0, 0, FLAG], got[PEERS, 0, FLAG]) > ROOM
    (chunks,) = call(choice_kernel, [chunk], place, got, send, smem=1)
    fitting = section_two(middle, to_blocks(chunks))

    def with_room():
        def dense(got):
            chunks = call(
                dense_kernel,
                [((PEERS, PLANES, CHUNK), f32)],
                place,
                got,
                holder,
                spot,
                smem=1,
                limit=16,
            )
            return to_blocks(chunks[0]).sum(axis=0)

        middle, sent = section_one(dense(first_got))
        return section_two(middle, dense(to_holders(sent)))

    accumulated, section_three = lax.cond(crowded, with_room, lambda: fitting)
    return (accumulated[None], section_three[None])


def solution(mesh):
    return jax.shard_map(
        shards,
        mesh=mesh,
        in_specs=(
            P("panel", None, None, "lat", "lon"),
            P("panel", "lat", "lon", None),
            P("panel", "lat", "lon", None, None),
            P("panel", "lat", "lon", None),
            P("panel", None),
            P(),
        ),
        out_specs=(P("panel", None, None, "lat", "lon"), P("panel", None, None, "lat", "lon")),
        check_vma=False,
    )
```

```python
import math

import jax
import jax.numpy as jnp
from jax import lax
from jax.experimental import pallas as pl
from jax.experimental.pallas import tpu as pltpu
from jax.sharding import PartitionSpec as P

GAMMA = 5.0 / 3.0
RADIAL_STEP = 0.65 / 32.0
FIELDS = 8
LEVELS = 4
PLANES = FIELDS * LEVELS
PAIRS = PLANES // 2
LOW_LEVEL = (0, 1)
HIGH_LEVEL = (3, 2)
ROWS = 16
COLS = 48
SLOTS = 33
LATS = 16
LONS = 16
ROOM = 63
WIDE = 128
HALF = 64
TALL = ROWS + 16
MID = ROWS + 8
BAND = 4 * HALF
SIDE = 4 * TALL
CHUNK = BAND + SIDE
PEERS = 16
PACKED = 32
MESSAGE = 9 * WIDE
TAIL = 8 * WIDE
FLAG = TAIL + HALF - 1
CHOICE_TILES = PEERS * PACKED // WIDE
CHOICE_DEPTH = (CHOICE_TILES + 1) * WIDE
DEPTH = PEERS * HALF
PANEL_ROWS = ROWS * LATS
PANEL_COLS = COLS * LONS
DTHETA = 0.5 * math.pi / PANEL_ROWS
DPHI = 1.5 * math.pi / PANEL_COLS
FINEST = min(DTHETA, DPHI)
TIME_STEP = 0.1 * FINEST
RADII = [0.35 + 0.65 * (k + 16 - LEVELS // 2 + 0.5) / 32.0 for k in range(LEVELS)]
VMEM = pl.BlockSpec(memory_space=pltpu.VMEM)
SMEM = pl.BlockSpec(memory_space=pltpu.SMEM)
MIB = 1024 * 1024


def iota(shape, axis):
    return lax.broadcasted_iota(jnp.int32, shape, axis)


def column_of(shape):
    return iota(shape, len(shape) - 1) & (HALF - 1)


def turn(value, lanes):
    return pltpu.roll(value, lanes % WIDE, 1) if lanes % WIDE else value


def three_parts(value):
    parts = []
    for _ in range(3):
        part = value.astype(jnp.bfloat16)
        value = value - part.astype(jnp.float32)
        parts.append(part)
    return parts


def donor_message(planes, pick, mix, spin):
    parts = jnp.concatenate(three_parts(planes), axis=1)
    chosen = jnp.dot(parts, pick, preferred_element_type=jnp.float32)
    chosen = chosen.reshape(PAIRS, MID, 2 * WIDE)
    both = jnp.sum(chosen * mix[None], axis=1)
    both = jnp.concatenate([both[:, :WIDE], both[:, WIDE:]], axis=0)
    mixed = both + pltpu.roll(both, HALF, 1)
    cosine = spin[0:1]
    sine = spin[1:2]
    at = (iota((PLANES, WIDE), 0) & (PAIRS - 1)) // 2
    theta = (at == 2) | (at == 5)
    phi = (at == 3) | (at == 6)
    other = jnp.where(theta, pltpu.roll(mixed, PLANES - 2, 0), -pltpu.roll(mixed, 2, 0))
    turned = jnp.where(theta | phi, cosine * mixed + sine * other, mixed)
    return jnp.where(iota((PAIRS, WIDE), 1) < HALF, turned[:PAIRS], turned[PAIRS:])


def post_message(place_ref, packed, flag, out_ref):
    panel = place_ref[0]
    lane = iota((16, WIDE), 1)
    column = lane & (HALF - 1)
    dense = jnp.where(column[:8] < PACKED, packed[:8], turn(packed[8:], PACKED))
    last = jnp.where(
        lane < HALF, packed[:, PACKED : PACKED + 1], packed[:, HALF + PACKED : HALF + PACKED + 1]
    )
    tail = jnp.sum(jnp.where(column == iota((16, WIDE), 0), last, 0.0), axis=0, keepdims=True)
    blank = jnp.where(lane[:1] == FLAG - TAIL, flag, 0.0)
    tail = jnp.where(lane[:1] == FLAG - TAIL, flag, tail)
    zero = jnp.zeros((1, WIDE), jnp.float32)
    for row in range(9):
        full = dense[row : row + 1] if row < 8 else tail
        empty = zero if row < 8 else blank
        at = slice(row * WIDE, (row + 1) * WIDE)
        out_ref[pl.ds((1 - panel) * PEERS, PEERS), :, at] = jnp.broadcast_to(
            full[None], (PEERS, 1, WIDE)
        )
        out_ref[pl.ds(panel * PEERS, PEERS), :, at] = jnp.broadcast_to(
            empty[None], (PEERS, 1, WIDE)
        )


def cut_kernel(state_ref, held_ref, south_ref, east_ref, corner_ref, plane_ref):
    for plane in range(PLANES):
        plane_ref[plane, :, :COLS] = state_ref[plane // LEVELS, plane % LEVELS]
    lane = iota((ROWS, WIDE), 1)
    column = column_of((ROWS, WIDE))
    own = (column >= 8) & (column < 8 + COLS)
    for pair in range(PAIRS):
        field, which = pair // 2, pair % 2
        low = turn(plane_ref[field * LEVELS + LOW_LEVEL[which]], 8)
        high = turn(plane_ref[field * LEVELS + HIGH_LEVEL[which]], HALF + 8)
        tile = jnp.where(own, jnp.where(lane < HALF, low, high), 0.0)
        held_ref[pair] = tile
        south_ref[pair] = tile[:8]
    for group in range(2):
        columns = jnp.zeros((ROWS, WIDE), jnp.float32)
        for which in range(8):
            moved = turn(held_ref[8 * group + which], 8 * which - 8)
            columns = jnp.where(column // 8 == which, moved, columns)
        east_ref[group] = columns
        corner_ref[group] = columns[:8]


def donor_tables(donor_ref, pick_ref, mix_ref, spin_ref, line_ref):
    late = iota((1, WIDE), 1) >= HALF

    def twice(value, fill):
        line_ref[...] = jnp.full((1, WIDE), fill, jnp.float32)
        line_ref[:, :SLOTS] = value
        line = line_ref[...]
        return jnp.where(late, pltpu.roll(line, HALF, 1), line)

    cell = twice(donor_ref[0:1], -10.0 * COLS)
    row_at = jnp.floor((cell + 0.5) * (1.0 / COLS))
    col_at = cell - row_at * COLS + jnp.where(late, 1.0, 0.0)
    upper = jnp.where(late, twice(donor_ref[2:3], 0.0), twice(donor_ref[1:2], 0.0))
    lower = jnp.where(late, twice(donor_ref[4:5], 0.0), twice(donor_ref[3:4], 0.0))
    angle = twice(donor_ref[5:6], 0.0)
    spin_ref[0:1] = jnp.cos(angle)
    spin_ref[1:2] = jnp.sin(angle)
    lane = iota((WIDE, WIDE), 0).astype(jnp.float32)
    real = jnp.where(row_at >= 0, col_at + 8.0, -1000.0)
    low = jnp.where(lane == real, 1.0, 0.0).astype(jnp.bfloat16)
    high = jnp.where(lane == real + HALF, 1.0, 0.0).astype(jnp.bfloat16)
    for part in range(3):
        pick_ref[part * WIDE : (part + 1) * WIDE, :WIDE] = low
        pick_ref[part * WIDE : (part + 1) * WIDE, WIDE:] = high
    row = iota((MID, WIDE), 0).astype(jnp.float32)
    mix = jnp.where(row == row_at, upper, 0.0) + jnp.where(row == row_at + 1.0, lower, 0.0)
    mix_ref[:, :WIDE] = mix
    mix_ref[:, WIDE:] = mix


def count_kernel(bands_ref, sides_ref, flag_ref):
    width = bands_ref.shape[1]
    column = iota((width, WIDE), 0) - 4
    start = iota((width, WIDE), 1) * COLS - 8
    within = (column >= start) & (column < start + 64) & (start < PANEL_COLS)
    columns = jnp.where(within, 1.0, 0.0).astype(jnp.bfloat16)
    row = iota((PANEL_ROWS, WIDE), 0)
    start = iota((PANEL_ROWS, WIDE), 1) * ROWS - 8
    within = (row >= start) & (row < start + TALL) & (start < PANEL_ROWS)
    rows = jnp.where(within, 1.0, 0.0).astype(jnp.bfloat16)

    def most(slots, windows):
        ones = []
        for which in range(LATS):
            first = which * LONS * SLOTS
            inside = (slots >= first) & (slots < first + LONS * SLOTS)
            ones.append(jnp.where(inside, 1.0, 0.0))
        ones = jnp.concatenate(ones, axis=0).astype(jnp.bfloat16)
        counts = jnp.dot(ones, windows, preferred_element_type=jnp.float32)
        return jnp.max(jnp.sum(counts.reshape(2 * LATS, 4, WIDE), axis=1))

    total = most(bands_ref[...], columns) + most(sides_ref[...], rows)
    flag_ref[...] = jnp.full(flag_ref.shape, total, jnp.float32)


def donor_kernel(
    place_ref, held_ref, south_ref, east_ref, corner_ref, pick_ref, mix_ref, spin_ref,
    lower_ref, north_ref, out_ref
):
    column = column_of((ROWS, WIDE))
    beyond = column >= 8 + COLS
    for pair in range(PAIRS):
        group, which = pair // 8, pair % 8
        east = turn(east_ref[group], 8 + COLS - 8 * which)
        corner = turn(corner_ref[group], 8 + COLS - 8 * which)
        lower_ref[pair, :ROWS] = jnp.where(beyond, east, held_ref[pair])
        lower_ref[pair, ROWS:] = jnp.where(beyond[:8], corner, south_ref[pair])
        north_ref[pair] = lower_ref[pair, 8:16]
    planes = lower_ref[...].reshape(PAIRS * MID, WIDE)
    packed = donor_message(planes, pick_ref[...], mix_ref[...], spin_ref[...])
    post_message(place_ref, packed, jnp.zeros((1, WIDE), jnp.float32), out_ref)


def split_parts(held):
    return jnp.concatenate(three_parts(held), axis=0)


def join_parts(terms):
    return terms[:PLANES] + terms[PLANES : 2 * PLANES] + terms[2 * PLANES :]


def from_row(place_ref, got_ref):
    base = (1 - place_ref[0]) * PEERS
    part = iota((8, WIDE), 1) // PACKED
    tiles = []
    tails = []
    for tile in range(CHOICE_TILES):
        rows = [jnp.zeros((8, WIDE), jnp.float32)] * 4
        for which in range(4):
            at = base + 4 * tile + which
            message = jnp.concatenate(
                [got_ref[at, :, row * WIDE : (row + 1) * WIDE] for row in range(8)], axis=0
            )
            tails.append(got_ref[at, :, TAIL:])
            for group in range(4):
                moved = turn(message, PACKED * (which - group))
                rows[group] = jnp.where(part == which, moved, rows[group])
        tiles.append(jnp.concatenate(rows, axis=0))
    tails.append(jnp.zeros((WIDE - PEERS, WIDE), jnp.float32))
    tails = jnp.concatenate(tails, axis=0).T
    tiles.append(jnp.concatenate([tails[:PAIRS], tails[HALF : HALF + PAIRS]], axis=0))
    return split_parts(jnp.concatenate(tiles, axis=1))


def rank_of(chosen):
    order = iota((CHUNK, CHUNK), 0) < iota((CHUNK, CHUNK), 1)
    order = jnp.where(order, 1.0, 0.0).astype(jnp.bfloat16)
    ones = jnp.where(chosen, 1.0, 0.0).astype(jnp.bfloat16)
    return jnp.dot(ones, order, preferred_element_type=jnp.float32)


def send_kernel(place_ref, holder_ref, spot_ref, send_ref):
    mine = holder_ref[...] == place_ref[1]
    spot = spot_ref[...].astype(jnp.float32)
    rank = rank_of(mine)
    key = jnp.where(mine & (rank < ROOM), rank, -1.0)
    place_at = iota((HALF, CHUNK), 0).astype(jnp.float32)
    eye = iota((WIDE, WIDE), 0) == iota((WIDE, WIDE), 1)
    depth = iota((CHOICE_DEPTH, WIDE), 0).astype(jnp.float32) + 1.0
    for pair in range(LATS // 2):
        tables = []
        for block in (2 * pair, 2 * pair + 1):
            found = place_at == key[block : block + 1]
            tables.append(
                jnp.sum(jnp.where(found, spot[block : block + 1] + 1.0, 0.0), axis=1, keepdims=True)
            )
        table = jnp.concatenate(tables, axis=0)
        line = jnp.sum(jnp.where(eye, table, 0.0), axis=0, keepdims=True)
        hot = jnp.where(depth == line, 1.0, 0.0).astype(jnp.bfloat16)
        send_ref[:, pair * WIDE : (pair + 1) * WIDE] = hot


def take_kernel(place_ref, holder_ref, take_ref, coef_ref):
    lat = place_ref[1]
    own = holder_ref[pl.ds(lat, 1)]
    masks = iota((PEERS, CHUNK), 0) == own
    rank = jnp.sum(jnp.where(masks, rank_of(masks), 0.0), axis=0, keepdims=True)
    fits = (own >= 0) & (rank < ROOM)
    index = jnp.where(fits, own.astype(jnp.float32) * HALF + rank, -1.0)
    hot = iota((DEPTH, CHUNK), 0).astype(jnp.float32) == index
    take_ref[...] = jnp.where(hot, 1.0, 0.0).astype(jnp.bfloat16)
    row = (lat * ROWS - 8 + iota((TALL, WIDE), 0)).astype(jnp.float32)
    column = (place_ref[2] * COLS - 8 + column_of((TALL, WIDE))).astype(jnp.float32)
    colatitude = 0.25 * math.pi + (row + 0.5) * DTHETA
    longitude = -0.75 * math.pi + (column + 0.5) * DPHI
    sine, cosine = jnp.sin(colatitude), jnp.cos(colatitude)
    twirl = 2.0 * 0.25 / TIME_STEP
    yang = place_ref[0] == 1
    coef_ref[0] = sine
    coef_ref[1] = 1.0 / sine
    coef_ref[2] = twirl * jnp.where(yang, sine * jnp.sin(longitude), cosine)
    coef_ref[3] = twirl * jnp.where(yang, cosine * jnp.sin(longitude), -sine)
    coef_ref[4] = twirl * jnp.where(yang, jnp.cos(longitude), 0.0)


def widen_kernel(place_ref, got_ref, send_ref, lower_ref, north_ref, out_ref, west_ref):
    column = column_of((TALL, WIDE))
    for group in range(2):
        columns = jnp.zeros((TALL, WIDE), jnp.float32)
        for which in range(8):
            pair = 8 * group + which
            rows = jnp.concatenate([north_ref[pair], lower_ref[pair]], axis=0)
            moved = turn(rows, 8 * which - COLS)
            columns = jnp.where(column // 8 == which, moved, columns)
        west_ref[group] = columns
    choice_kernel(place_ref, got_ref, send_ref, out_ref)


def choice_kernel(place_ref, got_ref, send_ref, out_ref):
    parts = from_row(place_ref, got_ref)
    terms = jnp.dot(parts, send_ref[...], preferred_element_type=jnp.float32)
    chosen = join_parts(terms)
    low = iota((16, WIDE), 1) < HALF
    for pair in range(PEERS // 2):
        tile = chosen[:, pair * WIDE : (pair + 1) * WIDE]
        top, end = tile[:16], tile[16:]
        out_ref[2 * pair] = jnp.where(low, top, pltpu.roll(end, HALF, 1))
        out_ref[2 * pair + 1] = jnp.where(low, pltpu.roll(top, HALF, 1), end)


def dense_kernel(place_ref, got_ref, holder_ref, spot_ref, out_ref):
    parts = from_row(place_ref, got_ref)
    index = jnp.where(holder_ref[...] == place_ref[1], spot_ref[...], -1)
    at = iota((CHOICE_DEPTH, CHUNK), 0)
    for block in range(LATS):
        hot = jnp.where(at == index[block : block + 1], 1.0, 0.0).astype(jnp.bfloat16)
        out_ref[block] = join_parts(jnp.dot(parts, hot, preferred_element_type=jnp.float32))


def ghost_values(got_ref, take_ref):
    if len(got_ref.shape) == 2:
        return got_ref[...]
    low = iota((16, WIDE), 1) < HALF
    tiles = []
    for pair in range(PEERS // 2):
        one = got_ref[2 * pair]
        two = got_ref[2 * pair + 1]
        top = jnp.where(low, one, pltpu.roll(two, HALF, 1))
        end = jnp.where(low, pltpu.roll(one, HALF, 1), two)
        tiles.append(jnp.concatenate([top, end], axis=0))
    parts = split_parts(jnp.concatenate(tiles, axis=1))
    return join_parts(jnp.dot(parts, take_ref[...], preferred_element_type=jnp.float32))


def fill_ghosts(place_ref, ghosts, work_ref, rows):
    lat, lon = place_ref[1], place_ref[2]
    trim = (TALL - rows) // 2
    top = 8 - trim
    half = PLANES // 2

    @pl.when((lon == 0) | (lon == LONS - 1))
    def _():
        side = ghosts[:, BAND:]
        first = jnp.where(lon == 0, 4, 8 + COLS)
        own = iota((rows, WIDE), 1) // 4 == iota((rows, WIDE), 0) + trim

        def spread(part):
            part = part.astype(jnp.float32)[:, None, :]
            return jnp.where(own[None], part, 0.0).astype(jnp.bfloat16).reshape(PAIRS * rows, WIDE)

        pieces = []
        for part in three_parts(side):
            pieces += [spread(part[:half]), spread(part[half:])]
        both = jnp.concatenate(pieces, axis=1)
        source = iota((6 * WIDE, WIDE), 0)
        target = first + (source & 3) + jnp.where((source & WIDE) != 0, HALF, 0)
        hot = jnp.where(target == iota((6 * WIDE, WIDE), 1), 1.0, 0.0).astype(jnp.bfloat16)
        moved = jnp.dot(both, hot, preferred_element_type=jnp.float32)
        moved = moved.reshape(PAIRS, rows, WIDE)
        column = column_of((rows, WIDE))
        ghost = (column >= first) & (column < first + 4)
        work_ref[...] = jnp.where(ghost[None], moved, work_ref[...])

    @pl.when((lat == 0) | (lat == LATS - 1))
    def _():
        low = iota((half, WIDE), 1) < HALF
        lines = []
        for which in range(2):
            piece = ghosts[:, which * WIDE : (which + 1) * WIDE]
            one, two = piece[:half], piece[half:]
            lines.append(jnp.where(low, one, pltpu.roll(two, HALF, 1)))
            lines.append(jnp.where(low, pltpu.roll(one, HALF, 1), two))

        def put(first):
            tile = first // 8 * 8
            row = iota((8, WIDE), 0)
            held = work_ref[:, tile : tile + 8, :]
            for which in range(4):
                mask = row == first - tile + which
                held = jnp.where(mask[None], lines[which][:, None, :], held)
            work_ref[:, tile : tile + 8, :] = held

        @pl.when(lat == 0)
        def _():
            put(top - 4)

        @pl.when(lat == LATS - 1)
        def _():
            put(top + ROWS)


def rates(load, rows, coef_ref, diffusion_ref):
    low = iota((rows, WIDE), 1) < HALF

    def levels(values):
        halves = [
            jnp.where(low, values[LOW_LEVEL[k]], values[HIGH_LEVEL[k]]).astype(jnp.float32)
            for k in range(2)
        ]
        return jnp.concatenate(halves, axis=0)

    def whole(which):
        value = coef_ref[which]
        if rows < TALL:
            value = pltpu.roll(value, TALL - (TALL - rows) // 2, 0)[:rows]
        return jnp.concatenate([value] * 2, axis=0)

    sine = whole(0)
    per_sine = whole(1)
    radius = levels(RADII)
    inverse = levels([1.0 / r for r in RADII])
    square = levels([r * r for r in RADII])
    per_square = levels([1.0 / (r * r) for r in RADII])
    sign = jnp.where(low, 1.0, -1.0)
    ends = sign * (1.0 / RADIAL_STEP)
    inner = sign * (1.0 / (2.0 * RADIAL_STEP))
    viscosity = diffusion_ref[0] * (FINEST * FINEST / TIME_STEP)
    resistivity = diffusion_ref[1] * (FINEST * FINEST / TIME_STEP)

    def slope(value, axis, step):
        size = value.shape[axis]
        near = pltpu.roll(value, size - 1, axis) - pltpu.roll(value, 1, axis)
        far = pltpu.roll(value, size - 2, axis) - pltpu.roll(value, 2, axis)
        return near * (8.0 / (12.0 * step)) - far * (1.0 / (12.0 * step))

    def d_theta(value):
        return slope(value, 0, DTHETA)

    def d_phi(value):
        return slope(value, 1, DPHI)

    def d_radius(value):
        one, two = value[:rows], value[rows:]
        return jnp.concatenate(
            [(two - one) * ends, (pltpu.roll(two, HALF, 1) - one) * inner], axis=0
        )

    def by_radius(value):
        return value * radius

    def per_radius(value):
        return value * inverse

    def curl(vector):
        part_r, part_t, part_p = vector
        return (
            per_radius((d_theta(sine * part_p) - d_phi(part_t)) * per_sine),
            per_radius(d_phi(part_r) * per_sine - d_radius(by_radius(part_p))),
            per_radius(d_radius(by_radius(part_t)) - d_theta(part_r)),
        )

    def gradient(value):
        return (
            d_radius(value),
            per_radius(d_theta(value)),
            per_radius(d_phi(value) * per_sine),
        )

    def cross(left, right):
        return (
            left[1] * right[2] - left[2] * right[1],
            left[2] * right[0] - left[0] * right[2],
            left[0] * right[1] - left[1] * right[0],
        )

    def advect(vector, slopes):
        return vector[0] * slopes[0] + vector[1] * slopes[1] + vector[2] * slopes[2]

    velocity = [load(which) for which in (1, 2, 3)]
    magnetic = [load(which) for which in (4, 5, 6)]
    vorticity = curl(velocity)
    current = curl(magnetic)
    spread = d_radius(square * velocity[0]) * per_square + per_radius(
        (d_theta(sine * velocity[1]) + d_phi(velocity[2])) * per_sine
    )
    induced = cross(velocity, magnetic)
    electric = [induced[k] - resistivity * current[k] for k in range(3)]
    kinetic = 0.5 * (
        velocity[0] * velocity[0] + velocity[1] * velocity[1] + velocity[2] * velocity[2]
    )
    curl_electric = curl(electric)
    log_rho = load(0)
    rho_rate = -advect(velocity, gradient(log_rho)) - spread
    pressure = load(7)
    slope_pressure = gradient(pressure)
    pressure_rate = -advect(velocity, slope_pressure) - GAMMA * pressure * spread
    lorentz = cross(current, magnetic)
    per_rho = jnp.exp(-log_rho)
    slope_kinetic = gradient(kinetic)
    curl_vorticity = curl(vorticity)
    lamb = cross(velocity, vorticity)
    turning = cross((whole(2), whole(3), whole(4)), velocity)
    momentum = [
        lamb[k]
        - slope_kinetic[k]
        + per_rho * (lorentz[k] - slope_pressure[k])
        - turning[k]
        - viscosity * curl_vorticity[k]
        for k in range(3)
    ]
    return [rho_rate, *momentum, *curl_electric, pressure_rate]


def first_kernel(
    place_ref,
    diffusion_ref,
    lower_ref,
    north_ref,
    west_ref,
    got_ref,
    take_ref,
    coef_ref,
    pick_ref,
    mix_ref,
    spin_ref,
    flag_ref,
    middle_ref,
    out_ref,
    work_ref,
    next_ref,
):
    column = column_of((TALL, WIDE))
    for pair in range(PAIRS):
        group, which = pair // 8, pair % 8
        west = turn(west_ref[group], -8 * which)
        rows = jnp.concatenate([north_ref[pair], lower_ref[pair]], axis=0)
        work_ref[pair] = jnp.where(column < 8, west, rows)
    ghosts = ghost_values(got_ref, take_ref)
    fill_ghosts(place_ref, ghosts, work_ref, TALL)

    def load(which):
        return work_ref[2 * which : 2 * which + 2].reshape(2 * TALL, WIDE)

    found = rates(load, TALL, coef_ref, diffusion_ref)
    row = iota((TALL, WIDE), 0)
    inside = (column >= 4) & (column < 12 + COLS) & (row >= 4) & (row < 12 + ROWS)
    for which in range(FIELDS):
        value = load(which) + (0.5 * TIME_STEP) * found[which]
        for half in range(2):
            part = jnp.where(inside, value[half * TALL : (half + 1) * TALL], 0.0)
            next_ref[2 * which + half] = part[8:]
            middle_ref[2 * which + half] = pltpu.roll(part, TALL - 4, 0)[:MID]
    planes = next_ref[...].reshape(PAIRS * MID, WIDE)
    packed = donor_message(planes, pick_ref[...], mix_ref[...], spin_ref[...])
    post_message(place_ref, packed, flag_ref[0:1], out_ref)


def second_kernel(
    place_ref,
    diffusion_ref,
    middle_ref,
    got_ref,
    take_ref,
    coef_ref,
    held_ref,
    whole_ref,
    third_ref,
    work_ref,
):
    work_ref[...] = middle_ref[...]
    ghosts = ghost_values(got_ref, take_ref)
    fill_ghosts(place_ref, ghosts, work_ref, MID)

    def load(which):
        return work_ref[2 * which : 2 * which + 2].reshape(2 * MID, WIDE)

    found = rates(load, MID, coef_ref, diffusion_ref)

    def centre(value):
        return pltpu.roll(value, MID - 4, 0)[:ROWS]

    def place(out_ref, pair, value):
        field, half = pair // 2, pair % 2
        out_ref[field, LOW_LEVEL[half]] = turn(value, -8)[:, :COLS]
        out_ref[field, HIGH_LEVEL[half]] = turn(value, -8 - HALF)[:, :COLS]

    for pair in range(PAIRS):
        field, half = pair // 2, pair % 2
        rate = found[field][half * MID : (half + 1) * MID]
        held = held_ref[pair]
        step = centre(rate) * (0.5 * TIME_STEP)
        middle = centre(middle_ref[pair])
        place(third_ref, pair, held + step)
        place(whole_ref, pair, held + ((middle - held) + 2.0 * step) * (1.0 / 3.0))


def shift(value, move_lat, move_lon):
    pairs = []
    for a in range(LATS):
        for b in range(LONS):
            goal_a, goal_b = a + move_lat, b + move_lon
            if 0 <= goal_a < LATS and 0 <= goal_b < LONS:
                pairs.append((a * LONS + b, goal_a * LONS + goal_b))
    return lax.ppermute(value, ("lat", "lon"), pairs)


def shards(state, donor_cell, donor_weights, donor_turn, border_source, diffusion):
    fields = state[0]
    panel = lax.axis_index("panel")
    lat = lax.axis_index("lat")
    lon = lax.axis_index("lon")
    place = jnp.stack([panel, lat, lon]).astype(jnp.int32)
    f32 = jnp.float32

    def call(kernel, outs, *args, smem=0, specs=None, scratch=(), limit=10):
        shapes = [jax.ShapeDtypeStruct(shape, dtype) for shape, dtype in outs]
        return pl.pallas_call(
            kernel,
            out_shape=shapes,
            in_specs=specs or [SMEM] * smem + [VMEM] * (len(args) - smem),
            out_specs=[VMEM] * len(outs),
            scratch_shapes=scratch,
            compiler_params=pltpu.CompilerParams(vmem_limit_bytes=limit * MIB),
        )(*args)

    bf16 = jnp.bfloat16
    held, south, east, corner = call(
        cut_kernel,
        [
            ((PAIRS, ROWS, WIDE), f32),
            ((PAIRS, 8, WIDE), f32),
            ((2, ROWS, WIDE), f32),
            ((2, 8, WIDE), f32),
        ],
        fields,
        scratch=[pltpu.VMEM((PLANES, ROWS, WIDE), f32)],
    )
    south = shift(south, -1, 0)
    east = shift(east, 0, -1)
    corner = shift(corner, -1, -1)

    donor = jnp.concatenate(
        [donor_cell[0, 0].astype(f32), donor_weights[0, 0, 0], donor_turn[0, 0]], axis=0
    )
    pick, mix, spin = call(
        donor_tables,
        [((3 * WIDE, 2 * WIDE), bf16), ((MID, 2 * WIDE), f32), ((2, WIDE), f32)],
        donor,
        scratch=[pltpu.VMEM((1, WIDE), f32)],
    )
    message = ((2 * PEERS, 1, MESSAGE), f32)
    lower, north, sent = call(
        donor_kernel,
        [((PAIRS, MID, WIDE), f32), ((PAIRS, 8, WIDE), f32), message],
        place,
        held,
        south,
        east,
        corner,
        pick,
        mix,
        spin,
        smem=1,
    )

    def to_holders(sent):
        return lax.all_to_all(sent, ("panel", "lon"), 0, 0, tiled=True)

    got = to_holders(sent)

    north, late_lat, late_lon, border, _ = lax.optimization_barrier(
        (north, lat, lon, border_source, sent)
    )
    border = lax.optimization_barrier(border[0])
    north = shift(north, 1, 0)

    ring = PANEL_COLS + 8
    row_slots = LONS * SLOTS
    bands = border[: 8 * ring].reshape(8, ring)
    sides = border[8 * ring :].reshape(PANEL_ROWS, 8)
    window = jnp.pad(bands, ((0, 0), (4, 4)), constant_values=-1)
    window = lax.dynamic_slice(window, (0, late_lon * COLS), (8, 64)).reshape(2, BAND)
    side = jnp.where(late_lon == 0, sides[:, :4], sides[:, 4:])
    side = jnp.where((late_lon == 0) | (late_lon == LONS - 1), side, -1)
    side = jnp.pad(side, ((8, 8), (0, 0)), constant_values=-1)
    side = jnp.concatenate(
        [
            side[:PANEL_ROWS].reshape(LATS, ROWS, 4),
            side[ROWS:].reshape(LATS, ROWS, 4),
        ],
        axis=1,
    ).reshape(LATS, SIDE)
    at_lat = jnp.arange(LATS)[:, None]
    band = jnp.where(at_lat == 0, window[:1], jnp.where(at_lat == LATS - 1, window[1:], -1))
    wanted = jnp.concatenate([band, side], axis=1)
    holder = jnp.where(wanted >= 0, wanted // row_slots, -1)
    local = wanted - late_lat * row_slots
    block = local // SLOTS
    slot = local % SLOTS
    spot = jnp.where(slot < PACKED, block * PACKED + slot, PEERS * PACKED + block)
    (send,) = call(
        send_kernel, [((CHOICE_DEPTH, DEPTH), bf16)], place, holder, spot, smem=1, limit=16
    )
    chunk = ((PEERS, 16, WIDE), f32)
    first_got = got
    chunks, west = call(
        widen_kernel, [chunk, ((2, TALL, WIDE), f32)], place, got, send, lower, north, smem=1
    )
    west = shift(west, 0, 1)
    late_holder, bands, sides, _ = lax.optimization_barrier((holder, bands, sides, chunks))
    take, coef = call(
        take_kernel,
        [((DEPTH, CHUNK), bf16), ((5, TALL, WIDE), f32)],
        place,
        late_holder,
        smem=1,
    )

    (flag,) = call(
        count_kernel,
        [((8, WIDE), f32)],
        jnp.pad(bands, ((0, 0), (0, 7 * WIDE - ring)), constant_values=-1),
        sides.T,
    )

    def to_blocks(chunks):
        return lax.all_to_all(chunks, "lat", 0, 0, tiled=True)

    def section_one(got):
        return call(
            first_kernel,
            [((PAIRS, MID, WIDE), f32), message],
            place,
            diffusion,
            lower,
            north,
            west,
            got,
            take,
            coef,
            pick,
            mix,
            spin,
            flag,
            smem=2,
            scratch=[pltpu.VMEM((PAIRS, TALL, WIDE), f32), pltpu.VMEM((PAIRS, MID, WIDE), f32)],
        )

    def section_two(middle, got):
        return call(
            second_kernel,
            [(fields.shape, f32), (fields.shape, f32)],
            place,
            diffusion,
            middle,
            got,
            take,
            coef,
            held,
            smem=2,
            scratch=[pltpu.VMEM((PAIRS, MID, WIDE), f32)],
        )

    middle, sent = section_one(to_blocks(chunks))
    got = to_holders(sent)
    crowded = jnp.maximum(got[0, 0, FLAG], got[PEERS, 0, FLAG]) > ROOM
    (chunks,) = call(choice_kernel, [chunk], place, got, send, smem=1)
    fitting = section_two(middle, to_blocks(chunks))

    def with_room():
        def dense(got):
            chunks = call(
                dense_kernel,
                [((PEERS, PLANES, CHUNK), f32)],
                place,
                got,
                holder,
                spot,
                smem=1,
                limit=16,
            )
            return to_blocks(chunks[0]).sum(axis=0)

        middle, sent = section_one(dense(first_got))
        return section_two(middle, dense(to_holders(sent)))

    accumulated, section_three = lax.cond(crowded, with_room, lambda: fitting)
    return (accumulated[None], section_three[None])


def solution(mesh):
    return jax.shard_map(
        shards,
        mesh=mesh,
        in_specs=(
            P("panel", None, None, "lat", "lon"),
            P("panel", "lat", "lon", None),
            P("panel", "lat", "lon", None, None),
            P("panel", "lat", "lon", None),
            P("panel", None),
            P(),
        ),
        out_specs=(P("panel", None, None, "lat", "lon"), P("panel", None, None, "lat", "lon")),
        check_vma=False,
    )
```

```python
import math

import jax
import jax.numpy as jnp
from jax import lax
from jax.experimental import pallas as pl
from jax.experimental.pallas import tpu as pltpu
from jax.sharding import PartitionSpec as P

GAMMA = 5.0 / 3.0
RADIAL_STEP = 0.65 / 32.0
FIELDS = 8
LEVELS = 4
PLANES = FIELDS * LEVELS
PAIRS = PLANES // 2
LOW_LEVEL = (0, 1)
HIGH_LEVEL = (3, 2)
ROWS = 16
COLS = 48
SLOTS = 33
LATS = 16
LONS = 16
ROOM = 63
WIDE = 128
HALF = 64
TALL = ROWS + 16
MID = ROWS + 8
BAND = 4 * HALF
SIDE = 4 * TALL
CHUNK = BAND + SIDE
PEERS = 16
PACKED = 32
MESSAGE = 9 * WIDE
TAIL = 8 * WIDE
FLAG = TAIL + HALF - 1
CHOICE_TILES = PEERS * PACKED // WIDE
CHOICE_DEPTH = (CHOICE_TILES + 1) * WIDE
DEPTH = PEERS * HALF
PANEL_ROWS = ROWS * LATS
PANEL_COLS = COLS * LONS
DTHETA = 0.5 * math.pi / PANEL_ROWS
DPHI = 1.5 * math.pi / PANEL_COLS
FINEST = min(DTHETA, DPHI)
TIME_STEP = 0.1 * FINEST
RADII = [0.35 + 0.65 * (k + 16 - LEVELS // 2 + 0.5) / 32.0 for k in range(LEVELS)]
VMEM = pl.BlockSpec(memory_space=pltpu.VMEM)
SMEM = pl.BlockSpec(memory_space=pltpu.SMEM)
MIB = 1024 * 1024


def iota(shape, axis):
    return lax.broadcasted_iota(jnp.int32, shape, axis)


def column_of(shape):
    return iota(shape, len(shape) - 1) & (HALF - 1)


def turn(value, lanes):
    return pltpu.roll(value, lanes % WIDE, 1) if lanes % WIDE else value


def three_parts(value):
    parts = []
    for _ in range(3):
        part = value.astype(jnp.bfloat16)
        value = value - part.astype(jnp.float32)
        parts.append(part)
    return parts


def donor_message(planes, pick, mix, spin):
    parts = jnp.concatenate(three_parts(planes), axis=1)
    chosen = jnp.dot(parts, pick, preferred_element_type=jnp.float32)
    chosen = chosen.reshape(PAIRS, MID, 2 * WIDE)
    both = jnp.sum(chosen * mix[None], axis=1)
    both = jnp.concatenate([both[:, :WIDE], both[:, WIDE:]], axis=0)
    mixed = both + pltpu.roll(both, HALF, 1)
    cosine = spin[0:1]
    sine = spin[1:2]
    at = (iota((PLANES, WIDE), 0) & (PAIRS - 1)) // 2
    theta = (at == 2) | (at == 5)
    phi = (at == 3) | (at == 6)
    other = jnp.where(theta, pltpu.roll(mixed, PLANES - 2, 0), -pltpu.roll(mixed, 2, 0))
    turned = jnp.where(theta | phi, cosine * mixed + sine * other, mixed)
    return jnp.where(iota((PAIRS, WIDE), 1) < HALF, turned[:PAIRS], turned[PAIRS:])


def post_message(place_ref, packed, flag, out_ref):
    panel = place_ref[0]
    lane = iota((16, WIDE), 1)
    column = lane & (HALF - 1)
    dense = jnp.where(column[:8] < PACKED, packed[:8], turn(packed[8:], PACKED))
    last = jnp.where(
        lane < HALF, packed[:, PACKED : PACKED + 1], packed[:, HALF + PACKED : HALF + PACKED + 1]
    )
    tail = jnp.sum(jnp.where(column == iota((16, WIDE), 0), last, 0.0), axis=0, keepdims=True)
    blank = jnp.where(lane[:1] == FLAG - TAIL, flag, 0.0)
    tail = jnp.where(lane[:1] == FLAG - TAIL, flag, tail)
    zero = jnp.zeros((1, WIDE), jnp.float32)
    for row in range(9):
        full = dense[row : row + 1] if row < 8 else tail
        empty = zero if row < 8 else blank
        at = slice(row * WIDE, (row + 1) * WIDE)
        out_ref[pl.ds((1 - panel) * PEERS, PEERS), :, at] = jnp.broadcast_to(
            full[None], (PEERS, 1, WIDE)
        )
        out_ref[pl.ds(panel * PEERS, PEERS), :, at] = jnp.broadcast_to(
            empty[None], (PEERS, 1, WIDE)
        )


def cut_kernel(state_ref, held_ref, south_ref, east_ref, corner_ref, plane_ref):
    for plane in range(PLANES):
        plane_ref[plane, :, :COLS] = state_ref[plane // LEVELS, plane % LEVELS]
    lane = iota((ROWS, WIDE), 1)
    column = column_of((ROWS, WIDE))
    own = (column >= 8) & (column < 8 + COLS)
    for pair in range(PAIRS):
        field, which = pair // 2, pair % 2
        low = turn(plane_ref[field * LEVELS + LOW_LEVEL[which]], 8)
        high = turn(plane_ref[field * LEVELS + HIGH_LEVEL[which]], HALF + 8)
        tile = jnp.where(own, jnp.where(lane < HALF, low, high), 0.0)
        held_ref[pair] = tile
        south_ref[pair] = tile[:8]
    for group in range(2):
        columns = jnp.zeros((ROWS, WIDE), jnp.float32)
        for which in range(8):
            moved = turn(held_ref[8 * group + which], 8 * which - 8)
            columns = jnp.where(column // 8 == which, moved, columns)
        east_ref[group] = columns
        corner_ref[group] = columns[:8]


def donor_tables(donor_ref, pick_ref, mix_ref, spin_ref, line_ref):
    late = iota((1, WIDE), 1) >= HALF

    def twice(value, fill):
        line_ref[...] = jnp.full((1, WIDE), fill, jnp.float32)
        line_ref[:, :SLOTS] = value
        line = line_ref[...]
        return jnp.where(late, pltpu.roll(line, HALF, 1), line)

    cell = twice(donor_ref[0:1], -10.0 * COLS)
    row_at = jnp.floor((cell + 0.5) * (1.0 / COLS))
    col_at = cell - row_at * COLS + jnp.where(late, 1.0, 0.0)
    upper = jnp.where(late, twice(donor_ref[2:3], 0.0), twice(donor_ref[1:2], 0.0))
    lower = jnp.where(late, twice(donor_ref[4:5], 0.0), twice(donor_ref[3:4], 0.0))
    angle = twice(donor_ref[5:6], 0.0)
    spin_ref[0:1] = jnp.cos(angle)
    spin_ref[1:2] = jnp.sin(angle)
    lane = iota((WIDE, WIDE), 0).astype(jnp.float32)
    real = jnp.where(row_at >= 0, col_at + 8.0, -1000.0)
    low = jnp.where(lane == real, 1.0, 0.0).astype(jnp.bfloat16)
    high = jnp.where(lane == real + HALF, 1.0, 0.0).astype(jnp.bfloat16)
    for part in range(3):
        pick_ref[part * WIDE : (part + 1) * WIDE, :WIDE] = low
        pick_ref[part * WIDE : (part + 1) * WIDE, WIDE:] = high
    row = iota((MID, WIDE), 0).astype(jnp.float32)
    mix = jnp.where(row == row_at, upper, 0.0) + jnp.where(row == row_at + 1.0, lower, 0.0)
    mix_ref[:, :WIDE] = mix
    mix_ref[:, WIDE:] = mix


def count_kernel(bands_ref, sides_ref, flag_ref):
    width = bands_ref.shape[1]
    column = iota((width, WIDE), 0) - 4
    start = iota((width, WIDE), 1) * COLS - 8
    within = (column >= start) & (column < start + 64) & (start < PANEL_COLS)
    columns = jnp.where(within, 1.0, 0.0).astype(jnp.bfloat16)
    row = iota((PANEL_ROWS, WIDE), 0)
    start = iota((PANEL_ROWS, WIDE), 1) * ROWS - 8
    within = (row >= start) & (row < start + TALL) & (start < PANEL_ROWS)
    rows = jnp.where(within, 1.0, 0.0).astype(jnp.bfloat16)

    def most(slots, windows):
        ones = []
        for which in range(LATS):
            first = which * LONS * SLOTS
            inside = (slots >= first) & (slots < first + LONS * SLOTS)
            ones.append(jnp.where(inside, 1.0, 0.0))
        ones = jnp.concatenate(ones, axis=0).astype(jnp.bfloat16)
        counts = jnp.dot(ones, windows, preferred_element_type=jnp.float32)
        return jnp.max(jnp.sum(counts.reshape(2 * LATS, 4, WIDE), axis=1))

    total = most(bands_ref[...], columns) + most(sides_ref[...], rows)
    flag_ref[...] = jnp.full(flag_ref.shape, total, jnp.float32)


def donor_kernel(
    place_ref, held_ref, south_ref, east_ref, corner_ref, pick_ref, mix_ref, spin_ref,
    lower_ref, north_ref, out_ref
):
    column = column_of((ROWS, WIDE))
    beyond = column >= 8 + COLS
    for pair in range(PAIRS):
        group, which = pair // 8, pair % 8
        east = turn(east_ref[group], 8 + COLS - 8 * which)
        corner = turn(corner_ref[group], 8 + COLS - 8 * which)
        lower_ref[pair, :ROWS] = jnp.where(beyond, east, held_ref[pair])
        lower_ref[pair, ROWS:] = jnp.where(beyond[:8], corner, south_ref[pair])
        north_ref[pair] = lower_ref[pair, 8:16]
    planes = lower_ref[...].reshape(PAIRS * MID, WIDE)
    packed = donor_message(planes, pick_ref[...], mix_ref[...], spin_ref[...])
    post_message(place_ref, packed, jnp.zeros((1, WIDE), jnp.float32), out_ref)


def split_parts(held):
    return jnp.concatenate(three_parts(held), axis=0)


def join_parts(terms):
    return terms[:PLANES] + terms[PLANES : 2 * PLANES] + terms[2 * PLANES :]


def from_row(place_ref, got_ref):
    base = (1 - place_ref[0]) * PEERS
    part = iota((8, WIDE), 1) // PACKED
    tiles = []
    tails = []
    for tile in range(CHOICE_TILES):
        rows = [jnp.zeros((8, WIDE), jnp.float32)] * 4
        for which in range(4):
            at = base + 4 * tile + which
            message = jnp.concatenate(
                [got_ref[at, :, row * WIDE : (row + 1) * WIDE] for row in range(8)], axis=0
            )
            tails.append(got_ref[at, :, TAIL:])
            for group in range(4):
                moved = turn(message, PACKED * (which - group))
                rows[group] = jnp.where(part == which, moved, rows[group])
        tiles.append(jnp.concatenate(rows, axis=0))
    tails.append(jnp.zeros((WIDE - PEERS, WIDE), jnp.float32))
    tails = jnp.concatenate(tails, axis=0).T
    tiles.append(jnp.concatenate([tails[:PAIRS], tails[HALF : HALF + PAIRS]], axis=0))
    return split_parts(jnp.concatenate(tiles, axis=1))


def rank_of(chosen):
    order = iota((CHUNK, CHUNK), 0) < iota((CHUNK, CHUNK), 1)
    order = jnp.where(order, 1.0, 0.0).astype(jnp.bfloat16)
    ones = jnp.where(chosen, 1.0, 0.0).astype(jnp.bfloat16)
    return jnp.dot(ones, order, preferred_element_type=jnp.float32)


def send_kernel(place_ref, holder_ref, spot_ref, send_ref):
    mine = holder_ref[...] == place_ref[1]
    spot = spot_ref[...].astype(jnp.float32)
    rank = rank_of(mine)
    key = jnp.where(mine & (rank < ROOM), rank, -1.0)
    place_at = iota((HALF, CHUNK), 0).astype(jnp.float32)
    eye = iota((WIDE, WIDE), 0) == iota((WIDE, WIDE), 1)
    depth = iota((CHOICE_DEPTH, WIDE), 0).astype(jnp.float32) + 1.0
    for pair in range(LATS // 2):
        tables = []
        for block in (2 * pair, 2 * pair + 1):
            found = place_at == key[block : block + 1]
            tables.append(
                jnp.sum(jnp.where(found, spot[block : block + 1] + 1.0, 0.0), axis=1, keepdims=True)
            )
        table = jnp.concatenate(tables, axis=0)
        line = jnp.sum(jnp.where(eye, table, 0.0), axis=0, keepdims=True)
        hot = jnp.where(depth == line, 1.0, 0.0).astype(jnp.bfloat16)
        send_ref[:, pair * WIDE : (pair + 1) * WIDE] = hot


def take_kernel(place_ref, holder_ref, take_ref, coef_ref):
    lat = place_ref[1]
    own = holder_ref[pl.ds(lat, 1)]
    masks = iota((PEERS, CHUNK), 0) == own
    rank = jnp.sum(jnp.where(masks, rank_of(masks), 0.0), axis=0, keepdims=True)
    fits = (own >= 0) & (rank < ROOM)
    index = jnp.where(fits, own.astype(jnp.float32) * HALF + rank, -1.0)
    hot = iota((DEPTH, CHUNK), 0).astype(jnp.float32) == index
    take_ref[...] = jnp.where(hot, 1.0, 0.0).astype(jnp.bfloat16)
    row = (lat * ROWS - 8 + iota((TALL, WIDE), 0)).astype(jnp.float32)
    column = (place_ref[2] * COLS - 8 + column_of((TALL, WIDE))).astype(jnp.float32)
    colatitude = 0.25 * math.pi + (row + 0.5) * DTHETA
    longitude = -0.75 * math.pi + (column + 0.5) * DPHI
    sine, cosine = jnp.sin(colatitude), jnp.cos(colatitude)
    twirl = 2.0 * 0.25 / TIME_STEP
    yang = place_ref[0] == 1
    coef_ref[0] = sine
    coef_ref[1] = 1.0 / sine
    coef_ref[2] = twirl * jnp.where(yang, sine * jnp.sin(longitude), cosine)
    coef_ref[3] = twirl * jnp.where(yang, cosine * jnp.sin(longitude), -sine)
    coef_ref[4] = twirl * jnp.where(yang, jnp.cos(longitude), 0.0)


def widen_kernel(place_ref, got_ref, send_ref, lower_ref, north_ref, out_ref, west_ref):
    column = column_of((TALL, WIDE))
    for group in range(2):
        columns = jnp.zeros((TALL, WIDE), jnp.float32)
        for which in range(8):
            pair = 8 * group + which
            rows = jnp.concatenate([north_ref[pair], lower_ref[pair]], axis=0)
            moved = turn(rows, 8 * which - COLS)
            columns = jnp.where(column // 8 == which, moved, columns)
        west_ref[group] = columns
    choice_kernel(place_ref, got_ref, send_ref, out_ref)


def choice_kernel(place_ref, got_ref, send_ref, out_ref):
    parts = from_row(place_ref, got_ref)
    terms = jnp.dot(parts, send_ref[...], preferred_element_type=jnp.float32)
    chosen = join_parts(terms)
    low = iota((16, WIDE), 1) < HALF
    for pair in range(PEERS // 2):
        tile = chosen[:, pair * WIDE : (pair + 1) * WIDE]
        top, end = tile[:16], tile[16:]
        out_ref[2 * pair] = jnp.where(low, top, pltpu.roll(end, HALF, 1))
        out_ref[2 * pair + 1] = jnp.where(low, pltpu.roll(top, HALF, 1), end)


def dense_kernel(place_ref, got_ref, holder_ref, spot_ref, out_ref):
    parts = from_row(place_ref, got_ref)
    index = jnp.where(holder_ref[...] == place_ref[1], spot_ref[...], -1)
    at = iota((CHOICE_DEPTH, CHUNK), 0)
    for block in range(LATS):
        hot = jnp.where(at == index[block : block + 1], 1.0, 0.0).astype(jnp.bfloat16)
        out_ref[block] = join_parts(jnp.dot(parts, hot, preferred_element_type=jnp.float32))


def ghost_values(got_ref, take_ref):
    if len(got_ref.shape) == 2:
        return got_ref[...]
    low = iota((16, WIDE), 1) < HALF
    tiles = []
    for pair in range(PEERS // 2):
        one = got_ref[2 * pair]
        two = got_ref[2 * pair + 1]
        top = jnp.where(low, one, pltpu.roll(two, HALF, 1))
        end = jnp.where(low, pltpu.roll(one, HALF, 1), two)
        tiles.append(jnp.concatenate([top, end], axis=0))
    parts = split_parts(jnp.concatenate(tiles, axis=1))
    return join_parts(jnp.dot(parts, take_ref[...], preferred_element_type=jnp.float32))


def fill_ghosts(place_ref, ghosts, work_ref, rows):
    lat, lon = place_ref[1], place_ref[2]
    trim = (TALL - rows) // 2
    top = 8 - trim
    half = PLANES // 2

    @pl.when((lon == 0) | (lon == LONS - 1))
    def _():
        side = ghosts[:, BAND:]
        first = jnp.where(lon == 0, 4, 8 + COLS)
        own = iota((rows, WIDE), 1) // 4 == iota((rows, WIDE), 0) + trim

        def spread(part):
            part = part.astype(jnp.float32)[:, None, :]
            return jnp.where(own[None], part, 0.0).astype(jnp.bfloat16).reshape(PAIRS * rows, WIDE)

        pieces = []
        for part in three_parts(side):
            pieces += [spread(part[:half]), spread(part[half:])]
        both = jnp.concatenate(pieces, axis=1)
        source = iota((6 * WIDE, WIDE), 0)
        target = first + (source & 3) + jnp.where((source & WIDE) != 0, HALF, 0)
        hot = jnp.where(target == iota((6 * WIDE, WIDE), 1), 1.0, 0.0).astype(jnp.bfloat16)
        moved = jnp.dot(both, hot, preferred_element_type=jnp.float32)
        moved = moved.reshape(PAIRS, rows, WIDE)
        column = column_of((rows, WIDE))
        ghost = (column >= first) & (column < first + 4)
        work_ref[...] = jnp.where(ghost[None], moved, work_ref[...])

    @pl.when((lat == 0) | (lat == LATS - 1))
    def _():
        low = iota((half, WIDE), 1) < HALF
        lines = []
        for which in range(2):
            piece = ghosts[:, which * WIDE : (which + 1) * WIDE]
            one, two = piece[:half], piece[half:]
            lines.append(jnp.where(low, one, pltpu.roll(two, HALF, 1)))
            lines.append(jnp.where(low, pltpu.roll(one, HALF, 1), two))

        def put(first):
            tile = first // 8 * 8
            row = iota((8, WIDE), 0)
            held = work_ref[:, tile : tile + 8, :]
            for which in range(4):
                mask = row == first - tile + which
                held = jnp.where(mask[None], lines[which][:, None, :], held)
            work_ref[:, tile : tile + 8, :] = held

        @pl.when(lat == 0)
        def _():
            put(top - 4)

        @pl.when(lat == LATS - 1)
        def _():
            put(top + ROWS)


def rates(load, rows, coef_ref, diffusion_ref):
    low = iota((rows, WIDE), 1) < HALF

    def levels(values):
        halves = [
            jnp.where(low, values[LOW_LEVEL[k]], values[HIGH_LEVEL[k]]).astype(jnp.float32)
            for k in range(2)
        ]
        return jnp.concatenate(halves, axis=0)

    def whole(which):
        value = coef_ref[which]
        if rows < TALL:
            value = pltpu.roll(value, TALL - (TALL - rows) // 2, 0)[:rows]
        return jnp.concatenate([value] * 2, axis=0)

    sine = whole(0)
    per_sine = whole(1)
    radius = levels(RADII)
    inverse = levels([1.0 / r for r in RADII])
    square = levels([r * r for r in RADII])
    per_square = levels([1.0 / (r * r) for r in RADII])
    sign = jnp.where(low, 1.0, -1.0)
    ends = sign * (1.0 / RADIAL_STEP)
    inner = sign * (1.0 / (2.0 * RADIAL_STEP))
    viscosity = diffusion_ref[0] * (FINEST * FINEST / TIME_STEP)
    resistivity = diffusion_ref[1] * (FINEST * FINEST / TIME_STEP)

    def slope(value, axis, step):
        size = value.shape[axis]
        near = pltpu.roll(value, size - 1, axis) - pltpu.roll(value, 1, axis)
        far = pltpu.roll(value, size - 2, axis) - pltpu.roll(value, 2, axis)
        return near * (8.0 / (12.0 * step)) - far * (1.0 / (12.0 * step))

    def d_theta(value):
        return slope(value, 0, DTHETA)

    def d_phi(value):
        return slope(value, 1, DPHI)

    def d_radius(value):
        one, two = value[:rows], value[rows:]
        return jnp.concatenate(
            [(two - one) * ends, (pltpu.roll(two, HALF, 1) - one) * inner], axis=0
        )

    def by_radius(value):
        return value * radius

    def per_radius(value):
        return value * inverse

    def curl(vector):
        part_r, part_t, part_p = vector
        return (
            per_radius((d_theta(sine * part_p) - d_phi(part_t)) * per_sine),
            per_radius(d_phi(part_r) * per_sine - d_radius(by_radius(part_p))),
            per_radius(d_radius(by_radius(part_t)) - d_theta(part_r)),
        )

    def gradient(value):
        return (
            d_radius(value),
            per_radius(d_theta(value)),
            per_radius(d_phi(value) * per_sine),
        )

    def cross(left, right):
        return (
            left[1] * right[2] - left[2] * right[1],
            left[2] * right[0] - left[0] * right[2],
            left[0] * right[1] - left[1] * right[0],
        )

    def advect(vector, slopes):
        return vector[0] * slopes[0] + vector[1] * slopes[1] + vector[2] * slopes[2]

    velocity = [load(which) for which in (1, 2, 3)]
    magnetic = [load(which) for which in (4, 5, 6)]
    vorticity = curl(velocity)
    current = curl(magnetic)
    spread = d_radius(square * velocity[0]) * per_square + per_radius(
        (d_theta(sine * velocity[1]) + d_phi(velocity[2])) * per_sine
    )
    induced = cross(velocity, magnetic)
    electric = [induced[k] - resistivity * current[k] for k in range(3)]
    kinetic = 0.5 * (
        velocity[0] * velocity[0] + velocity[1] * velocity[1] + velocity[2] * velocity[2]
    )
    curl_electric = curl(electric)
    log_rho = load(0)
    rho_rate = -advect(velocity, gradient(log_rho)) - spread
    pressure = load(7)
    slope_pressure = gradient(pressure)
    pressure_rate = -advect(velocity, slope_pressure) - GAMMA * pressure * spread
    lorentz = cross(current, magnetic)
    per_rho = jnp.exp(-log_rho)
    slope_kinetic = gradient(kinetic)
    curl_vorticity = curl(vorticity)
    lamb = cross(velocity, vorticity)
    turning = cross((whole(2), whole(3), whole(4)), velocity)
    momentum = [
        lamb[k]
        - slope_kinetic[k]
        + per_rho * (lorentz[k] - slope_pressure[k])
        - turning[k]
        - viscosity * curl_vorticity[k]
        for k in range(3)
    ]
    return [rho_rate, *momentum, *curl_electric, pressure_rate]


def first_kernel(
    place_ref,
    diffusion_ref,
    lower_ref,
    north_ref,
    west_ref,
    got_ref,
    take_ref,
    coef_ref,
    pick_ref,
    mix_ref,
    spin_ref,
    flag_ref,
    middle_ref,
    out_ref,
    work_ref,
    next_ref,
):
    column = column_of((TALL, WIDE))
    for pair in range(PAIRS):
        group, which = pair // 8, pair % 8
        west = turn(west_ref[group], -8 * which)
        rows = jnp.concatenate([north_ref[pair], lower_ref[pair]], axis=0)
        work_ref[pair] = jnp.where(column < 8, west, rows)
    ghosts = ghost_values(got_ref, take_ref)
    fill_ghosts(place_ref, ghosts, work_ref, TALL)

    def load(which):
        return work_ref[2 * which : 2 * which + 2].reshape(2 * TALL, WIDE)

    found = rates(load, TALL, coef_ref, diffusion_ref)
    row = iota((TALL, WIDE), 0)
    inside = (column >= 4) & (column < 12 + COLS) & (row >= 4) & (row < 12 + ROWS)
    for which in range(FIELDS):
        value = load(which) + (0.5 * TIME_STEP) * found[which]
        for half in range(2):
            part = jnp.where(inside, value[half * TALL : (half + 1) * TALL], 0.0)
            next_ref[2 * which + half] = part[8:]
            middle_ref[2 * which + half] = pltpu.roll(part, TALL - 4, 0)[:MID]
    planes = next_ref[...].reshape(PAIRS * MID, WIDE)
    packed = donor_message(planes, pick_ref[...], mix_ref[...], spin_ref[...])
    post_message(place_ref, packed, flag_ref[0:1], out_ref)


def second_kernel(
    place_ref,
    diffusion_ref,
    middle_ref,
    got_ref,
    take_ref,
    coef_ref,
    held_ref,
    whole_out,
    third_out,
    work_ref,
    whole_ref,
    third_ref,
    sems,
):
    work_ref[...] = middle_ref[...]
    ghosts = ghost_values(got_ref, take_ref)
    fill_ghosts(place_ref, ghosts, work_ref, MID)

    def load(which):
        return work_ref[2 * which : 2 * which + 2].reshape(2 * MID, WIDE)

    found = rates(load, MID, coef_ref, diffusion_ref)

    def centre(value):
        return pltpu.roll(value, MID - 4, 0)[:ROWS]

    def place(out_ref, pair, value):
        field, half = pair // 2, pair % 2
        out_ref[field, LOW_LEVEL[half]] = turn(value, -8)[:, :COLS]
        out_ref[field, HIGH_LEVEL[half]] = turn(value, -8 - HALF)[:, :COLS]

    copies = []
    for pair in range(PAIRS):
        field, half = pair // 2, pair % 2
        rate = found[field][half * MID : (half + 1) * MID]
        held = held_ref[pair]
        step = centre(rate) * (0.5 * TIME_STEP)
        middle = centre(middle_ref[pair])
        place(third_ref, pair, held + step)
        place(whole_ref, pair, held + ((middle - held) + 2.0 * step) * (1.0 / 3.0))
        if half == 1:
            for which, (source, target) in enumerate(
                [(third_ref, third_out), (whole_ref, whole_out)]
            ):
                copy = pltpu.make_async_copy(
                    source.at[field], target.at[field], sems.at[2 * field + which]
                )
                copy.start()
                copies.append(copy)
    for copy in copies:
        copy.wait()


def shift(value, move_lat, move_lon):
    pairs = []
    for a in range(LATS):
        for b in range(LONS):
            goal_a, goal_b = a + move_lat, b + move_lon
            if 0 <= goal_a < LATS and 0 <= goal_b < LONS:
                pairs.append((a * LONS + b, goal_a * LONS + goal_b))
    return lax.ppermute(value, ("lat", "lon"), pairs)


def shards(state, donor_cell, donor_weights, donor_turn, border_source, diffusion):
    fields = state[0]
    panel = lax.axis_index("panel")
    lat = lax.axis_index("lat")
    lon = lax.axis_index("lon")
    place = jnp.stack([panel, lat, lon]).astype(jnp.int32)
    f32 = jnp.float32

    def call(kernel, outs, *args, smem=0, specs=None, scratch=(), limit=10, out=VMEM):
        shapes = [jax.ShapeDtypeStruct(shape, dtype) for shape, dtype in outs]
        return pl.pallas_call(
            kernel,
            out_shape=shapes,
            in_specs=specs or [SMEM] * smem + [VMEM] * (len(args) - smem),
            out_specs=[out] * len(outs),
            scratch_shapes=scratch,
            compiler_params=pltpu.CompilerParams(vmem_limit_bytes=limit * MIB),
        )(*args)

    bf16 = jnp.bfloat16
    held, south, east, corner = call(
        cut_kernel,
        [
            ((PAIRS, ROWS, WIDE), f32),
            ((PAIRS, 8, WIDE), f32),
            ((2, ROWS, WIDE), f32),
            ((2, 8, WIDE), f32),
        ],
        fields,
        scratch=[pltpu.VMEM((PLANES, ROWS, WIDE), f32)],
    )
    south = shift(south, -1, 0)
    east = shift(east, 0, -1)
    corner = shift(corner, -1, -1)

    donor = jnp.concatenate(
        [donor_cell[0, 0].astype(f32), donor_weights[0, 0, 0], donor_turn[0, 0]], axis=0
    )
    pick, mix, spin = call(
        donor_tables,
        [((3 * WIDE, 2 * WIDE), bf16), ((MID, 2 * WIDE), f32), ((2, WIDE), f32)],
        donor,
        scratch=[pltpu.VMEM((1, WIDE), f32)],
    )
    message = ((2 * PEERS, 1, MESSAGE), f32)
    lower, north, sent = call(
        donor_kernel,
        [((PAIRS, MID, WIDE), f32), ((PAIRS, 8, WIDE), f32), message],
        place,
        held,
        south,
        east,
        corner,
        pick,
        mix,
        spin,
        smem=1,
    )

    def to_holders(sent):
        return lax.all_to_all(sent, ("panel", "lon"), 0, 0, tiled=True)

    got = to_holders(sent)

    north, late_lat, late_lon, border, _ = lax.optimization_barrier(
        (north, lat, lon, border_source, sent)
    )
    border = lax.optimization_barrier(border[0])
    north = shift(north, 1, 0)

    ring = PANEL_COLS + 8
    row_slots = LONS * SLOTS
    bands = border[: 8 * ring].reshape(8, ring)
    sides = border[8 * ring :].reshape(PANEL_ROWS, 8)
    window = jnp.pad(bands, ((0, 0), (4, 4)), constant_values=-1)
    window = lax.dynamic_slice(window, (0, late_lon * COLS), (8, 64)).reshape(2, BAND)
    side = jnp.where(late_lon == 0, sides[:, :4], sides[:, 4:])
    side = jnp.where((late_lon == 0) | (late_lon == LONS - 1), side, -1)
    side = jnp.pad(side, ((8, 8), (0, 0)), constant_values=-1)
    side = jnp.concatenate(
        [
            side[:PANEL_ROWS].reshape(LATS, ROWS, 4),
            side[ROWS:].reshape(LATS, ROWS, 4),
        ],
        axis=1,
    ).reshape(LATS, SIDE)
    at_lat = jnp.arange(LATS)[:, None]
    band = jnp.where(at_lat == 0, window[:1], jnp.where(at_lat == LATS - 1, window[1:], -1))
    wanted = jnp.concatenate([band, side], axis=1)
    holder = jnp.where(wanted >= 0, wanted // row_slots, -1)
    local = wanted - late_lat * row_slots
    block = local // SLOTS
    slot = local % SLOTS
    spot = jnp.where(slot < PACKED, block * PACKED + slot, PEERS * PACKED + block)
    (send,) = call(
        send_kernel, [((CHOICE_DEPTH, DEPTH), bf16)], place, holder, spot, smem=1, limit=16
    )
    chunk = ((PEERS, 16, WIDE), f32)
    first_got = got
    chunks, west = call(
        widen_kernel, [chunk, ((2, TALL, WIDE), f32)], place, got, send, lower, north, smem=1
    )
    west = shift(west, 0, 1)
    late_holder, bands, sides, _ = lax.optimization_barrier((holder, bands, sides, chunks))
    take, coef = call(
        take_kernel,
        [((DEPTH, CHUNK), bf16), ((5, TALL, WIDE), f32)],
        place,
        late_holder,
        smem=1,
    )

    (flag,) = call(
        count_kernel,
        [((8, WIDE), f32)],
        jnp.pad(bands, ((0, 0), (0, 7 * WIDE - ring)), constant_values=-1),
        sides.T,
    )

    def to_blocks(chunks):
        return lax.all_to_all(chunks, "lat", 0, 0, tiled=True)

    def section_one(got):
        return call(
            first_kernel,
            [((PAIRS, MID, WIDE), f32), message],
            place,
            diffusion,
            lower,
            north,
            west,
            got,
            take,
            coef,
            pick,
            mix,
            spin,
            flag,
            smem=2,
            scratch=[pltpu.VMEM((PAIRS, TALL, WIDE), f32), pltpu.VMEM((PAIRS, MID, WIDE), f32)],
        )

    def section_two(middle, got):
        return call(
            second_kernel,
            [(fields.shape, f32), (fields.shape, f32)],
            place,
            diffusion,
            middle,
            got,
            take,
            coef,
            held,
            smem=2,
            scratch=[
                pltpu.VMEM((PAIRS, MID, WIDE), f32),
                pltpu.VMEM(fields.shape, f32),
                pltpu.VMEM(fields.shape, f32),
                pltpu.SemaphoreType.DMA((2 * FIELDS,)),
            ],
            out=pl.BlockSpec(memory_space=pl.ANY),
        )

    middle, sent = section_one(to_blocks(chunks))
    got = to_holders(sent)
    crowded = jnp.maximum(got[0, 0, FLAG], got[PEERS, 0, FLAG]) > ROOM
    (chunks,) = call(choice_kernel, [chunk], place, got, send, smem=1)
    fitting = section_two(middle, to_blocks(chunks))

    def with_room():
        def dense(got):
            chunks = call(
                dense_kernel,
                [((PEERS, PLANES, CHUNK), f32)],
                place,
                got,
                holder,
                spot,
                smem=1,
                limit=16,
            )
            return to_blocks(chunks[0]).sum(axis=0)

        middle, sent = section_one(dense(first_got))
        return section_two(middle, dense(to_holders(sent)))

    accumulated, section_three = lax.cond(crowded, with_room, lambda: fitting)
    return (accumulated[None], section_three[None])


def solution(mesh):
    return jax.shard_map(
        shards,
        mesh=mesh,
        in_specs=(
            P("panel", None, None, "lat", "lon"),
            P("panel", "lat", "lon", None),
            P("panel", "lat", "lon", None, None),
            P("panel", "lat", "lon", None),
            P("panel", None),
            P(),
        ),
        out_specs=(P("panel", None, None, "lat", "lon"), P("panel", None, None, "lat", "lon")),
        check_vma=False,
    )
```

```python
import math

import jax
import jax.numpy as jnp
from jax import lax
from jax.experimental import pallas as pl
from jax.experimental.pallas import tpu as pltpu
from jax.sharding import PartitionSpec as P

GAMMA = 5.0 / 3.0
RADIAL_STEP = 0.65 / 32.0
FIELDS = 8
LEVELS = 4
PLANES = FIELDS * LEVELS
PAIRS = PLANES // 2
LOW_LEVEL = (0, 1)
HIGH_LEVEL = (3, 2)
ROWS = 16
COLS = 48
SLOTS = 33
LATS = 16
LONS = 16
ROOM = 63
WIDE = 128
HALF = 64
TALL = ROWS + 16
MID = ROWS + 8
BAND = 4 * HALF
SIDE = 4 * TALL
CHUNK = BAND + SIDE
PEERS = 16
PACKED = 32
MESSAGE = 9 * WIDE
TAIL = 8 * WIDE
FLAG = TAIL + HALF - 1
CHOICE_TILES = PEERS * PACKED // WIDE
CHOICE_DEPTH = (CHOICE_TILES + 1) * WIDE
DEPTH = PEERS * HALF
PANEL_ROWS = ROWS * LATS
PANEL_COLS = COLS * LONS
DTHETA = 0.5 * math.pi / PANEL_ROWS
DPHI = 1.5 * math.pi / PANEL_COLS
FINEST = min(DTHETA, DPHI)
TIME_STEP = 0.1 * FINEST
RADII = [0.35 + 0.65 * (k + 16 - LEVELS // 2 + 0.5) / 32.0 for k in range(LEVELS)]
VMEM = pl.BlockSpec(memory_space=pltpu.VMEM)
SMEM = pl.BlockSpec(memory_space=pltpu.SMEM)
MIB = 1024 * 1024


def iota(shape, axis):
    return lax.broadcasted_iota(jnp.int32, shape, axis)


def column_of(shape):
    return iota(shape, len(shape) - 1) & (HALF - 1)


def turn(value, lanes):
    return pltpu.roll(value, lanes % WIDE, 1) if lanes % WIDE else value


def three_parts(value):
    parts = []
    for _ in range(3):
        part = value.astype(jnp.bfloat16)
        value = value - part.astype(jnp.float32)
        parts.append(part)
    return parts


def donor_message(planes, pick, mix, spin):
    parts = jnp.concatenate(three_parts(planes), axis=1)
    chosen = jnp.dot(parts, pick, preferred_element_type=jnp.float32)
    chosen = chosen.reshape(PAIRS, MID, 2 * WIDE)
    both = jnp.sum(chosen * mix[None], axis=1)
    both = jnp.concatenate([both[:, :WIDE], both[:, WIDE:]], axis=0)
    mixed = both + pltpu.roll(both, HALF, 1)
    cosine = spin[0:1]
    sine = spin[1:2]
    at = (iota((PLANES, WIDE), 0) & (PAIRS - 1)) // 2
    theta = (at == 2) | (at == 5)
    phi = (at == 3) | (at == 6)
    other = jnp.where(theta, pltpu.roll(mixed, PLANES - 2, 0), -pltpu.roll(mixed, 2, 0))
    turned = jnp.where(theta | phi, cosine * mixed + sine * other, mixed)
    return jnp.where(iota((PAIRS, WIDE), 1) < HALF, turned[:PAIRS], turned[PAIRS:])


def post_message(place_ref, packed, flag, out_ref):
    panel = place_ref[0]
    lane = iota((16, WIDE), 1)
    column = lane & (HALF - 1)
    dense = jnp.where(column[:8] < PACKED, packed[:8], turn(packed[8:], PACKED))
    last = jnp.where(
        lane < HALF, packed[:, PACKED : PACKED + 1], packed[:, HALF + PACKED : HALF + PACKED + 1]
    )
    tail = jnp.sum(jnp.where(column == iota((16, WIDE), 0), last, 0.0), axis=0, keepdims=True)
    blank = jnp.where(lane[:1] == FLAG - TAIL, flag, 0.0)
    tail = jnp.where(lane[:1] == FLAG - TAIL, flag, tail)
    zero = jnp.zeros((1, WIDE), jnp.float32)
    for row in range(9):
        full = dense[row : row + 1] if row < 8 else tail
        empty = zero if row < 8 else blank
        at = slice(row * WIDE, (row + 1) * WIDE)
        out_ref[pl.ds((1 - panel) * PEERS, PEERS), :, at] = jnp.broadcast_to(
            full[None], (PEERS, 1, WIDE)
        )
        out_ref[pl.ds(panel * PEERS, PEERS), :, at] = jnp.broadcast_to(
            empty[None], (PEERS, 1, WIDE)
        )


def cut_kernel(state_ref, held_ref, south_ref, east_ref, corner_ref, plane_ref):
    for plane in range(PLANES):
        plane_ref[plane, :, :COLS] = state_ref[plane // LEVELS, plane % LEVELS]
    lane = iota((ROWS, WIDE), 1)
    column = column_of((ROWS, WIDE))
    own = (column >= 8) & (column < 8 + COLS)
    for pair in range(PAIRS):
        field, which = pair // 2, pair % 2
        low = turn(plane_ref[field * LEVELS + LOW_LEVEL[which]], 8)
        high = turn(plane_ref[field * LEVELS + HIGH_LEVEL[which]], HALF + 8)
        tile = jnp.where(own, jnp.where(lane < HALF, low, high), 0.0)
        held_ref[pair] = tile
        south_ref[pair] = tile[:8]
    for group in range(2):
        columns = jnp.zeros((ROWS, WIDE), jnp.float32)
        for which in range(8):
            moved = turn(held_ref[8 * group + which], 8 * which - 8)
            columns = jnp.where(column // 8 == which, moved, columns)
        east_ref[group] = columns
        corner_ref[group] = columns[:8]


def donor_tables(donor_ref, pick_ref, mix_ref, spin_ref, line_ref):
    late = iota((1, WIDE), 1) >= HALF

    def twice(value, fill):
        line_ref[...] = jnp.full((1, WIDE), fill, jnp.float32)
        line_ref[:, :SLOTS] = value
        line = line_ref[...]
        return jnp.where(late, pltpu.roll(line, HALF, 1), line)

    cell = twice(donor_ref[0:1], -10.0 * COLS)
    row_at = jnp.floor((cell + 0.5) * (1.0 / COLS))
    col_at = cell - row_at * COLS + jnp.where(late, 1.0, 0.0)
    upper = jnp.where(late, twice(donor_ref[2:3], 0.0), twice(donor_ref[1:2], 0.0))
    lower = jnp.where(late, twice(donor_ref[4:5], 0.0), twice(donor_ref[3:4], 0.0))
    angle = twice(donor_ref[5:6], 0.0)
    spin_ref[0:1] = jnp.cos(angle)
    spin_ref[1:2] = jnp.sin(angle)
    lane = iota((WIDE, WIDE), 0).astype(jnp.float32)
    real = jnp.where(row_at >= 0, col_at + 8.0, -1000.0)
    low = jnp.where(lane == real, 1.0, 0.0).astype(jnp.bfloat16)
    high = jnp.where(lane == real + HALF, 1.0, 0.0).astype(jnp.bfloat16)
    for part in range(3):
        pick_ref[part * WIDE : (part + 1) * WIDE, :WIDE] = low
        pick_ref[part * WIDE : (part + 1) * WIDE, WIDE:] = high
    row = iota((MID, WIDE), 0).astype(jnp.float32)
    mix = jnp.where(row == row_at, upper, 0.0) + jnp.where(row == row_at + 1.0, lower, 0.0)
    mix_ref[:, :WIDE] = mix
    mix_ref[:, WIDE:] = mix


def count_kernel(bands_ref, sides_ref, flag_ref):
    width = bands_ref.shape[1]
    column = iota((width, WIDE), 0) - 4
    start = iota((width, WIDE), 1) * COLS - 8
    within = (column >= start) & (column < start + 64) & (start < PANEL_COLS)
    columns = jnp.where(within, 1.0, 0.0).astype(jnp.bfloat16)
    row = iota((PANEL_ROWS, WIDE), 0)
    start = iota((PANEL_ROWS, WIDE), 1) * ROWS - 8
    within = (row >= start) & (row < start + TALL) & (start < PANEL_ROWS)
    rows = jnp.where(within, 1.0, 0.0).astype(jnp.bfloat16)

    def most(slots, windows):
        ones = []
        for which in range(LATS):
            first = which * LONS * SLOTS
            inside = (slots >= first) & (slots < first + LONS * SLOTS)
            ones.append(jnp.where(inside, 1.0, 0.0))
        ones = jnp.concatenate(ones, axis=0).astype(jnp.bfloat16)
        counts = jnp.dot(ones, windows, preferred_element_type=jnp.float32)
        return jnp.max(jnp.sum(counts.reshape(2 * LATS, 4, WIDE), axis=1))

    total = most(bands_ref[...], columns) + most(sides_ref[...], rows)
    flag_ref[...] = jnp.full(flag_ref.shape, total, jnp.float32)


def donor_kernel(
    place_ref, held_ref, south_ref, east_ref, corner_ref, pick_ref, mix_ref, spin_ref,
    lower_ref, north_ref, out_ref
):
    column = column_of((ROWS, WIDE))
    beyond = column >= 8 + COLS
    for pair in range(PAIRS):
        group, which = pair // 8, pair % 8
        east = turn(east_ref[group], 8 + COLS - 8 * which)
        corner = turn(corner_ref[group], 8 + COLS - 8 * which)
        lower_ref[pair, :ROWS] = jnp.where(beyond, east, held_ref[pair])
        lower_ref[pair, ROWS:] = jnp.where(beyond[:8], corner, south_ref[pair])
        north_ref[pair] = lower_ref[pair, 8:16]
    planes = lower_ref[...].reshape(PAIRS * MID, WIDE)
    packed = donor_message(planes, pick_ref[...], mix_ref[...], spin_ref[...])
    post_message(place_ref, packed, jnp.zeros((1, WIDE), jnp.float32), out_ref)


def split_parts(held):
    return jnp.concatenate(three_parts(held), axis=0)


def join_parts(terms):
    return terms[:PLANES] + terms[PLANES : 2 * PLANES] + terms[2 * PLANES :]


def from_row(place_ref, got_ref):
    base = (1 - place_ref[0]) * PEERS
    part = iota((8, WIDE), 1) // PACKED
    tiles = []
    tails = []
    for tile in range(CHOICE_TILES):
        rows = [jnp.zeros((8, WIDE), jnp.float32)] * 4
        for which in range(4):
            at = base + 4 * tile + which
            message = jnp.concatenate(
                [got_ref[at, :, row * WIDE : (row + 1) * WIDE] for row in range(8)], axis=0
            )
            tails.append(got_ref[at, :, TAIL:])
            for group in range(4):
                moved = turn(message, PACKED * (which - group))
                rows[group] = jnp.where(part == which, moved, rows[group])
        tiles.append(jnp.concatenate(rows, axis=0))
    tails.append(jnp.zeros((WIDE - PEERS, WIDE), jnp.float32))
    tails = jnp.concatenate(tails, axis=0).T
    tiles.append(jnp.concatenate([tails[:PAIRS], tails[HALF : HALF + PAIRS]], axis=0))
    return split_parts(jnp.concatenate(tiles, axis=1))


def rank_of(chosen):
    order = iota((CHUNK, CHUNK), 0) < iota((CHUNK, CHUNK), 1)
    order = jnp.where(order, 1.0, 0.0).astype(jnp.bfloat16)
    ones = jnp.where(chosen, 1.0, 0.0).astype(jnp.bfloat16)
    return jnp.dot(ones, order, preferred_element_type=jnp.float32)


def send_kernel(place_ref, holder_ref, spot_ref, send_ref):
    mine = holder_ref[...] == place_ref[1]
    spot = spot_ref[...].astype(jnp.float32)
    rank = rank_of(mine)
    key = jnp.where(mine & (rank < ROOM), rank, -1.0)
    place_at = iota((HALF, CHUNK), 0).astype(jnp.float32)
    eye = iota((WIDE, WIDE), 0) == iota((WIDE, WIDE), 1)
    depth = iota((CHOICE_DEPTH, WIDE), 0).astype(jnp.float32) + 1.0
    for pair in range(LATS // 2):
        tables = []
        for block in (2 * pair, 2 * pair + 1):
            found = place_at == key[block : block + 1]
            tables.append(
                jnp.sum(jnp.where(found, spot[block : block + 1] + 1.0, 0.0), axis=1, keepdims=True)
            )
        table = jnp.concatenate(tables, axis=0)
        line = jnp.sum(jnp.where(eye, table, 0.0), axis=0, keepdims=True)
        hot = jnp.where(depth == line, 1.0, 0.0).astype(jnp.bfloat16)
        send_ref[:, pair * WIDE : (pair + 1) * WIDE] = hot


def take_kernel(place_ref, holder_ref, take_ref, coef_ref):
    lat = place_ref[1]
    own = holder_ref[pl.ds(lat, 1)]
    masks = iota((PEERS, CHUNK), 0) == own
    rank = jnp.sum(jnp.where(masks, rank_of(masks), 0.0), axis=0, keepdims=True)
    fits = (own >= 0) & (rank < ROOM)
    index = jnp.where(fits, own.astype(jnp.float32) * HALF + rank, -1.0)
    hot = iota((DEPTH, CHUNK), 0).astype(jnp.float32) == index
    take_ref[...] = jnp.where(hot, 1.0, 0.0).astype(jnp.bfloat16)
    row = (lat * ROWS - 8 + iota((TALL, WIDE), 0)).astype(jnp.float32)
    column = (place_ref[2] * COLS - 8 + column_of((TALL, WIDE))).astype(jnp.float32)
    colatitude = 0.25 * math.pi + (row + 0.5) * DTHETA
    longitude = -0.75 * math.pi + (column + 0.5) * DPHI
    sine, cosine = jnp.sin(colatitude), jnp.cos(colatitude)
    twirl = 2.0 * 0.25 / TIME_STEP
    yang = place_ref[0] == 1
    coef_ref[0] = sine
    coef_ref[1] = 1.0 / sine
    coef_ref[2] = twirl * jnp.where(yang, sine * jnp.sin(longitude), cosine)
    coef_ref[3] = twirl * jnp.where(yang, cosine * jnp.sin(longitude), -sine)
    coef_ref[4] = twirl * jnp.where(yang, jnp.cos(longitude), 0.0)


def widen_kernel(place_ref, got_ref, send_ref, lower_ref, north_ref, out_ref, west_ref):
    column = column_of((TALL, WIDE))
    for group in range(2):
        columns = jnp.zeros((TALL, WIDE), jnp.float32)
        for which in range(8):
            pair = 8 * group + which
            rows = jnp.concatenate([north_ref[pair], lower_ref[pair]], axis=0)
            moved = turn(rows, 8 * which - COLS)
            columns = jnp.where(column // 8 == which, moved, columns)
        west_ref[group] = columns
    choice_kernel(place_ref, got_ref, send_ref, out_ref)


def choice_kernel(place_ref, got_ref, send_ref, out_ref):
    parts = from_row(place_ref, got_ref)
    terms = jnp.dot(parts, send_ref[...], preferred_element_type=jnp.float32)
    chosen = join_parts(terms)
    low = iota((16, WIDE), 1) < HALF
    for pair in range(PEERS // 2):
        tile = chosen[:, pair * WIDE : (pair + 1) * WIDE]
        top, end = tile[:16], tile[16:]
        out_ref[2 * pair] = jnp.where(low, top, pltpu.roll(end, HALF, 1))
        out_ref[2 * pair + 1] = jnp.where(low, pltpu.roll(top, HALF, 1), end)


def dense_kernel(place_ref, got_ref, holder_ref, spot_ref, out_ref):
    parts = from_row(place_ref, got_ref)
    index = jnp.where(holder_ref[...] == place_ref[1], spot_ref[...], -1)
    at = iota((CHOICE_DEPTH, CHUNK), 0)
    for block in range(LATS):
        hot = jnp.where(at == index[block : block + 1], 1.0, 0.0).astype(jnp.bfloat16)
        out_ref[block] = join_parts(jnp.dot(parts, hot, preferred_element_type=jnp.float32))


def ghost_values(got_ref, take_ref):
    if len(got_ref.shape) == 2:
        return got_ref[...]
    low = iota((16, WIDE), 1) < HALF
    tiles = []
    for pair in range(PEERS // 2):
        one = got_ref[2 * pair]
        two = got_ref[2 * pair + 1]
        top = jnp.where(low, one, pltpu.roll(two, HALF, 1))
        end = jnp.where(low, pltpu.roll(one, HALF, 1), two)
        tiles.append(jnp.concatenate([top, end], axis=0))
    parts = split_parts(jnp.concatenate(tiles, axis=1))
    return join_parts(jnp.dot(parts, take_ref[...], preferred_element_type=jnp.float32))


def fill_ghosts(place_ref, ghosts, work_ref, rows):
    lat, lon = place_ref[1], place_ref[2]
    trim = (TALL - rows) // 2
    top = 8 - trim
    half = PLANES // 2

    @pl.when((lon == 0) | (lon == LONS - 1))
    def _():
        side = ghosts[:, BAND:]
        first = jnp.where(lon == 0, 4, 8 + COLS)
        own = iota((rows, WIDE), 1) // 4 == iota((rows, WIDE), 0) + trim

        def spread(part):
            part = part.astype(jnp.float32)[:, None, :]
            return jnp.where(own[None], part, 0.0).astype(jnp.bfloat16).reshape(PAIRS * rows, WIDE)

        pieces = []
        for part in three_parts(side):
            pieces += [spread(part[:half]), spread(part[half:])]
        both = jnp.concatenate(pieces, axis=1)
        source = iota((6 * WIDE, WIDE), 0)
        target = first + (source & 3) + jnp.where((source & WIDE) != 0, HALF, 0)
        hot = jnp.where(target == iota((6 * WIDE, WIDE), 1), 1.0, 0.0).astype(jnp.bfloat16)
        moved = jnp.dot(both, hot, preferred_element_type=jnp.float32)
        moved = moved.reshape(PAIRS, rows, WIDE)
        column = column_of((rows, WIDE))
        ghost = (column >= first) & (column < first + 4)
        work_ref[...] = jnp.where(ghost[None], moved, work_ref[...])

    @pl.when((lat == 0) | (lat == LATS - 1))
    def _():
        low = iota((half, WIDE), 1) < HALF
        lines = []
        for which in range(2):
            piece = ghosts[:, which * WIDE : (which + 1) * WIDE]
            one, two = piece[:half], piece[half:]
            lines.append(jnp.where(low, one, pltpu.roll(two, HALF, 1)))
            lines.append(jnp.where(low, pltpu.roll(one, HALF, 1), two))

        def put(first):
            tile = first // 8 * 8
            row = iota((8, WIDE), 0)
            held = work_ref[:, tile : tile + 8, :]
            for which in range(4):
                mask = row == first - tile + which
                held = jnp.where(mask[None], lines[which][:, None, :], held)
            work_ref[:, tile : tile + 8, :] = held

        @pl.when(lat == 0)
        def _():
            put(top - 4)

        @pl.when(lat == LATS - 1)
        def _():
            put(top + ROWS)


def rates(load, rows, coef_ref, diffusion_ref):
    low = iota((rows, WIDE), 1) < HALF

    def levels(values):
        halves = [
            jnp.where(low, values[LOW_LEVEL[k]], values[HIGH_LEVEL[k]]).astype(jnp.float32)
            for k in range(2)
        ]
        return jnp.concatenate(halves, axis=0)

    def whole(which):
        value = coef_ref[which]
        if rows < TALL:
            value = pltpu.roll(value, TALL - (TALL - rows) // 2, 0)[:rows]
        return jnp.concatenate([value] * 2, axis=0)

    sine = whole(0)
    per_sine = whole(1)
    radius = levels(RADII)
    inverse = levels([1.0 / r for r in RADII])
    square = levels([r * r for r in RADII])
    per_square = levels([1.0 / (r * r) for r in RADII])
    sign = jnp.where(low, 1.0, -1.0)
    ends = sign * (1.0 / RADIAL_STEP)
    inner = sign * (1.0 / (2.0 * RADIAL_STEP))
    viscosity = diffusion_ref[0] * (FINEST * FINEST / TIME_STEP)
    resistivity = diffusion_ref[1] * (FINEST * FINEST / TIME_STEP)

    def slope(value, axis, step):
        size = value.shape[axis]
        near = pltpu.roll(value, size - 1, axis) - pltpu.roll(value, 1, axis)
        far = pltpu.roll(value, size - 2, axis) - pltpu.roll(value, 2, axis)
        return near * (8.0 / (12.0 * step)) - far * (1.0 / (12.0 * step))

    def d_theta(value):
        return slope(value, 0, DTHETA)

    def d_phi(value):
        return slope(value, 1, DPHI)

    def d_radius(value):
        one, two = value[:rows], value[rows:]
        return jnp.concatenate(
            [(two - one) * ends, (pltpu.roll(two, HALF, 1) - one) * inner], axis=0
        )

    def by_radius(value):
        return value * radius

    def per_radius(value):
        return value * inverse

    def curl(vector):
        part_r, part_t, part_p = vector
        return (
            per_radius((d_theta(sine * part_p) - d_phi(part_t)) * per_sine),
            per_radius(d_phi(part_r) * per_sine - d_radius(by_radius(part_p))),
            per_radius(d_radius(by_radius(part_t)) - d_theta(part_r)),
        )

    def gradient(value):
        return (
            d_radius(value),
            per_radius(d_theta(value)),
            per_radius(d_phi(value) * per_sine),
        )

    def cross(left, right):
        return (
            left[1] * right[2] - left[2] * right[1],
            left[2] * right[0] - left[0] * right[2],
            left[0] * right[1] - left[1] * right[0],
        )

    def advect(vector, slopes):
        return vector[0] * slopes[0] + vector[1] * slopes[1] + vector[2] * slopes[2]

    velocity = [load(which) for which in (1, 2, 3)]
    magnetic = [load(which) for which in (4, 5, 6)]
    vorticity = curl(velocity)
    current = curl(magnetic)
    spread = d_radius(square * velocity[0]) * per_square + per_radius(
        (d_theta(sine * velocity[1]) + d_phi(velocity[2])) * per_sine
    )
    induced = cross(velocity, magnetic)
    electric = [induced[k] - resistivity * current[k] for k in range(3)]
    kinetic = 0.5 * (
        velocity[0] * velocity[0] + velocity[1] * velocity[1] + velocity[2] * velocity[2]
    )
    curl_electric = curl(electric)
    log_rho = load(0)
    rho_rate = -advect(velocity, gradient(log_rho)) - spread
    pressure = load(7)
    slope_pressure = gradient(pressure)
    pressure_rate = -advect(velocity, slope_pressure) - GAMMA * pressure * spread
    lorentz = cross(current, magnetic)
    per_rho = jnp.exp(-log_rho)
    slope_kinetic = gradient(kinetic)
    curl_vorticity = curl(vorticity)
    lamb = cross(velocity, vorticity)
    turning = cross((whole(2), whole(3), whole(4)), velocity)
    momentum = [
        lamb[k]
        - slope_kinetic[k]
        + per_rho * (lorentz[k] - slope_pressure[k])
        - turning[k]
        - viscosity * curl_vorticity[k]
        for k in range(3)
    ]
    return [rho_rate, *momentum, *curl_electric, pressure_rate]


def first_kernel(
    place_ref,
    diffusion_ref,
    lower_ref,
    north_ref,
    west_ref,
    got_ref,
    take_ref,
    coef_ref,
    pick_ref,
    mix_ref,
    spin_ref,
    flag_ref,
    middle_ref,
    out_ref,
    work_ref,
    next_ref,
):
    column = column_of((TALL, WIDE))
    for pair in range(PAIRS):
        group, which = pair // 8, pair % 8
        west = turn(west_ref[group], -8 * which)
        rows = jnp.concatenate([north_ref[pair], lower_ref[pair]], axis=0)
        work_ref[pair] = jnp.where(column < 8, west, rows)
    ghosts = ghost_values(got_ref, take_ref)
    fill_ghosts(place_ref, ghosts, work_ref, TALL)

    def load(which):
        return work_ref[2 * which : 2 * which + 2].reshape(2 * TALL, WIDE)

    found = rates(load, TALL, coef_ref, diffusion_ref)
    row = iota((TALL, WIDE), 0)
    inside = (column >= 4) & (column < 12 + COLS) & (row >= 4) & (row < 12 + ROWS)
    for which in range(FIELDS):
        value = load(which) + (0.5 * TIME_STEP) * found[which]
        for half in range(2):
            part = jnp.where(inside, value[half * TALL : (half + 1) * TALL], 0.0)
            next_ref[2 * which + half] = part[8:]
            middle_ref[2 * which + half] = pltpu.roll(part, TALL - 4, 0)[:MID]
    planes = next_ref[...].reshape(PAIRS * MID, WIDE)
    packed = donor_message(planes, pick_ref[...], mix_ref[...], spin_ref[...])
    post_message(place_ref, packed, flag_ref[0:1], out_ref)


def second_kernel(
    place_ref,
    diffusion_ref,
    middle_ref,
    got_ref,
    take_ref,
    coef_ref,
    held_ref,
    whole_ref,
    third_ref,
    work_ref,
):
    work_ref[...] = middle_ref[...]
    ghosts = ghost_values(got_ref, take_ref)
    fill_ghosts(place_ref, ghosts, work_ref, MID)

    def load(which):
        return work_ref[2 * which : 2 * which + 2].reshape(2 * MID, WIDE)

    found = rates(load, MID, coef_ref, diffusion_ref)

    def centre(value):
        return pltpu.roll(value, MID - 4, 0)[:ROWS]

    def place(out_ref, pair, value):
        field, half = pair // 2, pair % 2
        out_ref[field, LOW_LEVEL[half]] = turn(value, -8)[:, :COLS]
        out_ref[field, HIGH_LEVEL[half]] = turn(value, -8 - HALF)[:, :COLS]

    for pair in range(PAIRS):
        field, half = pair // 2, pair % 2
        rate = found[field][half * MID : (half + 1) * MID]
        held = held_ref[pair]
        step = centre(rate) * (0.5 * TIME_STEP)
        middle = centre(middle_ref[pair])
        place(third_ref, pair, held + step)
        place(whole_ref, pair, held + ((middle - held) + 2.0 * step) * (1.0 / 3.0))


def shift(value, move_lat, move_lon):
    pairs = []
    for a in range(LATS):
        for b in range(LONS):
            goal_a, goal_b = a + move_lat, b + move_lon
            if 0 <= goal_a < LATS and 0 <= goal_b < LONS:
                pairs.append((a * LONS + b, goal_a * LONS + goal_b))
    return lax.ppermute(value, ("lat", "lon"), pairs)


def shards(state, donor_cell, donor_weights, donor_turn, border_source, diffusion):
    fields = state[0]
    panel = lax.axis_index("panel")
    lat = lax.axis_index("lat")
    lon = lax.axis_index("lon")
    place = jnp.stack([panel, lat, lon]).astype(jnp.int32)
    f32 = jnp.float32

    def call(kernel, outs, *args, smem=0, specs=None, scratch=(), limit=10):
        shapes = [jax.ShapeDtypeStruct(shape, dtype) for shape, dtype in outs]
        return pl.pallas_call(
            kernel,
            out_shape=shapes,
            in_specs=specs or [SMEM] * smem + [VMEM] * (len(args) - smem),
            out_specs=[VMEM] * len(outs),
            scratch_shapes=scratch,
            compiler_params=pltpu.CompilerParams(vmem_limit_bytes=limit * MIB),
        )(*args)

    bf16 = jnp.bfloat16
    held, south, east, corner = call(
        cut_kernel,
        [
            ((PAIRS, ROWS, WIDE), f32),
            ((PAIRS, 8, WIDE), f32),
            ((2, ROWS, WIDE), f32),
            ((2, 8, WIDE), f32),
        ],
        fields,
        scratch=[pltpu.VMEM((PLANES, ROWS, WIDE), f32)],
    )
    south = shift(south, -1, 0)
    east = shift(east, 0, -1)
    corner = shift(corner, -1, -1)

    donor = jnp.concatenate(
        [donor_cell[0, 0].astype(f32), donor_weights[0, 0, 0], donor_turn[0, 0]], axis=0
    )
    pick, mix, spin = call(
        donor_tables,
        [((3 * WIDE, 2 * WIDE), bf16), ((MID, 2 * WIDE), f32), ((2, WIDE), f32)],
        donor,
        scratch=[pltpu.VMEM((1, WIDE), f32)],
    )
    message = ((2 * PEERS, 1, MESSAGE), f32)
    lower, north, sent = call(
        donor_kernel,
        [((PAIRS, MID, WIDE), f32), ((PAIRS, 8, WIDE), f32), message],
        place,
        held,
        south,
        east,
        corner,
        pick,
        mix,
        spin,
        smem=1,
    )

    def to_holders(sent):
        return lax.all_to_all(sent, ("panel", "lon"), 0, 0, tiled=True)

    got = to_holders(sent)

    north, late_lat, late_lon, border, _ = lax.optimization_barrier(
        (north, lat, lon, border_source[0], sent)
    )
    north = shift(north, 1, 0)

    ring = PANEL_COLS + 8
    row_slots = LONS * SLOTS
    bands = border[: 8 * ring].reshape(8, ring)
    sides = border[8 * ring :].reshape(PANEL_ROWS, 8)
    window = jnp.pad(bands, ((0, 0), (4, 4)), constant_values=-1)
    window = lax.dynamic_slice(window, (0, late_lon * COLS), (8, 64)).reshape(2, BAND)
    side = jnp.where(late_lon == 0, sides[:, :4], sides[:, 4:])
    side = jnp.where((late_lon == 0) | (late_lon == LONS - 1), side, -1)
    side = jnp.pad(side, ((8, 8), (0, 0)), constant_values=-1)
    side = jnp.concatenate(
        [
            side[:PANEL_ROWS].reshape(LATS, ROWS, 4),
            side[ROWS:].reshape(LATS, ROWS, 4),
        ],
        axis=1,
    ).reshape(LATS, SIDE)
    at_lat = jnp.arange(LATS)[:, None]
    band = jnp.where(at_lat == 0, window[:1], jnp.where(at_lat == LATS - 1, window[1:], -1))
    wanted = jnp.concatenate([band, side], axis=1)
    holder = jnp.where(wanted >= 0, wanted // row_slots, -1)
    local = wanted - late_lat * row_slots
    block = local // SLOTS
    slot = local % SLOTS
    spot = jnp.where(slot < PACKED, block * PACKED + slot, PEERS * PACKED + block)
    (send,) = call(
        send_kernel, [((CHOICE_DEPTH, DEPTH), bf16)], place, holder, spot, smem=1, limit=16
    )
    chunk = ((PEERS, 16, WIDE), f32)
    first_got = got
    chunks, west = call(
        widen_kernel, [chunk, ((2, TALL, WIDE), f32)], place, got, send, lower, north, smem=1
    )
    west = shift(west, 0, 1)
    late_holder, bands, sides, _ = lax.optimization_barrier((holder, bands, sides, chunks))
    take, coef = call(
        take_kernel,
        [((DEPTH, CHUNK), bf16), ((5, TALL, WIDE), f32)],
        place,
        late_holder,
        smem=1,
    )

    (flag,) = call(
        count_kernel,
        [((8, WIDE), f32)],
        jnp.pad(bands, ((0, 0), (0, 7 * WIDE - ring)), constant_values=-1),
        sides.T,
    )

    def to_blocks(chunks):
        return lax.all_to_all(chunks, "lat", 0, 0, tiled=True)

    def section_one(got):
        return call(
            first_kernel,
            [((PAIRS, MID, WIDE), f32), message],
            place,
            diffusion,
            lower,
            north,
            west,
            got,
            take,
            coef,
            pick,
            mix,
            spin,
            flag,
            smem=2,
            scratch=[pltpu.VMEM((PAIRS, TALL, WIDE), f32), pltpu.VMEM((PAIRS, MID, WIDE), f32)],
        )

    def section_two(middle, got):
        return call(
            second_kernel,
            [(fields.shape, f32), (fields.shape, f32)],
            place,
            diffusion,
            middle,
            got,
            take,
            coef,
            held,
            smem=2,
            scratch=[pltpu.VMEM((PAIRS, MID, WIDE), f32)],
        )

    middle, sent = section_one(to_blocks(chunks))
    got = to_holders(sent)
    crowded = jnp.maximum(got[0, 0, FLAG], got[PEERS, 0, FLAG]) > ROOM
    (chunks,) = call(choice_kernel, [chunk], place, got, send, smem=1)
    fitting = section_two(middle, to_blocks(chunks))

    def with_room():
        def dense(got):
            chunks = call(
                dense_kernel,
                [((PEERS, PLANES, CHUNK), f32)],
                place,
                got,
                holder,
                spot,
                smem=1,
                limit=16,
            )
            return to_blocks(chunks[0]).sum(axis=0)

        middle, sent = section_one(dense(first_got))
        return section_two(middle, dense(to_holders(sent)))

    accumulated, section_three = lax.cond(crowded, with_room, lambda: fitting)
    return (accumulated[None], section_three[None])


def solution(mesh):
    return jax.shard_map(
        shards,
        mesh=mesh,
        in_specs=(
            P("panel", None, None, "lat", "lon"),
            P("panel", "lat", "lon", None),
            P("panel", "lat", "lon", None, None),
            P("panel", "lat", "lon", None),
            P("panel", None),
            P(),
        ),
        out_specs=(P("panel", None, None, "lat", "lon"), P("panel", None, None, "lat", "lon")),
        check_vma=False,
    )
```

```python
import math

import jax
import jax.numpy as jnp
from jax import lax
from jax.experimental import pallas as pl
from jax.experimental.pallas import tpu as pltpu
from jax.sharding import PartitionSpec as P

GAMMA = 5.0 / 3.0
RADIAL_STEP = 0.65 / 32.0
FIELDS = 8
LEVELS = 4
PLANES = FIELDS * LEVELS
PAIRS = PLANES // 2
LOW_LEVEL = (0, 1)
HIGH_LEVEL = (3, 2)
ROWS = 16
COLS = 48
SLOTS = 33
LATS = 16
LONS = 16
ROOM = 63
WIDE = 128
HALF = 64
TALL = ROWS + 16
MID = ROWS + 8
BAND = 4 * HALF
SIDE = 4 * TALL
CHUNK = BAND + SIDE
PEERS = 16
PACKED = 32
MESSAGE = 9 * WIDE
TAIL = 8 * WIDE
FLAG = TAIL + HALF - 1
CHOICE_TILES = PEERS * PACKED // WIDE
CHOICE_DEPTH = (CHOICE_TILES + 1) * WIDE
DEPTH = PEERS * HALF
PANEL_ROWS = ROWS * LATS
PANEL_COLS = COLS * LONS
DTHETA = 0.5 * math.pi / PANEL_ROWS
DPHI = 1.5 * math.pi / PANEL_COLS
FINEST = min(DTHETA, DPHI)
TIME_STEP = 0.1 * FINEST
RADII = [0.35 + 0.65 * (k + 16 - LEVELS // 2 + 0.5) / 32.0 for k in range(LEVELS)]
VMEM = pl.BlockSpec(memory_space=pltpu.VMEM)
SMEM = pl.BlockSpec(memory_space=pltpu.SMEM)
MIB = 1024 * 1024


def iota(shape, axis):
    return lax.broadcasted_iota(jnp.int32, shape, axis)


def column_of(shape):
    return iota(shape, len(shape) - 1) & (HALF - 1)


def turn(value, lanes):
    return pltpu.roll(value, lanes % WIDE, 1) if lanes % WIDE else value


def three_parts(value):
    parts = []
    for _ in range(3):
        part = value.astype(jnp.bfloat16)
        value = value - part.astype(jnp.float32)
        parts.append(part)
    return parts


def donor_message(planes, pick, mix, spin):
    parts = jnp.concatenate(three_parts(planes), axis=1)
    chosen = jnp.dot(parts, pick, preferred_element_type=jnp.float32)
    chosen = chosen.reshape(PAIRS, MID, 2 * WIDE)
    both = jnp.sum(chosen * mix[None], axis=1)
    both = jnp.concatenate([both[:, :WIDE], both[:, WIDE:]], axis=0)
    mixed = both + pltpu.roll(both, HALF, 1)
    cosine = spin[0:1]
    sine = spin[1:2]
    at = (iota((PLANES, WIDE), 0) & (PAIRS - 1)) // 2
    theta = (at == 2) | (at == 5)
    phi = (at == 3) | (at == 6)
    other = jnp.where(theta, pltpu.roll(mixed, PLANES - 2, 0), -pltpu.roll(mixed, 2, 0))
    turned = jnp.where(theta | phi, cosine * mixed + sine * other, mixed)
    return jnp.where(iota((PAIRS, WIDE), 1) < HALF, turned[:PAIRS], turned[PAIRS:])


def post_message(place_ref, packed, flag, out_ref):
    panel = place_ref[0]
    lane = iota((16, WIDE), 1)
    column = lane & (HALF - 1)
    dense = jnp.where(column[:8] < PACKED, packed[:8], turn(packed[8:], PACKED))
    last = jnp.where(
        lane < HALF, packed[:, PACKED : PACKED + 1], packed[:, HALF + PACKED : HALF + PACKED + 1]
    )
    tail = jnp.sum(jnp.where(column == iota((16, WIDE), 0), last, 0.0), axis=0, keepdims=True)
    blank = jnp.where(lane[:1] == FLAG - TAIL, flag, 0.0)
    tail = jnp.where(lane[:1] == FLAG - TAIL, flag, tail)
    zero = jnp.zeros((1, WIDE), jnp.float32)
    for row in range(9):
        full = dense[row : row + 1] if row < 8 else tail
        empty = zero if row < 8 else blank
        at = slice(row * WIDE, (row + 1) * WIDE)
        out_ref[pl.ds((1 - panel) * PEERS, PEERS), :, at] = jnp.broadcast_to(
            full[None], (PEERS, 1, WIDE)
        )
        out_ref[pl.ds(panel * PEERS, PEERS), :, at] = jnp.broadcast_to(
            empty[None], (PEERS, 1, WIDE)
        )


def cut_kernel(state_ref, held_ref, south_ref, east_ref, corner_ref, plane_ref):
    for plane in range(PLANES):
        plane_ref[plane, :, :COLS] = state_ref[plane // LEVELS, plane % LEVELS]
    lane = iota((ROWS, WIDE), 1)
    column = column_of((ROWS, WIDE))
    own = (column >= 8) & (column < 8 + COLS)
    for pair in range(PAIRS):
        field, which = pair // 2, pair % 2
        low = turn(plane_ref[field * LEVELS + LOW_LEVEL[which]], 8)
        high = turn(plane_ref[field * LEVELS + HIGH_LEVEL[which]], HALF + 8)
        tile = jnp.where(own, jnp.where(lane < HALF, low, high), 0.0)
        held_ref[pair] = tile
        south_ref[pair] = tile[:8]
    for group in range(2):
        columns = jnp.zeros((ROWS, WIDE), jnp.float32)
        for which in range(8):
            moved = turn(held_ref[8 * group + which], 8 * which - 8)
            columns = jnp.where(column // 8 == which, moved, columns)
        east_ref[group] = columns
        corner_ref[group] = columns[:8]


def donor_tables(donor_ref, pick_ref, mix_ref, spin_ref, line_ref):
    late = iota((1, WIDE), 1) >= HALF

    def twice(value, fill):
        line_ref[...] = jnp.full((1, WIDE), fill, jnp.float32)
        line_ref[:, :SLOTS] = value
        line = line_ref[...]
        return jnp.where(late, pltpu.roll(line, HALF, 1), line)

    cell = twice(donor_ref[0:1], -10.0 * COLS)
    row_at = jnp.floor((cell + 0.5) * (1.0 / COLS))
    col_at = cell - row_at * COLS + jnp.where(late, 1.0, 0.0)
    upper = jnp.where(late, twice(donor_ref[2:3], 0.0), twice(donor_ref[1:2], 0.0))
    lower = jnp.where(late, twice(donor_ref[4:5], 0.0), twice(donor_ref[3:4], 0.0))
    angle = twice(donor_ref[5:6], 0.0)
    spin_ref[0:1] = jnp.cos(angle)
    spin_ref[1:2] = jnp.sin(angle)
    lane = iota((WIDE, WIDE), 0).astype(jnp.float32)
    real = jnp.where(row_at >= 0, col_at + 8.0, -1000.0)
    low = jnp.where(lane == real, 1.0, 0.0).astype(jnp.bfloat16)
    high = jnp.where(lane == real + HALF, 1.0, 0.0).astype(jnp.bfloat16)
    for part in range(3):
        pick_ref[part * WIDE : (part + 1) * WIDE, :WIDE] = low
        pick_ref[part * WIDE : (part + 1) * WIDE, WIDE:] = high
    row = iota((MID, WIDE), 0).astype(jnp.float32)
    mix = jnp.where(row == row_at, upper, 0.0) + jnp.where(row == row_at + 1.0, lower, 0.0)
    mix_ref[:, :WIDE] = mix
    mix_ref[:, WIDE:] = mix


def count_kernel(bands_ref, sides_ref, flag_ref):
    width = bands_ref.shape[1]
    column = iota((width, WIDE), 0) - 4
    start = iota((width, WIDE), 1) * COLS - 8
    within = (column >= start) & (column < start + 64) & (start < PANEL_COLS)
    columns = jnp.where(within, 1.0, 0.0).astype(jnp.bfloat16)
    row = iota((PANEL_ROWS, WIDE), 0)
    start = iota((PANEL_ROWS, WIDE), 1) * ROWS - 8
    within = (row >= start) & (row < start + TALL) & (start < PANEL_ROWS)
    rows = jnp.where(within, 1.0, 0.0).astype(jnp.bfloat16)

    def most(slots, windows):
        ones = []
        for which in range(LATS):
            first = which * LONS * SLOTS
            inside = (slots >= first) & (slots < first + LONS * SLOTS)
            ones.append(jnp.where(inside, 1.0, 0.0))
        ones = jnp.concatenate(ones, axis=0).astype(jnp.bfloat16)
        counts = jnp.dot(ones, windows, preferred_element_type=jnp.float32)
        return jnp.max(jnp.sum(counts.reshape(2 * LATS, 4, WIDE), axis=1))

    total = most(bands_ref[...], columns) + most(sides_ref[...], rows)
    flag_ref[...] = jnp.full(flag_ref.shape, total, jnp.float32)


def donor_kernel(
    place_ref, held_ref, south_ref, east_ref, corner_ref, pick_ref, mix_ref, spin_ref,
    lower_ref, north_ref, out_ref
):
    column = column_of((ROWS, WIDE))
    beyond = column >= 8 + COLS
    for pair in range(PAIRS):
        group, which = pair // 8, pair % 8
        east = turn(east_ref[group], 8 + COLS - 8 * which)
        corner = turn(corner_ref[group], 8 + COLS - 8 * which)
        lower_ref[pair, :ROWS] = jnp.where(beyond, east, held_ref[pair])
        lower_ref[pair, ROWS:] = jnp.where(beyond[:8], corner, south_ref[pair])
        north_ref[pair] = lower_ref[pair, 8:16]
    planes = lower_ref[...].reshape(PAIRS * MID, WIDE)
    packed = donor_message(planes, pick_ref[...], mix_ref[...], spin_ref[...])
    post_message(place_ref, packed, jnp.zeros((1, WIDE), jnp.float32), out_ref)


def split_parts(held):
    return jnp.concatenate(three_parts(held), axis=0)


def join_parts(terms):
    return terms[:PLANES] + terms[PLANES : 2 * PLANES] + terms[2 * PLANES :]


def from_row(place_ref, got_ref):
    base = (1 - place_ref[0]) * PEERS
    part = iota((8, WIDE), 1) // PACKED
    tiles = []
    tails = []
    for tile in range(CHOICE_TILES):
        rows = [jnp.zeros((8, WIDE), jnp.float32)] * 4
        for which in range(4):
            at = base + 4 * tile + which
            message = jnp.concatenate(
                [got_ref[at, :, row * WIDE : (row + 1) * WIDE] for row in range(8)], axis=0
            )
            tails.append(got_ref[at, :, TAIL:])
            for group in range(4):
                moved = turn(message, PACKED * (which - group))
                rows[group] = jnp.where(part == which, moved, rows[group])
        tiles.append(jnp.concatenate(rows, axis=0))
    tails.append(jnp.zeros((WIDE - PEERS, WIDE), jnp.float32))
    tails = jnp.concatenate(tails, axis=0).T
    tiles.append(jnp.concatenate([tails[:PAIRS], tails[HALF : HALF + PAIRS]], axis=0))
    return split_parts(jnp.concatenate(tiles, axis=1))


def rank_of(chosen):
    order = iota((CHUNK, CHUNK), 0) < iota((CHUNK, CHUNK), 1)
    order = jnp.where(order, 1.0, 0.0).astype(jnp.bfloat16)
    ones = jnp.where(chosen, 1.0, 0.0).astype(jnp.bfloat16)
    return jnp.dot(ones, order, preferred_element_type=jnp.float32)


def send_kernel(place_ref, holder_ref, spot_ref, send_ref):
    mine = holder_ref[...] == place_ref[1]
    spot = spot_ref[...].astype(jnp.float32)
    rank = rank_of(mine)
    key = jnp.where(mine & (rank < ROOM), rank, -1.0)
    place_at = iota((HALF, CHUNK), 0).astype(jnp.float32)
    eye = iota((WIDE, WIDE), 0) == iota((WIDE, WIDE), 1)
    depth = iota((CHOICE_DEPTH, WIDE), 0).astype(jnp.float32) + 1.0
    for pair in range(LATS // 2):
        tables = []
        for block in (2 * pair, 2 * pair + 1):
            found = place_at == key[block : block + 1]
            tables.append(
                jnp.sum(jnp.where(found, spot[block : block + 1] + 1.0, 0.0), axis=1, keepdims=True)
            )
        table = jnp.concatenate(tables, axis=0)
        line = jnp.sum(jnp.where(eye, table, 0.0), axis=0, keepdims=True)
        hot = jnp.where(depth == line, 1.0, 0.0).astype(jnp.bfloat16)
        send_ref[:, pair * WIDE : (pair + 1) * WIDE] = hot


def take_kernel(place_ref, holder_ref, take_ref, coef_ref):
    lat = place_ref[1]
    own = holder_ref[pl.ds(lat, 1)]
    masks = iota((PEERS, CHUNK), 0) == own
    rank = jnp.sum(jnp.where(masks, rank_of(masks), 0.0), axis=0, keepdims=True)
    fits = (own >= 0) & (rank < ROOM)
    index = jnp.where(fits, own.astype(jnp.float32) * HALF + rank, -1.0)
    hot = iota((DEPTH, CHUNK), 0).astype(jnp.float32) == index
    take_ref[...] = jnp.where(hot, 1.0, 0.0).astype(jnp.bfloat16)
    row = (lat * ROWS - 8 + iota((TALL, WIDE), 0)).astype(jnp.float32)
    column = (place_ref[2] * COLS - 8 + column_of((TALL, WIDE))).astype(jnp.float32)
    colatitude = 0.25 * math.pi + (row + 0.5) * DTHETA
    longitude = -0.75 * math.pi + (column + 0.5) * DPHI
    sine, cosine = jnp.sin(colatitude), jnp.cos(colatitude)
    twirl = 2.0 * 0.25 / TIME_STEP
    yang = place_ref[0] == 1
    coef_ref[0] = sine
    coef_ref[1] = 1.0 / sine
    coef_ref[2] = twirl * jnp.where(yang, sine * jnp.sin(longitude), cosine)
    coef_ref[3] = twirl * jnp.where(yang, cosine * jnp.sin(longitude), -sine)
    coef_ref[4] = twirl * jnp.where(yang, jnp.cos(longitude), 0.0)


def widen_kernel(place_ref, got_ref, send_ref, lower_ref, north_ref, out_ref, west_ref):
    column = column_of((TALL, WIDE))
    for group in range(2):
        columns = jnp.zeros((TALL, WIDE), jnp.float32)
        for which in range(8):
            pair = 8 * group + which
            rows = jnp.concatenate([north_ref[pair], lower_ref[pair]], axis=0)
            moved = turn(rows, 8 * which - COLS)
            columns = jnp.where(column // 8 == which, moved, columns)
        west_ref[group] = columns
    choice_kernel(place_ref, got_ref, send_ref, out_ref)


def choice_kernel(place_ref, got_ref, send_ref, out_ref):
    parts = from_row(place_ref, got_ref)
    terms = jnp.dot(parts, send_ref[...], preferred_element_type=jnp.float32)
    chosen = join_parts(terms)
    low = iota((16, WIDE), 1) < HALF
    for pair in range(PEERS // 2):
        tile = chosen[:, pair * WIDE : (pair + 1) * WIDE]
        top, end = tile[:16], tile[16:]
        out_ref[2 * pair] = jnp.where(low, top, pltpu.roll(end, HALF, 1))
        out_ref[2 * pair + 1] = jnp.where(low, pltpu.roll(top, HALF, 1), end)


def dense_kernel(place_ref, got_ref, holder_ref, spot_ref, out_ref):
    parts = from_row(place_ref, got_ref)
    index = jnp.where(holder_ref[...] == place_ref[1], spot_ref[...], -1)
    at = iota((CHOICE_DEPTH, CHUNK), 0)
    for block in range(LATS):
        hot = jnp.where(at == index[block : block + 1], 1.0, 0.0).astype(jnp.bfloat16)
        out_ref[block] = join_parts(jnp.dot(parts, hot, preferred_element_type=jnp.float32))


def ghost_values(got_ref, take_ref):
    if len(got_ref.shape) == 2:
        return got_ref[...]
    low = iota((16, WIDE), 1) < HALF
    tiles = []
    for pair in range(PEERS // 2):
        one = got_ref[2 * pair]
        two = got_ref[2 * pair + 1]
        top = jnp.where(low, one, pltpu.roll(two, HALF, 1))
        end = jnp.where(low, pltpu.roll(one, HALF, 1), two)
        tiles.append(jnp.concatenate([top, end], axis=0))
    parts = split_parts(jnp.concatenate(tiles, axis=1))
    return join_parts(jnp.dot(parts, take_ref[...], preferred_element_type=jnp.float32))


def fill_ghosts(place_ref, ghosts, work_ref, rows):
    lat, lon = place_ref[1], place_ref[2]
    trim = (TALL - rows) // 2
    top = 8 - trim
    half = PLANES // 2

    @pl.when((lon == 0) | (lon == LONS - 1))
    def _():
        side = ghosts[:, BAND:]
        first = jnp.where(lon == 0, 4, 8 + COLS)
        own = iota((rows, WIDE), 1) // 4 == iota((rows, WIDE), 0) + trim

        def spread(part):
            part = part.astype(jnp.float32)[:, None, :]
            return jnp.where(own[None], part, 0.0).astype(jnp.bfloat16).reshape(PAIRS * rows, WIDE)

        pieces = []
        for part in three_parts(side):
            pieces += [spread(part[:half]), spread(part[half:])]
        both = jnp.concatenate(pieces, axis=1)
        source = iota((6 * WIDE, WIDE), 0)
        target = first + (source & 3) + jnp.where((source & WIDE) != 0, HALF, 0)
        hot = jnp.where(target == iota((6 * WIDE, WIDE), 1), 1.0, 0.0).astype(jnp.bfloat16)
        moved = jnp.dot(both, hot, preferred_element_type=jnp.float32)
        moved = moved.reshape(PAIRS, rows, WIDE)
        column = column_of((rows, WIDE))
        ghost = (column >= first) & (column < first + 4)
        work_ref[...] = jnp.where(ghost[None], moved, work_ref[...])

    @pl.when((lat == 0) | (lat == LATS - 1))
    def _():
        low = iota((half, WIDE), 1) < HALF
        lines = []
        for which in range(2):
            piece = ghosts[:, which * WIDE : (which + 1) * WIDE]
            one, two = piece[:half], piece[half:]
            lines.append(jnp.where(low, one, pltpu.roll(two, HALF, 1)))
            lines.append(jnp.where(low, pltpu.roll(one, HALF, 1), two))

        def put(first):
            tile = first // 8 * 8
            row = iota((8, WIDE), 0)
            held = work_ref[:, tile : tile + 8, :]
            for which in range(4):
                mask = row == first - tile + which
                held = jnp.where(mask[None], lines[which][:, None, :], held)
            work_ref[:, tile : tile + 8, :] = held

        @pl.when(lat == 0)
        def _():
            put(top - 4)

        @pl.when(lat == LATS - 1)
        def _():
            put(top + ROWS)


def rates(load, rows, coef_ref, diffusion_ref):
    low = iota((rows, WIDE), 1) < HALF

    def levels(values):
        halves = [
            jnp.where(low, values[LOW_LEVEL[k]], values[HIGH_LEVEL[k]]).astype(jnp.float32)
            for k in range(2)
        ]
        return jnp.concatenate(halves, axis=0)

    def whole(which):
        value = coef_ref[which]
        if rows < TALL:
            value = pltpu.roll(value, TALL - (TALL - rows) // 2, 0)[:rows]
        return jnp.concatenate([value] * 2, axis=0)

    sine = whole(0)
    per_sine = whole(1)
    radius = levels(RADII)
    inverse = levels([1.0 / r for r in RADII])
    square = levels([r * r for r in RADII])
    per_square = levels([1.0 / (r * r) for r in RADII])
    sign = jnp.where(low, 1.0, -1.0)
    ends = sign * (1.0 / RADIAL_STEP)
    inner = sign * (1.0 / (2.0 * RADIAL_STEP))
    viscosity = diffusion_ref[0] * (FINEST * FINEST / TIME_STEP)
    resistivity = diffusion_ref[1] * (FINEST * FINEST / TIME_STEP)

    def slope(value, axis, step):
        size = value.shape[axis]
        near = pltpu.roll(value, size - 1, axis) - pltpu.roll(value, 1, axis)
        far = pltpu.roll(value, size - 2, axis) - pltpu.roll(value, 2, axis)
        return near * (8.0 / (12.0 * step)) - far * (1.0 / (12.0 * step))

    def d_theta(value):
        return slope(value, 0, DTHETA)

    def d_phi(value):
        return slope(value, 1, DPHI)

    def d_radius(value):
        one, two = value[:rows], value[rows:]
        return jnp.concatenate(
            [(two - one) * ends, (pltpu.roll(two, HALF, 1) - one) * inner], axis=0
        )

    def by_radius(value):
        return value * radius

    def per_radius(value):
        return value * inverse

    def curl(vector):
        part_r, part_t, part_p = vector
        return (
            per_radius((d_theta(sine * part_p) - d_phi(part_t)) * per_sine),
            per_radius(d_phi(part_r) * per_sine - d_radius(by_radius(part_p))),
            per_radius(d_radius(by_radius(part_t)) - d_theta(part_r)),
        )

    def gradient(value):
        return (
            d_radius(value),
            per_radius(d_theta(value)),
            per_radius(d_phi(value) * per_sine),
        )

    def cross(left, right):
        return (
            left[1] * right[2] - left[2] * right[1],
            left[2] * right[0] - left[0] * right[2],
            left[0] * right[1] - left[1] * right[0],
        )

    def advect(vector, slopes):
        return vector[0] * slopes[0] + vector[1] * slopes[1] + vector[2] * slopes[2]

    velocity = [load(which) for which in (1, 2, 3)]
    magnetic = [load(which) for which in (4, 5, 6)]
    vorticity = curl(velocity)
    current = curl(magnetic)
    spread = d_radius(square * velocity[0]) * per_square + per_radius(
        (d_theta(sine * velocity[1]) + d_phi(velocity[2])) * per_sine
    )
    induced = cross(velocity, magnetic)
    electric = [induced[k] - resistivity * current[k] for k in range(3)]
    kinetic = 0.5 * (
        velocity[0] * velocity[0] + velocity[1] * velocity[1] + velocity[2] * velocity[2]
    )
    curl_electric = curl(electric)
    log_rho = load(0)
    rho_rate = -advect(velocity, gradient(log_rho)) - spread
    pressure = load(7)
    slope_pressure = gradient(pressure)
    pressure_rate = -advect(velocity, slope_pressure) - GAMMA * pressure * spread
    lorentz = cross(current, magnetic)
    per_rho = jnp.exp(-log_rho)
    slope_kinetic = gradient(kinetic)
    curl_vorticity = curl(vorticity)
    lamb = cross(velocity, vorticity)
    turning = cross((whole(2), whole(3), whole(4)), velocity)
    momentum = [
        lamb[k]
        - slope_kinetic[k]
        + per_rho * (lorentz[k] - slope_pressure[k])
        - turning[k]
        - viscosity * curl_vorticity[k]
        for k in range(3)
    ]
    return [rho_rate, *momentum, *curl_electric, pressure_rate]


def first_kernel(
    place_ref,
    diffusion_ref,
    lower_ref,
    north_ref,
    west_ref,
    got_ref,
    take_ref,
    coef_ref,
    pick_ref,
    mix_ref,
    spin_ref,
    flag_ref,
    middle_ref,
    out_ref,
    work_ref,
    next_ref,
):
    column = column_of((TALL, WIDE))
    for pair in range(PAIRS):
        group, which = pair // 8, pair % 8
        west = turn(west_ref[group], -8 * which)
        rows = jnp.concatenate([north_ref[pair], lower_ref[pair]], axis=0)
        work_ref[pair] = jnp.where(column < 8, west, rows)
    ghosts = ghost_values(got_ref, take_ref)
    fill_ghosts(place_ref, ghosts, work_ref, TALL)

    def load(which):
        return work_ref[2 * which : 2 * which + 2].reshape(2 * TALL, WIDE)

    found = rates(load, TALL, coef_ref, diffusion_ref)
    row = iota((TALL, WIDE), 0)
    inside = (column >= 4) & (column < 12 + COLS) & (row >= 4) & (row < 12 + ROWS)
    for which in range(FIELDS):
        value = load(which) + (0.5 * TIME_STEP) * found[which]
        for half in range(2):
            part = jnp.where(inside, value[half * TALL : (half + 1) * TALL], 0.0)
            next_ref[2 * which + half] = part[8:]
            middle_ref[2 * which + half] = pltpu.roll(part, TALL - 4, 0)[:MID]
    planes = next_ref[...].reshape(PAIRS * MID, WIDE)
    packed = donor_message(planes, pick_ref[...], mix_ref[...], spin_ref[...])
    post_message(place_ref, packed, flag_ref[0:1], out_ref)


def second_kernel(
    place_ref,
    diffusion_ref,
    middle_ref,
    got_ref,
    take_ref,
    coef_ref,
    held_ref,
    whole_ref,
    third_ref,
    work_ref,
):
    work_ref[...] = middle_ref[...]
    ghosts = ghost_values(got_ref, take_ref)
    fill_ghosts(place_ref, ghosts, work_ref, MID)

    def load(which):
        return work_ref[2 * which : 2 * which + 2].reshape(2 * MID, WIDE)

    found = rates(load, MID, coef_ref, diffusion_ref)

    def centre(value):
        return pltpu.roll(value, MID - 4, 0)[:ROWS]

    def place(out_ref, pair, value):
        field, half = pair // 2, pair % 2
        out_ref[field, LOW_LEVEL[half]] = turn(value, -8)[:, :COLS]
        out_ref[field, HIGH_LEVEL[half]] = turn(value, -8 - HALF)[:, :COLS]

    for pair in range(PAIRS):
        field, half = pair // 2, pair % 2
        rate = found[field][half * MID : (half + 1) * MID]
        held = held_ref[pair]
        step = centre(rate) * (0.5 * TIME_STEP)
        middle = centre(middle_ref[pair])
        place(third_ref, pair, held + step)
        place(whole_ref, pair, held + ((middle - held) + 2.0 * step) * (1.0 / 3.0))


def shift(value, move_lat, move_lon):
    pairs = []
    for a in range(LATS):
        for b in range(LONS):
            goal_a, goal_b = a + move_lat, b + move_lon
            if 0 <= goal_a < LATS and 0 <= goal_b < LONS:
                pairs.append((a * LONS + b, goal_a * LONS + goal_b))
    return lax.ppermute(value, ("lat", "lon"), pairs)


def shards(state, donor_cell, donor_weights, donor_turn, border_source, diffusion):
    fields = state[0]
    panel = lax.axis_index("panel")
    lat = lax.axis_index("lat")
    lon = lax.axis_index("lon")
    place = jnp.stack([panel, lat, lon]).astype(jnp.int32)
    f32 = jnp.float32

    def call(kernel, outs, *args, smem=0, specs=None, scratch=(), limit=10):
        shapes = [jax.ShapeDtypeStruct(shape, dtype) for shape, dtype in outs]
        return pl.pallas_call(
            kernel,
            out_shape=shapes,
            in_specs=specs or [SMEM] * smem + [VMEM] * (len(args) - smem),
            out_specs=[VMEM] * len(outs),
            scratch_shapes=scratch,
            compiler_params=pltpu.CompilerParams(vmem_limit_bytes=limit * MIB),
        )(*args)

    bf16 = jnp.bfloat16
    held, south, east, corner = call(
        cut_kernel,
        [
            ((PAIRS, ROWS, WIDE), f32),
            ((PAIRS, 8, WIDE), f32),
            ((2, ROWS, WIDE), f32),
            ((2, 8, WIDE), f32),
        ],
        fields,
        scratch=[pltpu.VMEM((PLANES, ROWS, WIDE), f32)],
    )
    east = shift(east, 0, -1)
    south = shift(south, -1, 0)
    corner = shift(corner, -1, -1)

    donor = jnp.concatenate(
        [donor_cell[0, 0].astype(f32), donor_weights[0, 0, 0], donor_turn[0, 0]], axis=0
    )
    pick, mix, spin = call(
        donor_tables,
        [((3 * WIDE, 2 * WIDE), bf16), ((MID, 2 * WIDE), f32), ((2, WIDE), f32)],
        donor,
        scratch=[pltpu.VMEM((1, WIDE), f32)],
    )
    message = ((2 * PEERS, 1, MESSAGE), f32)
    lower, north, sent = call(
        donor_kernel,
        [((PAIRS, MID, WIDE), f32), ((PAIRS, 8, WIDE), f32), message],
        place,
        held,
        south,
        east,
        corner,
        pick,
        mix,
        spin,
        smem=1,
    )

    def to_holders(sent):
        return lax.all_to_all(sent, ("panel", "lon"), 0, 0, tiled=True)

    got = to_holders(sent)

    north, late_lat, late_lon, border, _ = lax.optimization_barrier(
        (north, lat, lon, border_source, sent)
    )
    border = lax.optimization_barrier(border[0])
    north = shift(north, 1, 0)

    ring = PANEL_COLS + 8
    row_slots = LONS * SLOTS
    bands = border[: 8 * ring].reshape(8, ring)
    sides = border[8 * ring :].reshape(PANEL_ROWS, 8)
    window = jnp.pad(bands, ((0, 0), (4, 4)), constant_values=-1)
    window = lax.dynamic_slice(window, (0, late_lon * COLS), (8, 64)).reshape(2, BAND)
    side = jnp.where(late_lon == 0, sides[:, :4], sides[:, 4:])
    side = jnp.where((late_lon == 0) | (late_lon == LONS - 1), side, -1)
    side = jnp.pad(side, ((8, 8), (0, 0)), constant_values=-1)
    side = jnp.concatenate(
        [
            side[:PANEL_ROWS].reshape(LATS, ROWS, 4),
            side[ROWS:].reshape(LATS, ROWS, 4),
        ],
        axis=1,
    ).reshape(LATS, SIDE)
    at_lat = jnp.arange(LATS)[:, None]
    band = jnp.where(at_lat == 0, window[:1], jnp.where(at_lat == LATS - 1, window[1:], -1))
    wanted = jnp.concatenate([band, side], axis=1)
    holder = jnp.where(wanted >= 0, wanted // row_slots, -1)
    local = wanted - late_lat * row_slots
    block = local // SLOTS
    slot = local % SLOTS
    spot = jnp.where(slot < PACKED, block * PACKED + slot, PEERS * PACKED + block)
    (send,) = call(
        send_kernel, [((CHOICE_DEPTH, DEPTH), bf16)], place, holder, spot, smem=1, limit=16
    )
    chunk = ((PEERS, 16, WIDE), f32)
    first_got = got
    chunks, west = call(
        widen_kernel, [chunk, ((2, TALL, WIDE), f32)], place, got, send, lower, north, smem=1
    )
    west = shift(west, 0, 1)
    late_holder, bands, sides, _ = lax.optimization_barrier((holder, bands, sides, chunks))
    take, coef = call(
        take_kernel,
        [((DEPTH, CHUNK), bf16), ((5, TALL, WIDE), f32)],
        place,
        late_holder,
        smem=1,
    )

    (flag,) = call(
        count_kernel,
        [((8, WIDE), f32)],
        jnp.pad(bands, ((0, 0), (0, 7 * WIDE - ring)), constant_values=-1),
        sides.T,
    )

    def to_blocks(chunks):
        return lax.all_to_all(chunks, "lat", 0, 0, tiled=True)

    def section_one(got):
        return call(
            first_kernel,
            [((PAIRS, MID, WIDE), f32), message],
            place,
            diffusion,
            lower,
            north,
            west,
            got,
            take,
            coef,
            pick,
            mix,
            spin,
            flag,
            smem=2,
            scratch=[pltpu.VMEM((PAIRS, TALL, WIDE), f32), pltpu.VMEM((PAIRS, MID, WIDE), f32)],
        )

    def section_two(middle, got):
        return call(
            second_kernel,
            [(fields.shape, f32), (fields.shape, f32)],
            place,
            diffusion,
            middle,
            got,
            take,
            coef,
            held,
            smem=2,
            scratch=[pltpu.VMEM((PAIRS, MID, WIDE), f32)],
        )

    middle, sent = section_one(to_blocks(chunks))
    got = to_holders(sent)
    crowded = jnp.maximum(got[0, 0, FLAG], got[PEERS, 0, FLAG]) > ROOM
    (chunks,) = call(choice_kernel, [chunk], place, got, send, smem=1)
    fitting = section_two(middle, to_blocks(chunks))

    def with_room():
        def dense(got):
            chunks = call(
                dense_kernel,
                [((PEERS, PLANES, CHUNK), f32)],
                place,
                got,
                holder,
                spot,
                smem=1,
                limit=16,
            )
            return to_blocks(chunks[0]).sum(axis=0)

        middle, sent = section_one(dense(first_got))
        return section_two(middle, dense(to_holders(sent)))

    accumulated, section_three = lax.cond(crowded, with_room, lambda: fitting)
    return (accumulated[None], section_three[None])


def solution(mesh):
    return jax.shard_map(
        shards,
        mesh=mesh,
        in_specs=(
            P("panel", None, None, "lat", "lon"),
            P("panel", "lat", "lon", None),
            P("panel", "lat", "lon", None, None),
            P("panel", "lat", "lon", None),
            P("panel", None),
            P(),
        ),
        out_specs=(P("panel", None, None, "lat", "lon"), P("panel", None, None, "lat", "lon")),
        check_vma=False,
    )
```
